32 devices in a mesh: lon: 8 (over y, x, core), dep: 4 (over z).
Axes of the slice: x: 2, y: 2, z: 4, core: 2. Of those that a mesh axis runs over, the one named last changes fastest.
Arguments:
- tracers: float32 [2, 80, 64, 1024], P(None, 'dep', None, 'lon'), may hold values from -6 to 6
- u_east: float32 [80, 64, 1024], P('dep', None, 'lon'), may hold values from -0.24 to 0.24
- v_north: float32 [80, 64, 1024], P('dep', None, 'lon'), may hold values from -0.24 to 0.24
- kappa_h: float32 [80, 64, 1024], P('dep', None, 'lon'), may hold values from 0.05 to 0.25
- kappa_v: float32 [80, 64, 1024], P('dep', None, 'lon'), may hold values from 0.3 to 300
- bottom: int32 [64, 1024], P(None, 'lon'), may hold values from 0 to 80
Outputs:
- tracers_out: float32 [2, 80, 64, 1024], P(None, 'dep', None, 'lon')
The draws below stay inside these ranges and needn't reach their ends.
Inputs may be any that keep to these rules, and one draw needn't show every extreme that they name: Levels from bottom down are land; a column with 0 is all land.
All inputs are finite; a program needn't handle non-finite values.
Results may differ from the reference program's by a relative error of at most 0.0003.
Values sent between devices are 32-bit elements; how exact they have to be, the bound alone decides.
No kernel may reach another device: no remote copies, remote signals or barrier semaphores. Data moves between devices by JAX's collectives and lax.ppermute only.
A program may use at most 128 MiB of HBM per device.

```python
import math
import jax
import jax.numpy as jnp
from jax import lax

LAT = 64
SUB = 4
NLON = 1024
NLEV = 80


def with_ends(drawn, key, low, largest):
    dims = drawn.shape
    place = [jax.random.randint(jax.random.fold_in(key, axis), (), 0, dims[axis]) for axis in range(len(dims))]
    drawn = drawn.at[tuple(place)].set(low)
    longest = dims.index(max(dims))
    place[longest] = (place[longest] + 1) % dims[longest]
    return drawn.at[tuple(place)].set(largest)


def block_scale(stream_key, dims, cuts, least, largest):
    gain = 1.0
    for axis_at, blocks in cuts:
        steps = jax.random.uniform(jax.random.fold_in(jax.random.fold_in(stream_key, 6), axis_at), (blocks,), jnp.float32, least / len(cuts), largest / len(cuts))
        gain = gain * jnp.repeat(jnp.exp(steps), dims[axis_at] // blocks).reshape((-1,) + (1,) * (len(dims) - 1 - axis_at))
    return gain


def centred(key, extent, width, reach, split=(), kind=jnp.bfloat16):
    loudness = block_scale(key, extent, split, -0.22, 0.18) if split else 1.0
    values = jax.random.normal(key, extent, jnp.float32) * width * loudness
    return jnp.minimum(jnp.maximum(values, -reach), reach).astype(kind)


def setup_inputs(seed: int = 0) -> dict:
    seeds = jax.random.split(jax.random.key(seed), 7)
    return {
        "tracers": centred(seeds[0], (2, NLEV, LAT, NLON), 1.0, 6.0, ((1, 4), (3, 8)), jnp.float32),
        "u_east": jnp.clip(jax.random.uniform(seeds[1], (NLEV, LAT, NLON), jnp.float32, -0.24, 0.24) * block_scale(seeds[1], (NLEV, LAT, NLON), ((0, 4), (2, 8)), -0.4, 0.0), -0.24, 0.24),
        "v_north": jnp.clip(jax.random.uniform(seeds[2], (NLEV, LAT, NLON), jnp.float32, -0.24, 0.24) * block_scale(seeds[2], (NLEV, LAT, NLON), ((0, 4), (2, 8)), -0.4, 0.0), -0.24, 0.24),
        "kappa_h": jnp.clip(jnp.exp(math.log(0.25) - 1.609438 * jax.random.uniform(seeds[3], (NLEV, LAT, NLON), jnp.float32) ** block_scale(seeds[3], (NLEV, LAT, NLON), ((0, 4), (2, 8)), -0.2, 0.2)), 0.05, 0.25),
        "kappa_v": jnp.clip(jnp.exp(math.log(300.0) - 6.9077552 * jax.random.uniform(seeds[4], (NLEV, LAT, NLON), jnp.float32) ** block_scale(seeds[4], (NLEV, LAT, NLON), ((0, 4), (2, 8)), -0.2, 0.2)), 0.3, 300.0),
        "bottom": with_ends(jax.random.randint(seeds[5], (LAT, NLON), 0, NLEV + 1), jax.random.fold_in(seeds[5], 1), 0, NLEV).astype(jnp.int32),
    }


thermal_coef = 0.2
haline_coef = 0.8


def wrap_lon(field, margin):
    return jnp.concatenate([field[..., -margin:], field, field[..., :margin]], axis=-1)


def shift_north(field):
    return jnp.concatenate([field[..., 1:, :], jnp.zeros_like(field[..., :1, :])], axis=-2)


def shift_south(field):
    return jnp.concatenate([jnp.zeros_like(field[..., :1, :]), field[..., :-1, :]], axis=-2)


def upwind_step(tracer_ext, zonal_ext, merid_mid, wet_ext):
    face_wet = wet_ext[..., :-1] * wet_ext[..., 1:]
    zonal_face = zonal_ext[..., :-1]
    flux_all = face_wet * (jnp.maximum(zonal_face, 0.0) * tracer_ext[..., :-1] + jnp.minimum(zonal_face, 0.0) * tracer_ext[..., 1:])
    flux_east = flux_all[..., 1:]
    flux_west = flux_all[..., :-1]
    middle = tracer_ext[..., 1:-1]
    wet_mid = wet_ext[..., 1:-1]
    wet_north = wet_mid * shift_north(wet_mid)
    flux_north = wet_north * (jnp.maximum(merid_mid, 0.0) * middle + jnp.minimum(merid_mid, 0.0) * shift_north(middle))
    return middle - (flux_east - flux_west) - (flux_north - shift_south(flux_north))


def lon_diff(field):
    return 0.5 * (field[..., 2:] - field[..., :-2])


def lev_diff(field):
    return 0.5 * (field[..., 2:, :, :] - field[..., :-2, :, :])


def lat_diff(field):
    padded = jnp.concatenate([jnp.zeros_like(field[..., :1, :]), field, jnp.zeros_like(field[..., :1, :])], axis=-2)
    return 0.5 * (padded[..., 2:, :] - padded[..., :-2, :])


def isoneutral(tracer_ext, kappa_ext, wet_ext):
    mask_x = wet_ext[1:-1, :, 2:] * wet_ext[1:-1, :, :-2]
    mask_z = wet_ext[2:, :, 1:-1] * wet_ext[:-2, :, 1:-1]
    wet_pad = jnp.concatenate([jnp.zeros_like(wet_ext[:, :1, :]), wet_ext, jnp.zeros_like(wet_ext[:, :1, :])], axis=1)
    mask_y = (wet_pad[:, 2:, :] * wet_pad[:, :-2, :])[1:-1, :, 1:-1]
    grad_x = lon_diff(tracer_ext)[:, 1:-1] * mask_x
    grad_y = lat_diff(tracer_ext)[:, 1:-1, :, 1:-1] * mask_y
    grad_z = lev_diff(tracer_ext)[..., 1:-1] * mask_z
    dens_x = -thermal_coef * grad_x[0] + haline_coef * grad_x[1]
    dens_y = -thermal_coef * grad_y[0] + haline_coef * grad_y[1]
    dens_z = -thermal_coef * grad_z[0] + haline_coef * grad_z[1]
    denominator = 1.0 + dens_x * dens_x + dens_y * dens_y + dens_z * dens_z
    slope_x = dens_x * dens_z / denominator
    slope_y = dens_y * dens_z / denominator
    kappa_mid = kappa_ext[1:-1, :, 1:-1] * wet_ext[1:-1, :, 1:-1]
    flux_x = kappa_mid * (grad_x + slope_x * grad_z)
    flux_y = kappa_mid * (grad_y + slope_y * grad_z)
    flux_z = kappa_mid * (slope_x * grad_x + slope_y * grad_y + (slope_x * slope_x + slope_y * slope_y) * grad_z)
    tendency = lon_diff(flux_x)[:, 1:-1] + lat_diff(flux_y)[:, 1:-1, :, 1:-1] + lev_diff(flux_z)[..., 1:-1]
    return tracer_ext[:, 2:-2, :, 2:-2] + tendency * wet_ext[2:-2, :, 2:-2]


def forward_sweep(right_side, e_top, e_low, start_ratio, start_value):
    def advance(carry, level):
        ratio, value = carry
        source_k, top_k, low_k = level
        denominator = 1.0 + top_k + low_k + top_k * ratio
        new_ratio = -low_k / denominator
        new_value = (source_k + top_k * value) / denominator
        return (new_ratio, new_value), (new_ratio, new_value)
    return lax.scan(advance, (start_ratio, start_value), (right_side, e_top, e_low))


def back_sweep(ratios, values, start):
    def advance(below, level):
        ratio, value = level
        here = value - ratio * below
        return here, here
    _, result = lax.scan(advance, start, (ratios, values), reverse=True)
    return result


def column_solve(tracer, e_top):
    e_low = jnp.concatenate([e_top[1:], jnp.zeros_like(e_top[:1])], axis=0)
    right_side = jnp.moveaxis(tracer, 1, 0)
    start_ratio = jnp.zeros(e_top.shape[1:], jnp.float32)
    start_value = jnp.zeros(right_side.shape[1:], jnp.float32)
    _, (ratios, values) = forward_sweep(right_side, e_top, e_low, start_ratio, start_value)
    result = back_sweep(ratios, values, start_value)
    return jnp.moveaxis(result, 0, 1)


def reference(tracers, u_east, v_north, kappa_h, kappa_v, bottom):
    level_ids = jnp.arange(NLEV, dtype=jnp.int32)[:, None, None]
    wet = (level_ids < bottom[None]).astype(jnp.float32)
    tracer_now = tracers
    wet_cycle = wrap_lon(wet, 1)
    zonal_cycle = wrap_lon(u_east, 1)
    for substep in range(SUB):
        tracer_now = upwind_step(wrap_lon(tracer_now, 1), zonal_cycle, v_north, wet_cycle)
    tracer_ext = jnp.pad(wrap_lon(tracer_now, 2), ((0, 0), (2, 2), (0, 0), (0, 0)))
    kappa_ext = jnp.pad(wrap_lon(kappa_h, 2), ((2, 2), (0, 0), (0, 0)))
    wet_ext = jnp.pad(wrap_lon(wet, 2), ((2, 2), (0, 0), (0, 0)))
    tracer_now = isoneutral(tracer_ext, kappa_ext, wet_ext)
    e_top = kappa_v * ((level_ids >= 1) & (level_ids < bottom[None])).astype(jnp.float32)
    return column_solve(tracer_now, e_top)
```

```python
import functools

import jax
import jax.numpy as jnp
from jax import lax
from jax.experimental import pallas as pl
from jax.experimental.pallas import tpu as pltpu
from jax.sharding import PartitionSpec as P

SUB = 4
THERMAL = 0.2
HALINE = 0.8
GROUPS = 4
STRIP = 32
CHUNK = 16
PAD = 8
HUGE = 1e30
MIB = 1024 * 1024

VMEM = pl.BlockSpec(memory_space=pltpu.VMEM)


def lane_ids(rows):
    return lax.broadcasted_iota(jnp.int32, (rows, 128), 1)


def roll_lanes(x, amount):
    amount = amount % 128
    return x if amount == 0 else pltpu.roll(x, amount, 1)


def call(body, out_shape, scratch, args, flops, in_bytes, limit):
    return pl.pallas_call(
        body,
        out_shape=out_shape,
        in_specs=[VMEM] * len(args),
        out_specs=jax.tree.map(lambda _: VMEM, out_shape),
        scratch_shapes=scratch,
        compiler_params=pltpu.CompilerParams(vmem_limit_bytes=limit * MIB),
        cost_estimate=pl.CostEstimate(flops=flops, bytes_accessed=in_bytes, transcendentals=0),
    )(*args)


def f32(*shape):
    return jax.ShapeDtypeStruct(shape, jnp.float32)


def pack_kernel(t_ref, u_ref, v_ref, kh_ref, b_ref, sw_ref, se_ref):
    rows_e = t_ref.shape[1] // GROUPS
    lat = t_ref.shape[2]
    lane = lane_ids(lat)

    def body(r, _):
        low = jnp.zeros((lat, 128), jnp.float32)
        high = jnp.zeros((lat, 128), jnp.float32)
        for g in range(GROUPS):
            level = g * rows_e + r
            slabs = (t_ref[0, level], t_ref[1, level], u_ref[level], v_ref[level])
            for f, slab in enumerate(slabs):
                start = STRIP * g + 8 * f
                rolled = roll_lanes(slab, start)
                low = jnp.where(lane >= start, rolled, low)
                if start == 0:
                    first = rolled
                else:
                    high = jnp.where(lane >= start - 8, rolled, high)
        sw_ref[r] = low
        se_ref[r] = jnp.where(lane >= 120, first, high)
        return 0

    lax.fori_loop(0, rows_e, body, 0)
    low = jnp.zeros((lat, 128), jnp.float32)
    high = jnp.zeros((lat, 128), jnp.float32)
    bottom = b_ref[...].astype(jnp.float32)
    for g in range(GROUPS):
        for r in range(rows_e):
            place = STRIP * g + r
            rolled = roll_lanes(kh_ref[g * rows_e + r], place)
            low = jnp.where(lane == place, rolled, low)
            high = jnp.where(lane == (place - 1) % 128, rolled, high)
        place = STRIP * g + 16
        rolled = roll_lanes(bottom, place)
        low = jnp.where((lane >= place) & (lane < place + 8), rolled, low)
        high = jnp.where((lane >= place - 8) & (lane < place), rolled, high)
    sw_ref[rows_e] = low
    se_ref[rows_e] = high


def advect_block(slabs, get_c, get_u, get_v, get_level, bx, by, buf, coef, put):
    lat = bx.shape[0]
    for i, slab in enumerate(slabs):
        level = get_level(slab)
        um = jnp.where(level < bx, get_u(slab), 0.0)
        vm = jnp.where(level < by, get_v(slab), 0.0)
        uw = roll_lanes(um, 1)
        vs = pltpu.roll(vm, 1, 0)
        coef[0, i] = (
            1.0
            - jnp.maximum(um, 0.0)
            + jnp.minimum(uw, 0.0)
            - jnp.maximum(vm, 0.0)
            + jnp.minimum(vs, 0.0)
        )
        coef[1, i] = -jnp.minimum(um, 0.0)
        coef[2, i] = jnp.maximum(uw, 0.0)
        coef[3, i] = -jnp.minimum(vm, 0.0)
        coef[4, i] = jnp.maximum(vs, 0.0)
        for tr in range(2):
            buf[0, 2 * i + tr, PAD : PAD + lat] = get_c(tr, slab)
    for step in range(SUB):
        src, dst = step % 2, (step + 1) % 2
        for i, slab in enumerate(slabs):
            for j in range(0, lat, CHUNK):
                a = coef[0, i, j : j + CHUNK]
                b = coef[1, i, j : j + CHUNK]
                c = coef[2, i, j : j + CHUNK]
                d = coef[3, i, j : j + CHUNK]
                e = coef[4, i, j : j + CHUNK]
                for tr in range(2):
                    q = 2 * i + tr
                    here = buf[src, q, PAD + j : PAD + j + CHUNK]
                    north = buf[src, q, PAD + j + 1 : PAD + j + 1 + CHUNK]
                    south = buf[src, q, PAD + j - 1 : PAD + j - 1 + CHUNK]
                    new = (
                        a * here
                        + b * roll_lanes(here, -1)
                        + c * roll_lanes(here, 1)
                        + d * north
                        + e * south
                    )
                    if step < SUB - 1:
                        buf[dst, q, PAD + j : PAD + j + CHUNK] = new
                    else:
                        put(tr, slab, j, new)


def face_limits(bottom):
    lat = bottom.shape[0]
    rows = lax.broadcasted_iota(jnp.int32, bottom.shape, 0)
    north = jnp.where(rows == lat - 1, 0.0, pltpu.roll(bottom, lat - 1, 0))
    return jnp.minimum(bottom, roll_lanes(bottom, -1)), jnp.minimum(bottom, north)


def lat_limits(bottom):
    lat = bottom.shape[0]
    rows = lax.broadcasted_iota(jnp.int32, bottom.shape, 0)
    north = jnp.where(rows == lat - 1, 0.0, pltpu.roll(bottom, lat - 1, 0))
    south = jnp.where(rows == 0, 0.0, pltpu.roll(bottom, 1, 0))
    return jnp.minimum(north, south)


def clear_pads(ref, lat):
    lead = ref.shape[:-2]
    zero = jnp.zeros(lead + (PAD, 128), jnp.float32)
    ref[..., 0:PAD, :] = zero
    ref[..., PAD + lat : 2 * PAD + lat, :] = zero


def advect_kernel(t_ref, u_ref, v_ref, b_ref, out_ref, buf, coef):
    levels, lat = t_ref.shape[1], t_ref.shape[2]
    base = lax.axis_index("dep") * levels
    clear_pads(buf, lat)
    bx, by = face_limits(b_ref[...].astype(jnp.float32))
    block = coef.shape[1]

    def body(n, _):
        slabs = [n * block + i for i in range(block)]

        def put(tr, slab, j, new):
            out_ref[tr, slab, j : j + CHUNK] = new

        advect_block(
            slabs,
            lambda tr, s: t_ref[tr, s],
            lambda s: u_ref[s],
            lambda s: v_ref[s],
            lambda s: (base + s).astype(jnp.float32),
            bx,
            by,
            buf,
            coef,
            put,
        )
        return 0

    lax.fori_loop(0, levels // block, body, 0)


def join(lane_q, own_high, east, west, own_low):
    return jnp.where(
        lane_q < 16,
        jnp.where(lane_q < 8, own_high, east),
        jnp.where(lane_q < 24, west, own_low),
    )


def west_patch(slab, g):
    return roll_lanes(slab, -(STRIP * g + 24))


def east_patch(slab, g):
    return roll_lanes(slab, 120 - STRIP * g)


def patched(main, slab, g, lane):
    return jnp.where(
        lane < 4, west_patch(slab, g), jnp.where(lane >= 124, east_patch(slab, g), main)
    )


def edge_kernel(
    sw_ref, se_ref, re_ref, rw_ref, b_ref, adv_ref, kh_ref,
    ea_ref, ek_ref, eb_ref, bmx_ref, up_ref, down_ref,
    buf, coef, fields,
):
    levels, lat = adv_ref.shape[1], adv_ref.shape[2]
    rows_e = levels // GROUPS
    base = lax.axis_index("dep") * levels
    lane = lane_ids(lat)
    lane_q = lane % STRIP
    clear_pads(buf, lat)
    bottom = b_ref[...].astype(jnp.float32)
    eb = join(
        lane_q,
        roll_lanes(se_ref[rows_e], -8),
        roll_lanes(re_ref[rows_e], -8),
        roll_lanes(rw_ref[rows_e], 8),
        roll_lanes(sw_ref[rows_e], 8),
    )
    eb_ref[...] = eb
    b_west = roll_lanes(jnp.where(lane == 127, west_patch(eb, 0), bottom), 1)
    b_east = roll_lanes(jnp.where(lane == 0, east_patch(eb, 0), bottom), -1)
    bmx_ref[...] = jnp.minimum(b_west, b_east)
    for r in range(rows_e):
        ek_ref[r] = jnp.where(
            lane_q < 16,
            roll_lanes(re_ref[rows_e], 8 - r),
            roll_lanes(rw_ref[rows_e], 24 - r),
        )
        for f in range(4):
            fields[f, r] = join(
                lane_q,
                roll_lanes(se_ref[r], 8 - 8 * f),
                roll_lanes(re_ref[r], 8 - 8 * f),
                roll_lanes(rw_ref[r], 24 - 8 * f),
                roll_lanes(sw_ref[r], 24 - 8 * f),
            )
    bx, by = face_limits(eb)
    level0 = (base + (lane // STRIP) * rows_e).astype(jnp.float32)

    def put(tr, slab, j, new):
        ea_ref[tr, slab, j : j + CHUNK] = new

    advect_block(
        list(range(rows_e)),
        lambda tr, s: fields[tr, s],
        lambda s: fields[2, s],
        lambda s: fields[3, s],
        lambda s: level0 + float(s),
        bx,
        by,
        buf,
        coef,
        put,
    )
    top = rows_e - 1
    for tr in range(2):
        up_ref[tr] = patched(adv_ref[tr, 0], ea_ref[tr, 0], 0, lane)
        up_ref[2 + tr] = patched(adv_ref[tr, 1], ea_ref[tr, 1], 0, lane)
        down_ref[tr] = patched(adv_ref[tr, levels - 1], ea_ref[tr, top], 3, lane)
        down_ref[2 + tr] = patched(adv_ref[tr, levels - 2], ea_ref[tr, top - 1], 3, lane)
    up_ref[4] = jnp.where(lane < STRIP, ea_ref[0, 0], roll_lanes(ea_ref[1, 0], STRIP))
    down_ref[4] = jnp.where(
        lane >= 3 * STRIP, ea_ref[0, top], roll_lanes(ea_ref[1, top], -STRIP)
    )
    up_ref[5] = kh_ref[0]
    down_ref[5] = kh_ref[levels - 1]


def slopes(gx, gy, gz):
    rx, ry, rz = (-THERMAL * g[0] + HALINE * g[1] for g in (gx, gy, gz))
    scale = rz / (1.0 + rx * rx + ry * ry + rz * rz)
    return rx * scale, ry * scale


def flux_xyz(gx, gy, gz, kappa, need_xy=True):
    sx, sy = slopes(gx, gy, gz)
    kx, ky = kappa * sx, kappa * sy
    kz = kx * sx + ky * sy
    fz = [kx * gx[n] + ky * gy[n] + kz * gz[n] for n in range(2)]
    if not need_xy:
        return None, None, fz
    fx = [kappa * gx[n] + kx * gz[n] for n in range(2)]
    fy = [kappa * gy[n] + ky * gz[n] for n in range(2)]
    return fx, fy, fz


def flux_x_edge(gx, gy, gz, kappa):
    sx, _ = slopes(gx, gy, gz)
    kx = kappa * sx
    return [kappa * gx[n] + kx * gz[n] for n in range(2)]


def grad(mask, high, low):
    return jnp.where(mask, 0.5 * (high - low), 0.0)


def edge_flux_row(r, epad, ek, eb, ebx, eby, level0, out_ref, lat):
    for j in range(0, lat, CHUNK):
        js = slice(j, j + CHUNK)
        level = level0[js] + r
        mx = level < ebx[js]
        my = level < eby[js]
        mz = (level + 1.0 < eb[js]) & (level >= 1.0)
        kappa = jnp.where((level < eb[js]) & (level >= 0.0), ek[js], 0.0)
        gx, gy, gz = [], [], []
        for tr in range(2):
            here = epad[tr, r + 1, PAD + j : PAD + j + CHUNK]
            gx.append(grad(mx, roll_lanes(here, -1), roll_lanes(here, 1)))
            gy.append(
                grad(
                    my,
                    epad[tr, r + 1, PAD + j + 1 : PAD + j + 1 + CHUNK],
                    epad[tr, r + 1, PAD + j - 1 : PAD + j - 1 + CHUNK],
                )
            )
            gz.append(
                grad(
                    mz,
                    epad[tr, r + 2, PAD + j : PAD + j + CHUNK],
                    epad[tr, r, PAD + j : PAD + j + CHUNK],
                )
            )
        fx = flux_x_edge(gx, gy, gz, kappa)
        for tr in range(2):
            out_ref[tr, r, js] = fx[tr]


def edge_limits(eb):
    return (
        jnp.minimum(roll_lanes(eb, 1), roll_lanes(eb, -1)),
        lat_limits(eb),
    )


def flux_kernel(
    adv_ref, ea_ref, ek_ref, eb_ref, bmx_ref, b_ref, kh_ref,
    p_ref, q_ref, fz_ref,
    pad, epad, efx, gxs, fxs, fys,
):
    levels, lat = adv_ref.shape[1], adv_ref.shape[2]
    rows_e = levels // GROUPS
    base = lax.axis_index("dep") * levels
    lane = lane_ids(lat)
    clear_pads(epad, lat)
    clear_pads(pad, lat)
    clear_pads(fys, lat)
    eb = eb_ref[...]
    ebx, eby = edge_limits(eb)
    level0 = (base + (lane // STRIP) * rows_e).astype(jnp.float32)
    for tr in range(2):
        for r in range(rows_e):
            epad[tr, r + 1, PAD : PAD + lat] = ea_ref[tr, r]
        epad[tr, 0, PAD : PAD + lat] = roll_lanes(ea_ref[tr, rows_e - 1], STRIP)
        epad[tr, rows_e + 1, PAD : PAD + lat] = roll_lanes(ea_ref[tr, 0], -STRIP)
    for r in range(rows_e):
        edge_flux_row(r, epad, ek_ref[r], eb, ebx, eby, level0, efx, lat)

    bottom = b_ref[...].astype(jnp.float32)
    bmy = lat_limits(bottom)

    def patch(r, _):
        for g in range(GROUPS):
            k = g * rows_e + r
            for tr in range(2):
                slab = ea_ref[tr, r]
                west, east = west_patch(slab, g), east_patch(slab, g)
                full = jnp.where(
                    lane < 4, west, jnp.where(lane >= 124, east, adv_ref[tr, k])
                )
                p_ref[tr, k] = full
                pad[tr, k + 1, PAD : PAD + lat] = full
                gxs[tr, k] = roll_lanes(jnp.where(lane == 0, east, full), -1) - roll_lanes(
                    jnp.where(lane == 127, west, full), 1
                )
        return 0

    lax.fori_loop(0, rows_e, patch, 0)

    def fluxes(r, _):
        for g in range(GROUPS):
            k = g * rows_e + r
            level = (base + k).astype(jnp.float32)
            level_z = jnp.where(level >= 1.0, level + 1.0, HUGE)
            for j in range(0, lat, CHUNK):
                js = slice(j, j + CHUNK)
                mx = level < bmx_ref[js]
                my = level < bmy[js]
                mz = level_z < bottom[js]
                kappa = jnp.where(level < bottom[js], kh_ref[k, js], 0.0)
                gx, gy, gz = [], [], []
                for tr in range(2):
                    gx.append(jnp.where(mx, 0.5 * gxs[tr, k, js], 0.0))
                    gy.append(
                        grad(
                            my,
                            pad[tr, k + 1, PAD + j + 1 : PAD + j + 1 + CHUNK],
                            pad[tr, k + 1, PAD + j - 1 : PAD + j - 1 + CHUNK],
                        )
                    )
                    gz.append(
                        grad(
                            mz,
                            pad[tr, k + 2, PAD + j : PAD + j + CHUNK],
                            pad[tr, k, PAD + j : PAD + j + CHUNK],
                        )
                    )
                fx, fy, fz = flux_xyz(gx, gy, gz, kappa)
                for tr in range(2):
                    fxs[tr, k, js] = fx[tr]
                    fys[tr, k, PAD + j : PAD + j + CHUNK] = fy[tr]
                    fz_ref[tr, k, js] = fz[tr]
        return 0

    lax.fori_loop(0, rows_e, fluxes, 0)

    def spread(r, _):
        for g in range(GROUPS):
            k = g * rows_e + r
            for tr in range(2):
                slab = efx[tr, r]
                q_ref[tr, k] = divergence(
                    fxs[tr, k], slab, g, lane, fys, (tr, k), lat
                )
        return 0

    lax.fori_loop(0, rows_e, spread, 0)


def divergence(fx, slab, g, lane, fys, at, lat):
    east = roll_lanes(jnp.where(lane == 0, east_patch(slab, g), fx), -1)
    west = roll_lanes(jnp.where(lane == 127, west_patch(slab, g), fx), 1)
    north = fys[at + (slice(PAD + 1, PAD + 1 + lat),)]
    south = fys[at + (slice(PAD - 1, PAD - 1 + lat),)]
    return 0.5 * ((east - west) + (north - south))


def factor_kernel(kv_ref, b_ref, inv_ref, ei_ref, ratio_ref, a_ref, bb_ref, abc_ref):
    levels, lat = kv_ref.shape[0], kv_ref.shape[1]
    base = lax.axis_index("dep") * levels
    bottom = b_ref[...].astype(jnp.float32)

    def coupling(k):
        level = (base + k).astype(jnp.float32)
        level = jnp.where(level >= 1.0, level, HUGE)
        return jnp.where(level < bottom, kv_ref[k], 0.0)

    top = coupling(0)
    e = jnp.zeros((lat, 128), jnp.float32)
    q = e
    za = jnp.ones((lat, 128), jnp.float32)
    for k in range(levels):
        low = coupling(k + 1) if k + 1 < levels else jnp.zeros((lat, 128), jnp.float32)
        eq = 1.0 + e * q
        inv = 1.0 / (eq + low)
        inv_ref[k] = inv
        ei = e * inv
        ei_ref[k] = ei
        ratio_ref[k] = low * inv
        za = inv if k == 0 else za * ei
        a_ref[k] = za
        q = eq * inv
        e = low
    bb_ref[levels - 1] = inv
    b = inv
    a = za
    for k in range(levels - 2, -1, -1):
        ratio = ratio_ref[k]
        b = ratio * b
        a = a_ref[k] + ratio * a
        bb_ref[k] = b
        a_ref[k] = a
    abc_ref[0] = a + jnp.where(top > 0.0, 1.0 / jnp.maximum(top, 1e-30), HUGE)
    abc_ref[1] = inv
    abc_ref[2] = b


def solve_kernel(
    p_ref, q_ref, fz_ref, ea_ref, ek_ref, eb_ref, bmx_ref, b_ref, kh_ref,
    above_ref, below_ref, inv_ref, ei_ref, ratio_ref, *rest,
):
    dep = lax.axis_size("dep")
    abc_refs = rest[:dep]
    y_ref, send_ref, own_ref = rest[dep : dep + 3]
    pad, epad, efx, fxs, fys, fze, weights, table = rest[dep + 3 :]
    levels, lat = p_ref.shape[1], p_ref.shape[2]
    rows_e = levels // GROUPS
    last = levels - 1
    top = rows_e - 1
    me = lax.axis_index("dep")
    base = me * levels
    lane = lane_ids(lat)
    clear_pads(epad, lat)
    clear_pads(pad, lat)
    clear_pads(fys, lat)

    for shift in range(dep):
        table[lax.rem(me - shift + dep, dep)] = abc_refs[shift][...]
    zero = jnp.zeros((lat, 128), jnp.float32)
    one = jnp.ones((lat, 128), jnp.float32)
    rho, sigma, left, right = [zero] * dep, [zero] * dep, [None] * dep, [None] * dep
    beff = table[0, 1]
    for p in range(1, dep):
        left[p] = table[p, 0] + beff
        rho[p] = table[p, 2] / left[p]
        beff = table[p, 1] - table[p, 2] * rho[p]
    aeff = table[dep - 1, 0]
    for p in range(dep - 2, -1, -1):
        right[p] = table[p, 1] + aeff
        sigma[p] = table[p, 2] / right[p]
        aeff = table[p, 0] - table[p, 2] * sigma[p]
    for src in range(dep):
        for dst in range(dep):
            w = one
            if dst > src:
                for p in range(src + 1, dst):
                    w = w * rho[p]
            else:
                for p in range(dst + 1, src):
                    w = w * sigma[p]
            if src != dst:
                weights[src, dst] = w
        c = table[src, 2]
        if src == 0:
            m11, m12, m22 = zero, zero, 1.0 / right[src]
        elif src == dep - 1:
            m11, m12, m22 = 1.0 / left[src], zero, zero
        else:
            m11 = 1.0 / (left[src] - c * sigma[src])
            m12 = m11 * sigma[src]
            m22 = 1.0 / (right[src] - c * rho[src])
        for n, m in enumerate((m11, m12, m22, rho[src], sigma[src])):
            weights[src, dep + n] = m
    for n in range(3):
        own_ref[n] = weights[me, dep + n]
    rho_me, sigma_me = weights[me, dep + 3], weights[me, dep + 4]

    eb = eb_ref[...]
    ebx, eby = edge_limits(eb)
    level0 = (base + (lane // STRIP) * rows_e).astype(jnp.float32)
    for tr in range(2):
        for n, slab in enumerate(
            (
                above_ref[2 + tr], above_ref[tr], p_ref[tr, 0], p_ref[tr, 1], p_ref[tr, 2],
                p_ref[tr, last - 2], p_ref[tr, last - 1], p_ref[tr, last],
                below_ref[tr], below_ref[2 + tr],
            )
        ):
            pad[tr, n, PAD : PAD + lat] = slab
        for r in range(rows_e):
            epad[tr, r + 1, PAD : PAD + lat] = ea_ref[tr, r]
        corner_up = above_ref[4] if tr == 0 else roll_lanes(above_ref[4], STRIP)
        corner_dn = below_ref[4] if tr == 0 else roll_lanes(below_ref[4], -STRIP)
        epad[tr, 0, PAD : PAD + lat] = roll_lanes(
            jnp.where(lane >= 3 * STRIP, corner_up, ea_ref[tr, top]), STRIP
        )
        epad[tr, rows_e + 1, PAD : PAD + lat] = roll_lanes(
            jnp.where(lane < STRIP, corner_dn, ea_ref[tr, 0]), -STRIP
        )
    edge_flux_row(0, epad, ek_ref[0], eb, ebx, eby, level0, efx, lat)
    edge_flux_row(top, epad, ek_ref[top], eb, ebx, eby, level0, efx, lat)

    bottom = b_ref[...].astype(jnp.float32)
    bmy = lat_limits(bottom)
    bmx = bmx_ref[...]
    ends = (
        (1, -1, 0, 0, above_ref[5], True),
        (2, 0, 1, 0, kh_ref[0], False),
        (7, last, top + 1, 3, kh_ref[last], False),
        (8, last + 1, top + 2, 3, below_ref[5], True),
    )
    for m, (n, k, er, g, kappa_slab, only_z) in enumerate(ends):
        level = (base + k).astype(jnp.float32)
        level_z = jnp.where(level >= 1.0, level + 1.0, HUGE)
        level_h = jnp.where(level >= 0.0, level, HUGE)
        gx_full = []
        for tr in range(2):
            slab = epad[tr, er, PAD : PAD + lat]
            full = pad[tr, n, PAD : PAD + lat]
            gx_full.append(
                roll_lanes(jnp.where(lane == 0, east_patch(slab, g), full), -1)
                - roll_lanes(jnp.where(lane == 127, west_patch(slab, g), full), 1)
            )
        for j in range(0, lat, CHUNK):
            js = slice(j, j + CHUNK)
            mx = level_h < bmx[js]
            my = level_h < bmy[js]
            mz = level_z < bottom[js]
            kappa = jnp.where(level_h < bottom[js], kappa_slab[js], 0.0)
            gx = [jnp.where(mx, 0.5 * gx_full[tr][js], 0.0) for tr in range(2)]
            gy, gz = [], []
            for tr in range(2):
                gy.append(
                    grad(
                        my,
                        pad[tr, n, PAD + j + 1 : PAD + j + 1 + CHUNK],
                        pad[tr, n, PAD + j - 1 : PAD + j - 1 + CHUNK],
                    )
                )
                gz.append(
                    grad(
                        mz,
                        pad[tr, n + 1, PAD + j : PAD + j + CHUNK],
                        pad[tr, n - 1, PAD + j : PAD + j + CHUNK],
                    )
                )
            fx, fy, fz = flux_xyz(gx, gy, gz, kappa, not only_z)
            for tr in range(2):
                fze[tr, m, js] = fz[tr]
                if not only_z:
                    fxs[tr, m - 1, js] = fx[tr]
                    fys[tr, m - 1, PAD + j : PAD + j + CHUNK] = fy[tr]

    def vertical_flux(tr, k):
        place = {-1: 0, 0: 1, last: 2, last + 1: 3}.get(k)
        return fz_ref[tr, k] if place is None else fze[tr, place]

    z = [None, None]
    for k in range(levels):
        level = (base + k).astype(jnp.float32)
        wet = level < bottom
        for tr in range(2):
            if k == 0:
                spread = divergence(fxs[tr, 0], efx[tr, 0], 0, lane, fys, (tr, 0), lat)
            elif k == last:
                spread = divergence(fxs[tr, 1], efx[tr, top], 3, lane, fys, (tr, 1), lat)
            else:
                spread = q_ref[tr, k]
            change = spread + 0.5 * (vertical_flux(tr, k + 1) - vertical_flux(tr, k - 1))
            rhs = p_ref[tr, k] + jnp.where(wet, change, 0.0)
            z[tr] = rhs * inv_ref[k]
            if k > 0:
                z[tr] = z[tr] + ei_ref[k] * y_ref[tr, k - 1]
            y_ref[tr, k] = z[tr]
    low = list(z)
    for k in range(last - 1, -1, -1):
        ratio = ratio_ref[k]
        for tr in range(2):
            z[tr] = y_ref[tr, k] + ratio * z[tr]
            y_ref[tr, k] = z[tr]
    for shift in range(1, dep):
        dst = lax.rem(me + shift, dep)
        w = weights[me, dst]
        forward = me + shift < dep
        for tr in range(2):
            send_ref[shift - 1, tr] = w * jnp.where(
                forward, low[tr] - rho_me * z[tr], z[tr] - sigma_me * low[tr]
            )


def finish_kernel(y_ref, a_ref, bb_ref, own_ref, *rest):
    dep = lax.axis_size("dep")
    got = rest[: dep - 1]
    out_ref = rest[dep - 1]
    levels = y_ref.shape[1]
    me = lax.axis_index("dep")
    flux = []
    for tr in range(2):
        left = right = 0.0
        for shift in range(1, dep):
            here = got[shift - 1][tr]
            from_left = me >= shift
            left = left + jnp.where(from_left, here, 0.0)
            right = right + jnp.where(from_left, 0.0, here)
        upper = y_ref[tr, 0] - left
        lower = right - y_ref[tr, levels - 1]
        flux.append(
            (
                own_ref[0] * upper + own_ref[1] * lower,
                own_ref[1] * upper + own_ref[2] * lower,
            )
        )
    for k in range(levels):
        a, b = a_ref[k], bb_ref[k]
        for tr in range(2):
            out_ref[tr, k] = y_ref[tr, k] - flux[tr][0] * a + flux[tr][1] * b


def per_device(tracers, u_east, v_north, kappa_h, kappa_v, bottom):
    _, levels, lat, lon = tracers.shape
    rows_e = levels // GROUPS
    lon_n, dep_n = lax.axis_size("lon"), lax.axis_size("dep")
    east = [(i, (i + 1) % lon_n) for i in range(lon_n)]
    west = [(t, s) for s, t in east]
    slab = lat * lon * 4
    slabs = lambda *lead: f32(*lead, lat, lon)
    work = lambda *lead: pltpu.VMEM(lead + (lat, lon), jnp.float32)
    padded = lambda *lead: pltpu.VMEM(lead + (lat + 2 * PAD, lon), jnp.float32)

    with jax.named_scope("pack"):
        sw, se = call(
            pack_kernel, (slabs(rows_e + 1),) * 2, [],
            (tracers, u_east, v_north, kappa_h, bottom), 10**6, 6 * levels * slab, 16,
        )
    with jax.named_scope("lon_halo"):
        r_east = lax.ppermute(sw, "lon", west)
        r_west = lax.ppermute(se, "lon", east)
    with jax.named_scope("advect_inner"):
        adv = call(
            advect_kernel, slabs(2, levels),
            [padded(2, 2 * rows_e), work(5, rows_e)],
            (tracers, u_east, v_north, bottom), 10**7, 7 * levels * slab, 16,
        )
    with jax.named_scope("factor"):
        inv, ei, ratio, a_end, b_end, abc = call(
            factor_kernel, (slabs(levels),) * 5 + (slabs(3),), [],
            (kappa_v, bottom), 10**7, 6 * levels * slab, 16,
        )
    with jax.named_scope("advect_edge"):
        ea, ek, eb, bmx, up, down = call(
            edge_kernel,
            (slabs(2, rows_e), slabs(rows_e), slabs(), slabs(), slabs(6), slabs(6)),
            [padded(2, 2 * rows_e), work(5, rows_e), work(4, rows_e)],
            (sw, se, r_east, r_west, bottom, adv, kappa_h), 10**6, 3 * levels * slab, 16,
        )
    with jax.named_scope("dep_halo"):
        below = lax.ppermute(up, "dep", [(i + 1, i) for i in range(dep_n - 1)])
        above = lax.ppermute(down, "dep", [(i, i + 1) for i in range(dep_n - 1)])
    with jax.named_scope("coefficients"):
        abcs = [abc] + [
            lax.ppermute(abc, "dep", [(i, (i + s) % dep_n) for i in range(dep_n)])
            for s in range(1, dep_n)
        ]
    with jax.named_scope("fluxes"):
        p_adv, q_part, fz = call(
            flux_kernel, (slabs(2, levels),) * 3,
            [
                padded(2, levels + 2), padded(2, rows_e + 2), work(2, rows_e),
                work(2, levels), work(2, levels), padded(2, levels),
            ],
            (adv, ea, ek, eb, bmx, bottom, kappa_h), 10**7, 10 * levels * slab, 24,
        )
    with jax.named_scope("solve"):
        y, send, own = call(
            solve_kernel, (slabs(2, levels), slabs(dep_n - 1, 2), slabs(3)),
            [
                padded(2, 10), padded(2, rows_e + 2), work(2, rows_e),
                work(2, 2), padded(2, 2), work(2, 4), work(dep_n, dep_n + 5), work(dep_n, 3),
            ],
            (p_adv, q_part, fz, ea, ek, eb, bmx, bottom, kappa_h, above, below, inv, ei, ratio, *abcs),
            10**7, 12 * levels * slab, 24,
        )
    with jax.named_scope("interfaces"):
        got = [
            lax.ppermute(send[s - 1], "dep", [(i, (i + s) % dep_n) for i in range(dep_n)])
            for s in range(1, dep_n)
        ]
    with jax.named_scope("finish"):
        return call(
            finish_kernel, slabs(2, levels), [],
            (y, a_end, b_end, own, *got), 10**6, 6 * levels * slab, 16,
        )


def solution(mesh):
    in_specs = (
        P(None, "dep", None, "lon"),
        P("dep", None, "lon"),
        P("dep", None, "lon"),
        P("dep", None, "lon"),
        P("dep", None, "lon"),
        P(None, "lon"),
    )
    out_specs = P(None, "dep", None, "lon")
    return jax.shard_map(
        per_device, mesh=mesh, in_specs=in_specs, out_specs=out_specs, check_vma=False
    )
```

```python
import jax
import jax.numpy as jnp
from jax import lax
from jax.experimental import pallas as pl
from jax.experimental.pallas import tpu as pltpu
from jax.sharding import PartitionSpec as P

SUB = 4
THERMAL = 0.2
HALINE = 0.8
GROUPS = 4
STRIP = 32
CHUNK = 16
PAD = 8
HUGE = 1e30
MIB = 1024 * 1024

VMEM = pl.BlockSpec(memory_space=pltpu.VMEM)
HBM = pl.BlockSpec(memory_space=pltpu.HBM)


def lane_ids(rows):
    return lax.broadcasted_iota(jnp.int32, (rows, 128), 1)


def roll_lanes(x, amount):
    amount = amount % 128
    return x if amount == 0 else pltpu.roll(x, amount, 1)


def call(body, out_shape, scratch, args, flops, in_bytes, limit, in_specs=None, out_specs=None):
    return pl.pallas_call(
        body,
        out_shape=out_shape,
        in_specs=in_specs or [VMEM] * len(args),
        out_specs=out_specs or jax.tree.map(lambda _: VMEM, out_shape),
        scratch_shapes=scratch,
        compiler_params=pltpu.CompilerParams(vmem_limit_bytes=int(limit * MIB)),
        cost_estimate=pl.CostEstimate(flops=flops, bytes_accessed=in_bytes, transcendentals=0),
    )(*args)


def f32(*shape):
    return jax.ShapeDtypeStruct(shape, jnp.float32)


def pack_kernel(
    t_hbm, u_hbm, v_hbm, kh_hbm, b_hbm,
    sw_ref, se_ref, t0_ref, t1_ref, u_ref, v_ref,
    kh_buf, b_buf, first_buf, sems, more_sems,
):
    rows_e = u_ref.shape[0] // GROUPS
    lat = u_ref.shape[1]
    lane = lane_ids(lat)
    fields = ((t_hbm.at[0], t0_ref), (t_hbm.at[1], t1_ref), (u_hbm, u_ref), (v_hbm, v_ref))
    groups = [
        [
            pltpu.make_async_copy(
                src.at[pl.ds(g * rows_e, rows_e)], dst.at[pl.ds(g * rows_e, rows_e)], sems.at[g, n]
            )
            for n, (src, dst) in enumerate(fields)
        ]
        for g in range(GROUPS)
    ]
    tail = [
        pltpu.make_async_copy(b_hbm, b_buf, more_sems.at[0]),
        pltpu.make_async_copy(kh_hbm, kh_buf, more_sems.at[1]),
    ]
    for copy in sum(groups, []) + tail:
        copy.start()
    for g in range(GROUPS):
        for copy in groups[g]:
            copy.wait()
        for r in range(rows_e):
            level = g * rows_e + r
            slabs = (t0_ref[level], t1_ref[level], u_ref[level], v_ref[level])
            if g > 0:
                low, high = sw_ref[r], se_ref[r]
            for f, slab in enumerate(slabs):
                start = STRIP * g + 8 * f
                rolled = roll_lanes(slab, start)
                if start == 0:
                    first_buf[r] = rolled
                    low = rolled
                else:
                    low = jnp.where(lane >= start, rolled, low)
                    high = rolled if start == 8 else jnp.where(lane >= start - 8, rolled, high)
            if g == GROUPS - 1:
                high = jnp.where(lane >= 120, first_buf[r], high)
            sw_ref[r] = low
            se_ref[r] = high
    for copy in tail:
        copy.wait()
    low = jnp.zeros((lat, 128), jnp.float32)
    high = jnp.zeros((lat, 128), jnp.float32)
    bottom = b_buf[...].astype(jnp.float32)
    for g in range(GROUPS):
        for r in range(rows_e):
            place = STRIP * g + r
            rolled = roll_lanes(kh_buf[g * rows_e + r], place)
            low = jnp.where(lane == place, rolled, low)
            high = jnp.where(lane == (place - 1) % 128, rolled, high)
        place = STRIP * g + 16
        rolled = roll_lanes(bottom, place)
        low = jnp.where((lane >= place) & (lane < place + 8), rolled, low)
        high = jnp.where((lane >= place - 8) & (lane < place), rolled, high)
    sw_ref[rows_e] = low
    se_ref[rows_e] = high


def advect_block(slabs, get_c, get_u, get_v, get_level, bx, by, buf, coef, put):
    lat = bx.shape[0]
    for i, slab in enumerate(slabs):
        level = get_level(slab)
        um = jnp.where(level < bx, get_u(slab), 0.0)
        vm = jnp.where(level < by, get_v(slab), 0.0)
        uw = roll_lanes(um, 1)
        vs = pltpu.roll(vm, 1, 0)
        coef[0, i] = (
            1.0
            - jnp.maximum(um, 0.0)
            + jnp.minimum(uw, 0.0)
            - jnp.maximum(vm, 0.0)
            + jnp.minimum(vs, 0.0)
        )
        coef[1, i] = -jnp.minimum(um, 0.0)
        coef[2, i] = jnp.maximum(uw, 0.0)
        coef[3, i] = -jnp.minimum(vm, 0.0)
        coef[4, i] = jnp.maximum(vs, 0.0)
        for tr in range(2):
            buf[0, 2 * i + tr, PAD : PAD + lat] = get_c(tr, slab)
    for step in range(SUB):
        src, dst = step % 2, (step + 1) % 2
        for i, slab in enumerate(slabs):
            for j in range(0, lat, CHUNK):
                a = coef[0, i, j : j + CHUNK]
                b = coef[1, i, j : j + CHUNK]
                c = coef[2, i, j : j + CHUNK]
                d = coef[3, i, j : j + CHUNK]
                e = coef[4, i, j : j + CHUNK]
                for tr in range(2):
                    q = 2 * i + tr
                    here = buf[src, q, PAD + j : PAD + j + CHUNK]
                    north = buf[src, q, PAD + j + 1 : PAD + j + 1 + CHUNK]
                    south = buf[src, q, PAD + j - 1 : PAD + j - 1 + CHUNK]
                    new = (
                        a * here
                        + b * roll_lanes(here, -1)
                        + c * roll_lanes(here, 1)
                        + d * north
                        + e * south
                    )
                    if step < SUB - 1:
                        buf[dst, q, PAD + j : PAD + j + CHUNK] = new
                    else:
                        put(tr, slab, j, new)


def face_limits(bottom):
    lat = bottom.shape[0]
    rows = lax.broadcasted_iota(jnp.int32, bottom.shape, 0)
    north = jnp.where(rows == lat - 1, 0.0, pltpu.roll(bottom, lat - 1, 0))
    return jnp.minimum(bottom, roll_lanes(bottom, -1)), jnp.minimum(bottom, north)


def lat_limits(bottom):
    lat = bottom.shape[0]
    rows = lax.broadcasted_iota(jnp.int32, bottom.shape, 0)
    north = jnp.where(rows == lat - 1, 0.0, pltpu.roll(bottom, lat - 1, 0))
    south = jnp.where(rows == 0, 0.0, pltpu.roll(bottom, 1, 0))
    return jnp.minimum(north, south)


def clear_pads(ref, lat):
    lead = ref.shape[:-2]
    zero = jnp.zeros(lead + (PAD, 128), jnp.float32)
    ref[..., 0:PAD, :] = zero
    ref[..., PAD + lat : 2 * PAD + lat, :] = zero


def advect_kernel(t0_ref, t1_ref, u_ref, v_ref, b_ref, out_ref, buf, coef):
    levels, lat = out_ref.shape[1], out_ref.shape[2]
    base = lax.axis_index("dep") * levels
    block = coef.shape[1]
    clear_pads(buf, lat)
    bx, by = face_limits(b_ref[...].astype(jnp.float32))

    def body(n, _):
        slabs = [n * block + i for i in range(block)]

        def put(tr, slab, j, new):
            out_ref[tr, slab, j : j + CHUNK] = new

        advect_block(
            slabs,
            lambda tr, s: (t0_ref, t1_ref)[tr][s],
            lambda s: u_ref[s],
            lambda s: v_ref[s],
            lambda s: (base + s).astype(jnp.float32),
            bx,
            by,
            buf,
            coef,
            put,
        )
        return 0

    lax.fori_loop(0, levels // block, body, 0)


def join(lane_q, own_high, east, west, own_low):
    return jnp.where(
        lane_q < 16,
        jnp.where(lane_q < 8, own_high, east),
        jnp.where(lane_q < 24, west, own_low),
    )


def west_patch(slab, g):
    return roll_lanes(slab, -(STRIP * g + 24))


def east_patch(slab, g):
    return roll_lanes(slab, 120 - STRIP * g)


def patched(main, slab, g, lane):
    return jnp.where(
        lane < 4, west_patch(slab, g), jnp.where(lane >= 124, east_patch(slab, g), main)
    )


def edge_kernel(
    sw_ref, se_ref, re_ref, rw_ref, b_ref, adv_ref, kh_ref, abc_ref,
    ea_ref, ek_ref, eb_ref, bmx_ref, first_ref, second_ref,
    buf, coef, fields, pay,
):
    levels, lat = adv_ref.shape[1], adv_ref.shape[2]
    rows_e = levels // GROUPS
    me = lax.axis_index("dep")
    base = me * levels
    parity = lax.rem(me, 2)
    up_ref, down_ref = pay.at[1 - parity], pay.at[parity]
    lane = lane_ids(lat)
    lane_q = lane % STRIP
    clear_pads(buf, lat)
    bottom = b_ref[...].astype(jnp.float32)
    eb = join(
        lane_q,
        roll_lanes(se_ref[rows_e], -8),
        roll_lanes(re_ref[rows_e], -8),
        roll_lanes(rw_ref[rows_e], 8),
        roll_lanes(sw_ref[rows_e], 8),
    )
    eb_ref[...] = eb
    b_west = roll_lanes(jnp.where(lane == 127, west_patch(eb, 0), bottom), 1)
    b_east = roll_lanes(jnp.where(lane == 0, east_patch(eb, 0), bottom), -1)
    bmx_ref[...] = jnp.minimum(b_west, b_east)
    for r in range(rows_e):
        ek_ref[r] = jnp.where(
            lane_q < 16,
            roll_lanes(re_ref[rows_e], 8 - r),
            roll_lanes(rw_ref[rows_e], 24 - r),
        )
        for f in range(4):
            fields[f, r] = join(
                lane_q,
                roll_lanes(se_ref[r], 8 - 8 * f),
                roll_lanes(re_ref[r], 8 - 8 * f),
                roll_lanes(rw_ref[r], 24 - 8 * f),
                roll_lanes(sw_ref[r], 24 - 8 * f),
            )
    bx, by = face_limits(eb)
    level0 = (base + (lane // STRIP) * rows_e).astype(jnp.float32)

    def put(tr, slab, j, new):
        ea_ref[tr, slab, j : j + CHUNK] = new

    advect_block(
        list(range(rows_e)),
        lambda tr, s: fields[tr, s],
        lambda s: fields[2, s],
        lambda s: fields[3, s],
        lambda s: level0 + float(s),
        bx,
        by,
        buf,
        coef,
        put,
    )
    top = rows_e - 1
    for tr in range(2):
        up_ref[tr] = patched(adv_ref[tr, 0], ea_ref[tr, 0], 0, lane)
        up_ref[2 + tr] = patched(adv_ref[tr, 1], ea_ref[tr, 1], 0, lane)
        down_ref[tr] = patched(adv_ref[tr, levels - 1], ea_ref[tr, top], 3, lane)
        down_ref[2 + tr] = patched(adv_ref[tr, levels - 2], ea_ref[tr, top - 1], 3, lane)
    up_ref[4] = jnp.where(lane < STRIP, ea_ref[0, 0], roll_lanes(ea_ref[1, 0], STRIP))
    down_ref[4] = jnp.where(
        lane >= 3 * STRIP, ea_ref[0, top], roll_lanes(ea_ref[1, top], -STRIP)
    )
    up_ref[5] = kh_ref[0]
    down_ref[5] = kh_ref[levels - 1]
    first_ref[0:6] = pay[0]
    first_ref[6:9] = abc_ref[...]
    second_ref[...] = pay[1]


def slopes(gx, gy, gz):
    rx, ry, rz = (-0.5 * THERMAL * g[0] + 0.5 * HALINE * g[1] for g in (gx, gy, gz))
    scale = rz / (1.0 + rx * rx + ry * ry + rz * rz)
    return rx * scale, ry * scale


def flux_xyz(gx, gy, gz, kappa, need_xy=True):
    sx, sy = slopes(gx, gy, gz)
    kx, ky = kappa * sx, kappa * sy
    kz = kx * sx + ky * sy
    fz = [kx * gx[n] + ky * gy[n] + kz * gz[n] for n in range(2)]
    if not need_xy:
        return None, None, fz
    fx = [kappa * gx[n] + kx * gz[n] for n in range(2)]
    fy = [kappa * gy[n] + ky * gz[n] for n in range(2)]
    return fx, fy, fz


def flux_x_edge(gx, gy, gz, kappa):
    sx, _ = slopes(gx, gy, gz)
    kx = kappa * sx
    return [kappa * gx[n] + kx * gz[n] for n in range(2)]


def diff(mask, high, low):
    return jnp.where(mask, high - low, 0.0)


def edge_flux_row(r, epad, ek, eb, ebx, eby, level0, out_ref, lat):
    level = level0 + r
    mx = level < ebx
    my = level < eby
    mz = (level + 1.0 < eb) & (level >= 1.0)
    kappa = jnp.where((level < eb) & (level >= 0.0), 0.25 * ek, 0.0)
    rows = slice(PAD, PAD + lat)
    gx, gy, gz = [], [], []
    for tr in range(2):
        here = epad[tr, r + 1, rows]
        gx.append(diff(mx, roll_lanes(here, -1), roll_lanes(here, 1)))
        gy.append(
            diff(
                my,
                epad[tr, r + 1, PAD + 1 : PAD + 1 + lat],
                epad[tr, r + 1, PAD - 1 : PAD - 1 + lat],
            )
        )
        gz.append(diff(mz, epad[tr, r + 2, rows], epad[tr, r, rows]))
    fx = flux_x_edge(gx, gy, gz, kappa)
    for tr in range(2):
        out_ref[tr, r] = fx[tr]


def edge_limits(eb):
    return (
        jnp.minimum(roll_lanes(eb, 1), roll_lanes(eb, -1)),
        lat_limits(eb),
    )


def divergence(fx, slab, g, lane, fys, at, lat):
    east = roll_lanes(jnp.where(lane == 0, east_patch(slab, g), fx), -1)
    west = roll_lanes(jnp.where(lane == 127, west_patch(slab, g), fx), 1)
    north = fys[at + (slice(PAD + 1, PAD + 1 + lat),)]
    south = fys[at + (slice(PAD - 1, PAD - 1 + lat),)]
    return (east - west) + (north - south)


def flux_kernel(
    adv_ref, ea_ref, ek_ref, eb_ref, bmx_ref, b_ref, kh_ref,
    pe_ref, q_ref, fz_ref,
    pad, epad, efx, gxs, fxs, fys,
):
    levels, lat = adv_ref.shape[1], adv_ref.shape[2]
    rows_e = levels // GROUPS
    base = lax.axis_index("dep") * levels
    lane = lane_ids(lat)
    clear_pads(epad, lat)
    clear_pads(pad, lat)
    clear_pads(fys, lat)
    rows = slice(PAD, PAD + lat)
    eb = eb_ref[...]
    ebx, eby = edge_limits(eb)
    level0 = (base + (lane // STRIP) * rows_e).astype(jnp.float32)
    for tr in range(2):
        for r in range(rows_e):
            epad[tr, r + 1, rows] = ea_ref[tr, r]
        epad[tr, 0, rows] = roll_lanes(ea_ref[tr, rows_e - 1], STRIP)
        epad[tr, rows_e + 1, rows] = roll_lanes(ea_ref[tr, 0], -STRIP)
    for r in range(rows_e):
        edge_flux_row(r, epad, ek_ref[r], eb, ebx, eby, level0, efx, lat)

    bottom = b_ref[...].astype(jnp.float32)
    bmy = lat_limits(bottom)
    bmx = bmx_ref[...]

    def patch(r, _):
        for g in range(GROUPS):
            k = g * rows_e + r
            full, gx = [], []
            for tr in range(2):
                slab = ea_ref[tr, r]
                west, east = west_patch(slab, g), east_patch(slab, g)
                full.append(
                    jnp.where(lane < 4, west, jnp.where(lane >= 124, east, adv_ref[tr, k]))
                )
                gx.append(
                    roll_lanes(jnp.where(lane == 0, east, full[tr]), -1)
                    - roll_lanes(jnp.where(lane == 127, west, full[tr]), 1)
                )
            for tr in range(2):
                pad[tr, k + 1, rows] = full[tr]
                gxs[tr, k] = gx[tr]
        return 0

    lax.fori_loop(0, rows_e, patch, 0)
    for n, k in enumerate((0, 1, 2, levels - 3, levels - 2, levels - 1)):
        for tr in range(2):
            pe_ref[tr, n] = pad[tr, k + 1, rows]

    def fluxes(r, _):
        for g in range(GROUPS):
            k = g * rows_e + r
            level = (base + k).astype(jnp.float32)
            level_z = jnp.where(level >= 1.0, level + 1.0, HUGE)
            mx = level < bmx
            my = level < bmy
            mz = level_z < bottom
            kappa = jnp.where(level < bottom, 0.25 * kh_ref[k], 0.0)
            gx, gy, gz = [], [], []
            for tr in range(2):
                gx.append(jnp.where(mx, gxs[tr, k], 0.0))
                gy.append(
                    diff(
                        my,
                        pad[tr, k + 1, PAD + 1 : PAD + 1 + lat],
                        pad[tr, k + 1, PAD - 1 : PAD - 1 + lat],
                    )
                )
                gz.append(diff(mz, pad[tr, k + 2, rows], pad[tr, k, rows]))
            fx, fy, fz = flux_xyz(gx, gy, gz, kappa)
            for tr in range(2):
                fxs[tr, k] = fx[tr]
                fys[tr, k, rows] = fy[tr]
                fz_ref[tr, k] = fz[tr]
        return 0

    lax.fori_loop(0, rows_e, fluxes, 0)

    def spread(r, _):
        for g in range(GROUPS):
            k = g * rows_e + r
            wet = (base + k).astype(jnp.float32) < bottom
            new = []
            for tr in range(2):
                change = divergence(fxs[tr, k], efx[tr, r], g, lane, fys, (tr, k), lat)
                new.append(pad[tr, k + 1, rows] + jnp.where(wet, change, 0.0))
            for tr in range(2):
                q_ref[tr, k] = new[tr]
        return 0

    lax.fori_loop(0, rows_e, spread, 0)


def factor_kernel(kv_ref, b_ref, inv_ref, ei_ref, ratio_ref, a_ref, bb_ref, abc_ref):
    levels, lat = kv_ref.shape[0], kv_ref.shape[1]
    base = lax.axis_index("dep") * levels
    bottom = b_ref[...].astype(jnp.float32)

    def coupling(k):
        level = (base + k).astype(jnp.float32)
        level = jnp.where(level >= 1.0, level, HUGE)
        return jnp.where(level < bottom, kv_ref[k], 0.0)

    top = coupling(0)
    e = jnp.zeros((lat, 128), jnp.float32)
    q = e
    za = jnp.ones((lat, 128), jnp.float32)
    for k in range(levels):
        low = coupling(k + 1) if k + 1 < levels else jnp.zeros((lat, 128), jnp.float32)
        eq = 1.0 + e * q
        inv = 1.0 / (eq + low)
        inv_ref[k] = inv
        ei = e * inv
        ei_ref[k] = ei
        ratio_ref[k] = low * inv
        za = inv if k == 0 else za * ei
        a_ref[k] = za
        q = eq * inv
        e = low
    bb_ref[levels - 1] = inv
    b = inv
    a = za
    for k in range(levels - 2, -1, -1):
        ratio = ratio_ref[k]
        b = ratio * b
        a = a_ref[k] + ratio * a
        bb_ref[k] = b
        a_ref[k] = a
    abc_ref[0] = a + jnp.where(top > 0.0, 1.0 / jnp.maximum(top, 1e-30), HUGE)
    abc_ref[1] = inv
    abc_ref[2] = b


def solve_kernel(
    pe_ref, q_ref, fz_ref, ea_ref, ek_ref, eb_ref, bmx_ref, b_ref, kh_ref,
    first_ref, second_ref, inv_ref, ei_ref, ratio_ref, abc_ref,
    y_ref, m1_ref, m2_ref, m3_ref, own_ref,
    pad, epad, efx, fxs, fys, fze, halo,
):
    levels, lat = q_ref.shape[1], q_ref.shape[2]
    rows_e = levels // GROUPS
    last = levels - 1
    top = rows_e - 1
    me = lax.axis_index("dep")
    base = me * levels
    parity = lax.rem(me, 2)
    upper = parity == 0
    low_pair = me < 2
    lane = lane_ids(lat)
    rows = slice(PAD, PAD + lat)
    clear_pads(epad, lat)
    clear_pads(pad, lat)
    clear_pads(fys, lat)
    halo[0] = first_ref[0:6]
    halo[1] = second_ref[...]
    above_ref, below_ref = halo.at[1 - parity], halo.at[parity]

    b_u = jnp.where(upper, abc_ref[1], first_ref[7])
    a_l = jnp.where(upper, first_ref[6], abc_ref[0])
    a_u = jnp.where(upper, abc_ref[0], first_ref[6])
    b_l = jnp.where(upper, first_ref[7], abc_ref[1])
    inv_t = 1.0 / (b_u + a_l)
    c_pair = jnp.where(upper == low_pair, first_ref[8], abc_ref[2])
    share = c_pair * inv_t
    eff = jnp.where(low_pair, b_l, a_u) - c_pair * share
    own_ref[0] = share
    own_ref[1] = inv_t
    own_ref[2] = eff

    eb = eb_ref[...]
    ebx, eby = edge_limits(eb)
    level0 = (base + (lane // STRIP) * rows_e).astype(jnp.float32)
    for tr in range(2):
        pad[tr, 0, rows] = above_ref[2 + tr]
        pad[tr, 1, rows] = above_ref[tr]
        for n in range(6):
            pad[tr, n + 2, rows] = pe_ref[tr, n]
        pad[tr, 8, rows] = below_ref[tr]
        pad[tr, 9, rows] = below_ref[2 + tr]
        for r in range(rows_e):
            epad[tr, r + 1, rows] = ea_ref[tr, r]
        corner_up = above_ref[4] if tr == 0 else roll_lanes(above_ref[4], STRIP)
        corner_dn = below_ref[4] if tr == 0 else roll_lanes(below_ref[4], -STRIP)
        epad[tr, 0, rows] = roll_lanes(
            jnp.where(lane >= 3 * STRIP, corner_up, ea_ref[tr, top]), STRIP
        )
        epad[tr, rows_e + 1, rows] = roll_lanes(
            jnp.where(lane < STRIP, corner_dn, ea_ref[tr, 0]), -STRIP
        )
    edge_flux_row(0, epad, ek_ref[0], eb, ebx, eby, level0, efx, lat)
    edge_flux_row(top, epad, ek_ref[top], eb, ebx, eby, level0, efx, lat)

    bottom = b_ref[...].astype(jnp.float32)
    bmy = lat_limits(bottom)
    bmx = bmx_ref[...]
    ends = (
        (1, -1, 0, 0, above_ref[5], True),
        (2, 0, 1, 0, kh_ref[0], False),
        (7, last, top + 1, 3, kh_ref[last], False),
        (8, last + 1, top + 2, 3, below_ref[5], True),
    )
    for m, (n, k, er, g, kappa_slab, only_z) in enumerate(ends):
        level = (base + k).astype(jnp.float32)
        level_z = jnp.where(level >= 1.0, level + 1.0, HUGE)
        level_h = jnp.where(level >= 0.0, level, HUGE)
        mx = level_h < bmx
        my = level_h < bmy
        mz = level_z < bottom
        kappa = jnp.where(level_h < bottom, 0.25 * kappa_slab, 0.0)
        gx, gy, gz = [], [], []
        for tr in range(2):
            slab = epad[tr, er, rows]
            full = pad[tr, n, rows]
            gx.append(
                diff(
                    mx,
                    roll_lanes(jnp.where(lane == 0, east_patch(slab, g), full), -1),
                    roll_lanes(jnp.where(lane == 127, west_patch(slab, g), full), 1),
                )
            )
            gy.append(
                diff(
                    my,
                    pad[tr, n, PAD + 1 : PAD + 1 + lat],
                    pad[tr, n, PAD - 1 : PAD - 1 + lat],
                )
            )
            gz.append(diff(mz, pad[tr, n + 1, rows], pad[tr, n - 1, rows]))
        fx, fy, fz = flux_xyz(gx, gy, gz, kappa, not only_z)
        for tr in range(2):
            fze[tr, m] = fz[tr]
            if not only_z:
                fxs[tr, m - 1] = fx[tr]
                fys[tr, m - 1, rows] = fy[tr]

    def vertical_flux(tr, k):
        place = {-1: 0, 0: 1, last: 2, last + 1: 3}.get(k)
        return fz_ref[tr, k] if place is None else fze[tr, place]

    z = [None, None]
    for k in range(levels):
        level = (base + k).astype(jnp.float32)
        wet = level < bottom
        for tr in range(2):
            change = vertical_flux(tr, k + 1) - vertical_flux(tr, k - 1)
            if k == 0 or k == last:
                m, r, g, n = (0, 0, 0, 2) if k == 0 else (1, top, 3, 7)
                change = change + divergence(
                    fxs[tr, m], efx[tr, r], g, lane, fys, (tr, m), lat
                )
                start = pad[tr, n, rows]
            else:
                start = q_ref[tr, k]
            rhs = start + jnp.where(wet, change, 0.0)
            z[tr] = rhs * inv_ref[k]
            if k > 0:
                z[tr] = z[tr] + ei_ref[k] * y_ref[tr, k - 1]
            y_ref[tr, k] = z[tr]
    low = list(z)
    for k in range(last - 1, -1, -1):
        ratio = ratio_ref[k]
        for tr in range(2):
            z[tr] = y_ref[tr, k] + ratio * z[tr]
            y_ref[tr, k] = z[tr]
    m2_ref[2] = eff
    for tr in range(2):
        inner = share * jnp.where(upper, low[tr], z[tr])
        outer = jnp.where(upper, z[tr], low[tr])
        value = jnp.where(upper == low_pair, inner, outer - inner)
        m1_ref[tr] = z[tr]
        m1_ref[2 + tr] = low[tr]
        m2_ref[tr] = value
        m3_ref[tr] = value


def finish_kernel(
    y_ref, a_ref, bb_ref, own_ref, r1_ref, r2_ref, r3_ref, out_hbm, out, sems
):
    levels = y_ref.shape[1]
    me = lax.axis_index("dep")
    upper = lax.rem(me, 2) == 0
    low_pair = me < 2
    share, inv_t, eff = own_ref[0], own_ref[1], own_ref[2]
    middle = 1.0 / (eff + r2_ref[2])
    middle = jnp.where(low_pair, middle, -middle)
    tops, lows = [], []
    for tr in range(2):
        y_top, y_low = y_ref[tr, 0], y_ref[tr, levels - 1]
        p_top, p_low = r1_ref[tr], r1_ref[2 + tr]
        jump = jnp.where(upper, p_top - y_low, y_top - p_low)
        edge = jnp.where(
            low_pair, jnp.where(upper, p_low, y_low), jnp.where(upper, y_top, p_top)
        )
        edge = edge + jnp.where(low_pair, -share, share) * jump
        across = middle * (r2_ref[tr] + r3_ref[tr] - edge)
        inside = jump * inv_t + share * across
        tops.append(jnp.where(upper, jnp.where(low_pair, 0.0, across), inside))
        lows.append(jnp.where(upper, inside, jnp.where(low_pair, across, 0.0)))
    step = levels // GROUPS
    copies = []
    for part in range(GROUPS):
        for k in range(part * step, (part + 1) * step):
            a, b = a_ref[k], bb_ref[k]
            for tr in range(2):
                out[tr, k] = y_ref[tr, k] - tops[tr] * a + lows[tr] * b
        for tr in range(2):
            span = (tr, pl.ds(part * step, step))
            copies.append(
                pltpu.make_async_copy(out.at[span], out_hbm.at[span], sems.at[tr, part])
            )
            copies[-1].start()
    for copy in copies:
        copy.wait()


def per_device(tracers, u_east, v_north, kappa_h, kappa_v, bottom):
    _, levels, lat, lon = tracers.shape
    rows_e = levels // GROUPS
    lon_n, dep_n = lax.axis_size("lon"), lax.axis_size("dep")
    east = [(i, (i + 1) % lon_n) for i in range(lon_n)]
    west = [(t, s) for s, t in east]
    slab = lat * lon * 4
    slabs = lambda *lead: f32(*lead, lat, lon)
    work = lambda *lead: pltpu.VMEM(lead + (lat, lon), jnp.float32)
    padded = lambda *lead: pltpu.VMEM(lead + (lat + 2 * PAD, lon), jnp.float32)

    with jax.named_scope("pack"):
        sw, se, t0, t1, u, v = call(
            pack_kernel, (slabs(rows_e + 1),) * 2 + (slabs(levels),) * 4,
            [
                work(levels), pltpu.VMEM((lat, lon), jnp.int32), work(rows_e),
                pltpu.SemaphoreType.DMA((GROUPS, 4)), pltpu.SemaphoreType.DMA((2,)),
            ],
            (tracers, u_east, v_north, kappa_h, bottom), 10**6, 6 * levels * slab, 50.8,
            in_specs=[HBM] * 5,
        )
    with jax.named_scope("lon_halo"):
        r_east = lax.ppermute(sw, "lon", west)
        r_west = lax.ppermute(se, "lon", east)
    with jax.named_scope("advect_inner"):
        adv = call(
            advect_kernel, slabs(2, levels), [padded(2, 2 * rows_e), work(5, rows_e)],
            (t0, t1, u, v, bottom), 10**7, 7 * levels * slab, 16,
        )
    with jax.named_scope("factor"):
        inv, ei, ratio, a_end, b_end, abc = call(
            factor_kernel, (slabs(levels),) * 5 + (slabs(3),), [],
            (kappa_v, bottom), 10**7, 6 * levels * slab, 16,
        )
    with jax.named_scope("advect_edge"):
        ea, ek, eb, bmx, first, second = call(
            edge_kernel,
            (slabs(2, rows_e), slabs(rows_e), slabs(), slabs(), slabs(9), slabs(6)),
            [padded(2, 2 * rows_e), work(5, rows_e), work(4, rows_e), work(2, 6)],
            (sw, se, r_east, r_west, bottom, adv, kappa_h, abc), 10**6, 3 * levels * slab, 16,
        )
    swap = [(i, i ^ 1) for i in range(dep_n)]
    other = [(i, min(i + 1, dep_n - 1) if i % 2 else max(i - 1, 0)) for i in range(dep_n)]
    with jax.named_scope("dep_halo"):
        first = lax.ppermute(first, "dep", swap)
        second = lax.ppermute(second, "dep", other)
    with jax.named_scope("fluxes"):
        pe, q_part, fz = call(
            flux_kernel, (slabs(2, 6), slabs(2, levels), slabs(2, levels)),
            [
                padded(2, levels + 2), padded(2, rows_e + 2), work(2, rows_e),
                work(2, levels), work(2, levels), padded(2, levels),
            ],
            (adv, ea, ek, eb, bmx, bottom, kappa_h), 10**7, 10 * levels * slab, 24,
        )
    with jax.named_scope("solve"):
        y, m1, m2, m3, own = call(
            solve_kernel, (slabs(2, levels), slabs(4), slabs(3), slabs(2), slabs(3)),
            [
                padded(2, 10), padded(2, rows_e + 2), work(2, rows_e),
                work(2, 2), padded(2, 2), work(2, 4), work(2, 6),
            ],
            (pe, q_part, fz, ea, ek, eb, bmx, bottom, kappa_h, first, second, inv, ei, ratio, abc),
            10**7, 12 * levels * slab, 24,
        )
    with jax.named_scope("interfaces"):
        m3 = lax.ppermute(m3, "dep", [(i, i ^ 3) for i in range(dep_n)])
        m2 = lax.ppermute(m2, "dep", [(i, i ^ 2) for i in range(dep_n)])
        m1 = lax.ppermute(m1, "dep", swap)
    with jax.named_scope("finish"):
        return call(
            finish_kernel, slabs(2, levels),
            [work(2, levels), pltpu.SemaphoreType.DMA((2, GROUPS))],
            (y, a_end, b_end, own, m1, m2, m3), 10**6, 6 * levels * slab, 16,
            out_specs=HBM,
        )


def solution(mesh):
    in_specs = (
        P(None, "dep", None, "lon"),
        P("dep", None, "lon"),
        P("dep", None, "lon"),
        P("dep", None, "lon"),
        P("dep", None, "lon"),
        P(None, "lon"),
    )
    out_specs = P(None, "dep", None, "lon")
    return jax.shard_map(
        per_device, mesh=mesh, in_specs=in_specs, out_specs=out_specs, check_vma=False
    )
```

```python
import jax
import jax.numpy as jnp
from jax import lax
from jax.experimental import pallas as pl
from jax.experimental.pallas import tpu as pltpu
from jax.sharding import PartitionSpec as P

SUB = 4
THERMAL = 0.2
HALINE = 0.8
GROUPS = 4
STRIP = 32
CHUNK = 16
PAD = 8
HUGE = 1e30
MIB = 1024 * 1024

VMEM = pl.BlockSpec(memory_space=pltpu.VMEM)
HBM = pl.BlockSpec(memory_space=pltpu.HBM)


def lane_ids(rows):
    return lax.broadcasted_iota(jnp.int32, (rows, 128), 1)


def roll_lanes(x, amount):
    amount = amount % 128
    return x if amount == 0 else pltpu.roll(x, amount, 1)


def call(body, out_shape, scratch, args, flops, in_bytes, limit, in_specs=None, out_specs=None):
    return pl.pallas_call(
        body,
        out_shape=out_shape,
        in_specs=in_specs or [VMEM] * len(args),
        out_specs=out_specs or jax.tree.map(lambda _: VMEM, out_shape),
        scratch_shapes=scratch,
        compiler_params=pltpu.CompilerParams(vmem_limit_bytes=int(limit * MIB)),
        cost_estimate=pl.CostEstimate(flops=flops, bytes_accessed=in_bytes, transcendentals=0),
    )(*args)


def f32(*shape):
    return jax.ShapeDtypeStruct(shape, jnp.float32)


def pack_kernel(
    t_hbm, u_hbm, v_hbm, kh_hbm, b_hbm,
    sw_ref, se_ref, t0_ref, t1_ref, u_ref, v_ref,
    kh_buf, b_buf, first_buf, sems, more_sems,
):
    rows_e = u_ref.shape[0] // GROUPS
    lat = u_ref.shape[1]
    lane = lane_ids(lat)
    fields = ((t_hbm.at[0], t0_ref), (t_hbm.at[1], t1_ref), (u_hbm, u_ref), (v_hbm, v_ref))
    groups = [
        [
            pltpu.make_async_copy(
                src.at[pl.ds(g * rows_e, rows_e)], dst.at[pl.ds(g * rows_e, rows_e)], sems.at[g, n]
            )
            for n, (src, dst) in enumerate(fields)
        ]
        for g in range(GROUPS)
    ]
    tail = [
        pltpu.make_async_copy(b_hbm, b_buf, more_sems.at[0]),
        pltpu.make_async_copy(kh_hbm, kh_buf, more_sems.at[1]),
    ]
    for copy in sum(groups, []) + tail:
        copy.start()
    for g in range(GROUPS):
        for copy in groups[g]:
            copy.wait()
        for r in range(rows_e):
            level = g * rows_e + r
            slabs = (t0_ref[level], t1_ref[level], u_ref[level], v_ref[level])
            if g > 0:
                low, high = sw_ref[r], se_ref[r]
            for f, slab in enumerate(slabs):
                start = STRIP * g + 8 * f
                rolled = roll_lanes(slab, start)
                if start == 0:
                    first_buf[r] = rolled
                    low = rolled
                else:
                    low = jnp.where(lane >= start, rolled, low)
                    high = rolled if start == 8 else jnp.where(lane >= start - 8, rolled, high)
            if g == GROUPS - 1:
                high = jnp.where(lane >= 120, first_buf[r], high)
            sw_ref[r] = low
            se_ref[r] = high
    for copy in tail:
        copy.wait()
    low = jnp.zeros((lat, 128), jnp.float32)
    high = jnp.zeros((lat, 128), jnp.float32)
    bottom = b_buf[...].astype(jnp.float32)
    for g in range(GROUPS):
        for r in range(rows_e):
            place = STRIP * g + r
            rolled = roll_lanes(kh_buf[g * rows_e + r], place)
            low = jnp.where(lane == place, rolled, low)
            high = jnp.where(lane == (place - 1) % 128, rolled, high)
        place = STRIP * g + 16
        rolled = roll_lanes(bottom, place)
        low = jnp.where((lane >= place) & (lane < place + 8), rolled, low)
        high = jnp.where((lane >= place - 8) & (lane < place), rolled, high)
    sw_ref[rows_e] = low
    se_ref[rows_e] = high


def advect_block(slabs, get_c, get_u, get_v, get_level, bx, by, buf, coef, put):
    lat = bx.shape[0]
    for i, slab in enumerate(slabs):
        level = get_level(slab)
        um = jnp.where(level < bx, get_u(slab), 0.0)
        vm = jnp.where(level < by, get_v(slab), 0.0)
        uw = roll_lanes(um, 1)
        vs = pltpu.roll(vm, 1, 0)
        coef[0, i] = (
            1.0
            - jnp.maximum(um, 0.0)
            + jnp.minimum(uw, 0.0)
            - jnp.maximum(vm, 0.0)
            + jnp.minimum(vs, 0.0)
        )
        coef[1, i] = -jnp.minimum(um, 0.0)
        coef[2, i] = jnp.maximum(uw, 0.0)
        coef[3, i] = -jnp.minimum(vm, 0.0)
        coef[4, i] = jnp.maximum(vs, 0.0)
        for tr in range(2):
            buf[0, 2 * i + tr, PAD : PAD + lat] = get_c(tr, slab)
    for step in range(SUB):
        src, dst = step % 2, (step + 1) % 2
        for i, slab in enumerate(slabs):
            for j in range(0, lat, CHUNK):
                a = coef[0, i, j : j + CHUNK]
                b = coef[1, i, j : j + CHUNK]
                c = coef[2, i, j : j + CHUNK]
                d = coef[3, i, j : j + CHUNK]
                e = coef[4, i, j : j + CHUNK]
                for tr in range(2):
                    q = 2 * i + tr
                    here = buf[src, q, PAD + j : PAD + j + CHUNK]
                    north = buf[src, q, PAD + j + 1 : PAD + j + 1 + CHUNK]
                    south = buf[src, q, PAD + j - 1 : PAD + j - 1 + CHUNK]
                    new = (
                        a * here
                        + b * roll_lanes(here, -1)
                        + c * roll_lanes(here, 1)
                        + d * north
                        + e * south
                    )
                    if step < SUB - 1:
                        buf[dst, q, PAD + j : PAD + j + CHUNK] = new
                    else:
                        put(tr, slab, j, new)


def face_limits(bottom):
    lat = bottom.shape[0]
    rows = lax.broadcasted_iota(jnp.int32, bottom.shape, 0)
    north = jnp.where(rows == lat - 1, 0.0, pltpu.roll(bottom, lat - 1, 0))
    return jnp.minimum(bottom, roll_lanes(bottom, -1)), jnp.minimum(bottom, north)


def lat_limits(bottom):
    lat = bottom.shape[0]
    rows = lax.broadcasted_iota(jnp.int32, bottom.shape, 0)
    north = jnp.where(rows == lat - 1, 0.0, pltpu.roll(bottom, lat - 1, 0))
    south = jnp.where(rows == 0, 0.0, pltpu.roll(bottom, 1, 0))
    return jnp.minimum(north, south)


def clear_pads(ref, lat):
    lead = ref.shape[:-2]
    zero = jnp.zeros(lead + (PAD, 128), jnp.float32)
    ref[..., 0:PAD, :] = zero
    ref[..., PAD + lat : 2 * PAD + lat, :] = zero


def advect_kernel(t0_ref, t1_ref, u_ref, v_ref, b_ref, out_ref, buf, coef):
    levels, lat = out_ref.shape[1], out_ref.shape[2]
    base = lax.axis_index("dep") * levels
    block = coef.shape[1]
    clear_pads(buf, lat)
    bx, by = face_limits(b_ref[...].astype(jnp.float32))

    def body(n, _):
        slabs = [n * block + i for i in range(block)]

        def put(tr, slab, j, new):
            out_ref[tr, slab, j : j + CHUNK] = new

        advect_block(
            slabs,
            lambda tr, s: (t0_ref, t1_ref)[tr][s],
            lambda s: u_ref[s],
            lambda s: v_ref[s],
            lambda s: (base + s).astype(jnp.float32),
            bx,
            by,
            buf,
            coef,
            put,
        )
        return 0

    lax.fori_loop(0, levels // block, body, 0)


def join(lane_q, own_high, east, west, own_low):
    return jnp.where(
        lane_q < 16,
        jnp.where(lane_q < 8, own_high, east),
        jnp.where(lane_q < 24, west, own_low),
    )


def west_patch(slab, g):
    return roll_lanes(slab, -(STRIP * g + 24))


def east_patch(slab, g):
    return roll_lanes(slab, 120 - STRIP * g)


def patched(main, slab, g, lane):
    return jnp.where(
        lane < 4, west_patch(slab, g), jnp.where(lane >= 124, east_patch(slab, g), main)
    )


def edge_kernel(
    sw_ref, se_ref, re_ref, rw_ref, b_ref, adv_ref, kh_ref, abc_ref,
    ea_ref, ek_ref, eb_ref, bmx_ref, first_ref, second_ref,
    buf, coef, fields, pay,
):
    levels, lat = adv_ref.shape[1], adv_ref.shape[2]
    rows_e = levels // GROUPS
    me = lax.axis_index("dep")
    base = me * levels
    parity = lax.rem(me, 2)
    up_ref, down_ref = pay.at[1 - parity], pay.at[parity]
    lane = lane_ids(lat)
    lane_q = lane % STRIP
    clear_pads(buf, lat)
    bottom = b_ref[...].astype(jnp.float32)
    eb = join(
        lane_q,
        roll_lanes(se_ref[rows_e], -8),
        roll_lanes(re_ref[rows_e], -8),
        roll_lanes(rw_ref[rows_e], 8),
        roll_lanes(sw_ref[rows_e], 8),
    )
    eb_ref[...] = eb
    b_west = roll_lanes(jnp.where(lane == 127, west_patch(eb, 0), bottom), 1)
    b_east = roll_lanes(jnp.where(lane == 0, east_patch(eb, 0), bottom), -1)
    bmx_ref[...] = jnp.minimum(b_west, b_east)
    for r in range(rows_e):
        ek_ref[r] = jnp.where(
            lane_q < 16,
            roll_lanes(re_ref[rows_e], 8 - r),
            roll_lanes(rw_ref[rows_e], 24 - r),
        )
        for f in range(4):
            fields[f, r] = join(
                lane_q,
                roll_lanes(se_ref[r], 8 - 8 * f),
                roll_lanes(re_ref[r], 8 - 8 * f),
                roll_lanes(rw_ref[r], 24 - 8 * f),
                roll_lanes(sw_ref[r], 24 - 8 * f),
            )
    bx, by = face_limits(eb)
    level0 = (base + (lane // STRIP) * rows_e).astype(jnp.float32)

    def put(tr, slab, j, new):
        ea_ref[tr, slab, j : j + CHUNK] = new

    advect_block(
        list(range(rows_e)),
        lambda tr, s: fields[tr, s],
        lambda s: fields[2, s],
        lambda s: fields[3, s],
        lambda s: level0 + float(s),
        bx,
        by,
        buf,
        coef,
        put,
    )
    top = rows_e - 1
    for tr in range(2):
        up_ref[tr] = patched(adv_ref[tr, 0], ea_ref[tr, 0], 0, lane)
        up_ref[2 + tr] = patched(adv_ref[tr, 1], ea_ref[tr, 1], 0, lane)
        down_ref[tr] = patched(adv_ref[tr, levels - 1], ea_ref[tr, top], 3, lane)
        down_ref[2 + tr] = patched(adv_ref[tr, levels - 2], ea_ref[tr, top - 1], 3, lane)
    up_ref[4] = jnp.where(lane < STRIP, ea_ref[0, 0], roll_lanes(ea_ref[1, 0], STRIP))
    down_ref[4] = jnp.where(
        lane >= 3 * STRIP, ea_ref[0, top], roll_lanes(ea_ref[1, top], -STRIP)
    )
    up_ref[5] = kh_ref[0]
    down_ref[5] = kh_ref[levels - 1]
    first_ref[0:6] = pay[0]
    first_ref[6:9] = abc_ref[...]
    second_ref[...] = pay[1]


def slopes(gx, gy, gz):
    rx, ry, rz = (-0.5 * THERMAL * g[0] + 0.5 * HALINE * g[1] for g in (gx, gy, gz))
    scale = rz / (1.0 + rx * rx + ry * ry + rz * rz)
    return rx * scale, ry * scale


def flux_xyz(gx, gy, gz, kappa, need_xy=True):
    sx, sy = slopes(gx, gy, gz)
    kx, ky = kappa * sx, kappa * sy
    kz = kx * sx + ky * sy
    fz = [kx * gx[n] + ky * gy[n] + kz * gz[n] for n in range(2)]
    if not need_xy:
        return None, None, fz
    fx = [kappa * gx[n] + kx * gz[n] for n in range(2)]
    fy = [kappa * gy[n] + ky * gz[n] for n in range(2)]
    return fx, fy, fz


def flux_x_edge(gx, gy, gz, kappa):
    sx, _ = slopes(gx, gy, gz)
    kx = kappa * sx
    return [kappa * gx[n] + kx * gz[n] for n in range(2)]


def diff(mask, high, low):
    return jnp.where(mask, high - low, 0.0)


def edge_flux_row(r, epad, ek, eb, ebx, eby, level0, out_ref, lat):
    level = level0 + r
    mx = level < ebx
    my = level < eby
    mz = (level + 1.0 < eb) & (level >= 1.0)
    kappa = jnp.where((level < eb) & (level >= 0.0), 0.25 * ek, 0.0)
    rows = slice(PAD, PAD + lat)
    gx, gy, gz = [], [], []
    for tr in range(2):
        here = epad[tr, r + 1, rows]
        gx.append(diff(mx, roll_lanes(here, -1), roll_lanes(here, 1)))
        gy.append(
            diff(
                my,
                epad[tr, r + 1, PAD + 1 : PAD + 1 + lat],
                epad[tr, r + 1, PAD - 1 : PAD - 1 + lat],
            )
        )
        gz.append(diff(mz, epad[tr, r + 2, rows], epad[tr, r, rows]))
    fx = flux_x_edge(gx, gy, gz, kappa)
    for tr in range(2):
        out_ref[tr, r] = fx[tr]


def edge_limits(eb):
    return (
        jnp.minimum(roll_lanes(eb, 1), roll_lanes(eb, -1)),
        lat_limits(eb),
    )


def divergence(fx, slab, g, lane, fys, at, lat):
    east = roll_lanes(jnp.where(lane == 0, east_patch(slab, g), fx), -1)
    west = roll_lanes(jnp.where(lane == 127, west_patch(slab, g), fx), 1)
    north = fys[at + (slice(PAD + 1, PAD + 1 + lat),)]
    south = fys[at + (slice(PAD - 1, PAD - 1 + lat),)]
    return (east - west) + (north - south)


def flux_kernel(
    adv_ref, ea_ref, ek_ref, eb_ref, bmx_ref, b_ref, kh_ref,
    pe_ref, q_ref, fz_ref,
    pad, epad, efx, gxs, fxs, fys,
):
    levels, lat = adv_ref.shape[1], adv_ref.shape[2]
    rows_e = levels // GROUPS
    base = lax.axis_index("dep") * levels
    lane = lane_ids(lat)
    clear_pads(epad, lat)
    clear_pads(pad, lat)
    clear_pads(fys, lat)
    rows = slice(PAD, PAD + lat)
    eb = eb_ref[...]
    ebx, eby = edge_limits(eb)
    level0 = (base + (lane // STRIP) * rows_e).astype(jnp.float32)
    for tr in range(2):
        for r in range(rows_e):
            epad[tr, r + 1, rows] = ea_ref[tr, r]
        epad[tr, 0, rows] = roll_lanes(ea_ref[tr, rows_e - 1], STRIP)
        epad[tr, rows_e + 1, rows] = roll_lanes(ea_ref[tr, 0], -STRIP)
    for r in range(rows_e):
        edge_flux_row(r, epad, ek_ref[r], eb, ebx, eby, level0, efx, lat)

    bottom = b_ref[...].astype(jnp.float32)
    bmy = lat_limits(bottom)
    bmx = bmx_ref[...]

    for k in range(levels):
        g, r = divmod(k, rows_e)
        full, gx = [], []
        for tr in range(2):
            slab = ea_ref[tr, r]
            west, east = west_patch(slab, g), east_patch(slab, g)
            full.append(
                jnp.where(lane < 4, west, jnp.where(lane >= 124, east, adv_ref[tr, k]))
            )
            gx.append(
                roll_lanes(jnp.where(lane == 0, east, full[tr]), -1)
                - roll_lanes(jnp.where(lane == 127, west, full[tr]), 1)
            )
        for tr in range(2):
            pad[tr, k + 1, rows] = full[tr]
            gxs[tr, k] = gx[tr]
    for n, k in enumerate((0, 1, 2, levels - 3, levels - 2, levels - 1)):
        for tr in range(2):
            pe_ref[tr, n] = pad[tr, k + 1, rows]

    for k in range(levels):
        g, r = divmod(k, rows_e)
        level = (base + k).astype(jnp.float32)
        level_z = jnp.where(level >= 1.0, level + 1.0, HUGE)
        mx = level < bmx
        my = level < bmy
        mz = level_z < bottom
        kappa = jnp.where(level < bottom, 0.25 * kh_ref[k], 0.0)
        gx, gy, gz = [], [], []
        for tr in range(2):
            gx.append(jnp.where(mx, gxs[tr, k], 0.0))
            gy.append(
                diff(
                    my,
                    pad[tr, k + 1, PAD + 1 : PAD + 1 + lat],
                    pad[tr, k + 1, PAD - 1 : PAD - 1 + lat],
                )
            )
            gz.append(diff(mz, pad[tr, k + 2, rows], pad[tr, k, rows]))
        fx, fy, fz = flux_xyz(gx, gy, gz, kappa)
        for tr in range(2):
            fxs[tr, k] = fx[tr]
            fys[tr, k, rows] = fy[tr]
            fz_ref[tr, k] = fz[tr]

    for k in range(levels):
        g, r = divmod(k, rows_e)
        wet = (base + k).astype(jnp.float32) < bottom
        new = []
        for tr in range(2):
            change = divergence(fxs[tr, k], efx[tr, r], g, lane, fys, (tr, k), lat)
            new.append(pad[tr, k + 1, rows] + jnp.where(wet, change, 0.0))
        for tr in range(2):
            q_ref[tr, k] = new[tr]


def factor_kernel(kv_ref, b_ref, inv_ref, ei_ref, ratio_ref, a_ref, bb_ref, abc_ref):
    levels, lat = kv_ref.shape[0], kv_ref.shape[1]
    base = lax.axis_index("dep") * levels
    bottom = b_ref[...].astype(jnp.float32)

    def coupling(k):
        level = (base + k).astype(jnp.float32)
        level = jnp.where(level >= 1.0, level, HUGE)
        return jnp.where(level < bottom, kv_ref[k], 0.0)

    top = coupling(0)
    e = jnp.zeros((lat, 128), jnp.float32)
    q = e
    za = jnp.ones((lat, 128), jnp.float32)
    for k in range(levels):
        low = coupling(k + 1) if k + 1 < levels else jnp.zeros((lat, 128), jnp.float32)
        eq = 1.0 + e * q
        inv = 1.0 / (eq + low)
        inv_ref[k] = inv
        ei = e * inv
        ei_ref[k] = ei
        ratio_ref[k] = low * inv
        za = inv if k == 0 else za * ei
        a_ref[k] = za
        q = eq * inv
        e = low
    bb_ref[levels - 1] = inv
    b = inv
    a = za
    for k in range(levels - 2, -1, -1):
        ratio = ratio_ref[k]
        b = ratio * b
        a = a_ref[k] + ratio * a
        bb_ref[k] = b
        a_ref[k] = a
    abc_ref[0] = a + jnp.where(top > 0.0, 1.0 / jnp.maximum(top, 1e-30), HUGE)
    abc_ref[1] = inv
    abc_ref[2] = b


def solve_kernel(
    pe_ref, q_ref, fz_ref, ea_ref, ek_ref, eb_ref, bmx_ref, b_ref, kh_ref,
    first_ref, second_ref, inv_ref, ei_ref, ratio_ref, abc_ref,
    y_ref, m1_ref, m2_ref, m3_ref, own_ref,
    pad, epad, efx, fxs, fys, fze, halo,
):
    levels, lat = q_ref.shape[1], q_ref.shape[2]
    rows_e = levels // GROUPS
    last = levels - 1
    top = rows_e - 1
    me = lax.axis_index("dep")
    base = me * levels
    parity = lax.rem(me, 2)
    upper = parity == 0
    low_pair = me < 2
    lane = lane_ids(lat)
    rows = slice(PAD, PAD + lat)
    clear_pads(epad, lat)
    clear_pads(pad, lat)
    clear_pads(fys, lat)
    halo[0] = first_ref[0:6]
    halo[1] = second_ref[...]
    above_ref, below_ref = halo.at[1 - parity], halo.at[parity]

    b_u = jnp.where(upper, abc_ref[1], first_ref[7])
    a_l = jnp.where(upper, first_ref[6], abc_ref[0])
    a_u = jnp.where(upper, abc_ref[0], first_ref[6])
    b_l = jnp.where(upper, first_ref[7], abc_ref[1])
    inv_t = 1.0 / (b_u + a_l)
    c_pair = jnp.where(upper == low_pair, first_ref[8], abc_ref[2])
    share = c_pair * inv_t
    eff = jnp.where(low_pair, b_l, a_u) - c_pair * share
    own_ref[0] = share
    own_ref[1] = inv_t
    own_ref[2] = eff

    eb = eb_ref[...]
    ebx, eby = edge_limits(eb)
    level0 = (base + (lane // STRIP) * rows_e).astype(jnp.float32)
    for tr in range(2):
        pad[tr, 0, rows] = above_ref[2 + tr]
        pad[tr, 1, rows] = above_ref[tr]
        for n in range(6):
            pad[tr, n + 2, rows] = pe_ref[tr, n]
        pad[tr, 8, rows] = below_ref[tr]
        pad[tr, 9, rows] = below_ref[2 + tr]
        for r in range(rows_e):
            epad[tr, r + 1, rows] = ea_ref[tr, r]
        corner_up = above_ref[4] if tr == 0 else roll_lanes(above_ref[4], STRIP)
        corner_dn = below_ref[4] if tr == 0 else roll_lanes(below_ref[4], -STRIP)
        epad[tr, 0, rows] = roll_lanes(
            jnp.where(lane >= 3 * STRIP, corner_up, ea_ref[tr, top]), STRIP
        )
        epad[tr, rows_e + 1, rows] = roll_lanes(
            jnp.where(lane < STRIP, corner_dn, ea_ref[tr, 0]), -STRIP
        )
    edge_flux_row(0, epad, ek_ref[0], eb, ebx, eby, level0, efx, lat)
    edge_flux_row(top, epad, ek_ref[top], eb, ebx, eby, level0, efx, lat)

    bottom = b_ref[...].astype(jnp.float32)
    bmy = lat_limits(bottom)
    bmx = bmx_ref[...]
    ends = (
        (1, -1, 0, 0, above_ref[5], True),
        (2, 0, 1, 0, kh_ref[0], False),
        (7, last, top + 1, 3, kh_ref[last], False),
        (8, last + 1, top + 2, 3, below_ref[5], True),
    )
    for m, (n, k, er, g, kappa_slab, only_z) in enumerate(ends):
        level = (base + k).astype(jnp.float32)
        level_z = jnp.where(level >= 1.0, level + 1.0, HUGE)
        level_h = jnp.where(level >= 0.0, level, HUGE)
        mx = level_h < bmx
        my = level_h < bmy
        mz = level_z < bottom
        kappa = jnp.where(level_h < bottom, 0.25 * kappa_slab, 0.0)
        gx, gy, gz = [], [], []
        for tr in range(2):
            slab = epad[tr, er, rows]
            full = pad[tr, n, rows]
            gx.append(
                diff(
                    mx,
                    roll_lanes(jnp.where(lane == 0, east_patch(slab, g), full), -1),
                    roll_lanes(jnp.where(lane == 127, west_patch(slab, g), full), 1),
                )
            )
            gy.append(
                diff(
                    my,
                    pad[tr, n, PAD + 1 : PAD + 1 + lat],
                    pad[tr, n, PAD - 1 : PAD - 1 + lat],
                )
            )
            gz.append(diff(mz, pad[tr, n + 1, rows], pad[tr, n - 1, rows]))
        fx, fy, fz = flux_xyz(gx, gy, gz, kappa, not only_z)
        for tr in range(2):
            fze[tr, m] = fz[tr]
            if not only_z:
                fxs[tr, m - 1] = fx[tr]
                fys[tr, m - 1, rows] = fy[tr]

    def vertical_flux(tr, k):
        place = {-1: 0, 0: 1, last: 2, last + 1: 3}.get(k)
        return fz_ref[tr, k] if place is None else fze[tr, place]

    z = [None, None]
    for k in range(levels):
        level = (base + k).astype(jnp.float32)
        wet = level < bottom
        for tr in range(2):
            change = vertical_flux(tr, k + 1) - vertical_flux(tr, k - 1)
            if k == 0 or k == last:
                m, r, g, n = (0, 0, 0, 2) if k == 0 else (1, top, 3, 7)
                change = change + divergence(
                    fxs[tr, m], efx[tr, r], g, lane, fys, (tr, m), lat
                )
                start = pad[tr, n, rows]
            else:
                start = q_ref[tr, k]
            rhs = start + jnp.where(wet, change, 0.0)
            z[tr] = rhs * inv_ref[k]
            if k > 0:
                z[tr] = z[tr] + ei_ref[k] * y_ref[tr, k - 1]
            y_ref[tr, k] = z[tr]
    low = list(z)
    for k in range(last - 1, -1, -1):
        ratio = ratio_ref[k]
        for tr in range(2):
            z[tr] = y_ref[tr, k] + ratio * z[tr]
            y_ref[tr, k] = z[tr]
    m2_ref[2] = eff
    for tr in range(2):
        inner = share * jnp.where(upper, low[tr], z[tr])
        outer = jnp.where(upper, z[tr], low[tr])
        value = jnp.where(upper == low_pair, inner, outer - inner)
        m1_ref[tr] = z[tr]
        m1_ref[2 + tr] = low[tr]
        m2_ref[tr] = value
        m3_ref[tr] = value


def finish_kernel(
    y_ref, a_ref, bb_ref, own_ref, r1_ref, r2_ref, r3_ref, out_hbm, out, sems
):
    levels = y_ref.shape[1]
    me = lax.axis_index("dep")
    upper = lax.rem(me, 2) == 0
    low_pair = me < 2
    share, inv_t, eff = own_ref[0], own_ref[1], own_ref[2]
    middle = 1.0 / (eff + r2_ref[2])
    middle = jnp.where(low_pair, middle, -middle)
    tops, lows = [], []
    for tr in range(2):
        y_top, y_low = y_ref[tr, 0], y_ref[tr, levels - 1]
        p_top, p_low = r1_ref[tr], r1_ref[2 + tr]
        jump = jnp.where(upper, p_top - y_low, y_top - p_low)
        edge = jnp.where(
            low_pair, jnp.where(upper, p_low, y_low), jnp.where(upper, y_top, p_top)
        )
        edge = edge + jnp.where(low_pair, -share, share) * jump
        across = middle * (r2_ref[tr] + r3_ref[tr] - edge)
        inside = jump * inv_t + share * across
        tops.append(jnp.where(upper, jnp.where(low_pair, 0.0, across), inside))
        lows.append(jnp.where(upper, inside, jnp.where(low_pair, across, 0.0)))
    step = levels // GROUPS
    copies = []
    for part in range(GROUPS):
        for k in range(part * step, (part + 1) * step):
            a, b = a_ref[k], bb_ref[k]
            for tr in range(2):
                out[tr, k] = y_ref[tr, k] - tops[tr] * a + lows[tr] * b
        for tr in range(2):
            span = (tr, pl.ds(part * step, step))
            copies.append(
                pltpu.make_async_copy(out.at[span], out_hbm.at[span], sems.at[tr, part])
            )
            copies[-1].start()
    for copy in copies:
        copy.wait()


def per_device(tracers, u_east, v_north, kappa_h, kappa_v, bottom):
    _, levels, lat, lon = tracers.shape
    rows_e = levels // GROUPS
    lon_n, dep_n = lax.axis_size("lon"), lax.axis_size("dep")
    east = [(i, (i + 1) % lon_n) for i in range(lon_n)]
    west = [(t, s) for s, t in east]
    slab = lat * lon * 4
    slabs = lambda *lead: f32(*lead, lat, lon)
    work = lambda *lead: pltpu.VMEM(lead + (lat, lon), jnp.float32)
    padded = lambda *lead: pltpu.VMEM(lead + (lat + 2 * PAD, lon), jnp.float32)

    with jax.named_scope("pack"):
        sw, se, t0, t1, u, v = call(
            pack_kernel, (slabs(rows_e + 1),) * 2 + (slabs(levels),) * 4,
            [
                work(levels), pltpu.VMEM((lat, lon), jnp.int32), work(rows_e),
                pltpu.SemaphoreType.DMA((GROUPS, 4)), pltpu.SemaphoreType.DMA((2,)),
            ],
            (tracers, u_east, v_north, kappa_h, bottom), 10**6, 6 * levels * slab, 50.8,
            in_specs=[HBM] * 5,
        )
    with jax.named_scope("lon_halo"):
        r_east = lax.ppermute(sw, "lon", west)
        r_west = lax.ppermute(se, "lon", east)
    with jax.named_scope("advect_inner"):
        adv = call(
            advect_kernel, slabs(2, levels), [padded(2, 2 * rows_e), work(5, rows_e)],
            (t0, t1, u, v, bottom), 10**7, 7 * levels * slab, 16,
        )
    with jax.named_scope("factor"):
        inv, ei, ratio, a_end, b_end, abc = call(
            factor_kernel, (slabs(levels),) * 5 + (slabs(3),), [],
            (kappa_v, bottom), 10**7, 6 * levels * slab, 16,
        )
    with jax.named_scope("advect_edge"):
        ea, ek, eb, bmx, first, second = call(
            edge_kernel,
            (slabs(2, rows_e), slabs(rows_e), slabs(), slabs(), slabs(9), slabs(6)),
            [padded(2, 2 * rows_e), work(5, rows_e), work(4, rows_e), work(2, 6)],
            (sw, se, r_east, r_west, bottom, adv, kappa_h, abc), 10**6, 3 * levels * slab, 16,
        )
    swap = [(i, i ^ 1) for i in range(dep_n)]
    other = [(i, min(i + 1, dep_n - 1) if i % 2 else max(i - 1, 0)) for i in range(dep_n)]
    with jax.named_scope("dep_halo"):
        first = lax.ppermute(first, "dep", swap)
        second = lax.ppermute(second, "dep", other)
    with jax.named_scope("fluxes"):
        pe, q_part, fz = call(
            flux_kernel, (slabs(2, 6), slabs(2, levels), slabs(2, levels)),
            [
                padded(2, levels + 2), padded(2, rows_e + 2), work(2, rows_e),
                work(2, levels), work(2, levels), padded(2, levels),
            ],
            (adv, ea, ek, eb, bmx, bottom, kappa_h), 10**7, 10 * levels * slab, 24,
        )
    with jax.named_scope("solve"):
        y, m1, m2, m3, own = call(
            solve_kernel, (slabs(2, levels), slabs(4), slabs(3), slabs(2), slabs(3)),
            [
                padded(2, 10), padded(2, rows_e + 2), work(2, rows_e),
                work(2, 2), padded(2, 2), work(2, 4), work(2, 6),
            ],
            (pe, q_part, fz, ea, ek, eb, bmx, bottom, kappa_h, first, second, inv, ei, ratio, abc),
            10**7, 12 * levels * slab, 24,
        )
    with jax.named_scope("interfaces"):
        m1 = lax.ppermute(m1, "dep", swap)
        m2 = lax.ppermute(m2, "dep", [(i, i ^ 2) for i in range(dep_n)])
        m3 = lax.ppermute(m3, "dep", [(i, i ^ 3) for i in range(dep_n)])
    with jax.named_scope("finish"):
        return call(
            finish_kernel, slabs(2, levels),
            [work(2, levels), pltpu.SemaphoreType.DMA((2, GROUPS))],
            (y, a_end, b_end, own, m1, m2, m3), 10**6, 6 * levels * slab, 16,
            out_specs=HBM,
        )


def solution(mesh):
    in_specs = (
        P(None, "dep", None, "lon"),
        P("dep", None, "lon"),
        P("dep", None, "lon"),
        P("dep", None, "lon"),
        P("dep", None, "lon"),
        P(None, "lon"),
    )
    out_specs = P(None, "dep", None, "lon")
    return jax.shard_map(
        per_device, mesh=mesh, in_specs=in_specs, out_specs=out_specs, check_vma=False
    )
```

```python
import jax
import jax.numpy as jnp
from jax import lax
from jax.experimental import pallas as pl
from jax.experimental.pallas import tpu as pltpu
from jax.sharding import PartitionSpec as P

SUB = 4
THERMAL = 0.2
HALINE = 0.8
GROUPS = 4
STRIP = 32
HUGE = 1e30
MIB = 1024 * 1024

VMEM = pl.BlockSpec(memory_space=pltpu.VMEM)
HBM = pl.BlockSpec(memory_space=pltpu.HBM)


def lane_ids(rows):
    return lax.broadcasted_iota(jnp.int32, (rows, 128), 1)


def roll_lanes(x, amount):
    amount = amount % 128
    return x if amount == 0 else pltpu.roll(x, amount, 1)


def shift_north(x):
    return jnp.concatenate([x[8:], pltpu.roll(x[:8], 7, 0)], axis=0)


def shift_south(x):
    return jnp.concatenate([pltpu.roll(x[-8:], 1, 0), x[:-8]], axis=0)


def rows_of(ref, v, *lead):
    return ref[(*lead, pl.ds(v, 8, ref.shape[-2] // 8), slice(None))]


def slab_of(ref, *lead):
    return jnp.concatenate([rows_of(ref, v, *lead) for v in range(ref.shape[-2] // 8)], axis=0)


def call(body, out_shape, scratch, args, flops, in_bytes, limit, in_specs=None, out_specs=None):
    return pl.pallas_call(
        body,
        out_shape=out_shape,
        in_specs=in_specs or [VMEM] * len(args),
        out_specs=out_specs or jax.tree.map(lambda _: VMEM, out_shape),
        scratch_shapes=scratch,
        compiler_params=pltpu.CompilerParams(vmem_limit_bytes=int(limit * MIB)),
        cost_estimate=pl.CostEstimate(flops=flops, bytes_accessed=in_bytes, transcendentals=0),
    )(*args)


def f32(*shape):
    return jax.ShapeDtypeStruct(shape, jnp.float32)


def pack_kernel(
    t_hbm, u_hbm, v_hbm, kh_hbm, b_hbm,
    sw_ref, se_ref, t0_ref, t1_ref, u_ref, v_ref,
    kh_buf, b_buf, first_buf, sems, more_sems,
):
    rows_e = u_ref.shape[0] // GROUPS
    lat = u_ref.shape[1]
    lane = lane_ids(lat)
    fields = ((t_hbm.at[0], t0_ref), (t_hbm.at[1], t1_ref), (u_hbm, u_ref), (v_hbm, v_ref))
    groups = [
        [
            pltpu.make_async_copy(
                src.at[pl.ds(g * rows_e, rows_e)], dst.at[pl.ds(g * rows_e, rows_e)], sems.at[g, n]
            )
            for n, (src, dst) in enumerate(fields)
        ]
        for g in range(GROUPS)
    ]
    tail = [
        pltpu.make_async_copy(b_hbm, b_buf, more_sems.at[0]),
        pltpu.make_async_copy(kh_hbm, kh_buf, more_sems.at[1]),
    ]
    for copy in sum(groups, []) + tail:
        copy.start()
    for g in range(GROUPS):
        for copy in groups[g]:
            copy.wait()
        for r in range(rows_e):
            level = g * rows_e + r
            slabs = [slab_of(ref, level) for ref in (t0_ref, t1_ref, u_ref, v_ref)]
            if g > 0:
                low, high = sw_ref[r], se_ref[r]
            for f, slab in enumerate(slabs):
                start = STRIP * g + 8 * f
                rolled = roll_lanes(slab, start)
                if start == 0:
                    first_buf[r] = rolled
                    low = rolled
                else:
                    low = jnp.where(lane >= start, rolled, low)
                    high = rolled if start == 8 else jnp.where(lane >= start - 8, rolled, high)
            if g == GROUPS - 1:
                high = jnp.where(lane >= 120, first_buf[r], high)
            sw_ref[r] = low
            se_ref[r] = high
    for copy in tail:
        copy.wait()
    low = jnp.zeros((lat, 128), jnp.float32)
    high = jnp.zeros((lat, 128), jnp.float32)
    bottom = slab_of(b_buf).astype(jnp.float32)
    for g in range(GROUPS):
        for r in range(rows_e):
            place = STRIP * g + r
            rolled = roll_lanes(slab_of(kh_buf, g * rows_e + r), place)
            low = jnp.where(lane == place, rolled, low)
            high = jnp.where(lane == (place - 1) % 128, rolled, high)
        place = STRIP * g + 16
        rolled = roll_lanes(bottom, place)
        low = jnp.where((lane >= place) & (lane < place + 8), rolled, low)
        high = jnp.where((lane >= place - 8) & (lane < place), rolled, high)
    sw_ref[rows_e] = low
    se_ref[rows_e] = high


def advect_block(slabs, get_c, get_u, get_v, get_level, bx, by, buf, coef, put):
    regs = bx.shape[0] // 8
    for i, slab in enumerate(slabs):
        level = get_level(slab)
        um = jnp.where(level < bx, get_u(slab), 0.0)
        vm = jnp.where(level < by, get_v(slab), 0.0)
        uw = roll_lanes(um, 1)
        vs = shift_south(vm)
        coef[0, i] = (
            1.0
            - jnp.maximum(um, 0.0)
            + jnp.minimum(uw, 0.0)
            - jnp.maximum(vm, 0.0)
            + jnp.minimum(vs, 0.0)
        )
        coef[1, i] = -jnp.minimum(um, 0.0)
        coef[2, i] = jnp.maximum(uw, 0.0)
        coef[3, i] = -jnp.minimum(vm, 0.0)
        coef[4, i] = jnp.maximum(vs, 0.0)
        for tr in range(2):
            buf[0, 2 * i + tr] = get_c(tr, slab)
    for step in range(SUB):
        src, dst = step % 2, (step + 1) % 2
        for i, slab in enumerate(slabs):
            now = [
                [buf[src, 2 * i + tr, 8 * v : 8 * v + 8] for v in range(regs)] for tr in range(2)
            ]
            for v in range(regs):
                js = slice(8 * v, 8 * v + 8)
                a, b, c, d, e = (coef[n, i, js] for n in range(5))
                for tr in range(2):
                    here = now[tr][v]
                    north = now[tr][v + 1] if v + 1 < regs else pltpu.roll(now[tr][0], 7, 0)
                    south = now[tr][v - 1] if v > 0 else pltpu.roll(now[tr][regs - 1], 1, 0)
                    new = (
                        a * here
                        + b * roll_lanes(here, -1)
                        + c * roll_lanes(here, 1)
                        + d * north
                        + e * south
                    )
                    if step < SUB - 1:
                        buf[dst, 2 * i + tr, js] = new
                    else:
                        put(tr, slab, js, new)


def face_limits(bottom):
    lat = bottom.shape[0]
    rows = lax.broadcasted_iota(jnp.int32, bottom.shape, 0)
    north = jnp.where(rows == lat - 1, 0.0, shift_north(bottom))
    return jnp.minimum(bottom, roll_lanes(bottom, -1)), jnp.minimum(bottom, north)


def lat_limits(bottom):
    lat = bottom.shape[0]
    rows = lax.broadcasted_iota(jnp.int32, bottom.shape, 0)
    north = jnp.where(rows == lat - 1, 0.0, shift_north(bottom))
    south = jnp.where(rows == 0, 0.0, shift_south(bottom))
    return jnp.minimum(north, south)


def advect_kernel(t0_ref, t1_ref, u_ref, v_ref, b_ref, out_ref, buf, coef):
    levels, lat = out_ref.shape[1], out_ref.shape[2]
    base = lax.axis_index("dep") * levels
    block = coef.shape[1]
    bx, by = face_limits(slab_of(b_ref).astype(jnp.float32))

    def body(n, _):
        slabs = [n * block + i for i in range(block)]

        def put(tr, slab, js, new):
            out_ref[tr, slab, js] = new

        advect_block(
            slabs,
            lambda tr, s: slab_of((t0_ref, t1_ref)[tr], s),
            lambda s: slab_of(u_ref, s),
            lambda s: slab_of(v_ref, s),
            lambda s: (base + s).astype(jnp.float32),
            bx,
            by,
            buf,
            coef,
            put,
        )
        return 0

    lax.fori_loop(0, levels // block, body, 0)


def join(lane_q, own_high, east, west, own_low):
    return jnp.where(
        lane_q < 16,
        jnp.where(lane_q < 8, own_high, east),
        jnp.where(lane_q < 24, west, own_low),
    )


def west_patch(slab, g):
    return roll_lanes(slab, -(STRIP * g + 24))


def east_patch(slab, g):
    return roll_lanes(slab, 120 - STRIP * g)


def patched(main, slab, g, lane):
    return jnp.where(
        lane < 4, west_patch(slab, g), jnp.where(lane >= 124, east_patch(slab, g), main)
    )


def edge_kernel(
    sw_ref, se_ref, re_ref, rw_ref, b_ref, adv_ref, kh_ref, abc_ref,
    ea_ref, ek_ref, eb_ref, bmx_ref, first_ref, second_ref,
    buf, coef, fields, pay,
):
    levels, lat = adv_ref.shape[1], adv_ref.shape[2]
    rows_e = levels // GROUPS
    me = lax.axis_index("dep")
    base = me * levels
    parity = lax.rem(me, 2)
    up_ref, down_ref = pay.at[1 - parity], pay.at[parity]
    lane = lane_ids(lat)
    lane_q = lane % STRIP
    bottom = slab_of(b_ref).astype(jnp.float32)
    eb = join(
        lane_q,
        roll_lanes(se_ref[rows_e], -8),
        roll_lanes(re_ref[rows_e], -8),
        roll_lanes(rw_ref[rows_e], 8),
        roll_lanes(sw_ref[rows_e], 8),
    )
    eb_ref[...] = eb
    b_west = roll_lanes(jnp.where(lane == 127, west_patch(eb, 0), bottom), 1)
    b_east = roll_lanes(jnp.where(lane == 0, east_patch(eb, 0), bottom), -1)
    bmx_ref[...] = jnp.minimum(b_west, b_east)
    for r in range(rows_e):
        ek_ref[r] = jnp.where(
            lane_q < 16,
            roll_lanes(re_ref[rows_e], 8 - r),
            roll_lanes(rw_ref[rows_e], 24 - r),
        )
        for f in range(4):
            fields[f, r] = join(
                lane_q,
                roll_lanes(se_ref[r], 8 - 8 * f),
                roll_lanes(re_ref[r], 8 - 8 * f),
                roll_lanes(rw_ref[r], 24 - 8 * f),
                roll_lanes(sw_ref[r], 24 - 8 * f),
            )
    bx, by = face_limits(eb)
    level0 = (base + (lane // STRIP) * rows_e).astype(jnp.float32)

    def put(tr, slab, js, new):
        ea_ref[tr, slab, js] = new

    advect_block(
        list(range(rows_e)),
        lambda tr, s: fields[tr, s],
        lambda s: fields[2, s],
        lambda s: fields[3, s],
        lambda s: level0 + float(s),
        bx,
        by,
        buf,
        coef,
        put,
    )
    top = rows_e - 1
    for tr in range(2):
        up_ref[tr] = patched(adv_ref[tr, 0], ea_ref[tr, 0], 0, lane)
        up_ref[2 + tr] = patched(adv_ref[tr, 1], ea_ref[tr, 1], 0, lane)
        down_ref[tr] = patched(adv_ref[tr, levels - 1], ea_ref[tr, top], 3, lane)
        down_ref[2 + tr] = patched(adv_ref[tr, levels - 2], ea_ref[tr, top - 1], 3, lane)
    up_ref[4] = jnp.where(lane < STRIP, ea_ref[0, 0], roll_lanes(ea_ref[1, 0], STRIP))
    down_ref[4] = jnp.where(
        lane >= 3 * STRIP, ea_ref[0, top], roll_lanes(ea_ref[1, top], -STRIP)
    )
    up_ref[5] = slab_of(kh_ref, 0)
    down_ref[5] = slab_of(kh_ref, levels - 1)
    first_ref[0:6] = pay[0]
    first_ref[6:9] = abc_ref[...]
    second_ref[...] = pay[1]


def slopes(gx, gy, gz):
    rx, ry, rz = (-0.5 * THERMAL * g[0] + 0.5 * HALINE * g[1] for g in (gx, gy, gz))
    scale = rz / (1.0 + rx * rx + ry * ry + rz * rz)
    return rx * scale, ry * scale


def flux_xyz(gx, gy, gz, kappa, need_xy=True):
    sx, sy = slopes(gx, gy, gz)
    kx, ky = kappa * sx, kappa * sy
    kz = kx * sx + ky * sy
    fz = [kx * gx[n] + ky * gy[n] + kz * gz[n] for n in range(2)]
    if not need_xy:
        return None, None, fz
    fx = [kappa * gx[n] + kx * gz[n] for n in range(2)]
    fy = [kappa * gy[n] + ky * gz[n] for n in range(2)]
    return fx, fy, fz


def flux_x_edge(gx, gy, gz, kappa):
    sx, _ = slopes(gx, gy, gz)
    kx = kappa * sx
    return [kappa * gx[n] + kx * gz[n] for n in range(2)]


def diff(mask, high, low):
    return jnp.where(mask, high - low, 0.0)


def edge_flux_row(r, rows, ek, eb, ebx, eby, level0, out_ref):
    level = level0 + r
    mx = level < ebx
    my = level < eby
    mz = (level + 1.0 < eb) & (level >= 1.0)
    kappa = jnp.where((level < eb) & (level >= 0.0), 0.25 * ek, 0.0)
    gx, gy, gz = [], [], []
    for tr in range(2):
        here = rows[tr, r + 1]
        gx.append(diff(mx, roll_lanes(here, -1), roll_lanes(here, 1)))
        gy.append(diff(my, shift_north(here), shift_south(here)))
        gz.append(diff(mz, rows[tr, r + 2], rows[tr, r]))
    fx = flux_x_edge(gx, gy, gz, kappa)
    for tr in range(2):
        out_ref[tr, r] = fx[tr]


def edge_limits(eb):
    return (
        jnp.minimum(roll_lanes(eb, 1), roll_lanes(eb, -1)),
        lat_limits(eb),
    )


def zonal_change(fx, west, east, lane):
    return roll_lanes(jnp.where(lane == 0, east, fx), -1) - roll_lanes(
        jnp.where(lane == 127, west, fx), 1
    )


def divergence(fx, fy, slab, g, lane):
    return zonal_change(fx, west_patch(slab, g), east_patch(slab, g), lane) + (
        shift_north(fy) - shift_south(fy)
    )


def flux_kernel(
    adv_ref, ea_ref, ek_ref, eb_ref, bmx_ref, b_ref, kh_ref,
    pe_ref, q_ref, fz_ref,
    full, rows, efx, gxs, limits,
):
    levels, lat = adv_ref.shape[1], adv_ref.shape[2]
    rows_e = levels // GROUPS
    regs = lat // 8
    base = lax.axis_index("dep") * levels
    lane = lane_ids(lat)
    lane8 = lane_ids(8)
    eb = eb_ref[...]
    ebx, eby = edge_limits(eb)
    level0 = (base + (lane // STRIP) * rows_e).astype(jnp.float32)
    for tr in range(2):
        for r in range(rows_e):
            rows[tr, r + 1] = ea_ref[tr, r]
        rows[tr, 0] = roll_lanes(ea_ref[tr, rows_e - 1], STRIP)
        rows[tr, rows_e + 1] = roll_lanes(ea_ref[tr, 0], -STRIP)
    for r in range(rows_e):
        edge_flux_row(r, rows, ek_ref[r], eb, ebx, eby, level0, efx)

    bottom = slab_of(b_ref).astype(jnp.float32)
    limits[0] = bmx_ref[...]
    limits[1] = lat_limits(bottom)
    limits[2] = bottom

    def patch(r, _):
        for g in range(GROUPS):
            k = g * rows_e + r
            for v in range(regs):
                js = slice(8 * v, 8 * v + 8)
                for tr in range(2):
                    slab = ea_ref[tr, r, js]
                    west, east = west_patch(slab, g), east_patch(slab, g)
                    main = jnp.where(
                        lane8 < 4, west, jnp.where(lane8 >= 124, east, adv_ref[tr, k, js])
                    )
                    full[tr, k + 1, js] = main
                    gxs[tr, k, js] = zonal_change(main, west, east, lane8)
        return 0

    lax.fori_loop(0, rows_e, patch, 0)
    for n, k in enumerate((0, 1, 2, levels - 3, levels - 2, levels - 1)):
        for tr in range(2):
            pe_ref[tr, n] = full[tr, k + 1]

    def fluxes(r, _):
        for g in range(GROUPS):
            k = g * rows_e + r
            level = (base + k).astype(jnp.float32)
            level_z = jnp.where(level >= 1.0, level + 1.0, HUGE)
            change, fys = [[], []], [[], []]
            for v in range(regs):
                js = slice(8 * v, 8 * v + 8)
                mx = level < limits[0, js]
                my = level < limits[1, js]
                mz = level_z < limits[2, js]
                kappa = jnp.where(level < limits[2, js], 0.25 * rows_of(kh_ref, v, k), 0.0)
                gx, gy, gz = [], [], []
                for tr in range(2):
                    if v + 1 < regs:
                        north = full[tr, k + 1, 8 * v + 8 : 8 * v + 16]
                    else:
                        north = pltpu.roll(full[tr, k + 1, 0:8], 7, 0)
                    if v > 0:
                        south = full[tr, k + 1, 8 * v - 8 : 8 * v]
                    else:
                        south = pltpu.roll(full[tr, k + 1, lat - 8 : lat], 1, 0)
                    gx.append(jnp.where(mx, gxs[tr, k, js], 0.0))
                    gy.append(diff(my, north, south))
                    gz.append(diff(mz, full[tr, k + 2, js], full[tr, k, js]))
                fx, fy, fz = flux_xyz(gx, gy, gz, kappa)
                for tr in range(2):
                    slab = efx[tr, r, js]
                    change[tr].append(
                        zonal_change(fx[tr], west_patch(slab, g), east_patch(slab, g), lane8)
                    )
                    fys[tr].append(fy[tr])
                    fz_ref[tr, k, js] = fz[tr]
            for v in range(regs):
                js = slice(8 * v, 8 * v + 8)
                wet = level < limits[2, js]
                for tr in range(2):
                    fy = fys[tr]
                    north = fy[v + 1] if v + 1 < regs else pltpu.roll(fy[0], 7, 0)
                    south = fy[v - 1] if v > 0 else pltpu.roll(fy[regs - 1], 1, 0)
                    total = change[tr][v] + (north - south)
                    q_ref[tr, k, js] = full[tr, k + 1, js] + jnp.where(wet, total, 0.0)
        return 0

    lax.fori_loop(0, rows_e, fluxes, 0)


def factor_kernel(kv_ref, b_ref, inv_ref, ei_ref, ratio_ref, a_ref, bb_ref, abc_ref):
    levels, lat = kv_ref.shape[0], kv_ref.shape[1]
    base = lax.axis_index("dep") * levels
    bottom = slab_of(b_ref).astype(jnp.float32)

    def coupling(k):
        level = (base + k).astype(jnp.float32)
        level = jnp.where(level >= 1.0, level, HUGE)
        return jnp.where(level < bottom, slab_of(kv_ref, k), 0.0)

    top = coupling(0)
    e = jnp.zeros((lat, 128), jnp.float32)
    q = e
    za = jnp.ones((lat, 128), jnp.float32)
    for k in range(levels):
        low = coupling(k + 1) if k + 1 < levels else jnp.zeros((lat, 128), jnp.float32)
        eq = 1.0 + e * q
        inv = 1.0 / (eq + low)
        inv_ref[k] = inv
        ei = e * inv
        ei_ref[k] = ei
        ratio_ref[k] = low * inv
        za = inv if k == 0 else za * ei
        a_ref[k] = za
        q = eq * inv
        e = low
    bb_ref[levels - 1] = inv
    b = inv
    a = za
    for k in range(levels - 2, -1, -1):
        ratio = ratio_ref[k]
        b = ratio * b
        a = a_ref[k] + ratio * a
        bb_ref[k] = b
        a_ref[k] = a
    abc_ref[0] = a + jnp.where(top > 0.0, 1.0 / jnp.maximum(top, 1e-30), HUGE)
    abc_ref[1] = inv
    abc_ref[2] = b


def solve_kernel(
    pe_ref, q_ref, fz_ref, ea_ref, ek_ref, eb_ref, bmx_ref, b_ref, kh_ref,
    first_ref, second_ref, inv_ref, ei_ref, ratio_ref, abc_ref,
    y_ref, m1_ref, m2_ref, m3_ref, own_ref,
    pad, epad, efx, fze, halo,
):
    levels, lat = q_ref.shape[1], q_ref.shape[2]
    rows_e = levels // GROUPS
    last = levels - 1
    top = rows_e - 1
    me = lax.axis_index("dep")
    base = me * levels
    parity = lax.rem(me, 2)
    upper = parity == 0
    low_pair = me < 2
    lane = lane_ids(lat)
    halo[0] = first_ref[0:6]
    halo[1] = second_ref[...]
    above_ref, below_ref = halo.at[1 - parity], halo.at[parity]

    b_u = jnp.where(upper, abc_ref[1], first_ref[7])
    a_l = jnp.where(upper, first_ref[6], abc_ref[0])
    a_u = jnp.where(upper, abc_ref[0], first_ref[6])
    b_l = jnp.where(upper, first_ref[7], abc_ref[1])
    inv_t = 1.0 / (b_u + a_l)
    c_pair = jnp.where(upper == low_pair, first_ref[8], abc_ref[2])
    share = c_pair * inv_t
    eff = jnp.where(low_pair, b_l, a_u) - c_pair * share
    own_ref[0] = share
    own_ref[1] = inv_t
    own_ref[2] = eff

    eb = eb_ref[...]
    ebx, eby = edge_limits(eb)
    level0 = (base + (lane // STRIP) * rows_e).astype(jnp.float32)
    for tr in range(2):
        pad[tr, 0] = above_ref[2 + tr]
        pad[tr, 1] = above_ref[tr]
        for n in range(6):
            pad[tr, n + 2] = pe_ref[tr, n]
        pad[tr, 8] = below_ref[tr]
        pad[tr, 9] = below_ref[2 + tr]
        for r in range(rows_e):
            epad[tr, r + 1] = ea_ref[tr, r]
        corner_up = above_ref[4] if tr == 0 else roll_lanes(above_ref[4], STRIP)
        corner_dn = below_ref[4] if tr == 0 else roll_lanes(below_ref[4], -STRIP)
        epad[tr, 0] = roll_lanes(
            jnp.where(lane >= 3 * STRIP, corner_up, ea_ref[tr, top]), STRIP
        )
        epad[tr, rows_e + 1] = roll_lanes(
            jnp.where(lane < STRIP, corner_dn, ea_ref[tr, 0]), -STRIP
        )
    edge_flux_row(0, epad, ek_ref[0], eb, ebx, eby, level0, efx)
    edge_flux_row(top, epad, ek_ref[top], eb, ebx, eby, level0, efx)

    bottom = slab_of(b_ref).astype(jnp.float32)
    bmy = lat_limits(bottom)
    bmx = bmx_ref[...]
    ends = (
        (1, -1, 0, 0, above_ref[5], True),
        (2, 0, 1, 0, slab_of(kh_ref, 0), False),
        (7, last, top + 1, 3, slab_of(kh_ref, last), False),
        (8, last + 1, top + 2, 3, below_ref[5], True),
    )
    spread = {}
    for m, (n, k, er, g, kappa_slab, only_z) in enumerate(ends):
        level = (base + k).astype(jnp.float32)
        level_z = jnp.where(level >= 1.0, level + 1.0, HUGE)
        level_h = jnp.where(level >= 0.0, level, HUGE)
        mx = level_h < bmx
        my = level_h < bmy
        mz = level_z < bottom
        kappa = jnp.where(level_h < bottom, 0.25 * kappa_slab, 0.0)
        gx, gy, gz = [], [], []
        for tr in range(2):
            slab, main = epad[tr, er], pad[tr, n]
            change = zonal_change(main, west_patch(slab, g), east_patch(slab, g), lane)
            gx.append(jnp.where(mx, change, 0.0))
            gy.append(diff(my, shift_north(main), shift_south(main)))
            gz.append(diff(mz, pad[tr, n + 1], pad[tr, n - 1]))
        fx, fy, fz = flux_xyz(gx, gy, gz, kappa, not only_z)
        for tr in range(2):
            fze[tr, m] = fz[tr]
            if not only_z:
                spread[k, tr] = divergence(fx[tr], fy[tr], efx[tr, er - 1], g, lane)

    def vertical_flux(tr, k):
        place = {-1: 0, 0: 1, last: 2, last + 1: 3}.get(k)
        return fz_ref[tr, k] if place is None else fze[tr, place]

    z = [None, None]
    for k in range(levels):
        level = (base + k).astype(jnp.float32)
        wet = level < bottom
        for tr in range(2):
            change = vertical_flux(tr, k + 1) - vertical_flux(tr, k - 1)
            if k == 0 or k == last:
                change = change + spread[k, tr]
                start = pad[tr, 2 if k == 0 else 7]
            else:
                start = q_ref[tr, k]
            rhs = start + jnp.where(wet, change, 0.0)
            z[tr] = rhs * inv_ref[k]
            if k > 0:
                z[tr] = z[tr] + ei_ref[k] * y_ref[tr, k - 1]
            y_ref[tr, k] = z[tr]
    low = list(z)
    for k in range(last - 1, -1, -1):
        ratio = ratio_ref[k]
        for tr in range(2):
            z[tr] = y_ref[tr, k] + ratio * z[tr]
            y_ref[tr, k] = z[tr]
    m2_ref[2] = eff
    for tr in range(2):
        inner = share * jnp.where(upper, low[tr], z[tr])
        outer = jnp.where(upper, z[tr], low[tr])
        value = jnp.where(upper == low_pair, inner, outer - inner)
        m1_ref[tr] = z[tr]
        m1_ref[2 + tr] = low[tr]
        m2_ref[tr] = value
        m3_ref[tr] = value


def finish_kernel(
    y_ref, a_ref, bb_ref, own_ref, r1_ref, r2_ref, r3_ref, out_hbm, out, sems
):
    levels = y_ref.shape[1]
    me = lax.axis_index("dep")
    upper = lax.rem(me, 2) == 0
    low_pair = me < 2
    share, inv_t, eff = own_ref[0], own_ref[1], own_ref[2]
    middle = 1.0 / (eff + r2_ref[2])
    middle = jnp.where(low_pair, middle, -middle)
    tops, lows = [], []
    for tr in range(2):
        y_top, y_low = y_ref[tr, 0], y_ref[tr, levels - 1]
        p_top, p_low = r1_ref[tr], r1_ref[2 + tr]
        jump = jnp.where(upper, p_top - y_low, y_top - p_low)
        edge = jnp.where(
            low_pair, jnp.where(upper, p_low, y_low), jnp.where(upper, y_top, p_top)
        )
        edge = edge + jnp.where(low_pair, -share, share) * jump
        across = middle * (r2_ref[tr] + r3_ref[tr] - edge)
        inside = jump * inv_t + share * across
        tops.append(jnp.where(upper, jnp.where(low_pair, 0.0, across), inside))
        lows.append(jnp.where(upper, inside, jnp.where(low_pair, across, 0.0)))
    step, regs = levels // GROUPS, y_ref.shape[2] // 8
    copies = []
    for part in range(GROUPS):
        for k in range(part * step, (part + 1) * step):
            a, b = a_ref[k], bb_ref[k]
            for tr in range(2):
                new = y_ref[tr, k] - tops[tr] * a + lows[tr] * b
                for v in range(regs):
                    out[tr, k, pl.ds(v, 8, regs), :] = new[8 * v : 8 * v + 8]
        for tr in range(2):
            span = (tr, pl.ds(part * step, step))
            copies.append(
                pltpu.make_async_copy(out.at[span], out_hbm.at[span], sems.at[tr, part])
            )
            copies[-1].start()
    for copy in copies:
        copy.wait()


def per_device(tracers, u_east, v_north, kappa_h, kappa_v, bottom):
    _, levels, lat, lon = tracers.shape
    rows_e = levels // GROUPS
    lon_n, dep_n = lax.axis_size("lon"), lax.axis_size("dep")
    east = [(i, (i + 1) % lon_n) for i in range(lon_n)]
    west = [(t, s) for s, t in east]
    slab = lat * lon * 4
    slabs = lambda *lead: f32(*lead, lat, lon)
    work = lambda *lead: pltpu.VMEM(lead + (lat, lon), jnp.float32)

    with jax.named_scope("pack"):
        sw, se, t0, t1, u, v = call(
            pack_kernel, (slabs(rows_e + 1),) * 2 + (slabs(levels),) * 4,
            [
                work(levels), pltpu.VMEM((lat, lon), jnp.int32), work(rows_e),
                pltpu.SemaphoreType.DMA((GROUPS, 4)), pltpu.SemaphoreType.DMA((2,)),
            ],
            (tracers, u_east, v_north, kappa_h, bottom), 10**6, 6 * levels * slab, 50.8,
            in_specs=[HBM] * 5,
        )
    with jax.named_scope("lon_halo"):
        r_east = lax.ppermute(sw, "lon", west)
        r_west = lax.ppermute(se, "lon", east)
    with jax.named_scope("advect_inner"):
        adv = call(
            advect_kernel, slabs(2, levels), [work(2, 2 * rows_e), work(5, rows_e)],
            (t0, t1, u, v, bottom), 10**7, 7 * levels * slab, 16,
        )
    with jax.named_scope("factor"):
        inv, ei, ratio, a_end, b_end, abc = call(
            factor_kernel, (slabs(levels),) * 5 + (slabs(3),), [],
            (kappa_v, bottom), 10**7, 6 * levels * slab, 16,
        )
    with jax.named_scope("advect_edge"):
        ea, ek, eb, bmx, first, second = call(
            edge_kernel,
            (slabs(2, rows_e), slabs(rows_e), slabs(), slabs(), slabs(9), slabs(6)),
            [work(2, 2 * rows_e), work(5, rows_e), work(4, rows_e), work(2, 6)],
            (sw, se, r_east, r_west, bottom, adv, kappa_h, abc), 10**6, 3 * levels * slab, 16,
        )
    swap = [(i, i ^ 1) for i in range(dep_n)]
    other = [(i, min(i + 1, dep_n - 1) if i % 2 else max(i - 1, 0)) for i in range(dep_n)]
    with jax.named_scope("dep_halo"):
        first = lax.ppermute(first, "dep", swap)
        second = lax.ppermute(second, "dep", other)
    with jax.named_scope("fluxes"):
        pe, q_part, fz = call(
            flux_kernel, (slabs(2, 6), slabs(2, levels), slabs(2, levels)),
            [
                work(2, levels + 2), work(2, rows_e + 2), work(2, rows_e),
                work(2, levels), work(3),
            ],
            (adv, ea, ek, eb, bmx, bottom, kappa_h), 10**7, 10 * levels * slab, 24,
        )
    with jax.named_scope("solve"):
        y, m1, m2, m3, own = call(
            solve_kernel, (slabs(2, levels), slabs(4), slabs(3), slabs(2), slabs(3)),
            [
                work(2, 10), work(2, rows_e + 2), work(2, rows_e), work(2, 4), work(2, 6),
            ],
            (pe, q_part, fz, ea, ek, eb, bmx, bottom, kappa_h, first, second, inv, ei, ratio, abc),
            10**7, 12 * levels * slab, 24,
        )
    with jax.named_scope("interfaces"):
        m3 = lax.ppermute(m3, "dep", [(i, i ^ 3) for i in range(dep_n)])
        m2 = lax.ppermute(m2, "dep", [(i, i ^ 2) for i in range(dep_n)])
        m1 = lax.ppermute(m1, "dep", swap)
    with jax.named_scope("finish"):
        return call(
            finish_kernel, slabs(2, levels),
            [work(2, levels), pltpu.SemaphoreType.DMA((2, GROUPS))],
            (y, a_end, b_end, own, m1, m2, m3), 10**6, 6 * levels * slab, 16,
            out_specs=HBM,
        )


def solution(mesh):
    in_specs = (
        P(None, "dep", None, "lon"),
        P("dep", None, "lon"),
        P("dep", None, "lon"),
        P("dep", None, "lon"),
        P("dep", None, "lon"),
        P(None, "lon"),
    )
    out_specs = P(None, "dep", None, "lon")
    return jax.shard_map(
        per_device, mesh=mesh, in_specs=in_specs, out_specs=out_specs, check_vma=False
    )
```

```python
import jax
import jax.numpy as jnp
from jax import lax
from jax.experimental import pallas as pl
from jax.experimental.pallas import tpu as pltpu
from jax.sharding import PartitionSpec as P

SUB = 4
THERMAL = 0.2
HALINE = 0.8
GROUPS = 4
STRIP = 32
HUGE = 1e30
MIB = 1024 * 1024

VMEM = pl.BlockSpec(memory_space=pltpu.VMEM)
HBM = pl.BlockSpec(memory_space=pltpu.HBM)


def lane_ids(rows):
    return lax.broadcasted_iota(jnp.int32, (rows, 128), 1)


def roll_lanes(x, amount):
    amount = amount % 128
    return x if amount == 0 else pltpu.roll(x, amount, 1)


def shift_north(x):
    return jnp.concatenate([x[8:], pltpu.roll(x[:8], 7, 0)], axis=0)


def shift_south(x):
    return jnp.concatenate([pltpu.roll(x[-8:], 1, 0), x[:-8]], axis=0)


def rows_of(ref, v, *lead):
    return ref[(*lead, pl.ds(v, 8, ref.shape[-2] // 8), slice(None))]


def neighbours(regs, v):
    north = regs[v + 1] if v + 1 < len(regs) else pltpu.roll(regs[0], 7, 0)
    south = regs[v - 1] if v > 0 else pltpu.roll(regs[-1], 1, 0)
    return north, south


def slab_of(ref, *lead):
    return jnp.concatenate([rows_of(ref, v, *lead) for v in range(ref.shape[-2] // 8)], axis=0)


def call(body, out_shape, scratch, args, flops, in_bytes, limit, in_specs=None, out_specs=None):
    return pl.pallas_call(
        body,
        out_shape=out_shape,
        in_specs=in_specs or [VMEM] * len(args),
        out_specs=out_specs or jax.tree.map(lambda _: VMEM, out_shape),
        scratch_shapes=scratch,
        compiler_params=pltpu.CompilerParams(vmem_limit_bytes=int(limit * MIB)),
        cost_estimate=pl.CostEstimate(flops=flops, bytes_accessed=in_bytes, transcendentals=0),
    )(*args)


def f32(*shape):
    return jax.ShapeDtypeStruct(shape, jnp.float32)


def pack_kernel(
    t_hbm, u_hbm, v_hbm, kh_hbm, b_hbm,
    sw_ref, se_ref, t0_ref, t1_ref, u_ref, v_ref,
    kh_buf, b_buf, first_buf, sems, more_sems,
):
    rows_e = u_ref.shape[0] // GROUPS
    lat = u_ref.shape[1]
    lane = lane_ids(lat)
    fields = ((t_hbm.at[0], t0_ref), (t_hbm.at[1], t1_ref), (u_hbm, u_ref), (v_hbm, v_ref))
    groups = [
        [
            pltpu.make_async_copy(
                src.at[pl.ds(g * rows_e, rows_e)], dst.at[pl.ds(g * rows_e, rows_e)], sems.at[g, n]
            )
            for n, (src, dst) in enumerate(fields)
        ]
        for g in range(GROUPS)
    ]
    tail = [
        pltpu.make_async_copy(b_hbm, b_buf, more_sems.at[0]),
        pltpu.make_async_copy(kh_hbm, kh_buf, more_sems.at[1]),
    ]
    for copy in sum(groups, []) + tail:
        copy.start()
    for g in range(GROUPS):
        for copy in groups[g]:
            copy.wait()
        for r in range(rows_e):
            level = g * rows_e + r
            slabs = [slab_of(ref, level) for ref in (t0_ref, t1_ref, u_ref, v_ref)]
            if g > 0:
                low, high = sw_ref[r], se_ref[r]
            for f, slab in enumerate(slabs):
                start = STRIP * g + 8 * f
                rolled = roll_lanes(slab, start)
                if start == 0:
                    first_buf[r] = rolled
                    low = rolled
                else:
                    low = jnp.where(lane >= start, rolled, low)
                    high = rolled if start == 8 else jnp.where(lane >= start - 8, rolled, high)
            if g == GROUPS - 1:
                high = jnp.where(lane >= 120, first_buf[r], high)
            sw_ref[r] = low
            se_ref[r] = high
    for copy in tail:
        copy.wait()
    low = jnp.zeros((lat, 128), jnp.float32)
    high = jnp.zeros((lat, 128), jnp.float32)
    bottom = slab_of(b_buf).astype(jnp.float32)
    for g in range(GROUPS):
        for r in range(rows_e):
            place = STRIP * g + r
            rolled = roll_lanes(slab_of(kh_buf, g * rows_e + r), place)
            low = jnp.where(lane == place, rolled, low)
            high = jnp.where(lane == (place - 1) % 128, rolled, high)
        place = STRIP * g + 16
        rolled = roll_lanes(bottom, place)
        low = jnp.where((lane >= place) & (lane < place + 8), rolled, low)
        high = jnp.where((lane >= place - 8) & (lane < place), rolled, high)
    sw_ref[rows_e] = low
    se_ref[rows_e] = high


def advect_block(slabs, get_c, get_u, get_v, get_level, bx, by, buf, coef, put):
    regs = bx.shape[0] // 8
    for i, slab in enumerate(slabs):
        level = get_level(slab)
        um = jnp.where(level < bx, get_u(slab), 0.0)
        vm = jnp.where(level < by, get_v(slab), 0.0)
        uw = roll_lanes(um, 1)
        vs = shift_south(vm)
        coef[0, i] = (
            1.0
            - jnp.maximum(um, 0.0)
            + jnp.minimum(uw, 0.0)
            - jnp.maximum(vm, 0.0)
            + jnp.minimum(vs, 0.0)
        )
        coef[1, i] = -jnp.minimum(um, 0.0)
        coef[2, i] = jnp.maximum(uw, 0.0)
        coef[3, i] = -jnp.minimum(vm, 0.0)
        coef[4, i] = jnp.maximum(vs, 0.0)
        for tr in range(2):
            buf[0, 2 * i + tr] = get_c(tr, slab)
    for step in range(SUB):
        src, dst = step % 2, (step + 1) % 2
        for i, slab in enumerate(slabs):
            now = [
                [buf[src, 2 * i + tr, 8 * v : 8 * v + 8] for v in range(regs)] for tr in range(2)
            ]
            for v in range(regs):
                js = slice(8 * v, 8 * v + 8)
                a, b, c, d, e = (coef[n, i, js] for n in range(5))
                for tr in range(2):
                    here = now[tr][v]
                    north, south = neighbours(now[tr], v)
                    new = (
                        a * here
                        + b * roll_lanes(here, -1)
                        + c * roll_lanes(here, 1)
                        + d * north
                        + e * south
                    )
                    if step < SUB - 1:
                        buf[dst, 2 * i + tr, js] = new
                    else:
                        put(tr, slab, js, new)


def face_limits(bottom):
    lat = bottom.shape[0]
    rows = lax.broadcasted_iota(jnp.int32, bottom.shape, 0)
    north = jnp.where(rows == lat - 1, 0.0, shift_north(bottom))
    return jnp.minimum(bottom, roll_lanes(bottom, -1)), jnp.minimum(bottom, north)


def lat_limits(bottom):
    lat = bottom.shape[0]
    rows = lax.broadcasted_iota(jnp.int32, bottom.shape, 0)
    north = jnp.where(rows == lat - 1, 0.0, shift_north(bottom))
    south = jnp.where(rows == 0, 0.0, shift_south(bottom))
    return jnp.minimum(north, south)


def advect_kernel(t0_ref, t1_ref, u_ref, v_ref, b_ref, out_ref, buf, coef):
    levels, lat = out_ref.shape[1], out_ref.shape[2]
    base = lax.axis_index("dep") * levels
    block = coef.shape[1]
    bx, by = face_limits(slab_of(b_ref).astype(jnp.float32))

    def body(n, _):
        slabs = [n * block + i for i in range(block)]

        def put(tr, slab, js, new):
            out_ref[tr, slab, js] = new

        advect_block(
            slabs,
            lambda tr, s: slab_of((t0_ref, t1_ref)[tr], s),
            lambda s: slab_of(u_ref, s),
            lambda s: slab_of(v_ref, s),
            lambda s: (base + s).astype(jnp.float32),
            bx,
            by,
            buf,
            coef,
            put,
        )
        return 0

    lax.fori_loop(0, levels // block, body, 0)


def join(lane_q, own_high, east, west, own_low):
    return jnp.where(
        lane_q < 16,
        jnp.where(lane_q < 8, own_high, east),
        jnp.where(lane_q < 24, west, own_low),
    )


def west_patch(slab, g):
    return roll_lanes(slab, -(STRIP * g + 24))


def east_patch(slab, g):
    return roll_lanes(slab, 120 - STRIP * g)


def patched(main, slab, g, lane):
    return jnp.where(
        lane < 4, west_patch(slab, g), jnp.where(lane >= 124, east_patch(slab, g), main)
    )


def edge_kernel(
    sw_ref, se_ref, re_ref, rw_ref, b_ref, adv_ref, kh_ref, abc_ref,
    ea_ref, ek_ref, eb_ref, bmx_ref, first_ref, second_ref,
    buf, coef, fields, pay,
):
    levels, lat = adv_ref.shape[1], adv_ref.shape[2]
    rows_e = levels // GROUPS
    me = lax.axis_index("dep")
    base = me * levels
    parity = lax.rem(me, 2)
    up_ref, down_ref = pay.at[1 - parity], pay.at[parity]
    lane = lane_ids(lat)
    lane_q = lane % STRIP
    bottom = slab_of(b_ref).astype(jnp.float32)
    eb = join(
        lane_q,
        roll_lanes(se_ref[rows_e], -8),
        roll_lanes(re_ref[rows_e], -8),
        roll_lanes(rw_ref[rows_e], 8),
        roll_lanes(sw_ref[rows_e], 8),
    )
    eb_ref[...] = eb
    b_west = roll_lanes(jnp.where(lane == 127, west_patch(eb, 0), bottom), 1)
    b_east = roll_lanes(jnp.where(lane == 0, east_patch(eb, 0), bottom), -1)
    bmx_ref[...] = jnp.minimum(b_west, b_east)
    for r in range(rows_e):
        ek_ref[r] = jnp.where(
            lane_q < 16,
            roll_lanes(re_ref[rows_e], 8 - r),
            roll_lanes(rw_ref[rows_e], 24 - r),
        )
        for f in range(4):
            fields[f, r] = join(
                lane_q,
                roll_lanes(se_ref[r], 8 - 8 * f),
                roll_lanes(re_ref[r], 8 - 8 * f),
                roll_lanes(rw_ref[r], 24 - 8 * f),
                roll_lanes(sw_ref[r], 24 - 8 * f),
            )
    bx, by = face_limits(eb)
    level0 = (base + (lane // STRIP) * rows_e).astype(jnp.float32)

    def put(tr, slab, js, new):
        ea_ref[tr, slab, js] = new

    advect_block(
        list(range(rows_e)),
        lambda tr, s: fields[tr, s],
        lambda s: fields[2, s],
        lambda s: fields[3, s],
        lambda s: level0 + float(s),
        bx,
        by,
        buf,
        coef,
        put,
    )
    top = rows_e - 1
    for tr in range(2):
        up_ref[tr] = patched(adv_ref[tr, 0], ea_ref[tr, 0], 0, lane)
        up_ref[2 + tr] = patched(adv_ref[tr, 1], ea_ref[tr, 1], 0, lane)
        down_ref[tr] = patched(adv_ref[tr, levels - 1], ea_ref[tr, top], 3, lane)
        down_ref[2 + tr] = patched(adv_ref[tr, levels - 2], ea_ref[tr, top - 1], 3, lane)
    up_ref[4] = jnp.where(lane < STRIP, ea_ref[0, 0], roll_lanes(ea_ref[1, 0], STRIP))
    down_ref[4] = jnp.where(
        lane >= 3 * STRIP, ea_ref[0, top], roll_lanes(ea_ref[1, top], -STRIP)
    )
    up_ref[5] = slab_of(kh_ref, 0)
    down_ref[5] = slab_of(kh_ref, levels - 1)
    first_ref[0:6] = pay[0]
    first_ref[6:9] = abc_ref[...]
    second_ref[...] = pay[1]


def slopes(gx, gy, gz):
    rx, ry, rz = (-0.5 * THERMAL * g[0] + 0.5 * HALINE * g[1] for g in (gx, gy, gz))
    scale = rz / (1.0 + rx * rx + ry * ry + rz * rz)
    return rx * scale, ry * scale


def flux_xyz(gx, gy, gz, kappa, need_xy=True):
    sx, sy = slopes(gx, gy, gz)
    kx, ky = kappa * sx, kappa * sy
    kz = kx * sx + ky * sy
    fz = [kx * gx[n] + ky * gy[n] + kz * gz[n] for n in range(2)]
    if not need_xy:
        return None, None, fz
    fx = [kappa * gx[n] + kx * gz[n] for n in range(2)]
    fy = [kappa * gy[n] + ky * gz[n] for n in range(2)]
    return fx, fy, fz


def flux_x_edge(gx, gy, gz, kappa):
    sx, _ = slopes(gx, gy, gz)
    kx = kappa * sx
    return [kappa * gx[n] + kx * gz[n] for n in range(2)]


def diff(mask, high, low):
    return jnp.where(mask, high - low, 0.0)


def edge_flux_row(r, rows, ek, eb, ebx, eby, level0, out_ref):
    level = level0 + r
    mx = level < ebx
    my = level < eby
    mz = (level + 1.0 < eb) & (level >= 1.0)
    kappa = jnp.where((level < eb) & (level >= 0.0), 0.25 * ek, 0.0)
    gx, gy, gz = [], [], []
    for tr in range(2):
        here = rows[tr, r + 1]
        gx.append(diff(mx, roll_lanes(here, -1), roll_lanes(here, 1)))
        gy.append(diff(my, shift_north(here), shift_south(here)))
        gz.append(diff(mz, rows[tr, r + 2], rows[tr, r]))
    fx = flux_x_edge(gx, gy, gz, kappa)
    for tr in range(2):
        out_ref[tr, r] = fx[tr]


def edge_limits(eb):
    return (
        jnp.minimum(roll_lanes(eb, 1), roll_lanes(eb, -1)),
        lat_limits(eb),
    )


def zonal_change(fx, west, east, lane):
    return roll_lanes(jnp.where(lane == 0, east, fx), -1) - roll_lanes(
        jnp.where(lane == 127, west, fx), 1
    )


def divergence(fx, fy, slab, g, lane):
    return zonal_change(fx, west_patch(slab, g), east_patch(slab, g), lane) + (
        shift_north(fy) - shift_south(fy)
    )


def flux_kernel(
    adv_ref, ea_ref, ek_ref, eb_ref, bmx_ref, b_ref, kh_ref,
    pe_ref, q_ref, fz_ref,
    full, rows, efx, gxs, limits,
):
    levels, lat = adv_ref.shape[1], adv_ref.shape[2]
    rows_e = levels // GROUPS
    regs = lat // 8
    base = lax.axis_index("dep") * levels
    lane = lane_ids(lat)
    lane8 = lane_ids(8)
    eb = eb_ref[...]
    ebx, eby = edge_limits(eb)
    level0 = (base + (lane // STRIP) * rows_e).astype(jnp.float32)
    for tr in range(2):
        for r in range(rows_e):
            rows[tr, r + 1] = ea_ref[tr, r]
        rows[tr, 0] = roll_lanes(ea_ref[tr, rows_e - 1], STRIP)
        rows[tr, rows_e + 1] = roll_lanes(ea_ref[tr, 0], -STRIP)
    for r in range(rows_e):
        edge_flux_row(r, rows, ek_ref[r], eb, ebx, eby, level0, efx)

    bottom = slab_of(b_ref).astype(jnp.float32)
    limits[0] = bmx_ref[...]
    limits[1] = lat_limits(bottom)
    limits[2] = bottom

    def patch(r, _):
        for pair in range(0, GROUPS, 2):
            found = []
            for g in (pair, pair + 1):
                k = g * rows_e + r
                for tr in range(2):
                    slab = ea_ref[tr, r]
                    west, east = west_patch(slab, g), east_patch(slab, g)
                    main = jnp.where(
                        lane < 4, west, jnp.where(lane >= 124, east, adv_ref[tr, k])
                    )
                    found.append((tr, k, main, zonal_change(main, west, east, lane)))
            for tr, k, main, change in found:
                full[tr, k + 1] = main
                gxs[tr, k] = change
        return 0

    lax.fori_loop(0, rows_e, patch, 0)
    for n, k in enumerate((0, 1, 2, levels - 3, levels - 2, levels - 1)):
        for tr in range(2):
            pe_ref[tr, n] = full[tr, k + 1]

    def fluxes(r, _):
        for g in range(GROUPS):
            k = g * rows_e + r
            level = (base + k).astype(jnp.float32)
            level_z = jnp.where(level >= 1.0, level + 1.0, HUGE)
            here = [[full[tr, k + 1, 8 * v : 8 * v + 8] for v in range(regs)] for tr in range(2)]
            change, fys, fzs = [[], []], [[], []], [[], []]
            for v in range(regs):
                js = slice(8 * v, 8 * v + 8)
                mx = level < limits[0, js]
                my = level < limits[1, js]
                mz = level_z < limits[2, js]
                kappa = jnp.where(level < limits[2, js], 0.25 * rows_of(kh_ref, v, k), 0.0)
                gx, gy, gz = [], [], []
                for tr in range(2):
                    gx.append(jnp.where(mx, gxs[tr, k, js], 0.0))
                    gy.append(diff(my, *neighbours(here[tr], v)))
                    gz.append(diff(mz, full[tr, k + 2, js], full[tr, k, js]))
                fx, fy, fz = flux_xyz(gx, gy, gz, kappa)
                for tr in range(2):
                    slab = efx[tr, r, js]
                    change[tr].append(
                        zonal_change(fx[tr], west_patch(slab, g), east_patch(slab, g), lane8)
                    )
                    fys[tr].append(fy[tr])
                    fzs[tr].append(fz[tr])
            for v in range(regs):
                wet = level < limits[2, 8 * v : 8 * v + 8]
                for tr in range(2):
                    north, south = neighbours(fys[tr], v)
                    total = change[tr][v] + (north - south)
                    change[tr][v] = here[tr][v] + jnp.where(wet, total, 0.0)
            for v in range(regs):
                js = slice(8 * v, 8 * v + 8)
                for tr in range(2):
                    q_ref[tr, k, js] = change[tr][v]
                    fz_ref[tr, k, js] = fzs[tr][v]
        return 0

    lax.fori_loop(0, rows_e, fluxes, 0)


def factor_kernel(kv_ref, b_ref, inv_ref, ei_ref, ratio_ref, a_ref, bb_ref, abc_ref):
    levels, lat = kv_ref.shape[0], kv_ref.shape[1]
    base = lax.axis_index("dep") * levels
    bottom = slab_of(b_ref).astype(jnp.float32)

    def coupling(k):
        level = (base + k).astype(jnp.float32)
        level = jnp.where(level >= 1.0, level, HUGE)
        return jnp.where(level < bottom, slab_of(kv_ref, k), 0.0)

    top = coupling(0)
    e = jnp.zeros((lat, 128), jnp.float32)
    q = e
    za = jnp.ones((lat, 128), jnp.float32)
    for k in range(levels):
        low = coupling(k + 1) if k + 1 < levels else jnp.zeros((lat, 128), jnp.float32)
        eq = 1.0 + e * q
        inv = 1.0 / (eq + low)
        inv_ref[k] = inv
        ei = e * inv
        ei_ref[k] = ei
        ratio_ref[k] = low * inv
        za = inv if k == 0 else za * ei
        a_ref[k] = za
        q = eq * inv
        e = low
    bb_ref[levels - 1] = inv
    b = inv
    a = za
    for k in range(levels - 2, -1, -1):
        ratio = ratio_ref[k]
        b = ratio * b
        a = a_ref[k] + ratio * a
        bb_ref[k] = b
        a_ref[k] = a
    abc_ref[0] = a + jnp.where(top > 0.0, 1.0 / jnp.maximum(top, 1e-30), HUGE)
    abc_ref[1] = inv
    abc_ref[2] = b


def solve_kernel(
    pe_ref, q_ref, fz_ref, ea_ref, ek_ref, eb_ref, bmx_ref, b_ref, kh_ref,
    first_ref, second_ref, inv_ref, ei_ref, ratio_ref, abc_ref,
    y_ref, m1_ref, m2_ref, m3_ref, own_ref,
    pad, epad, efx, fze, halo,
):
    levels, lat = q_ref.shape[1], q_ref.shape[2]
    rows_e = levels // GROUPS
    last = levels - 1
    top = rows_e - 1
    me = lax.axis_index("dep")
    base = me * levels
    parity = lax.rem(me, 2)
    upper = parity == 0
    low_pair = me < 2
    lane = lane_ids(lat)
    halo[0] = first_ref[0:6]
    halo[1] = second_ref[...]
    above_ref, below_ref = halo.at[1 - parity], halo.at[parity]

    b_u = jnp.where(upper, abc_ref[1], first_ref[7])
    a_l = jnp.where(upper, first_ref[6], abc_ref[0])
    a_u = jnp.where(upper, abc_ref[0], first_ref[6])
    b_l = jnp.where(upper, first_ref[7], abc_ref[1])
    inv_t = 1.0 / (b_u + a_l)
    c_pair = jnp.where(upper == low_pair, first_ref[8], abc_ref[2])
    share = c_pair * inv_t
    eff = jnp.where(low_pair, b_l, a_u) - c_pair * share
    own_ref[0] = share
    own_ref[1] = inv_t
    own_ref[2] = eff

    eb = eb_ref[...]
    ebx, eby = edge_limits(eb)
    level0 = (base + (lane // STRIP) * rows_e).astype(jnp.float32)
    for tr in range(2):
        pad[tr, 0] = above_ref[2 + tr]
        pad[tr, 1] = above_ref[tr]
        for n in range(6):
            pad[tr, n + 2] = pe_ref[tr, n]
        pad[tr, 8] = below_ref[tr]
        pad[tr, 9] = below_ref[2 + tr]
        for r in range(rows_e):
            epad[tr, r + 1] = ea_ref[tr, r]
        corner_up = above_ref[4] if tr == 0 else roll_lanes(above_ref[4], STRIP)
        corner_dn = below_ref[4] if tr == 0 else roll_lanes(below_ref[4], -STRIP)
        epad[tr, 0] = roll_lanes(
            jnp.where(lane >= 3 * STRIP, corner_up, ea_ref[tr, top]), STRIP
        )
        epad[tr, rows_e + 1] = roll_lanes(
            jnp.where(lane < STRIP, corner_dn, ea_ref[tr, 0]), -STRIP
        )
    edge_flux_row(0, epad, ek_ref[0], eb, ebx, eby, level0, efx)
    edge_flux_row(top, epad, ek_ref[top], eb, ebx, eby, level0, efx)

    bottom = slab_of(b_ref).astype(jnp.float32)
    bmy = lat_limits(bottom)
    bmx = bmx_ref[...]
    ends = (
        (1, -1, 0, 0, above_ref[5], True),
        (2, 0, 1, 0, slab_of(kh_ref, 0), False),
        (7, last, top + 1, 3, slab_of(kh_ref, last), False),
        (8, last + 1, top + 2, 3, below_ref[5], True),
    )
    spread = {}
    for m, (n, k, er, g, kappa_slab, only_z) in enumerate(ends):
        level = (base + k).astype(jnp.float32)
        level_z = jnp.where(level >= 1.0, level + 1.0, HUGE)
        level_h = jnp.where(level >= 0.0, level, HUGE)
        mx = level_h < bmx
        my = level_h < bmy
        mz = level_z < bottom
        kappa = jnp.where(level_h < bottom, 0.25 * kappa_slab, 0.0)
        gx, gy, gz = [], [], []
        for tr in range(2):
            slab, main = epad[tr, er], pad[tr, n]
            change = zonal_change(main, west_patch(slab, g), east_patch(slab, g), lane)
            gx.append(jnp.where(mx, change, 0.0))
            gy.append(diff(my, shift_north(main), shift_south(main)))
            gz.append(diff(mz, pad[tr, n + 1], pad[tr, n - 1]))
        fx, fy, fz = flux_xyz(gx, gy, gz, kappa, not only_z)
        for tr in range(2):
            fze[tr, m] = fz[tr]
            if not only_z:
                spread[k, tr] = divergence(fx[tr], fy[tr], efx[tr, er - 1], g, lane)

    def vertical_flux(tr, k):
        place = {-1: 0, 0: 1, last: 2, last + 1: 3}.get(k)
        return fz_ref[tr, k] if place is None else fze[tr, place]

    z = [None, None]
    for k in range(levels):
        level = (base + k).astype(jnp.float32)
        wet = level < bottom
        for tr in range(2):
            change = vertical_flux(tr, k + 1) - vertical_flux(tr, k - 1)
            if k == 0 or k == last:
                change = change + spread[k, tr]
                start = pad[tr, 2 if k == 0 else 7]
            else:
                start = q_ref[tr, k]
            rhs = start + jnp.where(wet, change, 0.0)
            new = rhs * inv_ref[k]
            z[tr] = new if k == 0 else new + ei_ref[k] * z[tr]
        for tr in range(2):
            y_ref[tr, k] = z[tr]
    low = list(z)
    for k in range(last - 1, -1, -1):
        ratio = ratio_ref[k]
        z = [y_ref[tr, k] + ratio * z[tr] for tr in range(2)]
        for tr in range(2):
            y_ref[tr, k] = z[tr]
    m2_ref[2] = eff
    for tr in range(2):
        inner = share * jnp.where(upper, low[tr], z[tr])
        outer = jnp.where(upper, z[tr], low[tr])
        value = jnp.where(upper == low_pair, inner, outer - inner)
        m1_ref[tr] = z[tr]
        m1_ref[2 + tr] = low[tr]
        m2_ref[tr] = value
        m3_ref[tr] = value


def finish_kernel(
    y_ref, a_ref, bb_ref, own_ref, r1_ref, r2_ref, r3_ref, out_hbm, out, sems
):
    levels = y_ref.shape[1]
    me = lax.axis_index("dep")
    upper = lax.rem(me, 2) == 0
    low_pair = me < 2
    share, inv_t, eff = own_ref[0], own_ref[1], own_ref[2]
    middle = 1.0 / (eff + r2_ref[2])
    middle = jnp.where(low_pair, middle, -middle)
    tops, lows = [], []
    for tr in range(2):
        y_top, y_low = y_ref[tr, 0], y_ref[tr, levels - 1]
        p_top, p_low = r1_ref[tr], r1_ref[2 + tr]
        jump = jnp.where(upper, p_top - y_low, y_top - p_low)
        edge = jnp.where(
            low_pair, jnp.where(upper, p_low, y_low), jnp.where(upper, y_top, p_top)
        )
        edge = edge + jnp.where(low_pair, -share, share) * jump
        across = middle * (r2_ref[tr] + r3_ref[tr] - edge)
        inside = jump * inv_t + share * across
        tops.append(jnp.where(upper, jnp.where(low_pair, 0.0, across), inside))
        lows.append(jnp.where(upper, inside, jnp.where(low_pair, across, 0.0)))
    step, regs = levels // GROUPS, y_ref.shape[2] // 8
    copies = []
    for part in range(GROUPS):
        for k in range(part * step, (part + 1) * step):
            a, b = a_ref[k], bb_ref[k]
            for tr in range(2):
                new = y_ref[tr, k] - tops[tr] * a + lows[tr] * b
                for v in range(regs):
                    out[tr, k, pl.ds(v, 8, regs), :] = new[8 * v : 8 * v + 8]
        for tr in range(2):
            span = (tr, pl.ds(part * step, step))
            copies.append(
                pltpu.make_async_copy(out.at[span], out_hbm.at[span], sems.at[tr, part])
            )
            copies[-1].start()
    for copy in copies:
        copy.wait()


def per_device(tracers, u_east, v_north, kappa_h, kappa_v, bottom):
    _, levels, lat, lon = tracers.shape
    rows_e = levels // GROUPS
    lon_n, dep_n = lax.axis_size("lon"), lax.axis_size("dep")
    east = [(i, (i + 1) % lon_n) for i in range(lon_n)]
    west = [(t, s) for s, t in east]
    slab = lat * lon * 4
    slabs = lambda *lead: f32(*lead, lat, lon)
    work = lambda *lead: pltpu.VMEM(lead + (lat, lon), jnp.float32)

    with jax.named_scope("pack"):
        sw, se, t0, t1, u, v = call(
            pack_kernel, (slabs(rows_e + 1),) * 2 + (slabs(levels),) * 4,
            [
                work(levels), pltpu.VMEM((lat, lon), jnp.int32), work(rows_e),
                pltpu.SemaphoreType.DMA((GROUPS, 4)), pltpu.SemaphoreType.DMA((2,)),
            ],
            (tracers, u_east, v_north, kappa_h, bottom), 10**6, 6 * levels * slab, 50.8,
            in_specs=[HBM] * 5,
        )
    with jax.named_scope("lon_halo"):
        r_east = lax.ppermute(sw, "lon", west)
        r_west = lax.ppermute(se, "lon", east)
    with jax.named_scope("advect_inner"):
        adv = call(
            advect_kernel, slabs(2, levels), [work(2, 4 * rows_e), work(5, 2 * rows_e)],
            (t0, t1, u, v, bottom), 10**7, 7 * levels * slab, 16,
        )
    with jax.named_scope("factor"):
        inv, ei, ratio, a_end, b_end, abc = call(
            factor_kernel, (slabs(levels),) * 5 + (slabs(3),), [],
            (kappa_v, bottom), 10**7, 6 * levels * slab, 16,
        )
    with jax.named_scope("advect_edge"):
        ea, ek, eb, bmx, first, second = call(
            edge_kernel,
            (slabs(2, rows_e), slabs(rows_e), slabs(), slabs(), slabs(9), slabs(6)),
            [work(2, 2 * rows_e), work(5, rows_e), work(4, rows_e), work(2, 6)],
            (sw, se, r_east, r_west, bottom, adv, kappa_h, abc), 10**6, 3 * levels * slab, 16,
        )
    swap = [(i, i ^ 1) for i in range(dep_n)]
    other = [(i, min(i + 1, dep_n - 1) if i % 2 else max(i - 1, 0)) for i in range(dep_n)]
    with jax.named_scope("dep_halo"):
        first = lax.ppermute(first, "dep", swap)
        second = lax.ppermute(second, "dep", other)
    with jax.named_scope("fluxes"):
        pe, q_part, fz = call(
            flux_kernel, (slabs(2, 6), slabs(2, levels), slabs(2, levels)),
            [
                work(2, levels + 2), work(2, rows_e + 2), work(2, rows_e),
                work(2, levels), work(3),
            ],
            (adv, ea, ek, eb, bmx, bottom, kappa_h), 10**7, 10 * levels * slab, 24,
        )
    with jax.named_scope("solve"):
        y, m1, m2, m3, own = call(
            solve_kernel, (slabs(2, levels), slabs(4), slabs(3), slabs(2), slabs(3)),
            [
                work(2, 10), work(2, rows_e + 2), work(2, rows_e), work(2, 4), work(2, 6),
            ],
            (pe, q_part, fz, ea, ek, eb, bmx, bottom, kappa_h, first, second, inv, ei, ratio, abc),
            10**7, 12 * levels * slab, 24,
        )
    with jax.named_scope("interfaces"):
        m3 = lax.ppermute(m3, "dep", [(i, i ^ 3) for i in range(dep_n)])
        m2 = lax.ppermute(m2, "dep", [(i, i ^ 2) for i in range(dep_n)])
        m1 = lax.ppermute(m1, "dep", swap)
    with jax.named_scope("finish"):
        return call(
            finish_kernel, slabs(2, levels),
            [work(2, levels), pltpu.SemaphoreType.DMA((2, GROUPS))],
            (y, a_end, b_end, own, m1, m2, m3), 10**6, 6 * levels * slab, 16,
            out_specs=HBM,
        )


def solution(mesh):
    in_specs = (
        P(None, "dep", None, "lon"),
        P("dep", None, "lon"),
        P("dep", None, "lon"),
        P("dep", None, "lon"),
        P("dep", None, "lon"),
        P(None, "lon"),
    )
    out_specs = P(None, "dep", None, "lon")
    return jax.shard_map(
        per_device, mesh=mesh, in_specs=in_specs, out_specs=out_specs, check_vma=False
    )
```

```python
import jax
import jax.numpy as jnp
from jax import lax
from jax.experimental import pallas as pl
from jax.experimental.pallas import tpu as pltpu
from jax.sharding import PartitionSpec as P

SUB = 4
THERMAL = 0.2
HALINE = 0.8
GROUPS = 4
ROWS = 32
STRIP = 32
HUGE = 1e30
MIB = 1024 * 1024

VMEM = pl.BlockSpec(memory_space=pltpu.VMEM)
HBM = pl.BlockSpec(memory_space=pltpu.HBM)


def lane_ids(rows):
    return lax.broadcasted_iota(jnp.int32, (rows, 128), 1)


def roll_lanes(x, amount):
    amount = amount % 128
    return x if amount == 0 else pltpu.roll(x, amount, 1)


def shift_north(x):
    return jnp.concatenate([x[8:], pltpu.roll(x[:8], 7, 0)], axis=0)


def shift_south(x):
    return jnp.concatenate([pltpu.roll(x[-8:], 1, 0), x[:-8]], axis=0)


def rows_of(ref, v, *lead):
    return ref[(*lead, pl.ds(v, 8, ref.shape[-2] // 8), slice(None))]


def neighbours(regs, v):
    north = regs[v + 1] if v + 1 < len(regs) else pltpu.roll(regs[0], 7, 0)
    south = regs[v - 1] if v > 0 else pltpu.roll(regs[-1], 1, 0)
    return north, south


def slab_of(ref, *lead):
    return jnp.concatenate([rows_of(ref, v, *lead) for v in range(ref.shape[-2] // 8)], axis=0)


def call(body, out_shape, scratch, args, flops, in_bytes, limit, in_specs=None, out_specs=None):
    return pl.pallas_call(
        body,
        out_shape=out_shape,
        in_specs=in_specs or [VMEM] * len(args),
        out_specs=out_specs or jax.tree.map(lambda _: VMEM, out_shape),
        scratch_shapes=scratch,
        compiler_params=pltpu.CompilerParams(vmem_limit_bytes=int(limit * MIB)),
        cost_estimate=pl.CostEstimate(flops=flops, bytes_accessed=in_bytes, transcendentals=0),
    )(*args)


def f32(*shape):
    return jax.ShapeDtypeStruct(shape, jnp.float32)


def pack_kernel(
    t_hbm, u_hbm, v_hbm, kh_hbm, b_hbm,
    sw_ref, se_ref, t0_ref, t1_ref, u_ref, v_ref,
    kh_buf, b_buf, first_buf, sems, more_sems,
):
    rows_e = u_ref.shape[0] // GROUPS
    lat = u_ref.shape[1]
    lane = lane_ids(lat)
    fields = ((t_hbm.at[0], t0_ref), (t_hbm.at[1], t1_ref), (u_hbm, u_ref), (v_hbm, v_ref))
    groups = [
        [
            pltpu.make_async_copy(
                src.at[pl.ds(g * rows_e, rows_e)], dst.at[pl.ds(g * rows_e, rows_e)], sems.at[g, n]
            )
            for n, (src, dst) in enumerate(fields)
        ]
        for g in range(GROUPS)
    ]
    tail = [
        pltpu.make_async_copy(b_hbm, b_buf, more_sems.at[0]),
        pltpu.make_async_copy(kh_hbm, kh_buf, more_sems.at[1]),
    ]
    for copy in sum(groups, []) + tail:
        copy.start()
    for g in range(GROUPS):
        for copy in groups[g]:
            copy.wait()
        for r in range(rows_e):
            level = g * rows_e + r
            slabs = [slab_of(ref, level) for ref in (t0_ref, t1_ref, u_ref, v_ref)]
            if g > 0:
                low, high = sw_ref[r], se_ref[r]
            for f, slab in enumerate(slabs):
                start = STRIP * g + 8 * f
                rolled = roll_lanes(slab, start)
                if start == 0:
                    first_buf[r] = rolled
                    low = rolled
                else:
                    low = jnp.where(lane >= start, rolled, low)
                    high = rolled if start == 8 else jnp.where(lane >= start - 8, rolled, high)
            if g == GROUPS - 1:
                high = jnp.where(lane >= 120, first_buf[r], high)
            sw_ref[r] = low
            se_ref[r] = high
    for copy in tail:
        copy.wait()
    low = jnp.zeros((lat, 128), jnp.float32)
    high = jnp.zeros((lat, 128), jnp.float32)
    bottom = slab_of(b_buf).astype(jnp.float32)
    for g in range(GROUPS):
        for r in range(rows_e):
            place = STRIP * g + r
            rolled = roll_lanes(slab_of(kh_buf, g * rows_e + r), place)
            low = jnp.where(lane == place, rolled, low)
            high = jnp.where(lane == (place - 1) % 128, rolled, high)
        place = STRIP * g + 16
        rolled = roll_lanes(bottom, place)
        low = jnp.where((lane >= place) & (lane < place + 8), rolled, low)
        high = jnp.where((lane >= place - 8) & (lane < place), rolled, high)
    sw_ref[rows_e] = low
    se_ref[rows_e] = high


def advect_block(slabs, get_c, get_u, get_v, get_level, bx, by, buf, coef, put):
    regs = bx.shape[0] // 8
    for i, slab in enumerate(slabs):
        level = get_level(slab)
        um = jnp.where(level < bx, get_u(slab), 0.0)
        vm = jnp.where(level < by, get_v(slab), 0.0)
        uw = roll_lanes(um, 1)
        vs = shift_south(vm)
        coef[0, i] = (
            1.0
            - jnp.maximum(um, 0.0)
            + jnp.minimum(uw, 0.0)
            - jnp.maximum(vm, 0.0)
            + jnp.minimum(vs, 0.0)
        )
        coef[1, i] = -jnp.minimum(um, 0.0)
        coef[2, i] = jnp.maximum(uw, 0.0)
        coef[3, i] = -jnp.minimum(vm, 0.0)
        coef[4, i] = jnp.maximum(vs, 0.0)
        for tr in range(2):
            buf[0, 2 * i + tr] = get_c(tr, slab)
    for step in range(SUB):
        src, dst = step % 2, (step + 1) % 2
        for i, slab in enumerate(slabs):
            now = [
                [buf[src, 2 * i + tr, 8 * v : 8 * v + 8] for v in range(regs)] for tr in range(2)
            ]
            for v in range(regs):
                js = slice(8 * v, 8 * v + 8)
                a, b, c, d, e = (coef[n, i, js] for n in range(5))
                for tr in range(2):
                    here = now[tr][v]
                    north, south = neighbours(now[tr], v)
                    new = (
                        a * here
                        + b * roll_lanes(here, -1)
                        + c * roll_lanes(here, 1)
                        + d * north
                        + e * south
                    )
                    if step < SUB - 1:
                        buf[dst, 2 * i + tr, js] = new
                    else:
                        put(tr, slab, js, new)


def face_limits(bottom):
    lat = bottom.shape[0]
    rows = lax.broadcasted_iota(jnp.int32, bottom.shape, 0)
    north = jnp.where(rows == lat - 1, 0.0, shift_north(bottom))
    return jnp.minimum(bottom, roll_lanes(bottom, -1)), jnp.minimum(bottom, north)


def lat_limits(bottom):
    lat = bottom.shape[0]
    rows = lax.broadcasted_iota(jnp.int32, bottom.shape, 0)
    north = jnp.where(rows == lat - 1, 0.0, shift_north(bottom))
    south = jnp.where(rows == 0, 0.0, shift_south(bottom))
    return jnp.minimum(north, south)


def advect_kernel(t0_ref, t1_ref, u_ref, v_ref, b_ref, out_ref, buf, coef):
    levels, lat = out_ref.shape[1], out_ref.shape[2]
    base = lax.axis_index("dep") * levels
    block = coef.shape[1]
    bx, by = face_limits(slab_of(b_ref).astype(jnp.float32))

    def body(n, _):
        slabs = [n * block + i for i in range(block)]

        def put(tr, slab, js, new):
            out_ref[tr, slab, js] = new

        advect_block(
            slabs,
            lambda tr, s: slab_of((t0_ref, t1_ref)[tr], s),
            lambda s: slab_of(u_ref, s),
            lambda s: slab_of(v_ref, s),
            lambda s: (base + s).astype(jnp.float32),
            bx,
            by,
            buf,
            coef,
            put,
        )
        return 0

    lax.fori_loop(0, levels // block, body, 0)


def join(lane_q, own_high, east, west, own_low):
    return jnp.where(
        lane_q < 16,
        jnp.where(lane_q < 8, own_high, east),
        jnp.where(lane_q < 24, west, own_low),
    )


def west_patch(slab, g):
    return roll_lanes(slab, -(STRIP * g + 24))


def east_patch(slab, g):
    return roll_lanes(slab, 120 - STRIP * g)


def patched(main, slab, g, lane):
    return jnp.where(
        lane < 4, west_patch(slab, g), jnp.where(lane >= 124, east_patch(slab, g), main)
    )


def edge_kernel(
    sw_ref, se_ref, re_ref, rw_ref, b_ref, adv_ref, kh_ref, abc_ref,
    ea_ref, ek_ref, eb_ref, bmx_ref, first_ref, second_ref,
    buf, coef, fields, pay,
):
    levels, lat = adv_ref.shape[1], adv_ref.shape[2]
    rows_e = levels // GROUPS
    me = lax.axis_index("dep")
    base = me * levels
    parity = lax.rem(me, 2)
    up_ref, down_ref = pay.at[1 - parity], pay.at[parity]
    lane = lane_ids(lat)
    lane_q = lane % STRIP
    bottom = slab_of(b_ref).astype(jnp.float32)
    eb = join(
        lane_q,
        roll_lanes(se_ref[rows_e], -8),
        roll_lanes(re_ref[rows_e], -8),
        roll_lanes(rw_ref[rows_e], 8),
        roll_lanes(sw_ref[rows_e], 8),
    )
    eb_ref[...] = eb
    b_west = roll_lanes(jnp.where(lane == 127, west_patch(eb, 0), bottom), 1)
    b_east = roll_lanes(jnp.where(lane == 0, east_patch(eb, 0), bottom), -1)
    bmx_ref[...] = jnp.minimum(b_west, b_east)
    for r in range(rows_e):
        ek_ref[r] = jnp.where(
            lane_q < 16,
            roll_lanes(re_ref[rows_e], 8 - r),
            roll_lanes(rw_ref[rows_e], 24 - r),
        )
        for f in range(4):
            fields[f, r] = join(
                lane_q,
                roll_lanes(se_ref[r], 8 - 8 * f),
                roll_lanes(re_ref[r], 8 - 8 * f),
                roll_lanes(rw_ref[r], 24 - 8 * f),
                roll_lanes(sw_ref[r], 24 - 8 * f),
            )
    bx, by = face_limits(eb)
    level0 = (base + (lane // STRIP) * rows_e).astype(jnp.float32)

    def put(tr, slab, js, new):
        ea_ref[tr, slab, js] = new

    advect_block(
        list(range(rows_e)),
        lambda tr, s: fields[tr, s],
        lambda s: fields[2, s],
        lambda s: fields[3, s],
        lambda s: level0 + float(s),
        bx,
        by,
        buf,
        coef,
        put,
    )
    top = rows_e - 1
    for tr in range(2):
        up_ref[tr] = patched(adv_ref[tr, 0], ea_ref[tr, 0], 0, lane)
        up_ref[2 + tr] = patched(adv_ref[tr, 1], ea_ref[tr, 1], 0, lane)
        down_ref[tr] = patched(adv_ref[tr, levels - 1], ea_ref[tr, top], 3, lane)
        down_ref[2 + tr] = patched(adv_ref[tr, levels - 2], ea_ref[tr, top - 1], 3, lane)
    up_ref[4] = jnp.where(lane < STRIP, ea_ref[0, 0], roll_lanes(ea_ref[1, 0], STRIP))
    down_ref[4] = jnp.where(
        lane >= 3 * STRIP, ea_ref[0, top], roll_lanes(ea_ref[1, top], -STRIP)
    )
    up_ref[5] = slab_of(kh_ref, 0)
    down_ref[5] = slab_of(kh_ref, levels - 1)
    first_ref[0:6] = pay[0]
    first_ref[6:9] = abc_ref[...]
    second_ref[...] = pay[1]


def slopes(gx, gy, gz):
    rx, ry, rz = (-0.5 * THERMAL * g[0] + 0.5 * HALINE * g[1] for g in (gx, gy, gz))
    scale = rz / (1.0 + rx * rx + ry * ry + rz * rz)
    return rx * scale, ry * scale


def flux_xyz(gx, gy, gz, kappa, need_xy=True):
    sx, sy = slopes(gx, gy, gz)
    kx, ky = kappa * sx, kappa * sy
    kz = kx * sx + ky * sy
    fz = [kx * gx[n] + ky * gy[n] + kz * gz[n] for n in range(2)]
    if not need_xy:
        return None, None, fz
    fx = [kappa * gx[n] + kx * gz[n] for n in range(2)]
    fy = [kappa * gy[n] + ky * gz[n] for n in range(2)]
    return fx, fy, fz


def flux_x_edge(gx, gy, gz, kappa):
    sx, _ = slopes(gx, gy, gz)
    kx = kappa * sx
    return [kappa * gx[n] + kx * gz[n] for n in range(2)]


def diff(mask, high, low):
    return jnp.where(mask, high - low, 0.0)


def edge_flux_row(r, rows, ek, eb, ebx, eby, level0, out_ref):
    level = level0 + r
    mx = level < ebx
    my = level < eby
    mz = (level + 1.0 < eb) & (level >= 1.0)
    kappa = jnp.where((level < eb) & (level >= 0.0), 0.25 * ek, 0.0)
    gx, gy, gz = [], [], []
    for tr in range(2):
        here = rows[tr, r + 1]
        gx.append(diff(mx, roll_lanes(here, -1), roll_lanes(here, 1)))
        gy.append(diff(my, shift_north(here), shift_south(here)))
        gz.append(diff(mz, rows[tr, r + 2], rows[tr, r]))
    fx = flux_x_edge(gx, gy, gz, kappa)
    for tr in range(2):
        out_ref[tr, r] = fx[tr]


def edge_limits(eb):
    return (
        jnp.minimum(roll_lanes(eb, 1), roll_lanes(eb, -1)),
        lat_limits(eb),
    )


def zonal_change(fx, west, east, lane):
    return roll_lanes(jnp.where(lane == 0, east, fx), -1) - roll_lanes(
        jnp.where(lane == 127, west, fx), 1
    )


def divergence(fx, fy, slab, g, lane):
    return zonal_change(fx, west_patch(slab, g), east_patch(slab, g), lane) + (
        shift_north(fy) - shift_south(fy)
    )


def patch_kernel(
    adv_ref, ea_ref, ek_ref, eb_ref,
    full_ref, gx_ref, efx_ref,
    rows,
):
    levels, lat = adv_ref.shape[1], adv_ref.shape[2]
    rows_e = levels // GROUPS
    base = lax.axis_index("dep") * levels
    lane = lane_ids(lat)
    eb = eb_ref[...]
    ebx, eby = edge_limits(eb)
    level0 = (base + (lane // STRIP) * rows_e).astype(jnp.float32)
    for tr in range(2):
        for r in range(rows_e):
            rows[tr, r + 1] = ea_ref[tr, r]
        rows[tr, 0] = roll_lanes(ea_ref[tr, rows_e - 1], STRIP)
        rows[tr, rows_e + 1] = roll_lanes(ea_ref[tr, 0], -STRIP)
    for r in range(rows_e):
        edge_flux_row(r, rows, ek_ref[r], eb, ebx, eby, level0, efx_ref)

    def patch(r, _):
        for pair in range(0, GROUPS, 2):
            found = []
            for g in (pair, pair + 1):
                k = g * rows_e + r
                for tr in range(2):
                    slab = ea_ref[tr, r]
                    west, east = west_patch(slab, g), east_patch(slab, g)
                    main = jnp.where(
                        lane < 4, west, jnp.where(lane >= 124, east, adv_ref[tr, k])
                    )
                    found.append((tr, k, main, zonal_change(main, west, east, lane)))
            for tr, k, main, change in found:
                full_ref[tr, k] = main
                gx_ref[tr, k] = change
        return 0

    lax.fori_loop(0, rows_e, patch, 0)


def flux_kernel(
    full_ref, gx_ref, efx_ref, bmx_ref, b_ref, kh_ref,
    q_ref, fz_ref,
    limits,
):
    levels, lat = full_ref.shape[1], full_ref.shape[2]
    rows_e = levels // GROUPS
    base = lax.axis_index("dep") * levels
    lane = lane_ids(lat)
    bottom = slab_of(b_ref).astype(jnp.float32)
    limits[0] = bmx_ref[...]
    limits[1] = lat_limits(bottom)
    limits[2] = bottom

    def north_rows(tr, k, j):
        if j + 8 + ROWS <= lat:
            return full_ref[tr, k, j + 8 : j + 8 + ROWS]
        return jnp.concatenate(
            [full_ref[tr, k, j + 8 : lat], pltpu.roll(full_ref[tr, k, 0:8], 7, 0)], axis=0
        )

    def south_rows(tr, k, j):
        if j >= 8:
            return full_ref[tr, k, j - 8 : j - 8 + ROWS]
        return jnp.concatenate(
            [pltpu.roll(full_ref[tr, k, lat - 8 : lat], 1, 0), full_ref[tr, k, 0 : ROWS - 8]],
            axis=0,
        )

    def fluxes(r, _):
        for g in range(GROUPS):
            k = g * rows_e + r
            above, below = jnp.maximum(k - 1, 0), jnp.minimum(k + 1, levels - 1)
            level = (base + k).astype(jnp.float32)
            level_z = jnp.where(level >= 1.0, level + 1.0, HUGE)
            sides = [
                (west_patch(efx_ref[tr, r], g), east_patch(efx_ref[tr, r], g)) for tr in range(2)
            ]
            fxs, fys, fzs = [[], []], [[], []], [[], []]
            for j in range(0, lat, ROWS):
                js = slice(j, j + ROWS)
                mx = level < limits[0, js]
                my = level < limits[1, js]
                mz = level_z < limits[2, js]
                kh = jnp.concatenate(
                    [rows_of(kh_ref, v, k) for v in range(j // 8, (j + ROWS) // 8)], axis=0
                )
                kappa = jnp.where(level < limits[2, js], 0.25 * kh, 0.0)
                gx, gy, gz = [], [], []
                for tr in range(2):
                    gx.append(jnp.where(mx, gx_ref[tr, k, js], 0.0))
                    gy.append(diff(my, north_rows(tr, k, j), south_rows(tr, k, j)))
                    gz.append(diff(mz, full_ref[tr, below, js], full_ref[tr, above, js]))
                fx, fy, fz = flux_xyz(gx, gy, gz, kappa)
                for tr in range(2):
                    fxs[tr].append(fx[tr])
                    fys[tr].append(fy[tr])
                    fzs[tr].append(fz[tr])
            wet = level < limits[2]
            new = []
            for tr in range(2):
                fy = jnp.concatenate(fys[tr], axis=0)
                change = zonal_change(jnp.concatenate(fxs[tr], axis=0), *sides[tr], lane)
                change = change + (shift_north(fy) - shift_south(fy))
                new.append(full_ref[tr, k] + jnp.where(wet, change, 0.0))
            for tr in range(2):
                q_ref[tr, k] = new[tr]
                fz_ref[tr, k] = jnp.concatenate(fzs[tr], axis=0)
        return 0

    lax.fori_loop(0, rows_e, fluxes, 0)


def factor_kernel(kv_ref, b_ref, inv_ref, ei_ref, ratio_ref, a_ref, bb_ref, abc_ref):
    levels, lat = kv_ref.shape[0], kv_ref.shape[1]
    base = lax.axis_index("dep") * levels
    bottom = slab_of(b_ref).astype(jnp.float32)

    def coupling(k):
        level = (base + k).astype(jnp.float32)
        level = jnp.where(level >= 1.0, level, HUGE)
        return jnp.where(level < bottom, slab_of(kv_ref, k), 0.0)

    top = coupling(0)
    e = jnp.zeros((lat, 128), jnp.float32)
    q = e
    za = jnp.ones((lat, 128), jnp.float32)
    for k in range(levels):
        low = coupling(k + 1) if k + 1 < levels else jnp.zeros((lat, 128), jnp.float32)
        eq = 1.0 + e * q
        inv = 1.0 / (eq + low)
        inv_ref[k] = inv
        ei = e * inv
        ei_ref[k] = ei
        ratio_ref[k] = low * inv
        za = inv if k == 0 else za * ei
        a_ref[k] = za
        q = eq * inv
        e = low
    bb_ref[levels - 1] = inv
    b = inv
    a = za
    for k in range(levels - 2, -1, -1):
        ratio = ratio_ref[k]
        b = ratio * b
        a = a_ref[k] + ratio * a
        bb_ref[k] = b
        a_ref[k] = a
    abc_ref[0] = a + jnp.where(top > 0.0, 1.0 / jnp.maximum(top, 1e-30), HUGE)
    abc_ref[1] = inv
    abc_ref[2] = b


def solve_kernel(
    full_ref, q_ref, fz_ref, ea_ref, ek_ref, eb_ref, bmx_ref, b_ref, kh_ref,
    first_ref, second_ref, inv_ref, ei_ref, ratio_ref, abc_ref,
    y_ref, m1_ref, m2_ref, m3_ref, own_ref,
    pad, epad, efx, fze, halo,
):
    levels, lat = q_ref.shape[1], q_ref.shape[2]
    rows_e = levels // GROUPS
    last = levels - 1
    top = rows_e - 1
    me = lax.axis_index("dep")
    base = me * levels
    parity = lax.rem(me, 2)
    upper = parity == 0
    low_pair = me < 2
    lane = lane_ids(lat)
    halo[0] = first_ref[0:6]
    halo[1] = second_ref[...]
    above_ref, below_ref = halo.at[1 - parity], halo.at[parity]

    b_u = jnp.where(upper, abc_ref[1], first_ref[7])
    a_l = jnp.where(upper, first_ref[6], abc_ref[0])
    a_u = jnp.where(upper, abc_ref[0], first_ref[6])
    b_l = jnp.where(upper, first_ref[7], abc_ref[1])
    inv_t = 1.0 / (b_u + a_l)
    c_pair = jnp.where(upper == low_pair, first_ref[8], abc_ref[2])
    share = c_pair * inv_t
    eff = jnp.where(low_pair, b_l, a_u) - c_pair * share
    own_ref[0] = share
    own_ref[1] = inv_t
    own_ref[2] = eff

    eb = eb_ref[...]
    ebx, eby = edge_limits(eb)
    level0 = (base + (lane // STRIP) * rows_e).astype(jnp.float32)
    for tr in range(2):
        pad[tr, 0] = above_ref[2 + tr]
        pad[tr, 1] = above_ref[tr]
        for n, k in enumerate((0, 1, 2, last - 2, last - 1, last)):
            pad[tr, n + 2] = full_ref[tr, k]
        pad[tr, 8] = below_ref[tr]
        pad[tr, 9] = below_ref[2 + tr]
        for r in range(rows_e):
            epad[tr, r + 1] = ea_ref[tr, r]
        corner_up = above_ref[4] if tr == 0 else roll_lanes(above_ref[4], STRIP)
        corner_dn = below_ref[4] if tr == 0 else roll_lanes(below_ref[4], -STRIP)
        epad[tr, 0] = roll_lanes(
            jnp.where(lane >= 3 * STRIP, corner_up, ea_ref[tr, top]), STRIP
        )
        epad[tr, rows_e + 1] = roll_lanes(
            jnp.where(lane < STRIP, corner_dn, ea_ref[tr, 0]), -STRIP
        )
    edge_flux_row(0, epad, ek_ref[0], eb, ebx, eby, level0, efx)
    edge_flux_row(top, epad, ek_ref[top], eb, ebx, eby, level0, efx)

    bottom = slab_of(b_ref).astype(jnp.float32)
    bmy = lat_limits(bottom)
    bmx = bmx_ref[...]
    ends = (
        (1, -1, 0, 0, above_ref[5], True),
        (2, 0, 1, 0, slab_of(kh_ref, 0), False),
        (7, last, top + 1, 3, slab_of(kh_ref, last), False),
        (8, last + 1, top + 2, 3, below_ref[5], True),
    )
    spread = {}
    for m, (n, k, er, g, kappa_slab, only_z) in enumerate(ends):
        level = (base + k).astype(jnp.float32)
        level_z = jnp.where(level >= 1.0, level + 1.0, HUGE)
        level_h = jnp.where(level >= 0.0, level, HUGE)
        mx = level_h < bmx
        my = level_h < bmy
        mz = level_z < bottom
        kappa = jnp.where(level_h < bottom, 0.25 * kappa_slab, 0.0)
        gx, gy, gz = [], [], []
        for tr in range(2):
            slab, main = epad[tr, er], pad[tr, n]
            change = zonal_change(main, west_patch(slab, g), east_patch(slab, g), lane)
            gx.append(jnp.where(mx, change, 0.0))
            gy.append(diff(my, shift_north(main), shift_south(main)))
            gz.append(diff(mz, pad[tr, n + 1], pad[tr, n - 1]))
        fx, fy, fz = flux_xyz(gx, gy, gz, kappa, not only_z)
        for tr in range(2):
            fze[tr, m] = fz[tr]
            if not only_z:
                spread[k, tr] = divergence(fx[tr], fy[tr], efx[tr, er - 1], g, lane)

    def vertical_flux(tr, k):
        place = {-1: 0, 0: 1, last: 2, last + 1: 3}.get(k)
        return fz_ref[tr, k] if place is None else fze[tr, place]

    z = [None, None]
    for k in range(levels):
        level = (base + k).astype(jnp.float32)
        wet = level < bottom
        for tr in range(2):
            change = vertical_flux(tr, k + 1) - vertical_flux(tr, k - 1)
            if k == 0 or k == last:
                change = change + spread[k, tr]
                start = pad[tr, 2 if k == 0 else 7]
            else:
                start = q_ref[tr, k]
            rhs = start + jnp.where(wet, change, 0.0)
            new = rhs * inv_ref[k]
            z[tr] = new if k == 0 else new + ei_ref[k] * z[tr]
        for tr in range(2):
            y_ref[tr, k] = z[tr]
    low = list(z)
    for k in range(last - 1, -1, -1):
        ratio = ratio_ref[k]
        z = [y_ref[tr, k] + ratio * z[tr] for tr in range(2)]
        for tr in range(2):
            y_ref[tr, k] = z[tr]
    m2_ref[2] = eff
    for tr in range(2):
        inner = share * jnp.where(upper, low[tr], z[tr])
        outer = jnp.where(upper, z[tr], low[tr])
        value = jnp.where(upper == low_pair, inner, outer - inner)
        m1_ref[tr] = z[tr]
        m1_ref[2 + tr] = low[tr]
        m2_ref[tr] = value
        m3_ref[tr] = value


def finish_kernel(
    y_ref, a_ref, bb_ref, own_ref, r1_ref, r2_ref, r3_ref, out_hbm, out, sems
):
    levels = y_ref.shape[1]
    me = lax.axis_index("dep")
    upper = lax.rem(me, 2) == 0
    low_pair = me < 2
    share, inv_t, eff = own_ref[0], own_ref[1], own_ref[2]
    middle = 1.0 / (eff + r2_ref[2])
    middle = jnp.where(low_pair, middle, -middle)
    tops, lows = [], []
    for tr in range(2):
        y_top, y_low = y_ref[tr, 0], y_ref[tr, levels - 1]
        p_top, p_low = r1_ref[tr], r1_ref[2 + tr]
        jump = jnp.where(upper, p_top - y_low, y_top - p_low)
        edge = jnp.where(
            low_pair, jnp.where(upper, p_low, y_low), jnp.where(upper, y_top, p_top)
        )
        edge = edge + jnp.where(low_pair, -share, share) * jump
        across = middle * (r2_ref[tr] + r3_ref[tr] - edge)
        inside = jump * inv_t + share * across
        tops.append(jnp.where(upper, jnp.where(low_pair, 0.0, across), inside))
        lows.append(jnp.where(upper, inside, jnp.where(low_pair, across, 0.0)))
    step, regs = levels // GROUPS, y_ref.shape[2] // 8
    copies = []
    for part in range(GROUPS):
        for k in range(part * step, (part + 1) * step):
            a, b = a_ref[k], bb_ref[k]
            for tr in range(2):
                new = y_ref[tr, k] - tops[tr] * a + lows[tr] * b
                for v in range(regs):
                    out[tr, k, pl.ds(v, 8, regs), :] = new[8 * v : 8 * v + 8]
        for tr in range(2):
            span = (tr, pl.ds(part * step, step))
            copies.append(
                pltpu.make_async_copy(out.at[span], out_hbm.at[span], sems.at[tr, part])
            )
            copies[-1].start()
    for copy in copies:
        copy.wait()


def per_device(tracers, u_east, v_north, kappa_h, kappa_v, bottom):
    _, levels, lat, lon = tracers.shape
    rows_e = levels // GROUPS
    lon_n, dep_n = lax.axis_size("lon"), lax.axis_size("dep")
    east = [(i, (i + 1) % lon_n) for i in range(lon_n)]
    west = [(t, s) for s, t in east]
    slab = lat * lon * 4
    slabs = lambda *lead: f32(*lead, lat, lon)
    work = lambda *lead: pltpu.VMEM(lead + (lat, lon), jnp.float32)

    with jax.named_scope("pack"):
        sw, se, t0, t1, u, v = call(
            pack_kernel, (slabs(rows_e + 1),) * 2 + (slabs(levels),) * 4,
            [
                work(levels), pltpu.VMEM((lat, lon), jnp.int32), work(rows_e),
                pltpu.SemaphoreType.DMA((GROUPS, 4)), pltpu.SemaphoreType.DMA((2,)),
            ],
            (tracers, u_east, v_north, kappa_h, bottom), 10**6, 6 * levels * slab, 50.8,
            in_specs=[HBM] * 5,
        )
    with jax.named_scope("lon_halo"):
        r_east = lax.ppermute(sw, "lon", west)
        r_west = lax.ppermute(se, "lon", east)
    with jax.named_scope("advect_inner"):
        adv = call(
            advect_kernel, slabs(2, levels), [work(2, 4 * rows_e), work(5, 2 * rows_e)],
            (t0, t1, u, v, bottom), 10**7, 7 * levels * slab, 16,
        )
    with jax.named_scope("factor"):
        inv, ei, ratio, a_end, b_end, abc = call(
            factor_kernel, (slabs(levels),) * 5 + (slabs(3),), [],
            (kappa_v, bottom), 10**7, 6 * levels * slab, 16,
        )
    with jax.named_scope("advect_edge"):
        ea, ek, eb, bmx, first, second = call(
            edge_kernel,
            (slabs(2, rows_e), slabs(rows_e), slabs(), slabs(), slabs(9), slabs(6)),
            [work(2, 2 * rows_e), work(5, rows_e), work(4, rows_e), work(2, 6)],
            (sw, se, r_east, r_west, bottom, adv, kappa_h, abc), 10**6, 3 * levels * slab, 16,
        )
    swap = [(i, i ^ 1) for i in range(dep_n)]
    other = [(i, min(i + 1, dep_n - 1) if i % 2 else max(i - 1, 0)) for i in range(dep_n)]
    with jax.named_scope("dep_halo"):
        first = lax.ppermute(first, "dep", swap)
        second = lax.ppermute(second, "dep", other)
    with jax.named_scope("patch"):
        full, gx, efx = call(
            patch_kernel, (slabs(2, levels), slabs(2, levels), slabs(2, rows_e)),
            [work(2, rows_e + 2)],
            (adv, ea, ek, eb), 10**7, 8 * levels * slab, 16,
        )
    with jax.named_scope("fluxes"):
        q_part, fz = call(
            flux_kernel, (slabs(2, levels), slabs(2, levels)), [work(3)],
            (full, gx, efx, bmx, bottom, kappa_h), 10**7, 10 * levels * slab, 16,
        )
    with jax.named_scope("solve"):
        y, m1, m2, m3, own = call(
            solve_kernel, (slabs(2, levels), slabs(4), slabs(3), slabs(2), slabs(3)),
            [
                work(2, 10), work(2, rows_e + 2), work(2, rows_e), work(2, 4), work(2, 6),
            ],
            (full, q_part, fz, ea, ek, eb, bmx, bottom, kappa_h, first, second, inv, ei, ratio, abc),
            10**7, 12 * levels * slab, 24,
        )
    with jax.named_scope("interfaces"):
        m3 = lax.ppermute(m3, "dep", [(i, i ^ 3) for i in range(dep_n)])
        m2 = lax.ppermute(m2, "dep", [(i, i ^ 2) for i in range(dep_n)])
        m1 = lax.ppermute(m1, "dep", swap)
    with jax.named_scope("finish"):
        return call(
            finish_kernel, slabs(2, levels),
            [work(2, levels), pltpu.SemaphoreType.DMA((2, GROUPS))],
            (y, a_end, b_end, own, m1, m2, m3), 10**6, 6 * levels * slab, 16,
            out_specs=HBM,
        )


def solution(mesh):
    in_specs = (
        P(None, "dep", None, "lon"),
        P("dep", None, "lon"),
        P("dep", None, "lon"),
        P("dep", None, "lon"),
        P("dep", None, "lon"),
        P(None, "lon"),
    )
    out_specs = P(None, "dep", None, "lon")
    return jax.shard_map(
        per_device, mesh=mesh, in_specs=in_specs, out_specs=out_specs, check_vma=False
    )
```

```python
import jax
import jax.numpy as jnp
from jax import lax
from jax.experimental import pallas as pl
from jax.experimental.pallas import tpu as pltpu
from jax.sharding import PartitionSpec as P

SUB = 4
THERMAL = 0.2
HALINE = 0.8
GROUPS = 4
ROWS = 32
STRIP = 32
HUGE = 1e30
MIB = 1024 * 1024

VMEM = pl.BlockSpec(memory_space=pltpu.VMEM)
HBM = pl.BlockSpec(memory_space=pltpu.HBM)


def lane_ids(rows):
    return lax.broadcasted_iota(jnp.int32, (rows, 128), 1)


def roll_lanes(x, amount):
    amount = amount % 128
    return x if amount == 0 else pltpu.roll(x, amount, 1)


def shift_north(x):
    return jnp.concatenate([x[8:], pltpu.roll(x[:8], 7, 0)], axis=0)


def shift_south(x):
    return jnp.concatenate([pltpu.roll(x[-8:], 1, 0), x[:-8]], axis=0)


def rows_of(ref, v, *lead):
    return ref[(*lead, pl.ds(v, 8, ref.shape[-2] // 8), slice(None))]


def neighbours(regs, v):
    north = regs[v + 1] if v + 1 < len(regs) else pltpu.roll(regs[0], 7, 0)
    south = regs[v - 1] if v > 0 else pltpu.roll(regs[-1], 1, 0)
    return north, south


def slab_of(ref, *lead):
    return jnp.concatenate([rows_of(ref, v, *lead) for v in range(ref.shape[-2] // 8)], axis=0)


def call(body, out_shape, scratch, args, flops, in_bytes, limit, in_specs=None, out_specs=None):
    return pl.pallas_call(
        body,
        out_shape=out_shape,
        in_specs=in_specs or [VMEM] * len(args),
        out_specs=out_specs or jax.tree.map(lambda _: VMEM, out_shape),
        scratch_shapes=scratch,
        compiler_params=pltpu.CompilerParams(vmem_limit_bytes=int(limit * MIB)),
        cost_estimate=pl.CostEstimate(flops=flops, bytes_accessed=in_bytes, transcendentals=0),
    )(*args)


def f32(*shape):
    return jax.ShapeDtypeStruct(shape, jnp.float32)


def pack_kernel(
    t_hbm, u_hbm, v_hbm, kh_hbm, b_hbm,
    sw_ref, se_ref, t0_ref, t1_ref, u_ref, v_ref,
    kh_buf, b_buf, first_buf, sems, more_sems,
):
    rows_e = u_ref.shape[0] // GROUPS
    lat = u_ref.shape[1]
    lane = lane_ids(lat)
    fields = ((t_hbm.at[0], t0_ref), (t_hbm.at[1], t1_ref), (u_hbm, u_ref), (v_hbm, v_ref))
    groups = [
        [
            pltpu.make_async_copy(
                src.at[pl.ds(g * rows_e, rows_e)], dst.at[pl.ds(g * rows_e, rows_e)], sems.at[g, n]
            )
            for n, (src, dst) in enumerate(fields)
        ]
        for g in range(GROUPS)
    ]
    tail = [
        pltpu.make_async_copy(b_hbm, b_buf, more_sems.at[0]),
        pltpu.make_async_copy(kh_hbm, kh_buf, more_sems.at[1]),
    ]
    for copy in sum(groups, []) + tail:
        copy.start()
    for g in range(GROUPS):
        for copy in groups[g]:
            copy.wait()
        for r in range(rows_e):
            level = g * rows_e + r
            slabs = [slab_of(ref, level) for ref in (t0_ref, t1_ref, u_ref, v_ref)]
            if g > 0:
                low, high = sw_ref[r], se_ref[r]
            for f, slab in enumerate(slabs):
                start = STRIP * g + 8 * f
                rolled = roll_lanes(slab, start)
                if start == 0:
                    first_buf[r] = rolled
                    low = rolled
                else:
                    low = jnp.where(lane >= start, rolled, low)
                    high = rolled if start == 8 else jnp.where(lane >= start - 8, rolled, high)
            if g == GROUPS - 1:
                high = jnp.where(lane >= 120, first_buf[r], high)
            sw_ref[r] = low
            se_ref[r] = high
    for copy in tail:
        copy.wait()
    low = jnp.zeros((lat, 128), jnp.float32)
    high = jnp.zeros((lat, 128), jnp.float32)
    bottom = slab_of(b_buf).astype(jnp.float32)
    for g in range(GROUPS):
        for r in range(rows_e):
            place = STRIP * g + r
            rolled = roll_lanes(slab_of(kh_buf, g * rows_e + r), place)
            low = jnp.where(lane == place, rolled, low)
            high = jnp.where(lane == (place - 1) % 128, rolled, high)
        place = STRIP * g + 16
        rolled = roll_lanes(bottom, place)
        low = jnp.where((lane >= place) & (lane < place + 8), rolled, low)
        high = jnp.where((lane >= place - 8) & (lane < place), rolled, high)
    sw_ref[rows_e] = low
    se_ref[rows_e] = high


def advect_block(slabs, get_c, get_u, get_v, get_level, bx, by, buf, coef, put):
    regs = bx.shape[0] // 8
    for i, slab in enumerate(slabs):
        level = get_level(slab)
        um = jnp.where(level < bx, get_u(slab), 0.0)
        vm = jnp.where(level < by, get_v(slab), 0.0)
        uw = roll_lanes(um, 1)
        vs = shift_south(vm)
        coef[0, i] = (
            1.0
            - jnp.maximum(um, 0.0)
            + jnp.minimum(uw, 0.0)
            - jnp.maximum(vm, 0.0)
            + jnp.minimum(vs, 0.0)
        )
        coef[1, i] = -jnp.minimum(um, 0.0)
        coef[2, i] = jnp.maximum(uw, 0.0)
        coef[3, i] = -jnp.minimum(vm, 0.0)
        coef[4, i] = jnp.maximum(vs, 0.0)
        for tr in range(2):
            buf[0, 2 * i + tr] = get_c(tr, slab)
    for step in range(SUB):
        src, dst = step % 2, (step + 1) % 2
        for i, slab in enumerate(slabs):
            now = [
                [buf[src, 2 * i + tr, 8 * v : 8 * v + 8] for v in range(regs)] for tr in range(2)
            ]
            for v in range(regs):
                js = slice(8 * v, 8 * v + 8)
                a, b, c, d, e = (coef[n, i, js] for n in range(5))
                for tr in range(2):
                    here = now[tr][v]
                    north, south = neighbours(now[tr], v)
                    new = (
                        a * here
                        + b * roll_lanes(here, -1)
                        + c * roll_lanes(here, 1)
                        + d * north
                        + e * south
                    )
                    if step < SUB - 1:
                        buf[dst, 2 * i + tr, js] = new
                    else:
                        put(tr, slab, js, new)


def face_limits(bottom):
    lat = bottom.shape[0]
    rows = lax.broadcasted_iota(jnp.int32, bottom.shape, 0)
    north = jnp.where(rows == lat - 1, 0.0, shift_north(bottom))
    return jnp.minimum(bottom, roll_lanes(bottom, -1)), jnp.minimum(bottom, north)


def lat_limits(bottom):
    lat = bottom.shape[0]
    rows = lax.broadcasted_iota(jnp.int32, bottom.shape, 0)
    north = jnp.where(rows == lat - 1, 0.0, shift_north(bottom))
    south = jnp.where(rows == 0, 0.0, shift_south(bottom))
    return jnp.minimum(north, south)


def advect_kernel(t0_ref, t1_ref, u_ref, v_ref, b_ref, out_ref, buf, coef):
    levels, lat = out_ref.shape[1], out_ref.shape[2]
    base = lax.axis_index("dep") * levels
    block = coef.shape[1]
    bx, by = face_limits(slab_of(b_ref).astype(jnp.float32))

    def body(n, _):
        slabs = [n * block + i for i in range(block)]

        def put(tr, slab, js, new):
            out_ref[tr, slab, js] = new

        advect_block(
            slabs,
            lambda tr, s: slab_of((t0_ref, t1_ref)[tr], s),
            lambda s: slab_of(u_ref, s),
            lambda s: slab_of(v_ref, s),
            lambda s: (base + s).astype(jnp.float32),
            bx,
            by,
            buf,
            coef,
            put,
        )
        return 0

    lax.fori_loop(0, levels // block, body, 0)


def join(lane_q, own_high, east, west, own_low):
    return jnp.where(
        lane_q < 16,
        jnp.where(lane_q < 8, own_high, east),
        jnp.where(lane_q < 24, west, own_low),
    )


def west_patch(slab, g):
    return roll_lanes(slab, -(STRIP * g + 24))


def east_patch(slab, g):
    return roll_lanes(slab, 120 - STRIP * g)


def patched(main, slab, g, lane):
    return jnp.where(
        lane < 4, west_patch(slab, g), jnp.where(lane >= 124, east_patch(slab, g), main)
    )


def edge_kernel(
    sw_ref, se_ref, re_ref, rw_ref, b_ref, adv_ref, kh_ref,
    ea_ref, ek_ref, eb_ref, bmx_ref, first_ref, second_ref,
    buf, coef, fields, pay,
):
    levels, lat = adv_ref.shape[1], adv_ref.shape[2]
    rows_e = levels // GROUPS
    me = lax.axis_index("dep")
    base = me * levels
    parity = lax.rem(me, 2)
    up_ref, down_ref = pay.at[1 - parity], pay.at[parity]
    lane = lane_ids(lat)
    lane_q = lane % STRIP
    bottom = slab_of(b_ref).astype(jnp.float32)
    eb = join(
        lane_q,
        roll_lanes(se_ref[rows_e], -8),
        roll_lanes(re_ref[rows_e], -8),
        roll_lanes(rw_ref[rows_e], 8),
        roll_lanes(sw_ref[rows_e], 8),
    )
    eb_ref[...] = eb
    b_west = roll_lanes(jnp.where(lane == 127, west_patch(eb, 0), bottom), 1)
    b_east = roll_lanes(jnp.where(lane == 0, east_patch(eb, 0), bottom), -1)
    bmx_ref[...] = jnp.minimum(b_west, b_east)
    for r in range(rows_e):
        ek_ref[r] = jnp.where(
            lane_q < 16,
            roll_lanes(re_ref[rows_e], 8 - r),
            roll_lanes(rw_ref[rows_e], 24 - r),
        )
        for f in range(4):
            fields[f, r] = join(
                lane_q,
                roll_lanes(se_ref[r], 8 - 8 * f),
                roll_lanes(re_ref[r], 8 - 8 * f),
                roll_lanes(rw_ref[r], 24 - 8 * f),
                roll_lanes(sw_ref[r], 24 - 8 * f),
            )
    bx, by = face_limits(eb)
    level0 = (base + (lane // STRIP) * rows_e).astype(jnp.float32)

    def put(tr, slab, js, new):
        ea_ref[tr, slab, js] = new

    advect_block(
        list(range(rows_e)),
        lambda tr, s: fields[tr, s],
        lambda s: fields[2, s],
        lambda s: fields[3, s],
        lambda s: level0 + float(s),
        bx,
        by,
        buf,
        coef,
        put,
    )
    top = rows_e - 1
    for tr in range(2):
        up_ref[tr] = patched(adv_ref[tr, 0], ea_ref[tr, 0], 0, lane)
        up_ref[2 + tr] = patched(adv_ref[tr, 1], ea_ref[tr, 1], 0, lane)
        down_ref[tr] = patched(adv_ref[tr, levels - 1], ea_ref[tr, top], 3, lane)
        down_ref[2 + tr] = patched(adv_ref[tr, levels - 2], ea_ref[tr, top - 1], 3, lane)
    up_ref[4] = jnp.where(lane < STRIP, ea_ref[0, 0], roll_lanes(ea_ref[1, 0], STRIP))
    down_ref[4] = jnp.where(
        lane >= 3 * STRIP, ea_ref[0, top], roll_lanes(ea_ref[1, top], -STRIP)
    )
    up_ref[5] = slab_of(kh_ref, 0)
    down_ref[5] = slab_of(kh_ref, levels - 1)
    first_ref[...] = pay[0]
    second_ref[...] = pay[1]


def slopes(gx, gy, gz):
    rx, ry, rz = (-0.5 * THERMAL * g[0] + 0.5 * HALINE * g[1] for g in (gx, gy, gz))
    scale = rz / (1.0 + rx * rx + ry * ry + rz * rz)
    return rx * scale, ry * scale


def flux_xyz(gx, gy, gz, kappa, need_xy=True):
    sx, sy = slopes(gx, gy, gz)
    kx, ky = kappa * sx, kappa * sy
    kz = kx * sx + ky * sy
    fz = [kx * gx[n] + ky * gy[n] + kz * gz[n] for n in range(2)]
    if not need_xy:
        return None, None, fz
    fx = [kappa * gx[n] + kx * gz[n] for n in range(2)]
    fy = [kappa * gy[n] + ky * gz[n] for n in range(2)]
    return fx, fy, fz


def flux_x_edge(gx, gy, gz, kappa):
    sx, _ = slopes(gx, gy, gz)
    kx = kappa * sx
    return [kappa * gx[n] + kx * gz[n] for n in range(2)]


def diff(mask, high, low):
    return jnp.where(mask, high - low, 0.0)


def edge_flux_row(r, rows, ek, eb, ebx, eby, level0):
    level = level0 + r
    mx = level < ebx
    my = level < eby
    mz = (level + 1.0 < eb) & (level >= 1.0)
    kappa = jnp.where((level < eb) & (level >= 0.0), 0.25 * ek, 0.0)
    gx, gy, gz = [], [], []
    for tr in range(2):
        here = rows[tr, r + 1]
        gx.append(diff(mx, roll_lanes(here, -1), roll_lanes(here, 1)))
        gy.append(diff(my, shift_north(here), shift_south(here)))
        gz.append(diff(mz, rows[tr, r + 2], rows[tr, r]))
    return flux_x_edge(gx, gy, gz, kappa)


def edge_limits(eb):
    return (
        jnp.minimum(roll_lanes(eb, 1), roll_lanes(eb, -1)),
        lat_limits(eb),
    )


def zonal_change(fx, west, east, lane):
    return roll_lanes(jnp.where(lane == 0, east, fx), -1) - roll_lanes(
        jnp.where(lane == 127, west, fx), 1
    )


def divergence(fx, fy, slab, g, lane):
    return zonal_change(fx, west_patch(slab, g), east_patch(slab, g), lane) + (
        shift_north(fy) - shift_south(fy)
    )


def patch_kernel(
    adv_ref, ea_ref, ek_ref, eb_ref, second_ref,
    full_ref, gx_ref, efx_ref, later_ref,
    rows,
):
    levels, lat = adv_ref.shape[1], adv_ref.shape[2]
    rows_e = levels // GROUPS
    base = lax.axis_index("dep") * levels
    lane = lane_ids(lat)
    eb = eb_ref[...]
    ebx, eby = edge_limits(eb)
    level0 = (base + (lane // STRIP) * rows_e).astype(jnp.float32)
    for tr in range(2):
        for r in range(rows_e):
            rows[tr, r + 1] = ea_ref[tr, r]
        rows[tr, 0] = roll_lanes(ea_ref[tr, rows_e - 1], STRIP)
        rows[tr, rows_e + 1] = roll_lanes(ea_ref[tr, 0], -STRIP)
    found = [
        edge_flux_row(r, rows, ek_ref[r], eb, ebx, eby, level0) for r in range(rows_e)
    ]
    for r in range(rows_e):
        for tr in range(2):
            efx_ref[tr, r] = found[r][tr]

    lane = lane_ids(ROWS)
    units = [(g, slice(j, j + ROWS)) for g in range(GROUPS) for j in range(0, lat, ROWS)]

    def patch(r, _):
        def fetch(unit):
            g, js = unit
            strips = [ea_ref[tr, r, js] for tr in range(2)]
            mains = [adv_ref[tr, g * rows_e + r, js] for tr in range(2)]
            return [(west_patch(x, g), east_patch(x, g), y) for x, y in zip(strips, mains)]

        def put(unit, mains, rolled):
            g, js = unit
            for tr in range(2):
                full_ref[tr, g * rows_e + r, js] = mains[tr]
                gx_ref[tr, g * rows_e + r, js] = rolled[tr][0] - rolled[tr][1]

        waiting = None
        fetched = fetch(units[0])
        for n, unit in enumerate(units):
            now = fetched
            fetched = fetch(units[n + 1]) if n + 1 < len(units) else None
            mains, rolled = [], []
            for west, east, main in now:
                main = jnp.where(lane < 4, west, jnp.where(lane >= 124, east, main))
                mains.append(main)
                rolled.append(
                    (
                        roll_lanes(jnp.where(lane == 0, east, main), -1),
                        roll_lanes(jnp.where(lane == 127, west, main), 1),
                    )
                )
            if waiting is not None:
                put(*waiting)
            waiting = (unit, mains, rolled)
        put(*waiting)
        return 0

    lax.fori_loop(0, rows_e, patch, 0)
    later_ref[...] = second_ref[...]


def flux_kernel(
    full_ref, gx_ref, efx_ref, bmx_ref, b_ref, kh_ref,
    q_ref, fz_ref,
    limits,
):
    levels, lat = full_ref.shape[1], full_ref.shape[2]
    rows_e = levels // GROUPS
    base = lax.axis_index("dep") * levels
    lane = lane_ids(lat)
    bottom = slab_of(b_ref).astype(jnp.float32)
    limits[0] = bmx_ref[...]
    limits[1] = lat_limits(bottom)
    limits[2] = bottom

    def north_rows(tr, k, j):
        if j + 8 + ROWS <= lat:
            return full_ref[tr, k, j + 8 : j + 8 + ROWS]
        return jnp.concatenate(
            [full_ref[tr, k, j + 8 : lat], pltpu.roll(full_ref[tr, k, 0:8], 7, 0)], axis=0
        )

    def south_rows(tr, k, j):
        if j >= 8:
            return full_ref[tr, k, j - 8 : j - 8 + ROWS]
        return jnp.concatenate(
            [pltpu.roll(full_ref[tr, k, lat - 8 : lat], 1, 0), full_ref[tr, k, 0 : ROWS - 8]],
            axis=0,
        )

    def fluxes(r, _):
        for g in range(GROUPS):
            k = g * rows_e + r
            above, below = jnp.maximum(k - 1, 0), jnp.minimum(k + 1, levels - 1)
            level = (base + k).astype(jnp.float32)
            level_z = jnp.where(level >= 1.0, level + 1.0, HUGE)
            sides = [
                (west_patch(efx_ref[tr, r], g), east_patch(efx_ref[tr, r], g)) for tr in range(2)
            ]
            fxs, fys, fzs = [[], []], [[], []], [[], []]
            for j in range(0, lat, ROWS):
                js = slice(j, j + ROWS)
                mx = level < limits[0, js]
                my = level < limits[1, js]
                mz = level_z < limits[2, js]
                kh = jnp.concatenate(
                    [rows_of(kh_ref, v, k) for v in range(j // 8, (j + ROWS) // 8)], axis=0
                )
                kappa = jnp.where(level < limits[2, js], 0.25 * kh, 0.0)
                gx, gy, gz = [], [], []
                for tr in range(2):
                    gx.append(jnp.where(mx, gx_ref[tr, k, js], 0.0))
                    gy.append(diff(my, north_rows(tr, k, j), south_rows(tr, k, j)))
                    gz.append(diff(mz, full_ref[tr, below, js], full_ref[tr, above, js]))
                fx, fy, fz = flux_xyz(gx, gy, gz, kappa)
                for tr in range(2):
                    fxs[tr].append(fx[tr])
                    fys[tr].append(fy[tr])
                    fzs[tr].append(fz[tr])
            wet = level < limits[2]
            new = []
            for tr in range(2):
                fy = jnp.concatenate(fys[tr], axis=0)
                change = zonal_change(jnp.concatenate(fxs[tr], axis=0), *sides[tr], lane)
                change = change + (shift_north(fy) - shift_south(fy))
                new.append(full_ref[tr, k] + jnp.where(wet, change, 0.0))
            for tr in range(2):
                q_ref[tr, k] = new[tr]
                fz_ref[tr, k] = jnp.concatenate(fzs[tr], axis=0)
        return 0

    lax.fori_loop(0, rows_e, fluxes, 0)


def factor_kernel(kv_ref, b_ref, inv_ref, ei_ref, ratio_ref, a_ref, bb_ref, abc_ref):
    levels, lat = kv_ref.shape[0], kv_ref.shape[1]
    base = lax.axis_index("dep") * levels
    bottom = slab_of(b_ref).astype(jnp.float32)

    def coupling(k):
        level = (base + k).astype(jnp.float32)
        level = jnp.where(level >= 1.0, level, HUGE)
        return jnp.where(level < bottom, slab_of(kv_ref, k), 0.0)

    top = coupling(0)
    e = jnp.zeros((lat, 128), jnp.float32)
    q = e
    za = jnp.ones((lat, 128), jnp.float32)
    for k in range(levels):
        low = coupling(k + 1) if k + 1 < levels else jnp.zeros((lat, 128), jnp.float32)
        eq = 1.0 + e * q
        inv = 1.0 / (eq + low)
        inv_ref[k] = inv
        ei = e * inv
        ei_ref[k] = ei
        ratio_ref[k] = low * inv
        za = inv if k == 0 else za * ei
        a_ref[k] = za
        q = eq * inv
        e = low
    bb_ref[levels - 1] = inv
    b = inv
    a = za
    for k in range(levels - 2, -1, -1):
        ratio = ratio_ref[k]
        b = ratio * b
        a = a_ref[k] + ratio * a
        bb_ref[k] = b
        a_ref[k] = a
    abc_ref[0] = a + jnp.where(top > 0.0, 1.0 / jnp.maximum(top, 1e-30), HUGE)
    abc_ref[1] = inv
    abc_ref[2] = b


def solve_kernel(
    full_ref, q_ref, fz_ref, ea_ref, ek_ref, eb_ref, bmx_ref, b_ref, kh_ref,
    first_ref, second_ref, inv_ref, ei_ref, ratio_ref, abc_ref, pair_ref,
    y_ref, m1_ref, m2_ref, m3_ref, own_ref,
    pad, epad, fze, halo,
):
    levels, lat = q_ref.shape[1], q_ref.shape[2]
    rows_e = levels // GROUPS
    last = levels - 1
    top = rows_e - 1
    me = lax.axis_index("dep")
    base = me * levels
    parity = lax.rem(me, 2)
    upper = parity == 0
    low_pair = me < 2
    lane = lane_ids(lat)
    halo[0] = first_ref[...]
    halo[1] = second_ref[...]
    above_ref, below_ref = halo.at[1 - parity], halo.at[parity]

    b_u = jnp.where(upper, abc_ref[1], pair_ref[1])
    a_l = jnp.where(upper, pair_ref[0], abc_ref[0])
    a_u = jnp.where(upper, abc_ref[0], pair_ref[0])
    b_l = jnp.where(upper, pair_ref[1], abc_ref[1])
    inv_t = 1.0 / (b_u + a_l)
    c_pair = jnp.where(upper == low_pair, pair_ref[2], abc_ref[2])
    share = c_pair * inv_t
    eff = jnp.where(low_pair, b_l, a_u) - c_pair * share
    own_ref[0] = share
    own_ref[1] = inv_t
    own_ref[2] = eff

    eb = eb_ref[...]
    ebx, eby = edge_limits(eb)
    level0 = (base + (lane // STRIP) * rows_e).astype(jnp.float32)
    for tr in range(2):
        pad[tr, 0] = above_ref[2 + tr]
        pad[tr, 1] = above_ref[tr]
        for n, k in enumerate((0, 1, 2, last - 2, last - 1, last)):
            pad[tr, n + 2] = full_ref[tr, k]
        pad[tr, 8] = below_ref[tr]
        pad[tr, 9] = below_ref[2 + tr]
        for r in range(rows_e):
            epad[tr, r + 1] = ea_ref[tr, r]
        corner_up = above_ref[4] if tr == 0 else roll_lanes(above_ref[4], STRIP)
        corner_dn = below_ref[4] if tr == 0 else roll_lanes(below_ref[4], -STRIP)
        epad[tr, 0] = roll_lanes(
            jnp.where(lane >= 3 * STRIP, corner_up, ea_ref[tr, top]), STRIP
        )
        epad[tr, rows_e + 1] = roll_lanes(
            jnp.where(lane < STRIP, corner_dn, ea_ref[tr, 0]), -STRIP
        )
    efx = {
        r + 1: edge_flux_row(r, epad, ek_ref[r], eb, ebx, eby, level0) for r in (0, top)
    }

    bottom = slab_of(b_ref).astype(jnp.float32)
    bmy = lat_limits(bottom)
    bmx = bmx_ref[...]
    ends = (
        (1, -1, 0, 0, above_ref[5], True),
        (2, 0, 1, 0, slab_of(kh_ref, 0), False),
        (7, last, top + 1, 3, slab_of(kh_ref, last), False),
        (8, last + 1, top + 2, 3, below_ref[5], True),
    )
    spread = {}
    for m, (n, k, er, g, kappa_slab, only_z) in enumerate(ends):
        level = (base + k).astype(jnp.float32)
        level_z = jnp.where(level >= 1.0, level + 1.0, HUGE)
        level_h = jnp.where(level >= 0.0, level, HUGE)
        mx = level_h < bmx
        my = level_h < bmy
        mz = level_z < bottom
        kappa = jnp.where(level_h < bottom, 0.25 * kappa_slab, 0.0)
        gx, gy, gz = [], [], []
        for tr in range(2):
            slab, main = epad[tr, er], pad[tr, n]
            change = zonal_change(main, west_patch(slab, g), east_patch(slab, g), lane)
            gx.append(jnp.where(mx, change, 0.0))
            gy.append(diff(my, shift_north(main), shift_south(main)))
            gz.append(diff(mz, pad[tr, n + 1], pad[tr, n - 1]))
        fx, fy, fz = flux_xyz(gx, gy, gz, kappa, not only_z)
        for tr in range(2):
            fze[tr, m] = fz[tr]
            if not only_z:
                spread[k, tr] = divergence(fx[tr], fy[tr], efx[er][tr], g, lane)

    def vertical_flux(tr, k):
        place = {-1: 0, 0: 1, last: 2, last + 1: 3}.get(k)
        return fz_ref[tr, k] if place is None else fze[tr, place]

    z = [None, None]
    for k in range(levels):
        level = (base + k).astype(jnp.float32)
        wet = level < bottom
        for tr in range(2):
            change = vertical_flux(tr, k + 1) - vertical_flux(tr, k - 1)
            if k == 0 or k == last:
                change = change + spread[k, tr]
                start = pad[tr, 2 if k == 0 else 7]
            else:
                start = q_ref[tr, k]
            rhs = start + jnp.where(wet, change, 0.0)
            new = rhs * inv_ref[k]
            z[tr] = new if k == 0 else new + ei_ref[k] * z[tr]
        for tr in range(2):
            y_ref[tr, k] = z[tr]
    low = list(z)
    for k in range(last - 1, -1, -1):
        ratio = ratio_ref[k]
        z = [y_ref[tr, k] + ratio * z[tr] for tr in range(2)]
        for tr in range(2):
            y_ref[tr, k] = z[tr]
    m2_ref[2] = eff
    for tr in range(2):
        inner = share * jnp.where(upper, low[tr], z[tr])
        outer = jnp.where(upper, z[tr], low[tr])
        value = jnp.where(upper == low_pair, inner, outer - inner)
        m1_ref[tr] = z[tr]
        m1_ref[2 + tr] = low[tr]
        m2_ref[tr] = value
        m3_ref[tr] = value


def finish_kernel(
    y_ref, a_ref, bb_ref, own_ref, r1_ref, r2_ref, r3_ref, out_hbm, out, sems
):
    levels = y_ref.shape[1]
    me = lax.axis_index("dep")
    upper = lax.rem(me, 2) == 0
    low_pair = me < 2
    share, inv_t, eff = own_ref[0], own_ref[1], own_ref[2]
    middle = 1.0 / (eff + r2_ref[2])
    middle = jnp.where(low_pair, middle, -middle)
    tops, lows = [], []
    for tr in range(2):
        y_top, y_low = y_ref[tr, 0], y_ref[tr, levels - 1]
        p_top, p_low = r1_ref[tr], r1_ref[2 + tr]
        jump = jnp.where(upper, p_top - y_low, y_top - p_low)
        edge = jnp.where(
            low_pair, jnp.where(upper, p_low, y_low), jnp.where(upper, y_top, p_top)
        )
        edge = edge + jnp.where(low_pair, -share, share) * jump
        across = middle * (r2_ref[tr] + r3_ref[tr] - edge)
        inside = jump * inv_t + share * across
        tops.append(jnp.where(upper, jnp.where(low_pair, 0.0, across), inside))
        lows.append(jnp.where(upper, inside, jnp.where(low_pair, across, 0.0)))
    step, regs = levels // GROUPS, y_ref.shape[2] // 8
    copies = []
    for part in range(GROUPS):
        for k in range(part * step, (part + 1) * step):
            a, b = a_ref[k], bb_ref[k]
            for tr in range(2):
                new = y_ref[tr, k] - tops[tr] * a + lows[tr] * b
                for v in range(regs):
                    out[tr, k, pl.ds(v, 8, regs), :] = new[8 * v : 8 * v + 8]
        for tr in range(2):
            span = (tr, pl.ds(part * step, step))
            copies.append(
                pltpu.make_async_copy(out.at[span], out_hbm.at[span], sems.at[tr, part])
            )
            copies[-1].start()
    for copy in copies:
        copy.wait()


def per_device(tracers, u_east, v_north, kappa_h, kappa_v, bottom):
    _, levels, lat, lon = tracers.shape
    rows_e = levels // GROUPS
    lon_n, dep_n = lax.axis_size("lon"), lax.axis_size("dep")
    east = [(i, (i + 1) % lon_n) for i in range(lon_n)]
    west = [(t, s) for s, t in east]
    slab = lat * lon * 4
    slabs = lambda *lead: f32(*lead, lat, lon)
    work = lambda *lead: pltpu.VMEM(lead + (lat, lon), jnp.float32)

    with jax.named_scope("pack"):
        sw, se, t0, t1, u, v = call(
            pack_kernel, (slabs(rows_e + 1),) * 2 + (slabs(levels),) * 4,
            [
                work(levels), pltpu.VMEM((lat, lon), jnp.int32), work(rows_e),
                pltpu.SemaphoreType.DMA((GROUPS, 4)), pltpu.SemaphoreType.DMA((2,)),
            ],
            (tracers, u_east, v_north, kappa_h, bottom), 10**6, 6 * levels * slab, 50.8,
            in_specs=[HBM] * 5,
        )
    with jax.named_scope("lon_halo"):
        r_east = lax.ppermute(sw, "lon", west)
        r_west = lax.ppermute(se, "lon", east)
    with jax.named_scope("advect_inner"):
        adv = call(
            advect_kernel, slabs(2, levels), [work(2, 4 * rows_e), work(5, 2 * rows_e)],
            (t0, t1, u, v, bottom), 10**7, 7 * levels * slab, 16,
        )
    with jax.named_scope("factor"):
        inv, ei, ratio, a_end, b_end, abc = call(
            factor_kernel, (slabs(levels),) * 5 + (slabs(3),), [],
            (kappa_v, bottom), 10**7, 6 * levels * slab, 16,
        )
    swap = [(i, i ^ 1) for i in range(dep_n)]
    other = [(i, min(i + 1, dep_n - 1) if i % 2 else max(i - 1, 0)) for i in range(dep_n)]
    with jax.named_scope("coefficients"):
        pair = lax.ppermute(abc, "dep", swap)
    with jax.named_scope("advect_edge"):
        ea, ek, eb, bmx, first, second = call(
            edge_kernel,
            (slabs(2, rows_e), slabs(rows_e), slabs(), slabs(), slabs(6), slabs(6)),
            [work(2, 2 * rows_e), work(5, rows_e), work(4, rows_e), work(2, 6)],
            (sw, se, r_east, r_west, bottom, adv, kappa_h), 10**6, 3 * levels * slab, 16,
        )
    with jax.named_scope("dep_halo_first"):
        first = lax.ppermute(first, "dep", swap)
    with jax.named_scope("patch"):
        full, gx, efx, second = call(
            patch_kernel, (slabs(2, levels), slabs(2, levels), slabs(2, rows_e), slabs(6)),
            [work(2, rows_e + 2)],
            (adv, ea, ek, eb, second), 10**7, 8 * levels * slab, 16,
        )
    with jax.named_scope("dep_halo_second"):
        second = lax.ppermute(second, "dep", other)
    with jax.named_scope("fluxes"):
        q_part, fz = call(
            flux_kernel, (slabs(2, levels), slabs(2, levels)), [work(3)],
            (full, gx, efx, bmx, bottom, kappa_h), 10**7, 10 * levels * slab, 16,
        )
    with jax.named_scope("solve"):
        y, m1, m2, m3, own = call(
            solve_kernel, (slabs(2, levels), slabs(4), slabs(3), slabs(2), slabs(3)),
            [
                work(2, 10), work(2, rows_e + 2), work(2, 4), work(2, 6),
            ],
            (full, q_part, fz, ea, ek, eb, bmx, bottom, kappa_h, first, second, inv, ei, ratio, abc, pair),
            10**7, 12 * levels * slab, 24,
        )
    with jax.named_scope("interfaces"):
        m3 = lax.ppermute(m3, "dep", [(i, i ^ 3) for i in range(dep_n)])
        m2 = lax.ppermute(m2, "dep", [(i, i ^ 2) for i in range(dep_n)])
        m1 = lax.ppermute(m1, "dep", swap)
    with jax.named_scope("finish"):
        return call(
            finish_kernel, slabs(2, levels),
            [work(2, levels), pltpu.SemaphoreType.DMA((2, GROUPS))],
            (y, a_end, b_end, own, m1, m2, m3), 10**6, 6 * levels * slab, 16,
            out_specs=HBM,
        )


def solution(mesh):
    in_specs = (
        P(None, "dep", None, "lon"),
        P("dep", None, "lon"),
        P("dep", None, "lon"),
        P("dep", None, "lon"),
        P("dep", None, "lon"),
        P(None, "lon"),
    )
    out_specs = P(None, "dep", None, "lon")
    return jax.shard_map(
        per_device, mesh=mesh, in_specs=in_specs, out_specs=out_specs, check_vma=False
    )
```

```python
import jax
import jax.numpy as jnp
from jax import lax
from jax.experimental import pallas as pl
from jax.experimental.pallas import tpu as pltpu
from jax.sharding import PartitionSpec as P

SUB = 4
THERMAL = 0.2
HALINE = 0.8
GROUPS = 4
ROWS = 32
STRIP = 32
HUGE = 1e30
MIB = 1024 * 1024

VMEM = pl.BlockSpec(memory_space=pltpu.VMEM)
HBM = pl.BlockSpec(memory_space=pltpu.HBM)


def lane_ids(rows):
    return lax.broadcasted_iota(jnp.int32, (rows, 128), 1)


def roll_lanes(x, amount):
    amount = amount % 128
    return x if amount == 0 else pltpu.roll(x, amount, 1)


def shift_north(x):
    return jnp.concatenate([x[8:], pltpu.roll(x[:8], 7, 0)], axis=0)


def shift_south(x):
    return jnp.concatenate([pltpu.roll(x[-8:], 1, 0), x[:-8]], axis=0)


def rows_of(ref, v, *lead):
    return ref[(*lead, pl.ds(v, 8, ref.shape[-2] // 8), slice(None))]


def neighbours(regs, v):
    north = regs[v + 1] if v + 1 < len(regs) else pltpu.roll(regs[0], 7, 0)
    south = regs[v - 1] if v > 0 else pltpu.roll(regs[-1], 1, 0)
    return north, south


def slab_of(ref, *lead):
    return jnp.concatenate([rows_of(ref, v, *lead) for v in range(ref.shape[-2] // 8)], axis=0)


def call(body, out_shape, scratch, args, flops, in_bytes, limit, in_specs=None, out_specs=None):
    return pl.pallas_call(
        body,
        out_shape=out_shape,
        in_specs=in_specs or [VMEM] * len(args),
        out_specs=out_specs or jax.tree.map(lambda _: VMEM, out_shape),
        scratch_shapes=scratch,
        compiler_params=pltpu.CompilerParams(vmem_limit_bytes=int(limit * MIB)),
        cost_estimate=pl.CostEstimate(flops=flops, bytes_accessed=in_bytes, transcendentals=0),
    )(*args)


def f32(*shape):
    return jax.ShapeDtypeStruct(shape, jnp.float32)


def pack_kernel(
    t_hbm, u_hbm, v_hbm, kh_hbm, b_hbm,
    sw_ref, se_ref, t0_ref, t1_ref, u_ref, v_ref,
    kh_buf, b_buf, first_buf, sems, more_sems,
):
    rows_e = u_ref.shape[0] // GROUPS
    lat = u_ref.shape[1]
    lane = lane_ids(lat)
    fields = ((t_hbm.at[0], t0_ref), (t_hbm.at[1], t1_ref), (u_hbm, u_ref), (v_hbm, v_ref))
    groups = [
        [
            pltpu.make_async_copy(
                src.at[pl.ds(g * rows_e, rows_e)], dst.at[pl.ds(g * rows_e, rows_e)], sems.at[g, n]
            )
            for n, (src, dst) in enumerate(fields)
        ]
        for g in range(GROUPS)
    ]
    tail = [
        pltpu.make_async_copy(b_hbm, b_buf, more_sems.at[0]),
        pltpu.make_async_copy(kh_hbm, kh_buf, more_sems.at[1]),
    ]
    for copy in sum(groups, []) + tail:
        copy.start()
    for g in range(GROUPS):
        for copy in groups[g]:
            copy.wait()
        for r in range(rows_e):
            level = g * rows_e + r
            slabs = [slab_of(ref, level) for ref in (t0_ref, t1_ref, u_ref, v_ref)]
            if g > 0:
                low, high = sw_ref[r], se_ref[r]
            for f, slab in enumerate(slabs):
                start = STRIP * g + 8 * f
                rolled = roll_lanes(slab, start)
                if start == 0:
                    first_buf[r] = rolled
                    low = rolled
                else:
                    low = jnp.where(lane >= start, rolled, low)
                    high = rolled if start == 8 else jnp.where(lane >= start - 8, rolled, high)
            if g == GROUPS - 1:
                high = jnp.where(lane >= 120, first_buf[r], high)
            sw_ref[r] = low
            se_ref[r] = high
    for copy in tail:
        copy.wait()
    low = jnp.zeros((lat, 128), jnp.float32)
    high = jnp.zeros((lat, 128), jnp.float32)
    bottom = slab_of(b_buf).astype(jnp.float32)
    for g in range(GROUPS):
        for r in range(rows_e):
            place = STRIP * g + r
            rolled = roll_lanes(slab_of(kh_buf, g * rows_e + r), place)
            low = jnp.where(lane == place, rolled, low)
            high = jnp.where(lane == (place - 1) % 128, rolled, high)
        place = STRIP * g + 16
        rolled = roll_lanes(bottom, place)
        low = jnp.where((lane >= place) & (lane < place + 8), rolled, low)
        high = jnp.where((lane >= place - 8) & (lane < place), rolled, high)
    sw_ref[rows_e] = low
    se_ref[rows_e] = high


def advect_block(slabs, get_c, get_u, get_v, get_level, bx, by, buf, coef, put):
    regs = bx.shape[0] // 8
    for i, slab in enumerate(slabs):
        level = get_level(slab)
        um = jnp.where(level < bx, get_u(slab), 0.0)
        vm = jnp.where(level < by, get_v(slab), 0.0)
        uw = roll_lanes(um, 1)
        vs = shift_south(vm)
        coef[0, i] = (
            1.0
            - jnp.maximum(um, 0.0)
            + jnp.minimum(uw, 0.0)
            - jnp.maximum(vm, 0.0)
            + jnp.minimum(vs, 0.0)
        )
        coef[1, i] = -jnp.minimum(um, 0.0)
        coef[2, i] = jnp.maximum(uw, 0.0)
        coef[3, i] = -jnp.minimum(vm, 0.0)
        coef[4, i] = jnp.maximum(vs, 0.0)
        for tr in range(2):
            buf[0, 2 * i + tr] = get_c(tr, slab)
    for step in range(SUB):
        src, dst = step % 2, (step + 1) % 2
        for i, slab in enumerate(slabs):
            now = [
                [buf[src, 2 * i + tr, 8 * v : 8 * v + 8] for v in range(regs)] for tr in range(2)
            ]
            for v in range(regs):
                js = slice(8 * v, 8 * v + 8)
                a, b, c, d, e = (coef[n, i, js] for n in range(5))
                for tr in range(2):
                    here = now[tr][v]
                    north, south = neighbours(now[tr], v)
                    new = (
                        a * here
                        + b * roll_lanes(here, -1)
                        + c * roll_lanes(here, 1)
                        + d * north
                        + e * south
                    )
                    if step < SUB - 1:
                        buf[dst, 2 * i + tr, js] = new
                    else:
                        put(tr, slab, js, new)


def face_limits(bottom):
    lat = bottom.shape[0]
    rows = lax.broadcasted_iota(jnp.int32, bottom.shape, 0)
    north = jnp.where(rows == lat - 1, 0.0, shift_north(bottom))
    return jnp.minimum(bottom, roll_lanes(bottom, -1)), jnp.minimum(bottom, north)


def lat_limits(bottom):
    lat = bottom.shape[0]
    rows = lax.broadcasted_iota(jnp.int32, bottom.shape, 0)
    north = jnp.where(rows == lat - 1, 0.0, shift_north(bottom))
    south = jnp.where(rows == 0, 0.0, shift_south(bottom))
    return jnp.minimum(north, south)


def advect_kernel(t0_ref, t1_ref, u_ref, v_ref, b_ref, out_ref, buf, coef):
    levels, lat = out_ref.shape[1], out_ref.shape[2]
    base = lax.axis_index("dep") * levels
    block = coef.shape[1]
    bx, by = face_limits(slab_of(b_ref).astype(jnp.float32))

    def body(n, _):
        slabs = [n * block + i for i in range(block)]

        def put(tr, slab, js, new):
            out_ref[tr, slab, js] = new

        advect_block(
            slabs,
            lambda tr, s: slab_of((t0_ref, t1_ref)[tr], s),
            lambda s: slab_of(u_ref, s),
            lambda s: slab_of(v_ref, s),
            lambda s: (base + s).astype(jnp.float32),
            bx,
            by,
            buf,
            coef,
            put,
        )
        return 0

    lax.fori_loop(0, levels // block, body, 0)


def join(lane_q, own_high, east, west, own_low):
    return jnp.where(
        lane_q < 16,
        jnp.where(lane_q < 8, own_high, east),
        jnp.where(lane_q < 24, west, own_low),
    )


def west_patch(slab, g):
    return roll_lanes(slab, -(STRIP * g + 24))


def east_patch(slab, g):
    return roll_lanes(slab, 120 - STRIP * g)


def patched(main, slab, g, lane):
    return jnp.where(
        lane < 4, west_patch(slab, g), jnp.where(lane >= 124, east_patch(slab, g), main)
    )


def edge_kernel(
    sw_ref, se_ref, re_ref, rw_ref, b_ref, adv_ref, kh_ref, abc_ref,
    ea_ref, ek_ref, eb_ref, bmx_ref, first_ref, second_ref,
    buf, coef, fields, pay,
):
    levels, lat = adv_ref.shape[1], adv_ref.shape[2]
    rows_e = levels // GROUPS
    me = lax.axis_index("dep")
    base = me * levels
    parity = lax.rem(me, 2)
    up_ref, down_ref = pay.at[1 - parity], pay.at[parity]
    lane = lane_ids(lat)
    lane_q = lane % STRIP
    bottom = slab_of(b_ref).astype(jnp.float32)
    eb = join(
        lane_q,
        roll_lanes(se_ref[rows_e], -8),
        roll_lanes(re_ref[rows_e], -8),
        roll_lanes(rw_ref[rows_e], 8),
        roll_lanes(sw_ref[rows_e], 8),
    )
    eb_ref[...] = eb
    b_west = roll_lanes(jnp.where(lane == 127, west_patch(eb, 0), bottom), 1)
    b_east = roll_lanes(jnp.where(lane == 0, east_patch(eb, 0), bottom), -1)
    bmx_ref[...] = jnp.minimum(b_west, b_east)
    for r in range(rows_e):
        ek_ref[r] = jnp.where(
            lane_q < 16,
            roll_lanes(re_ref[rows_e], 8 - r),
            roll_lanes(rw_ref[rows_e], 24 - r),
        )
        for f in range(4):
            fields[f, r] = join(
                lane_q,
                roll_lanes(se_ref[r], 8 - 8 * f),
                roll_lanes(re_ref[r], 8 - 8 * f),
                roll_lanes(rw_ref[r], 24 - 8 * f),
                roll_lanes(sw_ref[r], 24 - 8 * f),
            )
    bx, by = face_limits(eb)
    level0 = (base + (lane // STRIP) * rows_e).astype(jnp.float32)

    def put(tr, slab, js, new):
        ea_ref[tr, slab, js] = new

    advect_block(
        list(range(rows_e)),
        lambda tr, s: fields[tr, s],
        lambda s: fields[2, s],
        lambda s: fields[3, s],
        lambda s: level0 + float(s),
        bx,
        by,
        buf,
        coef,
        put,
    )
    top = rows_e - 1
    for tr in range(2):
        up_ref[tr] = patched(adv_ref[tr, 0], ea_ref[tr, 0], 0, lane)
        up_ref[2 + tr] = patched(adv_ref[tr, 1], ea_ref[tr, 1], 0, lane)
        down_ref[tr] = patched(adv_ref[tr, levels - 1], ea_ref[tr, top], 3, lane)
        down_ref[2 + tr] = patched(adv_ref[tr, levels - 2], ea_ref[tr, top - 1], 3, lane)
    up_ref[4] = jnp.where(lane < STRIP, ea_ref[0, 0], roll_lanes(ea_ref[1, 0], STRIP))
    down_ref[4] = jnp.where(
        lane >= 3 * STRIP, ea_ref[0, top], roll_lanes(ea_ref[1, top], -STRIP)
    )
    up_ref[5] = slab_of(kh_ref, 0)
    down_ref[5] = slab_of(kh_ref, levels - 1)
    first_ref[0:6] = pay[0]
    first_ref[6:9] = abc_ref[...]
    second_ref[...] = pay[1]


def slopes(gx, gy, gz):
    rx, ry, rz = (-0.5 * THERMAL * g[0] + 0.5 * HALINE * g[1] for g in (gx, gy, gz))
    scale = rz / (1.0 + rx * rx + ry * ry + rz * rz)
    return rx * scale, ry * scale


def flux_xyz(gx, gy, gz, kappa, need_xy=True):
    sx, sy = slopes(gx, gy, gz)
    kx, ky = kappa * sx, kappa * sy
    kz = kx * sx + ky * sy
    fz = [kx * gx[n] + ky * gy[n] + kz * gz[n] for n in range(2)]
    if not need_xy:
        return None, None, fz
    fx = [kappa * gx[n] + kx * gz[n] for n in range(2)]
    fy = [kappa * gy[n] + ky * gz[n] for n in range(2)]
    return fx, fy, fz


def flux_x_edge(gx, gy, gz, kappa):
    sx, _ = slopes(gx, gy, gz)
    kx = kappa * sx
    return [kappa * gx[n] + kx * gz[n] for n in range(2)]


def diff(mask, high, low):
    return jnp.where(mask, high - low, 0.0)


def edge_flux_row(r, rows, ek, eb, ebx, eby, level0):
    level = level0 + r
    mx = level < ebx
    my = level < eby
    mz = (level + 1.0 < eb) & (level >= 1.0)
    kappa = jnp.where((level < eb) & (level >= 0.0), 0.25 * ek, 0.0)
    gx, gy, gz = [], [], []
    for tr in range(2):
        here = rows[tr, r + 1]
        gx.append(diff(mx, roll_lanes(here, -1), roll_lanes(here, 1)))
        gy.append(diff(my, shift_north(here), shift_south(here)))
        gz.append(diff(mz, rows[tr, r + 2], rows[tr, r]))
    return flux_x_edge(gx, gy, gz, kappa)


def edge_limits(eb):
    return (
        jnp.minimum(roll_lanes(eb, 1), roll_lanes(eb, -1)),
        lat_limits(eb),
    )


def zonal_change(fx, west, east, lane):
    return roll_lanes(jnp.where(lane == 0, east, fx), -1) - roll_lanes(
        jnp.where(lane == 127, west, fx), 1
    )


def divergence(fx, fy, slab, g, lane):
    return zonal_change(fx, west_patch(slab, g), east_patch(slab, g), lane) + (
        shift_north(fy) - shift_south(fy)
    )


def patch_kernel(
    adv_ref, ea_ref, ek_ref, eb_ref,
    full_ref, gx_ref, efx_ref,
    rows,
):
    levels, lat = adv_ref.shape[1], adv_ref.shape[2]
    rows_e = levels // GROUPS
    base = lax.axis_index("dep") * levels
    lane = lane_ids(lat)
    eb = eb_ref[...]
    ebx, eby = edge_limits(eb)
    level0 = (base + (lane // STRIP) * rows_e).astype(jnp.float32)
    for tr in range(2):
        for r in range(rows_e):
            rows[tr, r + 1] = ea_ref[tr, r]
        rows[tr, 0] = roll_lanes(ea_ref[tr, rows_e - 1], STRIP)
        rows[tr, rows_e + 1] = roll_lanes(ea_ref[tr, 0], -STRIP)
    found = [
        edge_flux_row(r, rows, ek_ref[r], eb, ebx, eby, level0) for r in range(rows_e)
    ]
    for r in range(rows_e):
        for tr in range(2):
            efx_ref[tr, r] = found[r][tr]

    lane = lane_ids(ROWS)
    units = [(g, slice(j, j + ROWS)) for g in range(GROUPS) for j in range(0, lat, ROWS)]

    def patch(r, _):
        def fetch(unit):
            g, js = unit
            strips = [ea_ref[tr, r, js] for tr in range(2)]
            mains = [adv_ref[tr, g * rows_e + r, js] for tr in range(2)]
            return [(west_patch(x, g), east_patch(x, g), y) for x, y in zip(strips, mains)]

        def put(unit, mains, rolled):
            g, js = unit
            for tr in range(2):
                full_ref[tr, g * rows_e + r, js] = mains[tr]
                gx_ref[tr, g * rows_e + r, js] = rolled[tr][0] - rolled[tr][1]

        waiting = None
        fetched = fetch(units[0])
        for n, unit in enumerate(units):
            now = fetched
            fetched = fetch(units[n + 1]) if n + 1 < len(units) else None
            mains, rolled = [], []
            for west, east, main in now:
                main = jnp.where(lane < 4, west, jnp.where(lane >= 124, east, main))
                mains.append(main)
                rolled.append(
                    (
                        roll_lanes(jnp.where(lane == 0, east, main), -1),
                        roll_lanes(jnp.where(lane == 127, west, main), 1),
                    )
                )
            if waiting is not None:
                put(*waiting)
            waiting = (unit, mains, rolled)
        put(*waiting)
        return 0

    lax.fori_loop(0, rows_e, patch, 0)


def flux_kernel(
    full_ref, gx_ref, efx_ref, bmx_ref, b_ref, kh_ref,
    q_ref, fz_ref,
    limits,
):
    levels, lat = full_ref.shape[1], full_ref.shape[2]
    rows_e = levels // GROUPS
    base = lax.axis_index("dep") * levels
    lane = lane_ids(lat)
    bottom = slab_of(b_ref).astype(jnp.float32)
    limits[0] = bmx_ref[...]
    limits[1] = lat_limits(bottom)
    limits[2] = bottom

    def north_rows(tr, k, j):
        if j + 8 + ROWS <= lat:
            return full_ref[tr, k, j + 8 : j + 8 + ROWS]
        return jnp.concatenate(
            [full_ref[tr, k, j + 8 : lat], pltpu.roll(full_ref[tr, k, 0:8], 7, 0)], axis=0
        )

    def south_rows(tr, k, j):
        if j >= 8:
            return full_ref[tr, k, j - 8 : j - 8 + ROWS]
        return jnp.concatenate(
            [pltpu.roll(full_ref[tr, k, lat - 8 : lat], 1, 0), full_ref[tr, k, 0 : ROWS - 8]],
            axis=0,
        )

    def fluxes(r, _):
        for g in range(GROUPS):
            k = g * rows_e + r
            above, below = jnp.maximum(k - 1, 0), jnp.minimum(k + 1, levels - 1)
            level = (base + k).astype(jnp.float32)
            level_z = jnp.where(level >= 1.0, level + 1.0, HUGE)
            sides = [
                (west_patch(efx_ref[tr, r], g), east_patch(efx_ref[tr, r], g)) for tr in range(2)
            ]
            fxs, fys, fzs = [[], []], [[], []], [[], []]
            for j in range(0, lat, ROWS):
                js = slice(j, j + ROWS)
                mx = level < limits[0, js]
                my = level < limits[1, js]
                mz = level_z < limits[2, js]
                kh = jnp.concatenate(
                    [rows_of(kh_ref, v, k) for v in range(j // 8, (j + ROWS) // 8)], axis=0
                )
                kappa = jnp.where(level < limits[2, js], 0.25 * kh, 0.0)
                gx, gy, gz = [], [], []
                for tr in range(2):
                    gx.append(jnp.where(mx, gx_ref[tr, k, js], 0.0))
                    gy.append(diff(my, north_rows(tr, k, j), south_rows(tr, k, j)))
                    gz.append(diff(mz, full_ref[tr, below, js], full_ref[tr, above, js]))
                fx, fy, fz = flux_xyz(gx, gy, gz, kappa)
                for tr in range(2):
                    fxs[tr].append(fx[tr])
                    fys[tr].append(fy[tr])
                    fzs[tr].append(fz[tr])
            wet = level < limits[2]
            new = []
            for tr in range(2):
                fy = jnp.concatenate(fys[tr], axis=0)
                change = zonal_change(jnp.concatenate(fxs[tr], axis=0), *sides[tr], lane)
                change = change + (shift_north(fy) - shift_south(fy))
                new.append(full_ref[tr, k] + jnp.where(wet, change, 0.0))
            for tr in range(2):
                q_ref[tr, k] = new[tr]
                fz_ref[tr, k] = jnp.concatenate(fzs[tr], axis=0)
        return 0

    lax.fori_loop(0, rows_e, fluxes, 0)


def factor_kernel(kv_ref, b_ref, inv_ref, ei_ref, ratio_ref, a_ref, bb_ref, abc_ref):
    levels, lat = kv_ref.shape[0], kv_ref.shape[1]
    base = lax.axis_index("dep") * levels
    bottom = slab_of(b_ref).astype(jnp.float32)

    def coupling(k):
        level = (base + k).astype(jnp.float32)
        level = jnp.where(level >= 1.0, level, HUGE)
        return jnp.where(level < bottom, slab_of(kv_ref, k), 0.0)

    top = coupling(0)
    e = jnp.zeros((lat, 128), jnp.float32)
    q = e
    za = jnp.ones((lat, 128), jnp.float32)
    for k in range(levels):
        low = coupling(k + 1) if k + 1 < levels else jnp.zeros((lat, 128), jnp.float32)
        eq = 1.0 + e * q
        inv = 1.0 / (eq + low)
        inv_ref[k] = inv
        ei = e * inv
        ei_ref[k] = ei
        ratio_ref[k] = low * inv
        za = inv if k == 0 else za * ei
        a_ref[k] = za
        q = eq * inv
        e = low
    bb_ref[levels - 1] = inv
    b = inv
    a = za
    for k in range(levels - 2, -1, -1):
        ratio = ratio_ref[k]
        b = ratio * b
        a = a_ref[k] + ratio * a
        bb_ref[k] = b
        a_ref[k] = a
    abc_ref[0] = a + jnp.where(top > 0.0, 1.0 / jnp.maximum(top, 1e-30), HUGE)
    abc_ref[1] = inv
    abc_ref[2] = b


def solve_kernel(
    full_ref, q_ref, fz_ref, ea_ref, ek_ref, eb_ref, bmx_ref, b_ref, kh_ref,
    first_ref, second_ref, inv_ref, ei_ref, ratio_ref, abc_ref,
    y_ref, m1_ref, m2_ref, m3_ref, own_ref,
    pad, epad, fze, halo,
):
    levels, lat = q_ref.shape[1], q_ref.shape[2]
    rows_e = levels // GROUPS
    last = levels - 1
    top = rows_e - 1
    me = lax.axis_index("dep")
    base = me * levels
    parity = lax.rem(me, 2)
    upper = parity == 0
    low_pair = me < 2
    lane = lane_ids(lat)
    halo[0] = first_ref[0:6]
    halo[1] = second_ref[...]
    above_ref, below_ref = halo.at[1 - parity], halo.at[parity]

    b_u = jnp.where(upper, abc_ref[1], first_ref[7])
    a_l = jnp.where(upper, first_ref[6], abc_ref[0])
    a_u = jnp.where(upper, abc_ref[0], first_ref[6])
    b_l = jnp.where(upper, first_ref[7], abc_ref[1])
    inv_t = 1.0 / (b_u + a_l)
    c_pair = jnp.where(upper == low_pair, first_ref[8], abc_ref[2])
    share = c_pair * inv_t
    eff = jnp.where(low_pair, b_l, a_u) - c_pair * share
    own_ref[0] = share
    own_ref[1] = inv_t
    own_ref[2] = eff

    eb = eb_ref[...]
    ebx, eby = edge_limits(eb)
    level0 = (base + (lane // STRIP) * rows_e).astype(jnp.float32)
    for tr in range(2):
        pad[tr, 0] = above_ref[2 + tr]
        pad[tr, 1] = above_ref[tr]
        for n, k in enumerate((0, 1, 2, last - 2, last - 1, last)):
            pad[tr, n + 2] = full_ref[tr, k]
        pad[tr, 8] = below_ref[tr]
        pad[tr, 9] = below_ref[2 + tr]
        for r in range(rows_e):
            epad[tr, r + 1] = ea_ref[tr, r]
        corner_up = above_ref[4] if tr == 0 else roll_lanes(above_ref[4], STRIP)
        corner_dn = below_ref[4] if tr == 0 else roll_lanes(below_ref[4], -STRIP)
        epad[tr, 0] = roll_lanes(
            jnp.where(lane >= 3 * STRIP, corner_up, ea_ref[tr, top]), STRIP
        )
        epad[tr, rows_e + 1] = roll_lanes(
            jnp.where(lane < STRIP, corner_dn, ea_ref[tr, 0]), -STRIP
        )
    efx = {
        r + 1: edge_flux_row(r, epad, ek_ref[r], eb, ebx, eby, level0) for r in (0, top)
    }

    bottom = slab_of(b_ref).astype(jnp.float32)
    bmy = lat_limits(bottom)
    bmx = bmx_ref[...]
    ends = (
        (1, -1, 0, 0, above_ref[5], True),
        (2, 0, 1, 0, slab_of(kh_ref, 0), False),
        (7, last, top + 1, 3, slab_of(kh_ref, last), False),
        (8, last + 1, top + 2, 3, below_ref[5], True),
    )
    spread = {}
    for m, (n, k, er, g, kappa_slab, only_z) in enumerate(ends):
        level = (base + k).astype(jnp.float32)
        level_z = jnp.where(level >= 1.0, level + 1.0, HUGE)
        level_h = jnp.where(level >= 0.0, level, HUGE)
        mx = level_h < bmx
        my = level_h < bmy
        mz = level_z < bottom
        kappa = jnp.where(level_h < bottom, 0.25 * kappa_slab, 0.0)
        gx, gy, gz = [], [], []
        for tr in range(2):
            slab, main = epad[tr, er], pad[tr, n]
            change = zonal_change(main, west_patch(slab, g), east_patch(slab, g), lane)
            gx.append(jnp.where(mx, change, 0.0))
            gy.append(diff(my, shift_north(main), shift_south(main)))
            gz.append(diff(mz, pad[tr, n + 1], pad[tr, n - 1]))
        fx, fy, fz = flux_xyz(gx, gy, gz, kappa, not only_z)
        for tr in range(2):
            fze[tr, m] = fz[tr]
            if not only_z:
                spread[k, tr] = divergence(fx[tr], fy[tr], efx[er][tr], g, lane)

    def vertical_flux(tr, k):
        place = {-1: 0, 0: 1, last: 2, last + 1: 3}.get(k)
        return fz_ref[tr, k] if place is None else fze[tr, place]

    z = [None, None]
    for k in range(levels):
        level = (base + k).astype(jnp.float32)
        wet = level < bottom
        for tr in range(2):
            change = vertical_flux(tr, k + 1) - vertical_flux(tr, k - 1)
            if k == 0 or k == last:
                change = change + spread[k, tr]
                start = pad[tr, 2 if k == 0 else 7]
            else:
                start = q_ref[tr, k]
            rhs = start + jnp.where(wet, change, 0.0)
            new = rhs * inv_ref[k]
            z[tr] = new if k == 0 else new + ei_ref[k] * z[tr]
        for tr in range(2):
            y_ref[tr, k] = z[tr]
    low = list(z)
    for k in range(last - 1, -1, -1):
        ratio = ratio_ref[k]
        z = [y_ref[tr, k] + ratio * z[tr] for tr in range(2)]
        for tr in range(2):
            y_ref[tr, k] = z[tr]
    m2_ref[2] = eff
    for tr in range(2):
        inner = share * jnp.where(upper, low[tr], z[tr])
        outer = jnp.where(upper, z[tr], low[tr])
        value = jnp.where(upper == low_pair, inner, outer - inner)
        m1_ref[tr] = z[tr]
        m1_ref[2 + tr] = low[tr]
        m2_ref[tr] = value
        m3_ref[tr] = value


def finish_kernel(
    y_ref, a_ref, bb_ref, own_ref, r1_ref, r2_ref, r3_ref, out_hbm, out, sems
):
    levels = y_ref.shape[1]
    me = lax.axis_index("dep")
    upper = lax.rem(me, 2) == 0
    low_pair = me < 2
    share, inv_t, eff = own_ref[0], own_ref[1], own_ref[2]
    middle = 1.0 / (eff + r2_ref[2])
    middle = jnp.where(low_pair, middle, -middle)
    tops, lows = [], []
    for tr in range(2):
        y_top, y_low = y_ref[tr, 0], y_ref[tr, levels - 1]
        p_top, p_low = r1_ref[tr], r1_ref[2 + tr]
        jump = jnp.where(upper, p_top - y_low, y_top - p_low)
        edge = jnp.where(
            low_pair, jnp.where(upper, p_low, y_low), jnp.where(upper, y_top, p_top)
        )
        edge = edge + jnp.where(low_pair, -share, share) * jump
        across = middle * (r2_ref[tr] + r3_ref[tr] - edge)
        inside = jump * inv_t + share * across
        tops.append(jnp.where(upper, jnp.where(low_pair, 0.0, across), inside))
        lows.append(jnp.where(upper, inside, jnp.where(low_pair, across, 0.0)))
    step, regs = levels // GROUPS, y_ref.shape[2] // 8
    copies = []
    for part in range(GROUPS):
        for k in range(part * step, (part + 1) * step):
            a, b = a_ref[k], bb_ref[k]
            for tr in range(2):
                new = y_ref[tr, k] - tops[tr] * a + lows[tr] * b
                for v in range(regs):
                    out[tr, k, pl.ds(v, 8, regs), :] = new[8 * v : 8 * v + 8]
        for tr in range(2):
            span = (tr, pl.ds(part * step, step))
            copies.append(
                pltpu.make_async_copy(out.at[span], out_hbm.at[span], sems.at[tr, part])
            )
            copies[-1].start()
    for copy in copies:
        copy.wait()


def per_device(tracers, u_east, v_north, kappa_h, kappa_v, bottom):
    _, levels, lat, lon = tracers.shape
    rows_e = levels // GROUPS
    lon_n, dep_n = lax.axis_size("lon"), lax.axis_size("dep")
    east = [(i, (i + 1) % lon_n) for i in range(lon_n)]
    west = [(t, s) for s, t in east]
    slab = lat * lon * 4
    slabs = lambda *lead: f32(*lead, lat, lon)
    work = lambda *lead: pltpu.VMEM(lead + (lat, lon), jnp.float32)

    with jax.named_scope("pack"):
        sw, se, t0, t1, u, v = call(
            pack_kernel, (slabs(rows_e + 1),) * 2 + (slabs(levels),) * 4,
            [
                work(levels), pltpu.VMEM((lat, lon), jnp.int32), work(rows_e),
                pltpu.SemaphoreType.DMA((GROUPS, 4)), pltpu.SemaphoreType.DMA((2,)),
            ],
            (tracers, u_east, v_north, kappa_h, bottom), 10**6, 6 * levels * slab, 50.8,
            in_specs=[HBM] * 5,
        )
    with jax.named_scope("lon_halo"):
        r_east = lax.ppermute(sw, "lon", west)
        r_west = lax.ppermute(se, "lon", east)
    with jax.named_scope("advect_inner"):
        adv = call(
            advect_kernel, slabs(2, levels), [work(2, 4 * rows_e), work(5, 2 * rows_e)],
            (t0, t1, u, v, bottom), 10**7, 7 * levels * slab, 16,
        )
    with jax.named_scope("factor"):
        inv, ei, ratio, a_end, b_end, abc = call(
            factor_kernel, (slabs(levels),) * 5 + (slabs(3),), [],
            (kappa_v, bottom), 10**7, 6 * levels * slab, 16,
        )
    swap = [(i, i ^ 1) for i in range(dep_n)]
    other = []
    for i in range(lon_n * dep_n):
        row, place = divmod(i, dep_n)
        if place in (0, dep_n - 1):
            other.append((i, (row ^ 1) * dep_n + place))
        else:
            other.append((i, i + 1 if place % 2 else i - 1))
    with jax.named_scope("advect_edge"):
        ea, ek, eb, bmx, first, second = call(
            edge_kernel,
            (slabs(2, rows_e), slabs(rows_e), slabs(), slabs(), slabs(9), slabs(6)),
            [work(2, 2 * rows_e), work(5, rows_e), work(4, rows_e), work(2, 6)],
            (sw, se, r_east, r_west, bottom, adv, kappa_h, abc), 10**6, 3 * levels * slab, 16,
        )
    with jax.named_scope("dep_halo"):
        first = lax.ppermute(first, "dep", swap)
        second = lax.ppermute(second, ("lon", "dep"), other)
    with jax.named_scope("patch"):
        full, gx, efx = call(
            patch_kernel, (slabs(2, levels), slabs(2, levels), slabs(2, rows_e)),
            [work(2, rows_e + 2)],
            (adv, ea, ek, eb), 10**7, 8 * levels * slab, 16,
        )
    with jax.named_scope("fluxes"):
        q_part, fz = call(
            flux_kernel, (slabs(2, levels), slabs(2, levels)), [work(3)],
            (full, gx, efx, bmx, bottom, kappa_h), 10**7, 10 * levels * slab, 16,
        )
    with jax.named_scope("solve"):
        y, m1, m2, m3, own = call(
            solve_kernel, (slabs(2, levels), slabs(4), slabs(3), slabs(2), slabs(3)),
            [
                work(2, 10), work(2, rows_e + 2), work(2, 4), work(2, 6),
            ],
            (full, q_part, fz, ea, ek, eb, bmx, bottom, kappa_h, first, second, inv, ei, ratio, abc),
            10**7, 12 * levels * slab, 24,
        )
    with jax.named_scope("interfaces"):
        m3 = lax.ppermute(m3, "dep", [(i, i ^ 3) for i in range(dep_n)])
        m2 = lax.ppermute(m2, "dep", [(i, i ^ 2) for i in range(dep_n)])
        m1 = lax.ppermute(m1, "dep", swap)
    with jax.named_scope("finish"):
        return call(
            finish_kernel, slabs(2, levels),
            [work(2, levels), pltpu.SemaphoreType.DMA((2, GROUPS))],
            (y, a_end, b_end, own, m1, m2, m3), 10**6, 6 * levels * slab, 16,
            out_specs=HBM,
        )


def solution(mesh):
    in_specs = (
        P(None, "dep", None, "lon"),
        P("dep", None, "lon"),
        P("dep", None, "lon"),
        P("dep", None, "lon"),
        P("dep", None, "lon"),
        P(None, "lon"),
    )
    out_specs = P(None, "dep", None, "lon")
    return jax.shard_map(
        per_device, mesh=mesh, in_specs=in_specs, out_specs=out_specs, check_vma=False
    )
```

```python
import functools

import jax
import jax.numpy as jnp
from jax import lax
from jax.experimental import pallas as pl
from jax.experimental.pallas import tpu as pltpu
from jax.sharding import PartitionSpec as P

SUB = 4
THERMAL = 0.2
HALINE = 0.8
GROUPS = 4
ROWS = 32
STRIP = 32
HUGE = 1e30
MIB = 1024 * 1024

VMEM = pl.BlockSpec(memory_space=pltpu.VMEM)
HBM = pl.BlockSpec(memory_space=pltpu.HBM)


def lane_ids(rows):
    return lax.broadcasted_iota(jnp.int32, (rows, 128), 1)


def roll_lanes(x, amount):
    amount = amount % 128
    return x if amount == 0 else pltpu.roll(x, amount, 1)


def shift_north(x):
    return jnp.concatenate([x[8:], pltpu.roll(x[:8], 7, 0)], axis=0)


def shift_south(x):
    return jnp.concatenate([pltpu.roll(x[-8:], 1, 0), x[:-8]], axis=0)


def rows_of(ref, v, *lead):
    return ref[(*lead, pl.ds(v, 8, ref.shape[-2] // 8), slice(None))]


def neighbours(regs, v):
    north = regs[v + 1] if v + 1 < len(regs) else pltpu.roll(regs[0], 7, 0)
    south = regs[v - 1] if v > 0 else pltpu.roll(regs[-1], 1, 0)
    return north, south


def slab_of(ref, *lead):
    return jnp.concatenate([rows_of(ref, v, *lead) for v in range(ref.shape[-2] // 8)], axis=0)


def call(body, out_shape, scratch, args, flops, in_bytes, limit, in_specs=None, out_specs=None):
    return pl.pallas_call(
        body,
        out_shape=out_shape,
        in_specs=in_specs or [VMEM] * len(args),
        out_specs=out_specs or jax.tree.map(lambda _: VMEM, out_shape),
        scratch_shapes=scratch,
        compiler_params=pltpu.CompilerParams(vmem_limit_bytes=int(limit * MIB)),
        cost_estimate=pl.CostEstimate(flops=flops, bytes_accessed=in_bytes, transcendentals=0),
    )(*args)


def f32(*shape):
    return jax.ShapeDtypeStruct(shape, jnp.float32)


def pack_kernel(
    t_hbm, u_hbm, v_hbm, kh_hbm, b_hbm,
    sw_ref, se_ref, t0_ref, t1_ref, u_ref, v_ref,
    kh_buf, b_buf, first_buf, sems, more_sems,
):
    rows_e = u_ref.shape[0] // GROUPS
    lat = u_ref.shape[1]
    lane = lane_ids(lat)
    fields = ((t_hbm.at[0], t0_ref), (t_hbm.at[1], t1_ref), (u_hbm, u_ref), (v_hbm, v_ref))
    groups = [
        [
            pltpu.make_async_copy(
                src.at[pl.ds(g * rows_e, rows_e)], dst.at[pl.ds(g * rows_e, rows_e)], sems.at[g, n]
            )
            for n, (src, dst) in enumerate(fields)
        ]
        for g in range(GROUPS)
    ]
    tail = [
        pltpu.make_async_copy(b_hbm, b_buf, more_sems.at[0]),
        pltpu.make_async_copy(kh_hbm, kh_buf, more_sems.at[1]),
    ]
    for copy in sum(groups, []) + tail:
        copy.start()
    for g in range(GROUPS):
        for copy in groups[g]:
            copy.wait()
        for r in range(rows_e):
            level = g * rows_e + r
            slabs = [slab_of(ref, level) for ref in (t0_ref, t1_ref, u_ref, v_ref)]
            if g > 0:
                low, high = sw_ref[r], se_ref[r]
            for f, slab in enumerate(slabs):
                start = STRIP * g + 8 * f
                rolled = roll_lanes(slab, start)
                if start == 0:
                    first_buf[r] = rolled
                    low = rolled
                else:
                    low = jnp.where(lane >= start, rolled, low)
                    high = rolled if start == 8 else jnp.where(lane >= start - 8, rolled, high)
            if g == GROUPS - 1:
                high = jnp.where(lane >= 120, first_buf[r], high)
            sw_ref[r] = low
            se_ref[r] = high
    for copy in tail:
        copy.wait()
    low = jnp.zeros((lat, 128), jnp.float32)
    high = jnp.zeros((lat, 128), jnp.float32)
    bottom = slab_of(b_buf).astype(jnp.float32)
    for g in range(GROUPS):
        for r in range(rows_e):
            place = STRIP * g + r
            rolled = roll_lanes(slab_of(kh_buf, g * rows_e + r), place)
            low = jnp.where(lane == place, rolled, low)
            high = jnp.where(lane == (place - 1) % 128, rolled, high)
        place = STRIP * g + 16
        rolled = roll_lanes(bottom, place)
        low = jnp.where((lane >= place) & (lane < place + 8), rolled, low)
        high = jnp.where((lane >= place - 8) & (lane < place), rolled, high)
    sw_ref[rows_e] = low
    se_ref[rows_e] = high


def advect_block(slabs, get_c, get_u, get_v, get_level, bx, by, buf, coef, put):
    regs = bx.shape[0] // 8
    for i, slab in enumerate(slabs):
        level = get_level(slab)
        um = jnp.where(level < bx, get_u(slab), 0.0)
        vm = jnp.where(level < by, get_v(slab), 0.0)
        uw = roll_lanes(um, 1)
        vs = shift_south(vm)
        coef[0, i] = (
            1.0
            - jnp.maximum(um, 0.0)
            + jnp.minimum(uw, 0.0)
            - jnp.maximum(vm, 0.0)
            + jnp.minimum(vs, 0.0)
        )
        coef[1, i] = -jnp.minimum(um, 0.0)
        coef[2, i] = jnp.maximum(uw, 0.0)
        coef[3, i] = -jnp.minimum(vm, 0.0)
        coef[4, i] = jnp.maximum(vs, 0.0)
        for tr in range(2):
            buf[0, 2 * i + tr] = get_c(tr, slab)
    for step in range(SUB):
        src, dst = step % 2, (step + 1) % 2
        for i, slab in enumerate(slabs):
            now = [
                [buf[src, 2 * i + tr, 8 * v : 8 * v + 8] for v in range(regs)] for tr in range(2)
            ]
            for v in range(regs):
                js = slice(8 * v, 8 * v + 8)
                a, b, c, d, e = (coef[n, i, js] for n in range(5))
                for tr in range(2):
                    here = now[tr][v]
                    north, south = neighbours(now[tr], v)
                    new = (
                        a * here
                        + b * roll_lanes(here, -1)
                        + c * roll_lanes(here, 1)
                        + d * north
                        + e * south
                    )
                    if step < SUB - 1:
                        buf[dst, 2 * i + tr, js] = new
                    else:
                        put(tr, slab, js, new)


def face_limits(bottom):
    lat = bottom.shape[0]
    rows = lax.broadcasted_iota(jnp.int32, bottom.shape, 0)
    north = jnp.where(rows == lat - 1, 0.0, shift_north(bottom))
    return jnp.minimum(bottom, roll_lanes(bottom, -1)), jnp.minimum(bottom, north)


def lat_limits(bottom):
    lat = bottom.shape[0]
    rows = lax.broadcasted_iota(jnp.int32, bottom.shape, 0)
    north = jnp.where(rows == lat - 1, 0.0, shift_north(bottom))
    south = jnp.where(rows == 0, 0.0, shift_south(bottom))
    return jnp.minimum(north, south)


def advect_kernel(start, t0_ref, t1_ref, u_ref, v_ref, b_ref, earlier_ref, out_ref, buf, coef):
    del earlier_ref
    count, lat = out_ref.shape[1], out_ref.shape[2]
    base = lax.axis_index("dep") * t0_ref.shape[0] + start
    bx, by = face_limits(slab_of(b_ref).astype(jnp.float32))

    def put(tr, slab, js, new):
        out_ref[tr, slab, js] = new

    advect_block(
        list(range(count)),
        lambda tr, s: slab_of((t0_ref, t1_ref)[tr], start + s),
        lambda s: slab_of(u_ref, start + s),
        lambda s: slab_of(v_ref, start + s),
        lambda s: (base + s).astype(jnp.float32),
        bx,
        by,
        buf,
        coef,
        put,
    )


def join(lane_q, own_high, east, west, own_low):
    return jnp.where(
        lane_q < 16,
        jnp.where(lane_q < 8, own_high, east),
        jnp.where(lane_q < 24, west, own_low),
    )


def west_patch(slab, g):
    return roll_lanes(slab, -(STRIP * g + 24))


def east_patch(slab, g):
    return roll_lanes(slab, 120 - STRIP * g)


def patched(main, slab, g, lane):
    return jnp.where(
        lane < 4, west_patch(slab, g), jnp.where(lane >= 124, east_patch(slab, g), main)
    )


def fold_strip(slab, place):
    lane = lane_ids(8)
    folded = jnp.zeros((8, 128), jnp.float32)
    for v in range(slab.shape[0] // 8):
        rolled = roll_lanes(slab[8 * v : 8 * v + 8], 16 * v - place)
        folded = jnp.where(lane >= 16 * v, rolled, folded)
    return folded


def unfold_strip(folded, place, regs):
    return jnp.concatenate([roll_lanes(folded, place - 16 * v) for v in range(regs)], axis=0)


def edge_kernel(
    sw_ref, se_ref, re_ref, rw_ref, b_ref, north_half, south_half, kh_ref, earlier_ref,
    ea_ref, ek_ref, eb_ref, bmx_ref, first_ref, second_ref,
    buf, coef, fields, pay,
):
    del earlier_ref
    levels, lat = kh_ref.shape[0], kh_ref.shape[1]
    rows_e = levels // GROUPS
    me = lax.axis_index("dep")
    base = me * levels
    parity = lax.rem(me, 2)
    up_ref, down_ref = pay.at[1 - parity], pay.at[parity]
    lane = lane_ids(lat)
    lane_q = lane % STRIP
    bottom = slab_of(b_ref).astype(jnp.float32)
    eb = join(
        lane_q,
        roll_lanes(se_ref[rows_e], -8),
        roll_lanes(re_ref[rows_e], -8),
        roll_lanes(rw_ref[rows_e], 8),
        roll_lanes(sw_ref[rows_e], 8),
    )
    eb_ref[...] = eb
    b_west = roll_lanes(jnp.where(lane == 127, west_patch(eb, 0), bottom), 1)
    b_east = roll_lanes(jnp.where(lane == 0, east_patch(eb, 0), bottom), -1)
    bmx_ref[...] = jnp.minimum(b_west, b_east)
    for r in range(rows_e):
        ek_ref[r] = jnp.where(
            lane_q < 16,
            roll_lanes(re_ref[rows_e], 8 - r),
            roll_lanes(rw_ref[rows_e], 24 - r),
        )
        for f in range(4):
            fields[f, r] = join(
                lane_q,
                roll_lanes(se_ref[r], 8 - 8 * f),
                roll_lanes(re_ref[r], 8 - 8 * f),
                roll_lanes(rw_ref[r], 24 - 8 * f),
                roll_lanes(sw_ref[r], 24 - 8 * f),
            )
    bx, by = face_limits(eb)
    level0 = (base + (lane // STRIP) * rows_e).astype(jnp.float32)

    def put(tr, slab, js, new):
        ea_ref[tr, slab, js] = new

    advect_block(
        list(range(rows_e)),
        lambda tr, s: fields[tr, s],
        lambda s: fields[2, s],
        lambda s: fields[3, s],
        lambda s: level0 + float(s),
        bx,
        by,
        buf,
        coef,
        put,
    )
    top, half = rows_e - 1, levels // 2
    for tr in range(2):
        for n, (k, slab) in enumerate(((0, ea_ref[tr, 0]), (1, ea_ref[tr, 1]))):
            at = (2 * n + tr) * lat
            up_ref[at : at + lat] = patched(north_half[tr, k], slab, 0, lane)
        for n, (k, slab) in enumerate(
            ((half - 1, ea_ref[tr, top]), (half - 2, ea_ref[tr, top - 1]))
        ):
            at = (2 * n + tr) * lat
            down_ref[at : at + lat] = patched(south_half[tr, k], slab, 3, lane)
        at = 5 * lat + 8 * tr
        up_ref[at : at + 8] = fold_strip(ea_ref[tr, 0], 8)
        down_ref[at : at + 8] = fold_strip(ea_ref[tr, top], 3 * STRIP + 8)
    up_ref[4 * lat : 5 * lat] = slab_of(kh_ref, 0)
    down_ref[4 * lat : 5 * lat] = slab_of(kh_ref, levels - 1)
    first_ref[...] = pay[0]
    second_ref[...] = pay[1]


def slopes(gx, gy, gz):
    rx, ry, rz = (-0.5 * THERMAL * g[0] + 0.5 * HALINE * g[1] for g in (gx, gy, gz))
    scale = rz / (1.0 + rx * rx + ry * ry + rz * rz)
    return rx * scale, ry * scale


def flux_xyz(gx, gy, gz, kappa, need_xy=True):
    sx, sy = slopes(gx, gy, gz)
    kx, ky = kappa * sx, kappa * sy
    kz = kx * sx + ky * sy
    fz = [kx * gx[n] + ky * gy[n] + kz * gz[n] for n in range(2)]
    if not need_xy:
        return None, None, fz
    fx = [kappa * gx[n] + kx * gz[n] for n in range(2)]
    fy = [kappa * gy[n] + ky * gz[n] for n in range(2)]
    return fx, fy, fz


def flux_x_edge(gx, gy, gz, kappa):
    sx, _ = slopes(gx, gy, gz)
    kx = kappa * sx
    return [kappa * gx[n] + kx * gz[n] for n in range(2)]


def diff(mask, high, low):
    return jnp.where(mask, high - low, 0.0)


def edge_flux_row(r, rows, ek, eb, ebx, eby, level0):
    level = level0 + r
    mx = level < ebx
    my = level < eby
    mz = (level + 1.0 < eb) & (level >= 1.0)
    kappa = jnp.where((level < eb) & (level >= 0.0), 0.25 * ek, 0.0)
    gx, gy, gz = [], [], []
    for tr in range(2):
        here = rows[tr, r + 1]
        gx.append(diff(mx, roll_lanes(here, -1), roll_lanes(here, 1)))
        gy.append(diff(my, shift_north(here), shift_south(here)))
        gz.append(diff(mz, rows[tr, r + 2], rows[tr, r]))
    return flux_x_edge(gx, gy, gz, kappa)


def edge_limits(eb):
    return (
        jnp.minimum(roll_lanes(eb, 1), roll_lanes(eb, -1)),
        lat_limits(eb),
    )


def zonal_change(fx, west, east, lane):
    return roll_lanes(jnp.where(lane == 0, east, fx), -1) - roll_lanes(
        jnp.where(lane == 127, west, fx), 1
    )


def divergence(fx, fy, slab, g, lane):
    return zonal_change(fx, west_patch(slab, g), east_patch(slab, g), lane) + (
        shift_north(fy) - shift_south(fy)
    )


def patch_kernel(
    north_half, south_half, ea_ref, ek_ref, eb_ref,
    full_ref, gx_ref, efx_ref,
    rows,
):
    levels, lat = full_ref.shape[1], full_ref.shape[2]
    rows_e = levels // GROUPS
    base = lax.axis_index("dep") * levels
    lane = lane_ids(lat)
    eb = eb_ref[...]
    ebx, eby = edge_limits(eb)
    level0 = (base + (lane // STRIP) * rows_e).astype(jnp.float32)
    for tr in range(2):
        for r in range(rows_e):
            rows[tr, r + 1] = ea_ref[tr, r]
        rows[tr, 0] = roll_lanes(ea_ref[tr, rows_e - 1], STRIP)
        rows[tr, rows_e + 1] = roll_lanes(ea_ref[tr, 0], -STRIP)
    found = [
        edge_flux_row(r, rows, ek_ref[r], eb, ebx, eby, level0) for r in range(rows_e)
    ]
    for r in range(rows_e):
        for tr in range(2):
            efx_ref[tr, r] = found[r][tr]

    lane = lane_ids(ROWS)
    units = [(g, slice(j, j + ROWS)) for g in range(GROUPS) for j in range(0, lat, ROWS)]

    def patch(r, _):
        def fetch(unit):
            g, js = unit
            strips = [ea_ref[tr, r, js] for tr in range(2)]
            half = (north_half, south_half)[2 * g // GROUPS]
            mains = [half[tr, g % (GROUPS // 2) * rows_e + r, js] for tr in range(2)]
            return [(west_patch(x, g), east_patch(x, g), y) for x, y in zip(strips, mains)]

        def put(unit, mains, rolled):
            g, js = unit
            for tr in range(2):
                full_ref[tr, g * rows_e + r, js] = mains[tr]
                gx_ref[tr, g * rows_e + r, js] = rolled[tr][0] - rolled[tr][1]

        waiting = None
        fetched = fetch(units[0])
        for n, unit in enumerate(units):
            now = fetched
            fetched = fetch(units[n + 1]) if n + 1 < len(units) else None
            mains, rolled = [], []
            for west, east, main in now:
                main = jnp.where(lane < 4, west, jnp.where(lane >= 124, east, main))
                mains.append(main)
                rolled.append(
                    (
                        roll_lanes(jnp.where(lane == 0, east, main), -1),
                        roll_lanes(jnp.where(lane == 127, west, main), 1),
                    )
                )
            if waiting is not None:
                put(*waiting)
            waiting = (unit, mains, rolled)
        put(*waiting)
        return 0

    lax.fori_loop(0, rows_e, patch, 0)


def flux_kernel(
    full_ref, gx_ref, efx_ref, bmx_ref, b_ref, kh_ref,
    q_ref, fz_ref,
    limits,
):
    levels, lat = full_ref.shape[1], full_ref.shape[2]
    rows_e = levels // GROUPS
    base = lax.axis_index("dep") * levels
    lane = lane_ids(lat)
    bottom = slab_of(b_ref).astype(jnp.float32)
    limits[0] = bmx_ref[...]
    limits[1] = lat_limits(bottom)
    limits[2] = bottom

    def north_rows(tr, k, j):
        if j + 8 + ROWS <= lat:
            return full_ref[tr, k, j + 8 : j + 8 + ROWS]
        return jnp.concatenate(
            [full_ref[tr, k, j + 8 : lat], pltpu.roll(full_ref[tr, k, 0:8], 7, 0)], axis=0
        )

    def south_rows(tr, k, j):
        if j >= 8:
            return full_ref[tr, k, j - 8 : j - 8 + ROWS]
        return jnp.concatenate(
            [pltpu.roll(full_ref[tr, k, lat - 8 : lat], 1, 0), full_ref[tr, k, 0 : ROWS - 8]],
            axis=0,
        )

    def fluxes(r, _):
        for g in range(GROUPS):
            k = g * rows_e + r
            above, below = jnp.maximum(k - 1, 0), jnp.minimum(k + 1, levels - 1)
            level = (base + k).astype(jnp.float32)
            level_z = jnp.where(level >= 1.0, level + 1.0, HUGE)
            sides = [
                (west_patch(efx_ref[tr, r], g), east_patch(efx_ref[tr, r], g)) for tr in range(2)
            ]
            fxs, fys, fzs = [[], []], [[], []], [[], []]
            for j in range(0, lat, ROWS):
                js = slice(j, j + ROWS)
                mx = level < limits[0, js]
                my = level < limits[1, js]
                mz = level_z < limits[2, js]
                kh = jnp.concatenate(
                    [rows_of(kh_ref, v, k) for v in range(j // 8, (j + ROWS) // 8)], axis=0
                )
                kappa = jnp.where(level < limits[2, js], 0.25 * kh, 0.0)
                gx, gy, gz = [], [], []
                for tr in range(2):
                    gx.append(jnp.where(mx, gx_ref[tr, k, js], 0.0))
                    gy.append(diff(my, north_rows(tr, k, j), south_rows(tr, k, j)))
                    gz.append(diff(mz, full_ref[tr, below, js], full_ref[tr, above, js]))
                fx, fy, fz = flux_xyz(gx, gy, gz, kappa)
                for tr in range(2):
                    fxs[tr].append(fx[tr])
                    fys[tr].append(fy[tr])
                    fzs[tr].append(fz[tr])
            wet = level < limits[2]
            new = []
            for tr in range(2):
                fy = jnp.concatenate(fys[tr], axis=0)
                change = zonal_change(jnp.concatenate(fxs[tr], axis=0), *sides[tr], lane)
                change = change + (shift_north(fy) - shift_south(fy))
                new.append(full_ref[tr, k] + jnp.where(wet, change, 0.0))
            for tr in range(2):
                q_ref[tr, k] = new[tr]
                fz_ref[tr, k] = jnp.concatenate(fzs[tr], axis=0)
        return 0

    lax.fori_loop(0, rows_e, fluxes, 0)


def factor_kernel(kv_ref, b_ref, inv_ref, ei_ref, ratio_ref, a_ref, bb_ref, abc_ref):
    levels, lat = kv_ref.shape[0], kv_ref.shape[1]
    base = lax.axis_index("dep") * levels
    bottom = slab_of(b_ref).astype(jnp.float32)

    def coupling(k):
        level = (base + k).astype(jnp.float32)
        level = jnp.where(level >= 1.0, level, HUGE)
        return jnp.where(level < bottom, slab_of(kv_ref, k), 0.0)

    top = coupling(0)
    e = jnp.zeros((lat, 128), jnp.float32)
    q = e
    za = jnp.ones((lat, 128), jnp.float32)
    for k in range(levels):
        low = coupling(k + 1) if k + 1 < levels else jnp.zeros((lat, 128), jnp.float32)
        eq = 1.0 + e * q
        inv = 1.0 / (eq + low)
        inv_ref[k] = inv
        ei = e * inv
        ei_ref[k] = ei
        ratio_ref[k] = low * inv
        za = inv if k == 0 else za * ei
        a_ref[k] = za
        q = eq * inv
        e = low
    bb_ref[levels - 1] = inv
    b = inv
    a = za
    for k in range(levels - 2, -1, -1):
        ratio = ratio_ref[k]
        b = ratio * b
        a = a_ref[k] + ratio * a
        bb_ref[k] = b
        a_ref[k] = a
    abc_ref[0] = a + jnp.where(top > 0.0, 1.0 / jnp.maximum(top, 1e-30), HUGE)
    abc_ref[1] = inv
    abc_ref[2] = b


def reduce_kernel(abc_ref, pair_ref, red_ref, eff_ref):
    me = lax.axis_index("dep")
    upper = lax.rem(me, 2) == 0
    low_pair = me < 2
    b_u = jnp.where(upper, abc_ref[1], pair_ref[1])
    a_l = jnp.where(upper, pair_ref[0], abc_ref[0])
    a_u = jnp.where(upper, abc_ref[0], pair_ref[0])
    b_l = jnp.where(upper, pair_ref[1], abc_ref[1])
    inv_t = 1.0 / (b_u + a_l)
    c_pair = jnp.where(upper == low_pair, pair_ref[2], abc_ref[2])
    share = c_pair * inv_t
    eff = jnp.where(low_pair, b_l, a_u) - c_pair * share
    red_ref[0] = share
    red_ref[1] = inv_t
    red_ref[2] = eff
    eff_ref[...] = eff


def solve_kernel(
    full_ref, q_ref, fz_ref, ea_ref, ek_ref, eb_ref, bmx_ref, b_ref, kh_ref,
    first_ref, second_ref, inv_ref, ei_ref, ratio_ref, red_ref, other_ref,
    y_ref, m1_ref, m2_ref, own_ref,
    pad, epad, fze, halo,
):
    levels, lat = q_ref.shape[1], q_ref.shape[2]
    rows_e = levels // GROUPS
    last = levels - 1
    top = rows_e - 1
    me = lax.axis_index("dep")
    base = me * levels
    parity = lax.rem(me, 2)
    outer = (me == 0) | (me == 3)
    upper = parity == 0
    sign = jnp.where(me < 2, 1.0, -1.0)
    lane = lane_ids(lat)
    halo[0] = first_ref[...]
    halo[1] = second_ref[...]
    above_ref, below_ref = halo.at[1 - parity], halo.at[parity]

    share = red_ref[0]
    inv_e = 1.0 / (red_ref[2] + other_ref[...])
    cross = share * inv_e
    inside = red_ref[1] + share * cross
    for n, value in enumerate((share, inv_e, cross, inside)):
        own_ref[n] = value

    eb = eb_ref[...]
    ebx, eby = edge_limits(eb)
    level0 = (base + (lane // STRIP) * rows_e).astype(jnp.float32)
    for tr in range(2):
        pad[tr, 0] = above_ref[(2 + tr) * lat : (3 + tr) * lat]
        pad[tr, 1] = above_ref[tr * lat : (1 + tr) * lat]
        for n, k in enumerate((0, 1, 2, last - 2, last - 1, last)):
            pad[tr, n + 2] = full_ref[tr, k]
        pad[tr, 8] = below_ref[tr * lat : (1 + tr) * lat]
        pad[tr, 9] = below_ref[(2 + tr) * lat : (3 + tr) * lat]
        for r in range(rows_e):
            epad[tr, r + 1] = ea_ref[tr, r]
        at = 5 * lat + 8 * tr
        corner_up = unfold_strip(above_ref[at : at + 8], 3 * STRIP + 8, lat // 8)
        corner_dn = unfold_strip(below_ref[at : at + 8], 8, lat // 8)
        epad[tr, 0] = roll_lanes(
            jnp.where(lane >= 3 * STRIP, corner_up, ea_ref[tr, top]), STRIP
        )
        epad[tr, rows_e + 1] = roll_lanes(
            jnp.where(lane < STRIP, corner_dn, ea_ref[tr, 0]), -STRIP
        )
    efx = {
        r + 1: edge_flux_row(r, epad, ek_ref[r], eb, ebx, eby, level0) for r in (0, top)
    }

    bottom = slab_of(b_ref).astype(jnp.float32)
    bmy = lat_limits(bottom)
    bmx = bmx_ref[...]
    ends = (
        (1, -1, 0, 0, above_ref[4 * lat : 5 * lat], True),
        (2, 0, 1, 0, slab_of(kh_ref, 0), False),
        (7, last, top + 1, 3, slab_of(kh_ref, last), False),
        (8, last + 1, top + 2, 3, below_ref[4 * lat : 5 * lat], True),
    )
    spread = {}
    for m, (n, k, er, g, kappa_slab, only_z) in enumerate(ends):
        level = (base + k).astype(jnp.float32)
        level_z = jnp.where(level >= 1.0, level + 1.0, HUGE)
        level_h = jnp.where(level >= 0.0, level, HUGE)
        mx = level_h < bmx
        my = level_h < bmy
        mz = level_z < bottom
        kappa = jnp.where(level_h < bottom, 0.25 * kappa_slab, 0.0)
        gx, gy, gz = [], [], []
        for tr in range(2):
            slab, main = epad[tr, er], pad[tr, n]
            change = zonal_change(main, west_patch(slab, g), east_patch(slab, g), lane)
            gx.append(jnp.where(mx, change, 0.0))
            gy.append(diff(my, shift_north(main), shift_south(main)))
            gz.append(diff(mz, pad[tr, n + 1], pad[tr, n - 1]))
        fx, fy, fz = flux_xyz(gx, gy, gz, kappa, not only_z)
        for tr in range(2):
            fze[tr, m] = fz[tr]
            if not only_z:
                spread[k, tr] = divergence(fx[tr], fy[tr], efx[er][tr], g, lane)

    def vertical_flux(tr, k):
        place = {-1: 0, 0: 1, last: 2, last + 1: 3}.get(k)
        return fz_ref[tr, k] if place is None else fze[tr, place]

    z = [None, None]
    for k in range(levels):
        level = (base + k).astype(jnp.float32)
        wet = level < bottom
        for tr in range(2):
            change = vertical_flux(tr, k + 1) - vertical_flux(tr, k - 1)
            if k == 0 or k == last:
                change = change + spread[k, tr]
                start = pad[tr, 2 if k == 0 else 7]
            else:
                start = q_ref[tr, k]
            rhs = start + jnp.where(wet, change, 0.0)
            new = rhs * inv_ref[k]
            z[tr] = new if k == 0 else new + ei_ref[k] * z[tr]
        for tr in range(2):
            y_ref[tr, k] = z[tr]
    low = list(z)
    for k in range(last - 1, -1, -1):
        ratio = ratio_ref[k]
        z = [y_ref[tr, k] + ratio * z[tr] for tr in range(2)]
        for tr in range(2):
            y_ref[tr, k] = z[tr]
    for tr in range(2):
        near = jnp.where(upper, low[tr], z[tr])
        far = jnp.where(upper, z[tr], low[tr])
        m1_ref[tr] = jnp.where(outer, near, sign * (inside * near - cross * far))
        m2_ref[tr] = jnp.where(outer, share * near, far - share * near)


def finish_kernel(
    y_ref, a_ref, bb_ref, own_ref, r1_ref, r2_ref, r3_ref, out_hbm, out, sems
):
    levels = y_ref.shape[1]
    me = lax.axis_index("dep")
    upper = lax.rem(me, 2) == 0
    outer = (me == 0) | (me == 3)
    sign = jnp.where(me < 2, 1.0, -1.0)
    share, inv_e, cross, inside = (own_ref[n] for n in range(4))
    tops, lows = [], []
    for tr in range(2):
        y_top, y_low = y_ref[tr, 0], y_ref[tr, levels - 1]
        near = jnp.where(upper, y_low, y_top)
        far = jnp.where(upper, y_top, y_low)
        mate, across = r1_ref[tr], r2_ref[tr] + r3_ref[tr]
        pair_flux = jnp.where(
            outer,
            mate + sign * (cross * across - inside * near),
            sign * (inside * (near - mate) + cross * (across - far)),
        )
        middle = sign * (inv_e * (across - far + share * near) - cross * mate)
        middle = jnp.where(outer, 0.0, middle)
        tops.append(jnp.where(upper, middle, pair_flux))
        lows.append(jnp.where(upper, pair_flux, middle))
    step, regs = levels // GROUPS, y_ref.shape[2] // 8
    copies = []
    for part in range(GROUPS):
        for k in range(part * step, (part + 1) * step):
            a, b = a_ref[k], bb_ref[k]
            new = [y_ref[tr, k] - tops[tr] * a + lows[tr] * b for tr in range(2)]
            for tr in range(2):
                for v in range(regs):
                    out[tr, k, pl.ds(v, 8, regs), :] = new[tr][8 * v : 8 * v + 8]
        for tr in range(2):
            span = (tr, pl.ds(part * step, step))
            copies.append(
                pltpu.make_async_copy(out.at[span], out_hbm.at[span], sems.at[tr, part])
            )
            copies[-1].start()
    for copy in copies:
        copy.wait()


def per_device(tracers, u_east, v_north, kappa_h, kappa_v, bottom):
    _, levels, lat, lon = tracers.shape
    rows_e = levels // GROUPS
    lon_n, dep_n = lax.axis_size("lon"), lax.axis_size("dep")
    east = [(i, (i + 1) % lon_n) for i in range(lon_n)]
    west = [(t, s) for s, t in east]
    slab = lat * lon * 4
    slabs = lambda *lead: f32(*lead, lat, lon)
    work = lambda *lead: pltpu.VMEM(lead + (lat, lon), jnp.float32)

    with jax.named_scope("pack"):
        sw, se, t0, t1, u, v = call(
            pack_kernel, (slabs(rows_e + 1),) * 2 + (slabs(levels),) * 4,
            [
                work(levels), pltpu.VMEM((lat, lon), jnp.int32), work(rows_e),
                pltpu.SemaphoreType.DMA((GROUPS, 4)), pltpu.SemaphoreType.DMA((2,)),
            ],
            (tracers, u_east, v_north, kappa_h, bottom), 10**6, 6 * levels * slab, 50.8,
            in_specs=[HBM] * 5,
        )
    with jax.named_scope("lon_halo"):
        r_east = lax.ppermute(sw, "lon", west)
        r_west = lax.ppermute(se, "lon", east)
    with jax.named_scope("factor"):
        inv, ei, ratio, a_end, b_end, abc = call(
            factor_kernel, (slabs(levels),) * 5 + (slabs(3),), [],
            (kappa_v, bottom), 10**7, 6 * levels * slab, 16,
        )
    swap = [(i, i ^ 1) for i in range(dep_n)]
    far = [(i, i ^ 2) for i in range(dep_n)]
    with jax.named_scope("pair_coefficients"):
        pair = lax.ppermute(abc, "dep", swap)
    half = levels // 2

    def advect_half(start, earlier):
        return call(
            functools.partial(advect_kernel, start), slabs(2, half),
            [work(2, 2 * half), work(5, half)],
            (t0, t1, u, v, bottom, earlier), 10**7, 4 * levels * slab, 16,
        )

    with jax.named_scope("advect_north"):
        north_half = advect_half(0, abc)
    with jax.named_scope("reduce"):
        red, eff = call(
            reduce_kernel, (slabs(3), slabs()), [], (abc, pair), 10**5, 10 * slab, 16
        )
    with jax.named_scope("cross_coefficients"):
        eff_other = lax.ppermute(eff, "dep", far)
    with jax.named_scope("advect_south"):
        south_half = advect_half(half, red)
    rows_pay = 5 * lat + 16
    with jax.named_scope("advect_edge"):
        ea, ek, eb, bmx, first, second = call(
            edge_kernel,
            (
                slabs(2, rows_e), slabs(rows_e), slabs(), slabs(),
                f32(rows_pay, lon), f32(rows_pay, lon),
            ),
            [
                work(2, 2 * rows_e), work(5, rows_e), work(4, rows_e),
                pltpu.VMEM((2, rows_pay, lon), jnp.float32),
            ],
            (sw, se, r_east, r_west, bottom, north_half, south_half, kappa_h, eff_other),
            10**6, 3 * levels * slab, 16,
        )
    other = []
    for i in range(lon_n * dep_n):
        row, place = divmod(i, dep_n)
        if place in (0, dep_n - 1):
            other.append((i, (row ^ 1) * dep_n + place))
        else:
            other.append((i, i + 1 if place % 2 else i - 1))
    with jax.named_scope("dep_halo"):
        first = lax.ppermute(first, "dep", swap)
        second = lax.ppermute(second, ("lon", "dep"), other)
    with jax.named_scope("patch"):
        full, gx, efx = call(
            patch_kernel, (slabs(2, levels), slabs(2, levels), slabs(2, rows_e)),
            [work(2, rows_e + 2)],
            (north_half, south_half, ea, ek, eb), 10**7, 8 * levels * slab, 16,
        )
    with jax.named_scope("fluxes"):
        q_part, fz = call(
            flux_kernel, (slabs(2, levels), slabs(2, levels)), [work(3)],
            (full, gx, efx, bmx, bottom, kappa_h), 10**7, 10 * levels * slab, 16,
        )
    with jax.named_scope("solve"):
        y, m1, m2, own = call(
            solve_kernel, (slabs(2, levels), slabs(2), slabs(2), slabs(4)),
            [
                work(2, 10), work(2, rows_e + 2), work(2, 4),
                pltpu.VMEM((2, rows_pay, lon), jnp.float32),
            ],
            (
                full, q_part, fz, ea, ek, eb, bmx, bottom, kappa_h, first, second,
                inv, ei, ratio, red, eff_other,
            ),
            10**7, 12 * levels * slab, 24,
        )
    with jax.named_scope("interfaces"):
        m1 = lax.ppermute(m1, "dep", swap)
        m3 = lax.ppermute(m2, "dep", [(i, i ^ 3) for i in range(dep_n)])
        m2 = lax.ppermute(m2, "dep", far)
    with jax.named_scope("finish"):
        return call(
            finish_kernel, slabs(2, levels),
            [work(2, levels), pltpu.SemaphoreType.DMA((2, GROUPS))],
            (y, a_end, b_end, own, m1, m2, m3), 10**6, 6 * levels * slab, 16,
            out_specs=HBM,
        )


def solution(mesh):
    in_specs = (
        P(None, "dep", None, "lon"),
        P("dep", None, "lon"),
        P("dep", None, "lon"),
        P("dep", None, "lon"),
        P("dep", None, "lon"),
        P(None, "lon"),
    )
    out_specs = P(None, "dep", None, "lon")
    return jax.shard_map(
        per_device, mesh=mesh, in_specs=in_specs, out_specs=out_specs, check_vma=False
    )
```

```python
import functools

import jax
import jax.numpy as jnp
from jax import lax
from jax.experimental import pallas as pl
from jax.experimental.pallas import tpu as pltpu
from jax.sharding import PartitionSpec as P

SUB = 4
THERMAL = 0.2
HALINE = 0.8
GROUPS = 4
ROWS = 32
STRIP = 32
HUGE = 1e30
MIB = 1024 * 1024

VMEM = pl.BlockSpec(memory_space=pltpu.VMEM)
HBM = pl.BlockSpec(memory_space=pltpu.HBM)


def lane_ids(rows):
    return lax.broadcasted_iota(jnp.int32, (rows, 128), 1)


def roll_lanes(x, amount):
    amount = amount % 128
    return x if amount == 0 else pltpu.roll(x, amount, 1)


def shift_north(x):
    return jnp.concatenate([x[8:], pltpu.roll(x[:8], 7, 0)], axis=0)


def shift_south(x):
    return jnp.concatenate([pltpu.roll(x[-8:], 1, 0), x[:-8]], axis=0)


def rows_of(ref, v, *lead):
    return ref[(*lead, pl.ds(v, 8, ref.shape[-2] // 8), slice(None))]


def neighbours(regs, v):
    north = regs[v + 1] if v + 1 < len(regs) else pltpu.roll(regs[0], 7, 0)
    south = regs[v - 1] if v > 0 else pltpu.roll(regs[-1], 1, 0)
    return north, south


def slab_of(ref, *lead):
    return jnp.concatenate([rows_of(ref, v, *lead) for v in range(ref.shape[-2] // 8)], axis=0)


def call(body, out_shape, scratch, args, flops, in_bytes, limit, in_specs=None, out_specs=None):
    return pl.pallas_call(
        body,
        out_shape=out_shape,
        in_specs=in_specs or [VMEM] * len(args),
        out_specs=out_specs or jax.tree.map(lambda _: VMEM, out_shape),
        scratch_shapes=scratch,
        compiler_params=pltpu.CompilerParams(vmem_limit_bytes=int(limit * MIB)),
        cost_estimate=pl.CostEstimate(flops=flops, bytes_accessed=in_bytes, transcendentals=0),
    )(*args)


def f32(*shape):
    return jax.ShapeDtypeStruct(shape, jnp.float32)


def pack_kernel(
    t_hbm, u_hbm, v_hbm, kh_hbm, b_hbm,
    sw_ref, se_ref, t0_ref, t1_ref, u_ref, v_ref,
    kh_buf, b_buf, first_buf, sems, more_sems,
):
    rows_e = u_ref.shape[0] // GROUPS
    lat = u_ref.shape[1]
    lane = lane_ids(lat)
    fields = ((t_hbm.at[0], t0_ref), (t_hbm.at[1], t1_ref), (u_hbm, u_ref), (v_hbm, v_ref))
    groups = [
        [
            pltpu.make_async_copy(
                src.at[pl.ds(g * rows_e, rows_e)], dst.at[pl.ds(g * rows_e, rows_e)], sems.at[g, n]
            )
            for n, (src, dst) in enumerate(fields)
        ]
        for g in range(GROUPS)
    ]
    tail = [
        pltpu.make_async_copy(b_hbm, b_buf, more_sems.at[0]),
        pltpu.make_async_copy(kh_hbm, kh_buf, more_sems.at[1]),
    ]
    for copy in sum(groups, []) + tail:
        copy.start()
    for g in range(GROUPS):
        for copy in groups[g]:
            copy.wait()
        for r in range(rows_e):
            level = g * rows_e + r
            slabs = [slab_of(ref, level) for ref in (t0_ref, t1_ref, u_ref, v_ref)]
            if g > 0:
                low, high = sw_ref[r], se_ref[r]
            for f, slab in enumerate(slabs):
                start = STRIP * g + 8 * f
                rolled = roll_lanes(slab, start)
                if start == 0:
                    first_buf[r] = rolled
                    low = rolled
                else:
                    low = jnp.where(lane >= start, rolled, low)
                    high = rolled if start == 8 else jnp.where(lane >= start - 8, rolled, high)
            if g == GROUPS - 1:
                high = jnp.where(lane >= 120, first_buf[r], high)
            sw_ref[r] = low
            se_ref[r] = high
    for copy in tail:
        copy.wait()
    low = jnp.zeros((lat, 128), jnp.float32)
    high = jnp.zeros((lat, 128), jnp.float32)
    bottom = slab_of(b_buf).astype(jnp.float32)
    for g in range(GROUPS):
        for r in range(rows_e):
            place = STRIP * g + r
            rolled = roll_lanes(slab_of(kh_buf, g * rows_e + r), place)
            low = jnp.where(lane == place, rolled, low)
            high = jnp.where(lane == (place - 1) % 128, rolled, high)
        place = STRIP * g + 16
        rolled = roll_lanes(bottom, place)
        low = jnp.where((lane >= place) & (lane < place + 8), rolled, low)
        high = jnp.where((lane >= place - 8) & (lane < place), rolled, high)
    sw_ref[rows_e] = low
    se_ref[rows_e] = high


def advect_block(slabs, get_c, get_u, get_v, get_level, bx, by, buf, coef, put):
    regs = bx.shape[0] // 8
    for i, slab in enumerate(slabs):
        level = get_level(slab)
        um = jnp.where(level < bx, get_u(slab), 0.0)
        vm = jnp.where(level < by, get_v(slab), 0.0)
        uw = roll_lanes(um, 1)
        vs = shift_south(vm)
        coef[0, i] = (
            1.0
            - jnp.maximum(um, 0.0)
            + jnp.minimum(uw, 0.0)
            - jnp.maximum(vm, 0.0)
            + jnp.minimum(vs, 0.0)
        )
        coef[1, i] = -jnp.minimum(um, 0.0)
        coef[2, i] = jnp.maximum(uw, 0.0)
        coef[3, i] = -jnp.minimum(vm, 0.0)
        coef[4, i] = jnp.maximum(vs, 0.0)
        for tr in range(2):
            buf[0, 2 * i + tr] = get_c(tr, slab)
    for step in range(SUB):
        src, dst = step % 2, (step + 1) % 2
        for i, slab in enumerate(slabs):
            now = [
                [buf[src, 2 * i + tr, 8 * v : 8 * v + 8] for v in range(regs)] for tr in range(2)
            ]
            for v in range(regs):
                js = slice(8 * v, 8 * v + 8)
                a, b, c, d, e = (coef[n, i, js] for n in range(5))
                for tr in range(2):
                    here = now[tr][v]
                    north, south = neighbours(now[tr], v)
                    new = (
                        a * here
                        + b * roll_lanes(here, -1)
                        + c * roll_lanes(here, 1)
                        + d * north
                        + e * south
                    )
                    if step < SUB - 1:
                        buf[dst, 2 * i + tr, js] = new
                    else:
                        put(tr, slab, js, new)


def face_limits(bottom):
    lat = bottom.shape[0]
    rows = lax.broadcasted_iota(jnp.int32, bottom.shape, 0)
    north = jnp.where(rows == lat - 1, 0.0, shift_north(bottom))
    return jnp.minimum(bottom, roll_lanes(bottom, -1)), jnp.minimum(bottom, north)


def lat_limits(bottom):
    lat = bottom.shape[0]
    rows = lax.broadcasted_iota(jnp.int32, bottom.shape, 0)
    north = jnp.where(rows == lat - 1, 0.0, shift_north(bottom))
    south = jnp.where(rows == 0, 0.0, shift_south(bottom))
    return jnp.minimum(north, south)


def advect_kernel(start, t0_ref, t1_ref, u_ref, v_ref, b_ref, earlier_ref, out_ref, buf, coef):
    del earlier_ref
    count, lat = out_ref.shape[1], out_ref.shape[2]
    base = lax.axis_index("dep") * t0_ref.shape[0] + start
    bx, by = face_limits(slab_of(b_ref).astype(jnp.float32))

    def put(tr, slab, js, new):
        out_ref[tr, slab, js] = new

    advect_block(
        list(range(count)),
        lambda tr, s: slab_of((t0_ref, t1_ref)[tr], start + s),
        lambda s: slab_of(u_ref, start + s),
        lambda s: slab_of(v_ref, start + s),
        lambda s: (base + s).astype(jnp.float32),
        bx,
        by,
        buf,
        coef,
        put,
    )


def join(lane_q, own_high, east, west, own_low):
    return jnp.where(
        lane_q < 16,
        jnp.where(lane_q < 8, own_high, east),
        jnp.where(lane_q < 24, west, own_low),
    )


def west_patch(slab, g):
    return roll_lanes(slab, -(STRIP * g + 24))


def east_patch(slab, g):
    return roll_lanes(slab, 120 - STRIP * g)


def patched(main, slab, g, lane):
    return jnp.where(
        lane < 4, west_patch(slab, g), jnp.where(lane >= 124, east_patch(slab, g), main)
    )


def pair_response(abc_ref, pair_ref, me):
    upper = lax.rem(me, 2) == 0
    low_pair = me < 2
    b_u = jnp.where(upper, abc_ref[1], pair_ref[1])
    a_l = jnp.where(upper, pair_ref[0], abc_ref[0])
    a_u = jnp.where(upper, abc_ref[0], pair_ref[0])
    b_l = jnp.where(upper, pair_ref[1], abc_ref[1])
    inv_t = 1.0 / (b_u + a_l)
    c_pair = jnp.where(upper == low_pair, pair_ref[2], abc_ref[2])
    share = c_pair * inv_t
    return share, inv_t, jnp.where(low_pair, b_l, a_u) - c_pair * share


def fold_strip(slab, place):
    lane = lane_ids(8)
    folded = jnp.zeros((8, 128), jnp.float32)
    for v in range(slab.shape[0] // 8):
        rolled = roll_lanes(slab[8 * v : 8 * v + 8], 16 * v - place)
        folded = jnp.where(lane >= 16 * v, rolled, folded)
    return folded


def unfold_strip(folded, place, regs):
    return jnp.concatenate([roll_lanes(folded, place - 16 * v) for v in range(regs)], axis=0)


def edge_kernel(
    sw_ref, se_ref, re_ref, rw_ref, b_ref, north_half, south_half, kh_ref, abc_ref, pair_ref,
    ea_ref, ek_ref, eb_ref, bmx_ref, first_ref, second_ref, red_ref,
    buf, coef, fields, pay,
):
    levels, lat = kh_ref.shape[0], kh_ref.shape[1]
    rows_e = levels // GROUPS
    me = lax.axis_index("dep")
    base = me * levels
    parity = lax.rem(me, 2)
    up_ref, down_ref = pay.at[1 - parity], pay.at[parity]
    lane = lane_ids(lat)
    lane_q = lane % STRIP
    bottom = slab_of(b_ref).astype(jnp.float32)
    eb = join(
        lane_q,
        roll_lanes(se_ref[rows_e], -8),
        roll_lanes(re_ref[rows_e], -8),
        roll_lanes(rw_ref[rows_e], 8),
        roll_lanes(sw_ref[rows_e], 8),
    )
    eb_ref[...] = eb
    b_west = roll_lanes(jnp.where(lane == 127, west_patch(eb, 0), bottom), 1)
    b_east = roll_lanes(jnp.where(lane == 0, east_patch(eb, 0), bottom), -1)
    bmx_ref[...] = jnp.minimum(b_west, b_east)
    for r in range(rows_e):
        ek_ref[r] = jnp.where(
            lane_q < 16,
            roll_lanes(re_ref[rows_e], 8 - r),
            roll_lanes(rw_ref[rows_e], 24 - r),
        )
        for f in range(4):
            fields[f, r] = join(
                lane_q,
                roll_lanes(se_ref[r], 8 - 8 * f),
                roll_lanes(re_ref[r], 8 - 8 * f),
                roll_lanes(rw_ref[r], 24 - 8 * f),
                roll_lanes(sw_ref[r], 24 - 8 * f),
            )
    bx, by = face_limits(eb)
    level0 = (base + (lane // STRIP) * rows_e).astype(jnp.float32)

    def put(tr, slab, js, new):
        ea_ref[tr, slab, js] = new

    advect_block(
        list(range(rows_e)),
        lambda tr, s: fields[tr, s],
        lambda s: fields[2, s],
        lambda s: fields[3, s],
        lambda s: level0 + float(s),
        bx,
        by,
        buf,
        coef,
        put,
    )
    top, half = rows_e - 1, levels // 2
    for tr in range(2):
        for n, (k, slab) in enumerate(((0, ea_ref[tr, 0]), (1, ea_ref[tr, 1]))):
            at = (2 * n + tr) * lat
            up_ref[at : at + lat] = patched(north_half[tr, k], slab, 0, lane)
        for n, (k, slab) in enumerate(
            ((half - 1, ea_ref[tr, top]), (half - 2, ea_ref[tr, top - 1]))
        ):
            at = (2 * n + tr) * lat
            down_ref[at : at + lat] = patched(south_half[tr, k], slab, 3, lane)
        at = 5 * lat + 8 * tr
        up_ref[at : at + 8] = fold_strip(ea_ref[tr, 0], 8)
        down_ref[at : at + 8] = fold_strip(ea_ref[tr, top], 3 * STRIP + 8)
    up_ref[4 * lat : 5 * lat] = slab_of(kh_ref, 0)
    down_ref[4 * lat : 5 * lat] = slab_of(kh_ref, levels - 1)
    first_ref[...] = pay[0]
    second_ref[0 : 5 * lat + 16] = pay[1]
    response = pair_response(abc_ref, pair_ref, me)
    for n in range(3):
        red_ref[n] = response[n]
    second_ref[5 * lat + 16 : 6 * lat + 16] = response[2]


def slopes(gx, gy, gz):
    rx, ry, rz = (-0.5 * THERMAL * g[0] + 0.5 * HALINE * g[1] for g in (gx, gy, gz))
    scale = rz / (1.0 + rx * rx + ry * ry + rz * rz)
    return rx * scale, ry * scale


def flux_xyz(gx, gy, gz, kappa, need_xy=True):
    sx, sy = slopes(gx, gy, gz)
    kx, ky = kappa * sx, kappa * sy
    kz = kx * sx + ky * sy
    fz = [kx * gx[n] + ky * gy[n] + kz * gz[n] for n in range(2)]
    if not need_xy:
        return None, None, fz
    fx = [kappa * gx[n] + kx * gz[n] for n in range(2)]
    fy = [kappa * gy[n] + ky * gz[n] for n in range(2)]
    return fx, fy, fz


def flux_x_edge(gx, gy, gz, kappa):
    sx, _ = slopes(gx, gy, gz)
    kx = kappa * sx
    return [kappa * gx[n] + kx * gz[n] for n in range(2)]


def diff(mask, high, low):
    return jnp.where(mask, high - low, 0.0)


def edge_flux_row(r, rows, ek, eb, ebx, eby, level0):
    level = level0 + r
    mx = level < ebx
    my = level < eby
    mz = (level + 1.0 < eb) & (level >= 1.0)
    kappa = jnp.where((level < eb) & (level >= 0.0), 0.25 * ek, 0.0)
    gx, gy, gz = [], [], []
    for tr in range(2):
        here = rows[tr, r + 1]
        gx.append(diff(mx, roll_lanes(here, -1), roll_lanes(here, 1)))
        gy.append(diff(my, shift_north(here), shift_south(here)))
        gz.append(diff(mz, rows[tr, r + 2], rows[tr, r]))
    return flux_x_edge(gx, gy, gz, kappa)


def edge_limits(eb):
    return (
        jnp.minimum(roll_lanes(eb, 1), roll_lanes(eb, -1)),
        lat_limits(eb),
    )


def zonal_change(fx, west, east, lane):
    return roll_lanes(jnp.where(lane == 0, east, fx), -1) - roll_lanes(
        jnp.where(lane == 127, west, fx), 1
    )


def divergence(fx, fy, slab, g, lane):
    return zonal_change(fx, west_patch(slab, g), east_patch(slab, g), lane) + (
        shift_north(fy) - shift_south(fy)
    )


def patch_kernel(
    north_half, south_half, ea_ref, ek_ref, eb_ref,
    full_ref, gx_ref, efx_ref,
    rows,
):
    levels, lat = full_ref.shape[1], full_ref.shape[2]
    rows_e = levels // GROUPS
    base = lax.axis_index("dep") * levels
    lane = lane_ids(lat)
    eb = eb_ref[...]
    ebx, eby = edge_limits(eb)
    level0 = (base + (lane // STRIP) * rows_e).astype(jnp.float32)
    for tr in range(2):
        for r in range(rows_e):
            rows[tr, r + 1] = ea_ref[tr, r]
        rows[tr, 0] = roll_lanes(ea_ref[tr, rows_e - 1], STRIP)
        rows[tr, rows_e + 1] = roll_lanes(ea_ref[tr, 0], -STRIP)
    found = [
        edge_flux_row(r, rows, ek_ref[r], eb, ebx, eby, level0) for r in range(rows_e)
    ]
    for r in range(rows_e):
        for tr in range(2):
            efx_ref[tr, r] = found[r][tr]

    lane = lane_ids(ROWS)
    units = [(g, slice(j, j + ROWS)) for g in range(GROUPS) for j in range(0, lat, ROWS)]

    def patch(r, _):
        def fetch(unit):
            g, js = unit
            strips = [ea_ref[tr, r, js] for tr in range(2)]
            half = (north_half, south_half)[2 * g // GROUPS]
            mains = [half[tr, g % (GROUPS // 2) * rows_e + r, js] for tr in range(2)]
            return [(west_patch(x, g), east_patch(x, g), y) for x, y in zip(strips, mains)]

        def put(unit, mains, rolled):
            g, js = unit
            for tr in range(2):
                full_ref[tr, g * rows_e + r, js] = mains[tr]
                gx_ref[tr, g * rows_e + r, js] = rolled[tr][0] - rolled[tr][1]

        waiting = None
        fetched = fetch(units[0])
        for n, unit in enumerate(units):
            now = fetched
            fetched = fetch(units[n + 1]) if n + 1 < len(units) else None
            mains, rolled = [], []
            for west, east, main in now:
                main = jnp.where(lane < 4, west, jnp.where(lane >= 124, east, main))
                mains.append(main)
                rolled.append(
                    (
                        roll_lanes(jnp.where(lane == 0, east, main), -1),
                        roll_lanes(jnp.where(lane == 127, west, main), 1),
                    )
                )
            if waiting is not None:
                put(*waiting)
            waiting = (unit, mains, rolled)
        put(*waiting)
        return 0

    lax.fori_loop(0, rows_e, patch, 0)


def flux_kernel(
    full_ref, gx_ref, efx_ref, bmx_ref, b_ref, kh_ref,
    q_ref, fz_ref,
    limits,
):
    levels, lat = full_ref.shape[1], full_ref.shape[2]
    rows_e = levels // GROUPS
    base = lax.axis_index("dep") * levels
    lane = lane_ids(lat)
    bottom = slab_of(b_ref).astype(jnp.float32)
    limits[0] = bmx_ref[...]
    limits[1] = lat_limits(bottom)
    limits[2] = bottom

    def north_rows(tr, k, j):
        if j + 8 + ROWS <= lat:
            return full_ref[tr, k, j + 8 : j + 8 + ROWS]
        return jnp.concatenate(
            [full_ref[tr, k, j + 8 : lat], pltpu.roll(full_ref[tr, k, 0:8], 7, 0)], axis=0
        )

    def south_rows(tr, k, j):
        if j >= 8:
            return full_ref[tr, k, j - 8 : j - 8 + ROWS]
        return jnp.concatenate(
            [pltpu.roll(full_ref[tr, k, lat - 8 : lat], 1, 0), full_ref[tr, k, 0 : ROWS - 8]],
            axis=0,
        )

    def fluxes(r, _):
        for g in range(GROUPS):
            k = g * rows_e + r
            above, below = jnp.maximum(k - 1, 0), jnp.minimum(k + 1, levels - 1)
            level = (base + k).astype(jnp.float32)
            level_z = jnp.where(level >= 1.0, level + 1.0, HUGE)
            sides = [
                (west_patch(efx_ref[tr, r], g), east_patch(efx_ref[tr, r], g)) for tr in range(2)
            ]
            fxs, fys, fzs = [[], []], [[], []], [[], []]
            for j in range(0, lat, ROWS):
                js = slice(j, j + ROWS)
                mx = level < limits[0, js]
                my = level < limits[1, js]
                mz = level_z < limits[2, js]
                kh = jnp.concatenate(
                    [rows_of(kh_ref, v, k) for v in range(j // 8, (j + ROWS) // 8)], axis=0
                )
                kappa = jnp.where(level < limits[2, js], 0.25 * kh, 0.0)
                gx, gy, gz = [], [], []
                for tr in range(2):
                    gx.append(jnp.where(mx, gx_ref[tr, k, js], 0.0))
                    gy.append(diff(my, north_rows(tr, k, j), south_rows(tr, k, j)))
                    gz.append(diff(mz, full_ref[tr, below, js], full_ref[tr, above, js]))
                fx, fy, fz = flux_xyz(gx, gy, gz, kappa)
                for tr in range(2):
                    fxs[tr].append(fx[tr])
                    fys[tr].append(fy[tr])
                    fzs[tr].append(fz[tr])
            wet = level < limits[2]
            new = []
            for tr in range(2):
                fy = jnp.concatenate(fys[tr], axis=0)
                change = zonal_change(jnp.concatenate(fxs[tr], axis=0), *sides[tr], lane)
                change = change + (shift_north(fy) - shift_south(fy))
                new.append(full_ref[tr, k] + jnp.where(wet, change, 0.0))
            for tr in range(2):
                q_ref[tr, k] = new[tr]
                fz_ref[tr, k] = jnp.concatenate(fzs[tr], axis=0)
        return 0

    lax.fori_loop(0, rows_e, fluxes, 0)


def factor_kernel(kv_ref, b_ref, inv_ref, ei_ref, ratio_ref, a_ref, bb_ref, abc_ref):
    levels, lat = kv_ref.shape[0], kv_ref.shape[1]
    base = lax.axis_index("dep") * levels
    bottom = slab_of(b_ref).astype(jnp.float32)

    def coupling(k):
        level = (base + k).astype(jnp.float32)
        level = jnp.where(level >= 1.0, level, HUGE)
        return jnp.where(level < bottom, slab_of(kv_ref, k), 0.0)

    top = coupling(0)
    e = jnp.zeros((lat, 128), jnp.float32)
    q = e
    za = jnp.ones((lat, 128), jnp.float32)
    for k in range(levels):
        low = coupling(k + 1) if k + 1 < levels else jnp.zeros((lat, 128), jnp.float32)
        eq = 1.0 + e * q
        inv = 1.0 / (eq + low)
        inv_ref[k] = inv
        ei = e * inv
        ei_ref[k] = ei
        ratio_ref[k] = low * inv
        za = inv if k == 0 else za * ei
        a_ref[k] = za
        q = eq * inv
        e = low
    bb_ref[levels - 1] = inv
    b = inv
    a = za
    for k in range(levels - 2, -1, -1):
        ratio = ratio_ref[k]
        b = ratio * b
        a = a_ref[k] + ratio * a
        bb_ref[k] = b
        a_ref[k] = a
    abc_ref[0] = a + jnp.where(top > 0.0, 1.0 / jnp.maximum(top, 1e-30), HUGE)
    abc_ref[1] = inv
    abc_ref[2] = b


def solve_kernel(
    full_ref, q_ref, fz_ref, ea_ref, ek_ref, eb_ref, bmx_ref, b_ref, kh_ref,
    first_ref, second_ref, inv_ref, ei_ref, ratio_ref, red_ref,
    y_ref, m1_ref, m2_ref, own_ref,
    pad, epad, fze, halo,
):
    levels, lat = q_ref.shape[1], q_ref.shape[2]
    rows_e = levels // GROUPS
    last = levels - 1
    top = rows_e - 1
    me = lax.axis_index("dep")
    base = me * levels
    parity = lax.rem(me, 2)
    outer = (me == 0) | (me == 3)
    upper = parity == 0
    sign = jnp.where(me < 2, 1.0, -1.0)
    lane = lane_ids(lat)
    halo[0] = first_ref[...]
    halo[1] = second_ref[0 : 5 * lat + 16]
    above_ref, below_ref = halo.at[1 - parity], halo.at[parity]

    share = red_ref[0]
    both = red_ref[2] + second_ref[5 * lat + 16 : 6 * lat + 16]
    cross = share / both
    inside = red_ref[1] + share * cross
    for n, value in enumerate((share, red_ref[1], both)):
        own_ref[n] = value
    m1_ref[2] = both

    eb = eb_ref[...]
    ebx, eby = edge_limits(eb)
    level0 = (base + (lane // STRIP) * rows_e).astype(jnp.float32)
    for tr in range(2):
        pad[tr, 0] = above_ref[(2 + tr) * lat : (3 + tr) * lat]
        pad[tr, 1] = above_ref[tr * lat : (1 + tr) * lat]
        for n, k in enumerate((0, 1, 2, last - 2, last - 1, last)):
            pad[tr, n + 2] = full_ref[tr, k]
        pad[tr, 8] = below_ref[tr * lat : (1 + tr) * lat]
        pad[tr, 9] = below_ref[(2 + tr) * lat : (3 + tr) * lat]
        for r in range(rows_e):
            epad[tr, r + 1] = ea_ref[tr, r]
        at = 5 * lat + 8 * tr
        corner_up = unfold_strip(above_ref[at : at + 8], 3 * STRIP + 8, lat // 8)
        corner_dn = unfold_strip(below_ref[at : at + 8], 8, lat // 8)
        epad[tr, 0] = roll_lanes(
            jnp.where(lane >= 3 * STRIP, corner_up, ea_ref[tr, top]), STRIP
        )
        epad[tr, rows_e + 1] = roll_lanes(
            jnp.where(lane < STRIP, corner_dn, ea_ref[tr, 0]), -STRIP
        )
    efx = {
        r + 1: edge_flux_row(r, epad, ek_ref[r], eb, ebx, eby, level0) for r in (0, top)
    }

    bottom = slab_of(b_ref).astype(jnp.float32)
    bmy = lat_limits(bottom)
    bmx = bmx_ref[...]
    ends = (
        (1, -1, 0, 0, above_ref[4 * lat : 5 * lat], True),
        (2, 0, 1, 0, slab_of(kh_ref, 0), False),
        (7, last, top + 1, 3, slab_of(kh_ref, last), False),
        (8, last + 1, top + 2, 3, below_ref[4 * lat : 5 * lat], True),
    )
    spread = {}
    for m, (n, k, er, g, kappa_slab, only_z) in enumerate(ends):
        level = (base + k).astype(jnp.float32)
        level_z = jnp.where(level >= 1.0, level + 1.0, HUGE)
        level_h = jnp.where(level >= 0.0, level, HUGE)
        mx = level_h < bmx
        my = level_h < bmy
        mz = level_z < bottom
        kappa = jnp.where(level_h < bottom, 0.25 * kappa_slab, 0.0)
        gx, gy, gz = [], [], []
        for tr in range(2):
            slab, main = epad[tr, er], pad[tr, n]
            change = zonal_change(main, west_patch(slab, g), east_patch(slab, g), lane)
            gx.append(jnp.where(mx, change, 0.0))
            gy.append(diff(my, shift_north(main), shift_south(main)))
            gz.append(diff(mz, pad[tr, n + 1], pad[tr, n - 1]))
        fx, fy, fz = flux_xyz(gx, gy, gz, kappa, not only_z)
        for tr in range(2):
            fze[tr, m] = fz[tr]
            if not only_z:
                spread[k, tr] = divergence(fx[tr], fy[tr], efx[er][tr], g, lane)

    def vertical_flux(tr, k):
        place = {-1: 0, 0: 1, last: 2, last + 1: 3}.get(k)
        return fz_ref[tr, k] if place is None else fze[tr, place]

    z = [None, None]
    for k in range(levels):
        level = (base + k).astype(jnp.float32)
        wet = level < bottom
        for tr in range(2):
            change = vertical_flux(tr, k + 1) - vertical_flux(tr, k - 1)
            if k == 0 or k == last:
                change = change + spread[k, tr]
                start = pad[tr, 2 if k == 0 else 7]
            else:
                start = q_ref[tr, k]
            rhs = start + jnp.where(wet, change, 0.0)
            new = rhs * inv_ref[k]
            z[tr] = new if k == 0 else new + ei_ref[k] * z[tr]
        for tr in range(2):
            y_ref[tr, k] = z[tr]
    low = list(z)
    for k in range(last - 1, -1, -1):
        ratio = ratio_ref[k]
        z = [y_ref[tr, k] + ratio * z[tr] for tr in range(2)]
        for tr in range(2):
            y_ref[tr, k] = z[tr]
    for tr in range(2):
        near = jnp.where(upper, low[tr], z[tr])
        far = jnp.where(upper, z[tr], low[tr])
        m1_ref[tr] = jnp.where(outer, near, sign * (inside * near - cross * far))
        m2_ref[tr] = jnp.where(outer, share * near, far - share * near)


def finish_kernel(
    y_ref, a_ref, bb_ref, own_ref, r1_ref, r2_ref, r3_ref, out_hbm, out, sems
):
    levels = y_ref.shape[1]
    me = lax.axis_index("dep")
    upper = lax.rem(me, 2) == 0
    outer = (me == 0) | (me == 3)
    sign = jnp.where(me < 2, 1.0, -1.0)
    share, inv_t = own_ref[0], own_ref[1]
    inv_e = 1.0 / jnp.where(outer, r1_ref[2], own_ref[2])
    cross = share * inv_e
    inside = inv_t + share * cross
    tops, lows = [], []
    for tr in range(2):
        y_top, y_low = y_ref[tr, 0], y_ref[tr, levels - 1]
        near = jnp.where(upper, y_low, y_top)
        far = jnp.where(upper, y_top, y_low)
        mate, across = r1_ref[tr], r2_ref[tr] + r3_ref[tr]
        pair_flux = jnp.where(
            outer,
            mate + sign * (cross * across - inside * near),
            sign * (inside * (near - mate) + cross * (across - far)),
        )
        middle = sign * (inv_e * (across - far + share * near) - cross * mate)
        middle = jnp.where(outer, 0.0, middle)
        tops.append(jnp.where(upper, middle, pair_flux))
        lows.append(jnp.where(upper, pair_flux, middle))
    step, regs = levels // GROUPS, y_ref.shape[2] // 8
    copies = []
    for part in range(GROUPS):
        for k in range(part * step, (part + 1) * step):
            a, b = a_ref[k], bb_ref[k]
            new = [y_ref[tr, k] - tops[tr] * a + lows[tr] * b for tr in range(2)]
            for tr in range(2):
                for v in range(regs):
                    out[tr, k, pl.ds(v, 8, regs), :] = new[tr][8 * v : 8 * v + 8]
        for tr in range(2):
            span = (tr, pl.ds(part * step, step))
            copies.append(
                pltpu.make_async_copy(out.at[span], out_hbm.at[span], sems.at[tr, part])
            )
            copies[-1].start()
    for copy in copies:
        copy.wait()


def per_device(tracers, u_east, v_north, kappa_h, kappa_v, bottom):
    _, levels, lat, lon = tracers.shape
    rows_e = levels // GROUPS
    lon_n, dep_n = lax.axis_size("lon"), lax.axis_size("dep")
    east = [(i, (i + 1) % lon_n) for i in range(lon_n)]
    west = [(t, s) for s, t in east]
    slab = lat * lon * 4
    slabs = lambda *lead: f32(*lead, lat, lon)
    work = lambda *lead: pltpu.VMEM(lead + (lat, lon), jnp.float32)

    with jax.named_scope("pack"):
        sw, se, t0, t1, u, v = call(
            pack_kernel, (slabs(rows_e + 1),) * 2 + (slabs(levels),) * 4,
            [
                work(levels), pltpu.VMEM((lat, lon), jnp.int32), work(rows_e),
                pltpu.SemaphoreType.DMA((GROUPS, 4)), pltpu.SemaphoreType.DMA((2,)),
            ],
            (tracers, u_east, v_north, kappa_h, bottom), 10**6, 6 * levels * slab, 50.8,
            in_specs=[HBM] * 5,
        )
    with jax.named_scope("lon_halo"):
        r_east = lax.ppermute(sw, "lon", west)
        r_west = lax.ppermute(se, "lon", east)
    with jax.named_scope("factor"):
        inv, ei, ratio, a_end, b_end, abc = call(
            factor_kernel, (slabs(levels),) * 5 + (slabs(3),), [],
            (kappa_v, bottom), 10**7, 6 * levels * slab, 16,
        )
    swap = [(i, i ^ 1) for i in range(dep_n)]
    with jax.named_scope("pair_coefficients"):
        pair = lax.ppermute(abc, "dep", swap)
    half = levels // 2

    def advect_half(start, earlier):
        return call(
            functools.partial(advect_kernel, start), slabs(2, half),
            [work(2, 2 * half), work(5, half)],
            (t0, t1, u, v, bottom, earlier), 10**7, 4 * levels * slab, 16,
        )

    with jax.named_scope("advect_north"):
        north_half = advect_half(0, abc)
    with jax.named_scope("advect_south"):
        south_half = advect_half(half, abc)
    rows_pay = 5 * lat + 16
    with jax.named_scope("advect_edge"):
        ea, ek, eb, bmx, first, second, red = call(
            edge_kernel,
            (
                slabs(2, rows_e), slabs(rows_e), slabs(), slabs(),
                f32(rows_pay, lon), f32(rows_pay + lat, lon), slabs(3),
            ),
            [
                work(2, 2 * rows_e), work(5, rows_e), work(4, rows_e),
                pltpu.VMEM((2, rows_pay, lon), jnp.float32),
            ],
            (sw, se, r_east, r_west, bottom, north_half, south_half, kappa_h, abc, pair),
            10**6, 3 * levels * slab, 16,
        )
    other = []
    for i in range(lon_n * dep_n):
        row, place = divmod(i, dep_n)
        if place in (0, dep_n - 1):
            other.append((i, (row ^ 1) * dep_n + place))
        else:
            other.append((i, i + 1 if place % 2 else i - 1))
    with jax.named_scope("dep_halo"):
        first = lax.ppermute(first, "dep", swap)
        second = lax.ppermute(second, ("lon", "dep"), other)
    with jax.named_scope("patch"):
        full, gx, efx = call(
            patch_kernel, (slabs(2, levels), slabs(2, levels), slabs(2, rows_e)),
            [work(2, rows_e + 2)],
            (north_half, south_half, ea, ek, eb), 10**7, 8 * levels * slab, 16,
        )
    with jax.named_scope("fluxes"):
        q_part, fz = call(
            flux_kernel, (slabs(2, levels), slabs(2, levels)), [work(3)],
            (full, gx, efx, bmx, bottom, kappa_h), 10**7, 10 * levels * slab, 16,
        )
    with jax.named_scope("solve"):
        y, m1, m2, own = call(
            solve_kernel, (slabs(2, levels), slabs(3), slabs(2), slabs(3)),
            [
                work(2, 10), work(2, rows_e + 2), work(2, 4),
                pltpu.VMEM((2, rows_pay, lon), jnp.float32),
            ],
            (
                full, q_part, fz, ea, ek, eb, bmx, bottom, kappa_h, first, second,
                inv, ei, ratio, red,
            ),
            10**7, 12 * levels * slab, 24,
        )
    with jax.named_scope("interfaces"):
        m1 = lax.ppermute(m1, "dep", swap)
        m3 = lax.ppermute(m2, "dep", [(i, i ^ 3) for i in range(dep_n)])
        m2 = lax.ppermute(m2, "dep", [(i, i ^ 2) for i in range(dep_n)])
    with jax.named_scope("finish"):
        return call(
            finish_kernel, slabs(2, levels),
            [work(2, levels), pltpu.SemaphoreType.DMA((2, GROUPS))],
            (y, a_end, b_end, own, m1, m2, m3), 10**6, 6 * levels * slab, 16,
            out_specs=HBM,
        )


def solution(mesh):
    in_specs = (
        P(None, "dep", None, "lon"),
        P("dep", None, "lon"),
        P("dep", None, "lon"),
        P("dep", None, "lon"),
        P("dep", None, "lon"),
        P(None, "lon"),
    )
    out_specs = P(None, "dep", None, "lon")
    return jax.shard_map(
        per_device, mesh=mesh, in_specs=in_specs, out_specs=out_specs, check_vma=False
    )
```

```python
import functools

import jax
import jax.numpy as jnp
from jax import lax
from jax.experimental import pallas as pl
from jax.experimental.pallas import tpu as pltpu
from jax.sharding import PartitionSpec as P

SUB = 4
THERMAL = 0.2
HALINE = 0.8
GROUPS = 4
ROWS = 32
STRIP = 32
HUGE = 1e30
MIB = 1024 * 1024

VMEM = pl.BlockSpec(memory_space=pltpu.VMEM)
HBM = pl.BlockSpec(memory_space=pltpu.HBM)


def lane_ids(rows):
    return lax.broadcasted_iota(jnp.int32, (rows, 128), 1)


def roll_lanes(x, amount):
    amount = amount % 128
    return x if amount == 0 else pltpu.roll(x, amount, 1)


def shift_north(x):
    return jnp.concatenate([x[8:], pltpu.roll(x[:8], 7, 0)], axis=0)


def shift_south(x):
    return jnp.concatenate([pltpu.roll(x[-8:], 1, 0), x[:-8]], axis=0)


def rows_of(ref, v, *lead):
    return ref[(*lead, pl.ds(v, 8, ref.shape[-2] // 8), slice(None))]


def neighbours(regs, v):
    north = regs[v + 1] if v + 1 < len(regs) else pltpu.roll(regs[0], 7, 0)
    south = regs[v - 1] if v > 0 else pltpu.roll(regs[-1], 1, 0)
    return north, south


def slab_of(ref, *lead):
    return jnp.concatenate([rows_of(ref, v, *lead) for v in range(ref.shape[-2] // 8)], axis=0)


def call(body, out_shape, scratch, args, flops, in_bytes, limit, in_specs=None, out_specs=None):
    return pl.pallas_call(
        body,
        out_shape=out_shape,
        in_specs=in_specs or [VMEM] * len(args),
        out_specs=out_specs or jax.tree.map(lambda _: VMEM, out_shape),
        scratch_shapes=scratch,
        compiler_params=pltpu.CompilerParams(vmem_limit_bytes=int(limit * MIB)),
        cost_estimate=pl.CostEstimate(flops=flops, bytes_accessed=in_bytes, transcendentals=0),
    )(*args)


def f32(*shape):
    return jax.ShapeDtypeStruct(shape, jnp.float32)


def pack_kernel(
    t_hbm, u_hbm, v_hbm, kh_hbm, b_hbm,
    sw_ref, se_ref, bp_ref, ww_ref, we_ref, t0_ref, t1_ref, u_ref, v_ref,
    kh_buf, b_buf, first_buf, sems, more_sems,
):
    rows_e = u_ref.shape[0] // GROUPS
    lat = u_ref.shape[1]
    lane = lane_ids(lat)
    fields = ((t_hbm.at[0], t0_ref), (t_hbm.at[1], t1_ref), (u_hbm, u_ref), (v_hbm, v_ref))
    groups = [
        [
            pltpu.make_async_copy(
                src.at[pl.ds(g * rows_e, rows_e)], dst.at[pl.ds(g * rows_e, rows_e)], sems.at[g, n]
            )
            for n, (src, dst) in enumerate(fields)
        ]
        for g in range(GROUPS)
    ]
    tail = [
        pltpu.make_async_copy(b_hbm, b_buf, more_sems.at[0]),
        pltpu.make_async_copy(kh_hbm, kh_buf, more_sems.at[1]),
    ]
    for copy in sum(groups, []) + tail:
        copy.start()
    for g in range(GROUPS):
        for copy in groups[g]:
            copy.wait()
        for batch in (range(0, rows_e // 2), range(rows_e // 2, rows_e)):
            rolled = {
                (r, f): roll_lanes(slab_of(ref, g * rows_e + r), STRIP * g + 8 * f)
                for r in batch
                for f, ref in enumerate((t0_ref, t1_ref, u_ref, v_ref))
            }
            done = []
            for r in batch:
                low = rolled[r, 0]
                high = None
                if g > 0:
                    low = jnp.where(lane >= STRIP * g, low, sw_ref[r])
                    high = jnp.where(lane >= STRIP * g - 8, rolled[r, 0], se_ref[r])
                for f in range(1, 4):
                    start = STRIP * g + 8 * f
                    low = jnp.where(lane >= start, rolled[r, f], low)
                    if high is None:
                        high = rolled[r, f]
                    else:
                        high = jnp.where(lane >= start - 8, rolled[r, f], high)
                if g == GROUPS - 1:
                    high = jnp.where(lane >= 120, first_buf[r], high)
                done.append((r, low, high))
            for r, low, high in done:
                if g == 0:
                    first_buf[r] = rolled[r, 0]
                sw_ref[r] = low
                se_ref[r] = high
    for copy in tail:
        copy.wait()
    bottom = slab_of(b_buf).astype(jnp.float32)
    place = bottom
    for g in range(1, GROUPS):
        place = jnp.where(lane >= STRIP * g - 8, roll_lanes(bottom, STRIP * g), place)
    place = jnp.where(lane >= 120, bottom, place)
    bp_ref[...] = place

    def kappa(r):
        out = None
        for g in range(GROUPS):
            rolled = roll_lanes(slab_of(kh_buf, g * rows_e + r), STRIP * g + 23)
            out = rolled if g == 0 else jnp.where(lane >= STRIP * g + 8, rolled, out)
        return out

    last = rows_e - 1
    kappa_last = kappa(last)
    lane_q = lane % STRIP
    low_last, high_last = sw_ref[last], se_ref[last]
    wires = []
    for r in range(last):
        k = kappa(r)
        low, high = sw_ref[r], se_ref[r]
        west = (low, roll_lanes(low, -2), roll_lanes(low, -4), roll_lanes(low, -6), k)
        east = (
            roll_lanes(high, 6), roll_lanes(high, 4), roll_lanes(high, 2), roll_lanes(high, -1),
            roll_lanes(k, 1),
        )
        west += (roll_lanes(low_last, 24 - 8 * r),)
        east += (roll_lanes(high_last, 5 if r == 3 else 30 - 8 * r),)
        if r == 3:
            west += (roll_lanes(kappa_last, 6),)
            east += (roll_lanes(kappa_last, 7),)
        else:
            west += (roll_lanes(place, 30 - 2 * r),)
            east += (roll_lanes(place, 36 - 2 * r),)
        starts = (6, 12, 18, 23, 24, 29 if r == 3 else 30)
        for ref, parts in ((ww_ref, west), (we_ref, east)):
            wire = parts[0]
            for start, part in zip(starts, parts[1:]):
                wire = jnp.where(lane_q >= start, part, wire)
            wires.append((ref, r, wire))
    for ref, r, wire in wires:
        ref[r] = wire


def advect_block(slabs, get_c, get_u, get_v, get_level, bx, by, buf, coef, put):
    regs = bx.shape[0] // 8
    for i, slab in enumerate(slabs):
        level = get_level(slab)
        um = jnp.where(level < bx, get_u(slab), 0.0)
        vm = jnp.where(level < by, get_v(slab), 0.0)
        uw = roll_lanes(um, 1)
        vs = shift_south(vm)
        coef[0, i] = (
            1.0
            - jnp.maximum(um, 0.0)
            + jnp.minimum(uw, 0.0)
            - jnp.maximum(vm, 0.0)
            + jnp.minimum(vs, 0.0)
        )
        coef[1, i] = -jnp.minimum(um, 0.0)
        coef[2, i] = jnp.maximum(uw, 0.0)
        coef[3, i] = -jnp.minimum(vm, 0.0)
        coef[4, i] = jnp.maximum(vs, 0.0)
        for tr in range(2):
            buf[0, 2 * i + tr] = get_c(tr, slab)
    for step in range(SUB):
        src, dst = step % 2, (step + 1) % 2
        for i, slab in enumerate(slabs):
            now = [
                [buf[src, 2 * i + tr, 8 * v : 8 * v + 8] for v in range(regs)] for tr in range(2)
            ]
            for v in range(regs):
                js = slice(8 * v, 8 * v + 8)
                a, b, c, d, e = (coef[n, i, js] for n in range(5))
                for tr in range(2):
                    here = now[tr][v]
                    north, south = neighbours(now[tr], v)
                    new = (
                        a * here
                        + b * roll_lanes(here, -1)
                        + c * roll_lanes(here, 1)
                        + d * north
                        + e * south
                    )
                    if step < SUB - 1:
                        buf[dst, 2 * i + tr, js] = new
                    else:
                        put(tr, slab, js, new)


def face_limits(bottom):
    lat = bottom.shape[0]
    rows = lax.broadcasted_iota(jnp.int32, bottom.shape, 0)
    north = jnp.where(rows == lat - 1, 0.0, shift_north(bottom))
    return jnp.minimum(bottom, roll_lanes(bottom, -1)), jnp.minimum(bottom, north)


def lat_limits(bottom):
    lat = bottom.shape[0]
    rows = lax.broadcasted_iota(jnp.int32, bottom.shape, 0)
    north = jnp.where(rows == lat - 1, 0.0, shift_north(bottom))
    south = jnp.where(rows == 0, 0.0, shift_south(bottom))
    return jnp.minimum(north, south)


def advect_kernel(start, t0_ref, t1_ref, u_ref, v_ref, b_ref, earlier_ref, out_ref, buf, coef):
    del earlier_ref
    count, lat = out_ref.shape[1], out_ref.shape[2]
    base = lax.axis_index("dep") * t0_ref.shape[0] + start
    bx, by = face_limits(slab_of(b_ref).astype(jnp.float32))

    def put(tr, slab, js, new):
        out_ref[tr, slab, js] = new

    advect_block(
        list(range(count)),
        lambda tr, s: slab_of((t0_ref, t1_ref)[tr], start + s),
        lambda s: slab_of(u_ref, start + s),
        lambda s: slab_of(v_ref, start + s),
        lambda s: (base + s).astype(jnp.float32),
        bx,
        by,
        buf,
        coef,
        put,
    )


def join(lane_q, own_high, east, west, own_low):
    return jnp.where(
        lane_q < 16,
        jnp.where(lane_q < 8, own_high, east),
        jnp.where(lane_q < 24, west, own_low),
    )


def west_patch(slab, g):
    return roll_lanes(slab, -(STRIP * g + 24))


def east_patch(slab, g):
    return roll_lanes(slab, 120 - STRIP * g)


def patched(main, slab, g, lane):
    return jnp.where(
        lane < 4, west_patch(slab, g), jnp.where(lane >= 124, east_patch(slab, g), main)
    )


def pair_response(abc_ref, pair_ref, me):
    upper = lax.rem(me, 2) == 0
    low_pair = me < 2
    b_u = jnp.where(upper, abc_ref[1], pair_ref[1])
    a_l = jnp.where(upper, pair_ref[0], abc_ref[0])
    a_u = jnp.where(upper, abc_ref[0], pair_ref[0])
    b_l = jnp.where(upper, pair_ref[1], abc_ref[1])
    inv_t = 1.0 / (b_u + a_l)
    c_pair = jnp.where(upper == low_pair, pair_ref[2], abc_ref[2])
    share = c_pair * inv_t
    return share, inv_t, jnp.where(low_pair, b_l, a_u) - c_pair * share


def fold_strip(slab, place):
    lane = lane_ids(8)
    folded = jnp.zeros((8, 128), jnp.float32)
    for v in range(slab.shape[0] // 8):
        rolled = roll_lanes(slab[8 * v : 8 * v + 8], 16 * v - place)
        folded = jnp.where(lane >= 16 * v, rolled, folded)
    return folded


def unfold_strip(folded, place, regs):
    return jnp.concatenate([roll_lanes(folded, place - 16 * v) for v in range(regs)], axis=0)


def edge_kernel(
    sw_ref, se_ref, bp_ref, re_ref, rw_ref, b_ref, north_half, south_half, kh_ref, abc_ref, pair_ref,
    ea_ref, ek_ref, eb_ref, bmx_ref, first_ref, second_ref, red_ref,
    buf, coef, fields, pay,
):
    levels, lat = kh_ref.shape[0], kh_ref.shape[1]
    rows_e = levels // GROUPS
    me = lax.axis_index("dep")
    base = me * levels
    parity = lax.rem(me, 2)
    up_ref, down_ref = pay.at[1 - parity], pay.at[parity]
    lane = lane_ids(lat)
    lane_q = lane % STRIP
    bottom = slab_of(b_ref).astype(jnp.float32)
    place = bp_ref[...]
    east = [roll_lanes(re_ref[r], 2 * r - 22) for r in range(3)]
    west = [roll_lanes(rw_ref[r], 2 * r - 12) for r in range(3)]
    eb = join(
        lane_q,
        roll_lanes(place, 8),
        jnp.where(lane_q < 10, east[0], jnp.where(lane_q < 12, east[1], east[2])),
        jnp.where(lane_q < 20, west[0], jnp.where(lane_q < 22, west[1], west[2])),
        roll_lanes(place, 24),
    )
    eb_ref[...] = eb
    b_west = roll_lanes(jnp.where(lane == 127, west_patch(eb, 0), bottom), 1)
    b_east = roll_lanes(jnp.where(lane == 0, east_patch(eb, 0), bottom), -1)
    bmx_ref[...] = jnp.minimum(b_west, b_east)
    last = rows_e - 1
    for r in range(rows_e):
        at, shift_e, shift_w = (3, -21, -6) if r == last else (r, -15, 0)
        ek_ref[r] = jnp.where(
            lane_q < 16, roll_lanes(re_ref[at], shift_e), roll_lanes(rw_ref[at], shift_w)
        )
        for f in range(4):
            at, start = (f, 24) if r == last else (r, 6 * f)
            fields[f, r] = join(
                lane_q,
                roll_lanes(se_ref[r], 8 - 8 * f),
                roll_lanes(re_ref[at], 8 - start),
                roll_lanes(rw_ref[at], (19 if f == 3 else 18) - start),
                roll_lanes(sw_ref[r], 24 - 8 * f),
            )
    bx, by = face_limits(eb)
    level0 = (base + (lane // STRIP) * rows_e).astype(jnp.float32)

    def put(tr, slab, js, new):
        ea_ref[tr, slab, js] = new

    advect_block(
        list(range(rows_e)),
        lambda tr, s: fields[tr, s],
        lambda s: fields[2, s],
        lambda s: fields[3, s],
        lambda s: level0 + float(s),
        bx,
        by,
        buf,
        coef,
        put,
    )
    top, half = rows_e - 1, levels // 2
    for tr in range(2):
        for n, (k, slab) in enumerate(((0, ea_ref[tr, 0]), (1, ea_ref[tr, 1]))):
            at = (2 * n + tr) * lat
            up_ref[at : at + lat] = patched(north_half[tr, k], slab, 0, lane)
        for n, (k, slab) in enumerate(
            ((half - 1, ea_ref[tr, top]), (half - 2, ea_ref[tr, top - 1]))
        ):
            at = (2 * n + tr) * lat
            down_ref[at : at + lat] = patched(south_half[tr, k], slab, 3, lane)
        at = 5 * lat + 8 * tr
        up_ref[at : at + 8] = fold_strip(ea_ref[tr, 0], 8)
        down_ref[at : at + 8] = fold_strip(ea_ref[tr, top], 3 * STRIP + 8)
    up_ref[4 * lat : 5 * lat] = slab_of(kh_ref, 0)
    down_ref[4 * lat : 5 * lat] = slab_of(kh_ref, levels - 1)
    first_ref[...] = pay[0]
    second_ref[0 : 5 * lat + 16] = pay[1]
    response = pair_response(abc_ref, pair_ref, me)
    for n in range(3):
        red_ref[n] = response[n]
    second_ref[5 * lat + 16 : 6 * lat + 16] = response[2]


def slopes(gx, gy, gz):
    rx, ry, rz = (-0.5 * THERMAL * g[0] + 0.5 * HALINE * g[1] for g in (gx, gy, gz))
    scale = rz / (1.0 + rx * rx + ry * ry + rz * rz)
    return rx * scale, ry * scale


def flux_xyz(gx, gy, gz, kappa, need_xy=True):
    sx, sy = slopes(gx, gy, gz)
    kx, ky = kappa * sx, kappa * sy
    kz = kx * sx + ky * sy
    fz = [kx * gx[n] + ky * gy[n] + kz * gz[n] for n in range(2)]
    if not need_xy:
        return None, None, fz
    fx = [kappa * gx[n] + kx * gz[n] for n in range(2)]
    fy = [kappa * gy[n] + ky * gz[n] for n in range(2)]
    return fx, fy, fz


def flux_x_edge(gx, gy, gz, kappa):
    sx, _ = slopes(gx, gy, gz)
    kx = kappa * sx
    return [kappa * gx[n] + kx * gz[n] for n in range(2)]


def diff(mask, high, low):
    return jnp.where(mask, high - low, 0.0)


def edge_flux_row(r, rows, ek, eb, ebx, eby, level0):
    level = level0 + r
    mx = level < ebx
    my = level < eby
    mz = (level + 1.0 < eb) & (level >= 1.0)
    kappa = jnp.where((level < eb) & (level >= 0.0), 0.25 * ek, 0.0)
    gx, gy, gz = [], [], []
    for tr in range(2):
        here = rows[tr, r + 1]
        gx.append(diff(mx, roll_lanes(here, -1), roll_lanes(here, 1)))
        gy.append(diff(my, shift_north(here), shift_south(here)))
        gz.append(diff(mz, rows[tr, r + 2], rows[tr, r]))
    return flux_x_edge(gx, gy, gz, kappa)


def edge_limits(eb):
    return (
        jnp.minimum(roll_lanes(eb, 1), roll_lanes(eb, -1)),
        lat_limits(eb),
    )


def zonal_change(fx, west, east, lane):
    return roll_lanes(jnp.where(lane == 0, east, fx), -1) - roll_lanes(
        jnp.where(lane == 127, west, fx), 1
    )


def divergence(fx, fy, slab, g, lane):
    return zonal_change(fx, west_patch(slab, g), east_patch(slab, g), lane) + (
        shift_north(fy) - shift_south(fy)
    )


def patch_kernel(
    north_half, south_half, ea_ref, ek_ref, eb_ref,
    full_ref, gx_ref, efx_ref,
    rows,
):
    levels, lat = full_ref.shape[1], full_ref.shape[2]
    rows_e = levels // GROUPS
    base = lax.axis_index("dep") * levels
    lane = lane_ids(lat)
    eb = eb_ref[...]
    ebx, eby = edge_limits(eb)
    level0 = (base + (lane // STRIP) * rows_e).astype(jnp.float32)
    for tr in range(2):
        for r in range(rows_e):
            rows[tr, r + 1] = ea_ref[tr, r]
        rows[tr, 0] = roll_lanes(ea_ref[tr, rows_e - 1], STRIP)
        rows[tr, rows_e + 1] = roll_lanes(ea_ref[tr, 0], -STRIP)
    found = [
        edge_flux_row(r, rows, ek_ref[r], eb, ebx, eby, level0) for r in range(rows_e)
    ]
    for r in range(rows_e):
        for tr in range(2):
            efx_ref[tr, r] = found[r][tr]

    lane = lane_ids(ROWS)
    units = [(g, slice(j, j + ROWS)) for g in range(GROUPS) for j in range(0, lat, ROWS)]

    def patch(r, _):
        def fetch(unit):
            g, js = unit
            strips = [ea_ref[tr, r, js] for tr in range(2)]
            half = (north_half, south_half)[2 * g // GROUPS]
            mains = [half[tr, g % (GROUPS // 2) * rows_e + r, js] for tr in range(2)]
            return [(west_patch(x, g), east_patch(x, g), y) for x, y in zip(strips, mains)]

        def put(unit, mains, rolled):
            g, js = unit
            for tr in range(2):
                full_ref[tr, g * rows_e + r, js] = mains[tr]
                gx_ref[tr, g * rows_e + r, js] = rolled[tr][0] - rolled[tr][1]

        waiting = None
        fetched = fetch(units[0])
        for n, unit in enumerate(units):
            now = fetched
            fetched = fetch(units[n + 1]) if n + 1 < len(units) else None
            mains, rolled = [], []
            for west, east, main in now:
                main = jnp.where(lane < 4, west, jnp.where(lane >= 124, east, main))
                mains.append(main)
                rolled.append(
                    (
                        roll_lanes(jnp.where(lane == 0, east, main), -1),
                        roll_lanes(jnp.where(lane == 127, west, main), 1),
                    )
                )
            if waiting is not None:
                put(*waiting)
            waiting = (unit, mains, rolled)
        put(*waiting)
        return 0

    lax.fori_loop(0, rows_e, patch, 0)


def flux_kernel(
    full_ref, gx_ref, efx_ref, bmx_ref, b_ref, kh_ref,
    q_ref, fz_ref,
    limits,
):
    levels, lat = full_ref.shape[1], full_ref.shape[2]
    rows_e = levels // GROUPS
    base = lax.axis_index("dep") * levels
    lane = lane_ids(lat)
    bottom = slab_of(b_ref).astype(jnp.float32)
    limits[0] = bmx_ref[...]
    limits[1] = lat_limits(bottom)
    limits[2] = bottom

    def north_rows(tr, k, j):
        if j + 8 + ROWS <= lat:
            return full_ref[tr, k, j + 8 : j + 8 + ROWS]
        return jnp.concatenate(
            [full_ref[tr, k, j + 8 : lat], pltpu.roll(full_ref[tr, k, 0:8], 7, 0)], axis=0
        )

    def south_rows(tr, k, j):
        if j >= 8:
            return full_ref[tr, k, j - 8 : j - 8 + ROWS]
        return jnp.concatenate(
            [pltpu.roll(full_ref[tr, k, lat - 8 : lat], 1, 0), full_ref[tr, k, 0 : ROWS - 8]],
            axis=0,
        )

    def fluxes(r, _):
        for g in range(GROUPS):
            k = g * rows_e + r
            above, below = jnp.maximum(k - 1, 0), jnp.minimum(k + 1, levels - 1)
            level = (base + k).astype(jnp.float32)
            level_z = jnp.where(level >= 1.0, level + 1.0, HUGE)
            sides = [
                (west_patch(efx_ref[tr, r], g), east_patch(efx_ref[tr, r], g)) for tr in range(2)
            ]
            fxs, fys, fzs = [[], []], [[], []], [[], []]
            for j in range(0, lat, ROWS):
                js = slice(j, j + ROWS)
                mx = level < limits[0, js]
                my = level < limits[1, js]
                mz = level_z < limits[2, js]
                kh = jnp.concatenate(
                    [rows_of(kh_ref, v, k) for v in range(j // 8, (j + ROWS) // 8)], axis=0
                )
                kappa = jnp.where(level < limits[2, js], 0.25 * kh, 0.0)
                gx, gy, gz = [], [], []
                for tr in range(2):
                    gx.append(jnp.where(mx, gx_ref[tr, k, js], 0.0))
                    gy.append(diff(my, north_rows(tr, k, j), south_rows(tr, k, j)))
                    gz.append(diff(mz, full_ref[tr, below, js], full_ref[tr, above, js]))
                fx, fy, fz = flux_xyz(gx, gy, gz, kappa)
                for tr in range(2):
                    fxs[tr].append(fx[tr])
                    fys[tr].append(fy[tr])
                    fzs[tr].append(fz[tr])
            wet = level < limits[2]
            new = []
            for tr in range(2):
                fy = jnp.concatenate(fys[tr], axis=0)
                change = zonal_change(jnp.concatenate(fxs[tr], axis=0), *sides[tr], lane)
                change = change + (shift_north(fy) - shift_south(fy))
                new.append(full_ref[tr, k] + jnp.where(wet, change, 0.0))
            for tr in range(2):
                q_ref[tr, k] = new[tr]
                fz_ref[tr, k] = jnp.concatenate(fzs[tr], axis=0)
        return 0

    lax.fori_loop(0, rows_e, fluxes, 0)


def factor_kernel(kv_ref, b_ref, inv_ref, ei_ref, ratio_ref, a_ref, bb_ref, abc_ref):
    levels, lat = kv_ref.shape[0], kv_ref.shape[1]
    base = lax.axis_index("dep") * levels
    bottom = slab_of(b_ref).astype(jnp.float32)

    def coupling(k):
        level = (base + k).astype(jnp.float32)
        level = jnp.where(level >= 1.0, level, HUGE)
        return jnp.where(level < bottom, slab_of(kv_ref, k), 0.0)

    top = coupling(0)
    e = jnp.zeros((lat, 128), jnp.float32)
    q = e
    za = jnp.ones((lat, 128), jnp.float32)
    for k in range(levels):
        low = coupling(k + 1) if k + 1 < levels else jnp.zeros((lat, 128), jnp.float32)
        eq = 1.0 + e * q
        inv = 1.0 / (eq + low)
        inv_ref[k] = inv
        ei = e * inv
        ei_ref[k] = ei
        ratio_ref[k] = low * inv
        za = inv if k == 0 else za * ei
        a_ref[k] = za
        q = eq * inv
        e = low
    bb_ref[levels - 1] = inv
    b = inv
    a = za
    for k in range(levels - 2, -1, -1):
        ratio = ratio_ref[k]
        b = ratio * b
        a = a_ref[k] + ratio * a
        bb_ref[k] = b
        a_ref[k] = a
    abc_ref[0] = a + jnp.where(top > 0.0, 1.0 / jnp.maximum(top, 1e-30), HUGE)
    abc_ref[1] = inv
    abc_ref[2] = b


def solve_kernel(
    full_ref, q_ref, fz_ref, ea_ref, ek_ref, eb_ref, bmx_ref, b_ref, kh_ref,
    first_ref, second_ref, inv_ref, ei_ref, ratio_ref, red_ref,
    y_ref, m1_ref, m2_ref, own_ref,
    pad, epad, fze, halo,
):
    levels, lat = q_ref.shape[1], q_ref.shape[2]
    rows_e = levels // GROUPS
    last = levels - 1
    top = rows_e - 1
    me = lax.axis_index("dep")
    base = me * levels
    parity = lax.rem(me, 2)
    outer = (me == 0) | (me == 3)
    upper = parity == 0
    sign = jnp.where(me < 2, 1.0, -1.0)
    lane = lane_ids(lat)
    halo[0] = first_ref[...]
    halo[1] = second_ref[0 : 5 * lat + 16]
    above_ref, below_ref = halo.at[1 - parity], halo.at[parity]

    share = red_ref[0]
    both = red_ref[2] + second_ref[5 * lat + 16 : 6 * lat + 16]
    cross = share / both
    inside = red_ref[1] + share * cross
    for n, value in enumerate((share, red_ref[1], both)):
        own_ref[n] = value
    m1_ref[2] = both

    eb = eb_ref[...]
    ebx, eby = edge_limits(eb)
    level0 = (base + (lane // STRIP) * rows_e).astype(jnp.float32)
    for tr in range(2):
        pad[tr, 0] = above_ref[(2 + tr) * lat : (3 + tr) * lat]
        pad[tr, 1] = above_ref[tr * lat : (1 + tr) * lat]
        for n, k in enumerate((0, 1, 2, last - 2, last - 1, last)):
            pad[tr, n + 2] = full_ref[tr, k]
        pad[tr, 8] = below_ref[tr * lat : (1 + tr) * lat]
        pad[tr, 9] = below_ref[(2 + tr) * lat : (3 + tr) * lat]
        for r in range(rows_e):
            epad[tr, r + 1] = ea_ref[tr, r]
        at = 5 * lat + 8 * tr
        corner_up = unfold_strip(above_ref[at : at + 8], 3 * STRIP + 8, lat // 8)
        corner_dn = unfold_strip(below_ref[at : at + 8], 8, lat // 8)
        epad[tr, 0] = roll_lanes(
            jnp.where(lane >= 3 * STRIP, corner_up, ea_ref[tr, top]), STRIP
        )
        epad[tr, rows_e + 1] = roll_lanes(
            jnp.where(lane < STRIP, corner_dn, ea_ref[tr, 0]), -STRIP
        )
    efx = {
        r + 1: edge_flux_row(r, epad, ek_ref[r], eb, ebx, eby, level0) for r in (0, top)
    }

    bottom = slab_of(b_ref).astype(jnp.float32)
    bmy = lat_limits(bottom)
    bmx = bmx_ref[...]
    ends = (
        (1, -1, 0, 0, above_ref[4 * lat : 5 * lat], True),
        (2, 0, 1, 0, slab_of(kh_ref, 0), False),
        (7, last, top + 1, 3, slab_of(kh_ref, last), False),
        (8, last + 1, top + 2, 3, below_ref[4 * lat : 5 * lat], True),
    )
    spread = {}
    for m, (n, k, er, g, kappa_slab, only_z) in enumerate(ends):
        level = (base + k).astype(jnp.float32)
        level_z = jnp.where(level >= 1.0, level + 1.0, HUGE)
        level_h = jnp.where(level >= 0.0, level, HUGE)
        mx = level_h < bmx
        my = level_h < bmy
        mz = level_z < bottom
        kappa = jnp.where(level_h < bottom, 0.25 * kappa_slab, 0.0)
        gx, gy, gz = [], [], []
        for tr in range(2):
            slab, main = epad[tr, er], pad[tr, n]
            change = zonal_change(main, west_patch(slab, g), east_patch(slab, g), lane)
            gx.append(jnp.where(mx, change, 0.0))
            gy.append(diff(my, shift_north(main), shift_south(main)))
            gz.append(diff(mz, pad[tr, n + 1], pad[tr, n - 1]))
        fx, fy, fz = flux_xyz(gx, gy, gz, kappa, not only_z)
        for tr in range(2):
            fze[tr, m] = fz[tr]
            if not only_z:
                spread[k, tr] = divergence(fx[tr], fy[tr], efx[er][tr], g, lane)

    def vertical_flux(tr, k):
        place = {-1: 0, 0: 1, last: 2, last + 1: 3}.get(k)
        return fz_ref[tr, k] if place is None else fze[tr, place]

    z = [None, None]
    for k in range(levels):
        level = (base + k).astype(jnp.float32)
        wet = level < bottom
        for tr in range(2):
            change = vertical_flux(tr, k + 1) - vertical_flux(tr, k - 1)
            if k == 0 or k == last:
                change = change + spread[k, tr]
                start = pad[tr, 2 if k == 0 else 7]
            else:
                start = q_ref[tr, k]
            rhs = start + jnp.where(wet, change, 0.0)
            new = rhs * inv_ref[k]
            z[tr] = new if k == 0 else new + ei_ref[k] * z[tr]
        for tr in range(2):
            y_ref[tr, k] = z[tr]
    low = list(z)
    for k in range(last - 1, -1, -1):
        ratio = ratio_ref[k]
        z = [y_ref[tr, k] + ratio * z[tr] for tr in range(2)]
        for tr in range(2):
            y_ref[tr, k] = z[tr]
    for tr in range(2):
        near = jnp.where(upper, low[tr], z[tr])
        far = jnp.where(upper, z[tr], low[tr])
        m1_ref[tr] = jnp.where(outer, near, sign * (inside * near - cross * far))
        m2_ref[tr] = jnp.where(outer, share * near, far - share * near)


def finish_kernel(
    y_ref, a_ref, bb_ref, own_ref, r1_ref, r2_ref, r3_ref, out_hbm, out, sems
):
    levels = y_ref.shape[1]
    me = lax.axis_index("dep")
    upper = lax.rem(me, 2) == 0
    outer = (me == 0) | (me == 3)
    sign = jnp.where(me < 2, 1.0, -1.0)
    share, inv_t = own_ref[0], own_ref[1]
    inv_e = 1.0 / jnp.where(outer, r1_ref[2], own_ref[2])
    cross = share * inv_e
    inside = inv_t + share * cross
    tops, lows = [], []
    for tr in range(2):
        y_top, y_low = y_ref[tr, 0], y_ref[tr, levels - 1]
        near = jnp.where(upper, y_low, y_top)
        far = jnp.where(upper, y_top, y_low)
        mate, across = r1_ref[tr], r2_ref[tr] + r3_ref[tr]
        pair_flux = jnp.where(
            outer,
            mate + sign * (cross * across - inside * near),
            sign * (inside * (near - mate) + cross * (across - far)),
        )
        middle = sign * (inv_e * (across - far + share * near) - cross * mate)
        middle = jnp.where(outer, 0.0, middle)
        tops.append(jnp.where(upper, middle, pair_flux))
        lows.append(jnp.where(upper, pair_flux, middle))
    step, regs = levels // GROUPS, y_ref.shape[2] // 8
    copies = []
    for part in range(GROUPS):
        for k in range(part * step, (part + 1) * step):
            a, b = a_ref[k], bb_ref[k]
            new = [y_ref[tr, k] - tops[tr] * a + lows[tr] * b for tr in range(2)]
            for tr in range(2):
                for v in range(regs):
                    out[tr, k, pl.ds(v, 8, regs), :] = new[tr][8 * v : 8 * v + 8]
        for tr in range(2):
            span = (tr, pl.ds(part * step, step))
            copies.append(
                pltpu.make_async_copy(out.at[span], out_hbm.at[span], sems.at[tr, part])
            )
            copies[-1].start()
    for copy in copies:
        copy.wait()


def per_device(tracers, u_east, v_north, kappa_h, kappa_v, bottom):
    _, levels, lat, lon = tracers.shape
    rows_e = levels // GROUPS
    lon_n, dep_n = lax.axis_size("lon"), lax.axis_size("dep")
    east = [(i, (i + 1) % lon_n) for i in range(lon_n)]
    west = [(t, s) for s, t in east]
    slab = lat * lon * 4
    slabs = lambda *lead: f32(*lead, lat, lon)
    work = lambda *lead: pltpu.VMEM(lead + (lat, lon), jnp.float32)

    with jax.named_scope("pack"):
        sw, se, bp, ww, we, t0, t1, u, v = call(
            pack_kernel,
            (slabs(rows_e),) * 2 + (slabs(),) + (slabs(rows_e - 1),) * 2 + (slabs(levels),) * 4,
            [
                work(levels), pltpu.VMEM((lat, lon), jnp.int32), work(rows_e),
                pltpu.SemaphoreType.DMA((GROUPS, 4)), pltpu.SemaphoreType.DMA((2,)),
            ],
            (tracers, u_east, v_north, kappa_h, bottom), 10**6, 6 * levels * slab, 50.8,
            in_specs=[HBM] * 5,
        )
    with jax.named_scope("lon_halo"):
        r_east = lax.ppermute(ww, "lon", west)
        r_west = lax.ppermute(we, "lon", east)
    with jax.named_scope("factor"):
        inv, ei, ratio, a_end, b_end, abc = call(
            factor_kernel, (slabs(levels),) * 5 + (slabs(3),), [],
            (kappa_v, bottom), 10**7, 6 * levels * slab, 16,
        )
    swap = [(i, i ^ 1) for i in range(dep_n)]
    with jax.named_scope("pair_coefficients"):
        pair = lax.ppermute(abc, "dep", swap)
    half = levels // 2

    def advect_half(start, earlier):
        return call(
            functools.partial(advect_kernel, start), slabs(2, half),
            [work(2, 2 * half), work(5, half)],
            (t0, t1, u, v, bottom, earlier), 10**7, 4 * levels * slab, 16,
        )

    with jax.named_scope("advect_north"):
        north_half = advect_half(0, abc)
    with jax.named_scope("advect_south"):
        south_half = advect_half(half, abc)
    rows_pay = 5 * lat + 16
    with jax.named_scope("advect_edge"):
        ea, ek, eb, bmx, first, second, red = call(
            edge_kernel,
            (
                slabs(2, rows_e), slabs(rows_e), slabs(), slabs(),
                f32(rows_pay, lon), f32(rows_pay + lat, lon), slabs(3),
            ),
            [
                work(2, 2 * rows_e), work(5, rows_e), work(4, rows_e),
                pltpu.VMEM((2, rows_pay, lon), jnp.float32),
            ],
            (sw, se, bp, r_east, r_west, bottom, north_half, south_half, kappa_h, abc, pair),
            10**6, 3 * levels * slab, 16,
        )
    other = []
    for i in range(lon_n * dep_n):
        row, place = divmod(i, dep_n)
        if place in (0, dep_n - 1):
            other.append((i, (row ^ 1) * dep_n + place))
        else:
            other.append((i, i + 1 if place % 2 else i - 1))
    with jax.named_scope("dep_halo"):
        first = lax.ppermute(first, "dep", swap)
        second = lax.ppermute(second, ("lon", "dep"), other)
    with jax.named_scope("patch"):
        full, gx, efx = call(
            patch_kernel, (slabs(2, levels), slabs(2, levels), slabs(2, rows_e)),
            [work(2, rows_e + 2)],
            (north_half, south_half, ea, ek, eb), 10**7, 8 * levels * slab, 16,
        )
    with jax.named_scope("fluxes"):
        q_part, fz = call(
            flux_kernel, (slabs(2, levels), slabs(2, levels)), [work(3)],
            (full, gx, efx, bmx, bottom, kappa_h), 10**7, 10 * levels * slab, 16,
        )
    with jax.named_scope("solve"):
        y, m1, m2, own = call(
            solve_kernel, (slabs(2, levels), slabs(3), slabs(2), slabs(3)),
            [
                work(2, 10), work(2, rows_e + 2), work(2, 4),
                pltpu.VMEM((2, rows_pay, lon), jnp.float32),
            ],
            (
                full, q_part, fz, ea, ek, eb, bmx, bottom, kappa_h, first, second,
                inv, ei, ratio, red,
            ),
            10**7, 12 * levels * slab, 24,
        )
    with jax.named_scope("interfaces"):
        m1 = lax.ppermute(m1, "dep", swap)
        m3 = lax.ppermute(m2, "dep", [(i, i ^ 3) for i in range(dep_n)])
        m2 = lax.ppermute(m2, "dep", [(i, i ^ 2) for i in range(dep_n)])
    with jax.named_scope("finish"):
        return call(
            finish_kernel, slabs(2, levels),
            [work(2, levels), pltpu.SemaphoreType.DMA((2, GROUPS))],
            (y, a_end, b_end, own, m1, m2, m3), 10**6, 6 * levels * slab, 16,
            out_specs=HBM,
        )


def solution(mesh):
    in_specs = (
        P(None, "dep", None, "lon"),
        P("dep", None, "lon"),
        P("dep", None, "lon"),
        P("dep", None, "lon"),
        P("dep", None, "lon"),
        P(None, "lon"),
    )
    out_specs = P(None, "dep", None, "lon")
    return jax.shard_map(
        per_device, mesh=mesh, in_specs=in_specs, out_specs=out_specs, check_vma=False
    )
```

```python
import functools

import jax
import jax.numpy as jnp
from jax import lax
from jax.experimental import pallas as pl
from jax.experimental.pallas import tpu as pltpu
from jax.sharding import PartitionSpec as P

SUB = 4
THERMAL = 0.2
HALINE = 0.8
GROUPS = 4
ROWS = 32
STRIP = 32
HUGE = 1e30
MIB = 1024 * 1024

VMEM = pl.BlockSpec(memory_space=pltpu.VMEM)
HBM = pl.BlockSpec(memory_space=pltpu.HBM)


def lane_ids(rows):
    return lax.broadcasted_iota(jnp.int32, (rows, 128), 1)


def roll_lanes(x, amount):
    amount = amount % 128
    return x if amount == 0 else pltpu.roll(x, amount, 1)


def shift_north(x):
    return jnp.concatenate([x[8:], pltpu.roll(x[:8], 7, 0)], axis=0)


def shift_south(x):
    return jnp.concatenate([pltpu.roll(x[-8:], 1, 0), x[:-8]], axis=0)


def rows_of(ref, v, *lead):
    return ref[(*lead, pl.ds(v, 8, ref.shape[-2] // 8), slice(None))]


def neighbours(regs, v):
    north = regs[v + 1] if v + 1 < len(regs) else pltpu.roll(regs[0], 7, 0)
    south = regs[v - 1] if v > 0 else pltpu.roll(regs[-1], 1, 0)
    return north, south


def slab_of(ref, *lead):
    return jnp.concatenate([rows_of(ref, v, *lead) for v in range(ref.shape[-2] // 8)], axis=0)


def call(body, out_shape, scratch, args, flops, in_bytes, limit, in_specs=None, out_specs=None):
    return pl.pallas_call(
        body,
        out_shape=out_shape,
        in_specs=in_specs or [VMEM] * len(args),
        out_specs=out_specs or jax.tree.map(lambda _: VMEM, out_shape),
        scratch_shapes=scratch,
        compiler_params=pltpu.CompilerParams(vmem_limit_bytes=int(limit * MIB)),
        cost_estimate=pl.CostEstimate(flops=flops, bytes_accessed=in_bytes, transcendentals=0),
    )(*args)


def f32(*shape):
    return jax.ShapeDtypeStruct(shape, jnp.float32)


def pack_kernel(
    t_hbm, u_hbm, v_hbm, kh_hbm, b_hbm,
    sw_ref, se_ref, bp_ref, ww_ref, we_ref, t0_ref, t1_ref, u_ref, v_ref, khb_ref,
    kh_buf, b_buf, first_buf, kappa_buf, sems, more_sems,
):
    rows_e = u_ref.shape[0] // GROUPS
    lat = u_ref.shape[1]
    lane = lane_ids(lat)
    fields = ((t_hbm.at[0], t0_ref), (t_hbm.at[1], t1_ref), (u_hbm, u_ref), (v_hbm, v_ref))
    groups = [
        [
            pltpu.make_async_copy(
                src.at[pl.ds(g * rows_e, rows_e)], dst.at[pl.ds(g * rows_e, rows_e)], sems.at[g, n]
            )
            for n, (src, dst) in enumerate(fields)
        ]
        for g in range(GROUPS)
    ]
    tail = [
        pltpu.make_async_copy(b_hbm, b_buf, more_sems.at[0]),
        pltpu.make_async_copy(kh_hbm, kh_buf, more_sems.at[1]),
    ]
    for copy in tail + sum(groups, []):
        copy.start()
    for copy in tail:
        copy.wait()
    bottom = slab_of(b_buf).astype(jnp.float32)
    place = bottom
    for g in range(1, GROUPS):
        place = jnp.where(lane >= STRIP * g - 8, roll_lanes(bottom, STRIP * g), place)
    place = jnp.where(lane >= 120, bottom, place)
    bp_ref[...] = place

    def kappa(r):
        out = None
        for g in range(GROUPS):
            rolled = roll_lanes(slab_of(kh_buf, g * rows_e + r), STRIP * g + 23)
            out = rolled if g == 0 else jnp.where(lane >= STRIP * g + 8, rolled, out)
        return out

    kh_refs = [kappa(r) for r in range(rows_e)]
    for r in range(rows_e):
        kappa_buf[r] = kh_refs[r]
    khb_ref[0] = slab_of(kh_buf, 0)
    khb_ref[1] = slab_of(kh_buf, GROUPS * rows_e - 1)
    for g in range(GROUPS):
        for copy in groups[g]:
            copy.wait()
        for batch in (range(0, rows_e // 2), range(rows_e // 2, rows_e)):
            rolled = {
                (r, f): roll_lanes(slab_of(ref, g * rows_e + r), STRIP * g + 8 * f)
                for r in batch
                for f, ref in enumerate((t0_ref, t1_ref, u_ref, v_ref))
            }
            done = []
            for r in batch:
                low = rolled[r, 0]
                high = None
                if g > 0:
                    low = jnp.where(lane >= STRIP * g, low, sw_ref[r])
                    high = jnp.where(lane >= STRIP * g - 8, rolled[r, 0], se_ref[r])
                for f in range(1, 4):
                    start = STRIP * g + 8 * f
                    low = jnp.where(lane >= start, rolled[r, f], low)
                    if high is None:
                        high = rolled[r, f]
                    else:
                        high = jnp.where(lane >= start - 8, rolled[r, f], high)
                if g == GROUPS - 1:
                    high = jnp.where(lane >= 120, first_buf[r], high)
                done.append((r, low, high))
            for r, low, high in done:
                if g == 0:
                    first_buf[r] = rolled[r, 0]
                sw_ref[r] = low
                se_ref[r] = high
    last = rows_e - 1
    kappa_last = kappa_buf[last]
    lane_q = lane % STRIP
    low_last, high_last = sw_ref[last], se_ref[last]
    wires = []
    for r in range(last):
        k = kappa_buf[r]
        low, high = sw_ref[r], se_ref[r]
        west = (low, roll_lanes(low, -2), roll_lanes(low, -4), roll_lanes(low, -6), k)
        east = (
            roll_lanes(high, 6), roll_lanes(high, 4), roll_lanes(high, 2), roll_lanes(high, -1),
            roll_lanes(k, 1),
        )
        west += (roll_lanes(low_last, 24 - 8 * r),)
        east += (roll_lanes(high_last, 5 if r == 3 else 30 - 8 * r),)
        if r == 3:
            west += (roll_lanes(kappa_last, 6),)
            east += (roll_lanes(kappa_last, 7),)
        else:
            west += (roll_lanes(place, 30 - 2 * r),)
            east += (roll_lanes(place, 36 - 2 * r),)
        starts = (6, 12, 18, 23, 24, 29 if r == 3 else 30)
        for ref, parts in ((ww_ref, west), (we_ref, east)):
            wire = parts[0]
            for start, part in zip(starts, parts[1:]):
                wire = jnp.where(lane_q >= start, part, wire)
            wires.append((ref, r, wire))
    for ref, r, wire in wires:
        ref[r] = wire


def advect_block(slabs, get_c, get_u, get_v, get_level, bx, by, buf, coef, put):
    regs = bx.shape[0] // 8
    for i, slab in enumerate(slabs):
        level = get_level(slab)
        um = jnp.where(level < bx, get_u(slab), 0.0)
        vm = jnp.where(level < by, get_v(slab), 0.0)
        uw = roll_lanes(um, 1)
        vs = shift_south(vm)
        coef[0, i] = (
            1.0
            - jnp.maximum(um, 0.0)
            + jnp.minimum(uw, 0.0)
            - jnp.maximum(vm, 0.0)
            + jnp.minimum(vs, 0.0)
        )
        coef[1, i] = -jnp.minimum(um, 0.0)
        coef[2, i] = jnp.maximum(uw, 0.0)
        coef[3, i] = -jnp.minimum(vm, 0.0)
        coef[4, i] = jnp.maximum(vs, 0.0)
        for tr in range(2):
            buf[0, 2 * i + tr] = get_c(tr, slab)
    for step in range(SUB):
        src, dst = step % 2, (step + 1) % 2
        for i, slab in enumerate(slabs):
            now = [
                [buf[src, 2 * i + tr, 8 * v : 8 * v + 8] for v in range(regs)] for tr in range(2)
            ]
            for v in range(regs):
                js = slice(8 * v, 8 * v + 8)
                a, b, c, d, e = (coef[n, i, js] for n in range(5))
                for tr in range(2):
                    here = now[tr][v]
                    north, south = neighbours(now[tr], v)
                    new = (
                        a * here
                        + b * roll_lanes(here, -1)
                        + c * roll_lanes(here, 1)
                        + d * north
                        + e * south
                    )
                    if step < SUB - 1:
                        buf[dst, 2 * i + tr, js] = new
                    else:
                        put(tr, slab, js, new)


def face_limits(bottom):
    lat = bottom.shape[0]
    rows = lax.broadcasted_iota(jnp.int32, bottom.shape, 0)
    north = jnp.where(rows == lat - 1, 0.0, shift_north(bottom))
    return jnp.minimum(bottom, roll_lanes(bottom, -1)), jnp.minimum(bottom, north)


def lat_limits(bottom):
    lat = bottom.shape[0]
    rows = lax.broadcasted_iota(jnp.int32, bottom.shape, 0)
    north = jnp.where(rows == lat - 1, 0.0, shift_north(bottom))
    south = jnp.where(rows == 0, 0.0, shift_south(bottom))
    return jnp.minimum(north, south)


def advect_kernel(start, t0_ref, t1_ref, u_ref, v_ref, b_ref, earlier_ref, out_ref, buf, coef):
    del earlier_ref
    count, lat = out_ref.shape[1], out_ref.shape[2]
    base = lax.axis_index("dep") * t0_ref.shape[0] + start
    bx, by = face_limits(slab_of(b_ref).astype(jnp.float32))

    def put(tr, slab, js, new):
        out_ref[tr, slab, js] = new

    advect_block(
        list(range(count)),
        lambda tr, s: slab_of((t0_ref, t1_ref)[tr], start + s),
        lambda s: slab_of(u_ref, start + s),
        lambda s: slab_of(v_ref, start + s),
        lambda s: (base + s).astype(jnp.float32),
        bx,
        by,
        buf,
        coef,
        put,
    )


def join(lane_q, own, east, west):
    halo = jnp.where(lane_q < 16, east, west)
    return jnp.where((lane_q >= 8) & (lane_q < 24), halo, own)


def west_patch(slab, g):
    return roll_lanes(slab, -(STRIP * g + 24))


def east_patch(slab, g):
    return roll_lanes(slab, 120 - STRIP * g)


def patched(main, slab, g, lane):
    return jnp.where(
        lane < 4, west_patch(slab, g), jnp.where(lane >= 124, east_patch(slab, g), main)
    )


def own_kernel(sw_ref, se_ref, bp_ref, earlier_ref, own_ref, ownb_ref):
    del earlier_ref
    rows_e, lat = sw_ref.shape[0], sw_ref.shape[1]
    lane_q = lane_ids(lat) % STRIP
    for r in range(rows_e):
        made = [
            jnp.where(
                lane_q < 16, roll_lanes(se_ref[r], 8 - 8 * f), roll_lanes(sw_ref[r], 24 - 8 * f)
            )
            for f in range(4)
        ]
        for f in range(4):
            own_ref[f, r] = made[f]
    place = bp_ref[...]
    ownb_ref[...] = jnp.where(lane_q < 16, roll_lanes(place, 8), roll_lanes(place, 24))


def pair_response(abc_ref, pair_ref, me):
    upper = lax.rem(me, 2) == 0
    low_pair = me < 2
    inv_t = 1.0 / (pair_ref[0] + jnp.where(upper, abc_ref[1], abc_ref[0]))
    c_pair = jnp.where(upper == low_pair, pair_ref[1], abc_ref[2])
    share = c_pair * inv_t
    return share, inv_t, jnp.where(upper, abc_ref[0], abc_ref[1]) - c_pair * share


def fold_strip(slab, place):
    lane = lane_ids(8)
    folded = jnp.zeros((8, 128), jnp.float32)
    for v in range(slab.shape[0] // 8):
        rolled = roll_lanes(slab[8 * v : 8 * v + 8], 16 * v - place)
        folded = jnp.where(lane >= 16 * v, rolled, folded)
    return folded


def unfold_strip(folded, place, regs):
    return jnp.concatenate([roll_lanes(folded, place - 16 * v) for v in range(regs)], axis=0)


def edge_kernel(
    own_ref, ownb_ref, re_ref, rw_ref, b_ref, north_half, south_half, kh_ref, abc_ref, pair_ref,
    ea_ref, ek_ref, eb_ref, bmx_ref, first_ref, second_ref, red_ref,
    buf, coef, fields, pay,
):
    levels, lat = kh_ref.shape[0], kh_ref.shape[1]
    rows_e = levels // GROUPS
    me = lax.axis_index("dep")
    base = me * levels
    parity = lax.rem(me, 2)
    up_ref, down_ref = pay.at[1 - parity], pay.at[parity]
    lane = lane_ids(lat)
    lane_q = lane % STRIP
    bottom = slab_of(b_ref).astype(jnp.float32)
    east = [roll_lanes(re_ref[r], 2 * r - 22) for r in range(3)]
    west = [roll_lanes(rw_ref[r], 2 * r - 12) for r in range(3)]
    eb = join(
        lane_q,
        ownb_ref[...],
        jnp.where(lane_q < 10, east[0], jnp.where(lane_q < 12, east[1], east[2])),
        jnp.where(lane_q < 20, west[0], jnp.where(lane_q < 22, west[1], west[2])),
    )
    eb_ref[...] = eb
    b_west = roll_lanes(jnp.where(lane == 127, west_patch(eb, 0), bottom), 1)
    b_east = roll_lanes(jnp.where(lane == 0, east_patch(eb, 0), bottom), -1)
    bmx_ref[...] = jnp.minimum(b_west, b_east)
    last = rows_e - 1
    for r in range(rows_e):
        at, shift_e, shift_w = (3, -21, -6) if r == last else (r, -15, 0)
        ek_ref[r] = jnp.where(
            lane_q < 16, roll_lanes(re_ref[at], shift_e), roll_lanes(rw_ref[at], shift_w)
        )
        made = []
        for f in range(4):
            at, start = (f, 24) if r == last else (r, 6 * f)
            made.append(
                join(
                    lane_q,
                    own_ref[f, r],
                    roll_lanes(re_ref[at], 8 - start),
                    roll_lanes(rw_ref[at], (19 if f == 3 else 18) - start),
                )
            )
        for f in range(4):
            fields[f, r] = made[f]
    bx, by = face_limits(eb)
    level0 = (base + (lane // STRIP) * rows_e).astype(jnp.float32)

    def put(tr, slab, js, new):
        ea_ref[tr, slab, js] = new

    advect_block(
        list(range(rows_e)),
        lambda tr, s: fields[tr, s],
        lambda s: fields[2, s],
        lambda s: fields[3, s],
        lambda s: level0 + float(s),
        bx,
        by,
        buf,
        coef,
        put,
    )
    top, half = rows_e - 1, levels // 2
    for tr in range(2):
        for n, (k, slab) in enumerate(((0, ea_ref[tr, 0]), (1, ea_ref[tr, 1]))):
            at = (2 * n + tr) * lat
            up_ref[at : at + lat] = patched(north_half[tr, k], slab, 0, lane)
        for n, (k, slab) in enumerate(
            ((half - 1, ea_ref[tr, top]), (half - 2, ea_ref[tr, top - 1]))
        ):
            at = (2 * n + tr) * lat
            down_ref[at : at + lat] = patched(south_half[tr, k], slab, 3, lane)
        at = 4 * lat + 8 * tr
        up_ref[at : at + 8] = fold_strip(ea_ref[tr, 0], 8)
        down_ref[at : at + 8] = fold_strip(ea_ref[tr, top], 3 * STRIP + 8)
    up_ref[4 * lat + 16 : 5 * lat + 16] = slab_of(kh_ref, 0)
    down_ref[4 * lat + 16 : 5 * lat + 16] = slab_of(kh_ref, levels - 1)
    first_ref[...] = pay[0, 0 : 4 * lat + 16]
    second_ref[0 : 5 * lat + 16] = pay[1]
    response = pair_response(abc_ref, pair_ref, me)
    for n in range(3):
        red_ref[n] = response[n]
    second_ref[5 * lat + 16 : 6 * lat + 16] = response[2]


def slopes(gx, gy, gz):
    rx, ry, rz = (-0.5 * THERMAL * g[0] + 0.5 * HALINE * g[1] for g in (gx, gy, gz))
    scale = rz / (1.0 + rx * rx + ry * ry + rz * rz)
    return rx * scale, ry * scale


def flux_xyz(gx, gy, gz, kappa, need_xy=True):
    sx, sy = slopes(gx, gy, gz)
    kx, ky = kappa * sx, kappa * sy
    kz = kx * sx + ky * sy
    fz = [kx * gx[n] + ky * gy[n] + kz * gz[n] for n in range(2)]
    if not need_xy:
        return None, None, fz
    fx = [kappa * gx[n] + kx * gz[n] for n in range(2)]
    fy = [kappa * gy[n] + ky * gz[n] for n in range(2)]
    return fx, fy, fz


def flux_x_edge(gx, gy, gz, kappa):
    sx, _ = slopes(gx, gy, gz)
    kx = kappa * sx
    return [kappa * gx[n] + kx * gz[n] for n in range(2)]


def diff(mask, high, low):
    return jnp.where(mask, high - low, 0.0)


def edge_flux_row(r, rows, ek, eb, ebx, eby, level0):
    level = level0 + r
    mx = level < ebx
    my = level < eby
    mz = (level + 1.0 < eb) & (level >= 1.0)
    kappa = jnp.where((level < eb) & (level >= 0.0), 0.25 * ek, 0.0)
    gx, gy, gz = [], [], []
    for tr in range(2):
        here = rows[tr, r + 1]
        gx.append(diff(mx, roll_lanes(here, -1), roll_lanes(here, 1)))
        gy.append(diff(my, shift_north(here), shift_south(here)))
        gz.append(diff(mz, rows[tr, r + 2], rows[tr, r]))
    return flux_x_edge(gx, gy, gz, kappa)


def edge_limits(eb):
    return (
        jnp.minimum(roll_lanes(eb, 1), roll_lanes(eb, -1)),
        lat_limits(eb),
    )


def zonal_change(fx, west, east, lane):
    return roll_lanes(jnp.where(lane == 0, east, fx), -1) - roll_lanes(
        jnp.where(lane == 127, west, fx), 1
    )


def divergence(fx, fy, slab, g, lane):
    return zonal_change(fx, west_patch(slab, g), east_patch(slab, g), lane) + (
        shift_north(fy) - shift_south(fy)
    )


def patch_kernel(
    north_half, south_half, ea_ref, ek_ref, eb_ref,
    full_ref, gx_ref, efx_ref,
    rows,
):
    levels, lat = full_ref.shape[1], full_ref.shape[2]
    rows_e = levels // GROUPS
    base = lax.axis_index("dep") * levels
    lane = lane_ids(lat)
    eb = eb_ref[...]
    ebx, eby = edge_limits(eb)
    level0 = (base + (lane // STRIP) * rows_e).astype(jnp.float32)
    for tr in range(2):
        for r in range(rows_e):
            rows[tr, r + 1] = ea_ref[tr, r]
        rows[tr, 0] = roll_lanes(ea_ref[tr, rows_e - 1], STRIP)
        rows[tr, rows_e + 1] = roll_lanes(ea_ref[tr, 0], -STRIP)
    found = [
        edge_flux_row(r, rows, ek_ref[r], eb, ebx, eby, level0) for r in range(rows_e)
    ]
    for r in range(rows_e):
        for tr in range(2):
            efx_ref[tr, r] = found[r][tr]

    lane = lane_ids(ROWS)
    units = [(g, slice(j, j + ROWS)) for g in range(GROUPS) for j in range(0, lat, ROWS)]

    def patch(r, _):
        def fetch(unit):
            g, js = unit
            strips = [ea_ref[tr, r, js] for tr in range(2)]
            half = (north_half, south_half)[2 * g // GROUPS]
            mains = [half[tr, g % (GROUPS // 2) * rows_e + r, js] for tr in range(2)]
            return [(west_patch(x, g), east_patch(x, g), y) for x, y in zip(strips, mains)]

        def put(unit, mains, rolled):
            g, js = unit
            for tr in range(2):
                full_ref[tr, g * rows_e + r, js] = mains[tr]
                gx_ref[tr, g * rows_e + r, js] = rolled[tr][0] - rolled[tr][1]

        waiting = None
        fetched = fetch(units[0])
        for n, unit in enumerate(units):
            now = fetched
            fetched = fetch(units[n + 1]) if n + 1 < len(units) else None
            mains, rolled = [], []
            for west, east, main in now:
                main = jnp.where(lane < 4, west, jnp.where(lane >= 124, east, main))
                mains.append(main)
                rolled.append(
                    (
                        roll_lanes(jnp.where(lane == 0, east, main), -1),
                        roll_lanes(jnp.where(lane == 127, west, main), 1),
                    )
                )
            if waiting is not None:
                put(*waiting)
            waiting = (unit, mains, rolled)
        put(*waiting)
        return 0

    lax.fori_loop(0, rows_e, patch, 0)


def flux_kernel(
    full_ref, gx_ref, efx_ref, bmx_ref, b_ref, kh_ref,
    q_ref, fz_ref,
    limits,
):
    levels, lat = full_ref.shape[1], full_ref.shape[2]
    rows_e = levels // GROUPS
    base = lax.axis_index("dep") * levels
    lane = lane_ids(lat)
    bottom = slab_of(b_ref).astype(jnp.float32)
    limits[0] = bmx_ref[...]
    limits[1] = lat_limits(bottom)
    limits[2] = bottom

    def north_rows(tr, k, j):
        if j + 8 + ROWS <= lat:
            return full_ref[tr, k, j + 8 : j + 8 + ROWS]
        return jnp.concatenate(
            [full_ref[tr, k, j + 8 : lat], pltpu.roll(full_ref[tr, k, 0:8], 7, 0)], axis=0
        )

    def south_rows(tr, k, j):
        if j >= 8:
            return full_ref[tr, k, j - 8 : j - 8 + ROWS]
        return jnp.concatenate(
            [pltpu.roll(full_ref[tr, k, lat - 8 : lat], 1, 0), full_ref[tr, k, 0 : ROWS - 8]],
            axis=0,
        )

    def fluxes(r, _):
        for g in range(GROUPS):
            k = g * rows_e + r
            above, below = jnp.maximum(k - 1, 0), jnp.minimum(k + 1, levels - 1)
            level = (base + k).astype(jnp.float32)
            level_z = jnp.where(level >= 1.0, level + 1.0, HUGE)
            sides = [
                (west_patch(efx_ref[tr, r], g), east_patch(efx_ref[tr, r], g)) for tr in range(2)
            ]
            fxs, fys, fzs = [[], []], [[], []], [[], []]
            for j in range(0, lat, ROWS):
                js = slice(j, j + ROWS)
                mx = level < limits[0, js]
                my = level < limits[1, js]
                mz = level_z < limits[2, js]
                kh = jnp.concatenate(
                    [rows_of(kh_ref, v, k) for v in range(j // 8, (j + ROWS) // 8)], axis=0
                )
                kappa = jnp.where(level < limits[2, js], 0.25 * kh, 0.0)
                gx, gy, gz = [], [], []
                for tr in range(2):
                    gx.append(jnp.where(mx, gx_ref[tr, k, js], 0.0))
                    gy.append(diff(my, north_rows(tr, k, j), south_rows(tr, k, j)))
                    gz.append(diff(mz, full_ref[tr, below, js], full_ref[tr, above, js]))
                fx, fy, fz = flux_xyz(gx, gy, gz, kappa)
                for tr in range(2):
                    fxs[tr].append(fx[tr])
                    fys[tr].append(fy[tr])
                    fzs[tr].append(fz[tr])
            wet = level < limits[2]
            new = []
            for tr in range(2):
                fy = jnp.concatenate(fys[tr], axis=0)
                change = zonal_change(jnp.concatenate(fxs[tr], axis=0), *sides[tr], lane)
                change = change + (shift_north(fy) - shift_south(fy))
                new.append(full_ref[tr, k] + jnp.where(wet, change, 0.0))
            for tr in range(2):
                q_ref[tr, k] = new[tr]
                fz_ref[tr, k] = jnp.concatenate(fzs[tr], axis=0)
        return 0

    lax.fori_loop(0, rows_e, fluxes, 0)


def factor_kernel(
    kv_ref, b_ref, khb_ref, inv_ref, ei_ref, ratio_ref, a_ref, bb_ref, abc_ref, msg_ref
):
    levels, lat = kv_ref.shape[0], kv_ref.shape[1]
    base = lax.axis_index("dep") * levels
    bottom = slab_of(b_ref).astype(jnp.float32)

    def coupling(k):
        level = (base + k).astype(jnp.float32)
        level = jnp.where(level >= 1.0, level, HUGE)
        return jnp.where(level < bottom, slab_of(kv_ref, k), 0.0)

    top = coupling(0)
    e = jnp.zeros((lat, 128), jnp.float32)
    q = e
    za = jnp.ones((lat, 128), jnp.float32)
    for k in range(levels):
        low = coupling(k + 1) if k + 1 < levels else jnp.zeros((lat, 128), jnp.float32)
        eq = 1.0 + e * q
        inv = 1.0 / (eq + low)
        inv_ref[k] = inv
        ei = e * inv
        ei_ref[k] = ei
        ratio_ref[k] = low * inv
        za = inv if k == 0 else za * ei
        a_ref[k] = za
        q = eq * inv
        e = low
    bb_ref[levels - 1] = inv
    b = inv
    a = za
    for k in range(levels - 2, -1, -1):
        ratio = ratio_ref[k]
        b = ratio * b
        a = a_ref[k] + ratio * a
        bb_ref[k] = b
        a_ref[k] = a
    a = a + jnp.where(top > 0.0, 1.0 / jnp.maximum(top, 1e-30), HUGE)
    abc_ref[0] = a
    abc_ref[1] = inv
    abc_ref[2] = b
    upper = lax.rem(lax.axis_index("dep"), 2) == 0
    msg_ref[0] = jnp.where(upper, inv, a)
    msg_ref[1] = b
    msg_ref[2] = jnp.where(upper, khb_ref[1], khb_ref[0])


def solve_kernel(
    full_ref, q_ref, fz_ref, ea_ref, ek_ref, eb_ref, bmx_ref, b_ref, kh_ref,
    first_ref, second_ref, inv_ref, ei_ref, ratio_ref, red_ref, pair_ref,
    y_ref, m1_ref, m2_ref, own_ref,
    pad, epad, fze, halo,
):
    levels, lat = q_ref.shape[1], q_ref.shape[2]
    rows_e = levels // GROUPS
    last = levels - 1
    top = rows_e - 1
    me = lax.axis_index("dep")
    base = me * levels
    parity = lax.rem(me, 2)
    outer = (me == 0) | (me == 3)
    upper = parity == 0
    sign = jnp.where(me < 2, 1.0, -1.0)
    lane = lane_ids(lat)
    halo[0, 0 : 4 * lat + 16] = first_ref[...]
    halo[0, 4 * lat + 16 : 5 * lat + 16] = pair_ref[2]
    halo[1] = second_ref[0 : 5 * lat + 16]
    above_ref, below_ref = halo.at[1 - parity], halo.at[parity]

    share = red_ref[0]
    both = red_ref[2] + second_ref[5 * lat + 16 : 6 * lat + 16]
    cross = share / both
    inside = red_ref[1] + share * cross
    for n, value in enumerate((share, red_ref[1], both)):
        own_ref[n] = value
    m1_ref[2] = both

    eb = eb_ref[...]
    ebx, eby = edge_limits(eb)
    level0 = (base + (lane // STRIP) * rows_e).astype(jnp.float32)
    for tr in range(2):
        pad[tr, 0] = above_ref[(2 + tr) * lat : (3 + tr) * lat]
        pad[tr, 1] = above_ref[tr * lat : (1 + tr) * lat]
        for n, k in enumerate((0, 1, 2, last - 2, last - 1, last)):
            pad[tr, n + 2] = full_ref[tr, k]
        pad[tr, 8] = below_ref[tr * lat : (1 + tr) * lat]
        pad[tr, 9] = below_ref[(2 + tr) * lat : (3 + tr) * lat]
        for r in range(rows_e):
            epad[tr, r + 1] = ea_ref[tr, r]
        at = 4 * lat + 8 * tr
        corner_up = unfold_strip(above_ref[at : at + 8], 3 * STRIP + 8, lat // 8)
        corner_dn = unfold_strip(below_ref[at : at + 8], 8, lat // 8)
        epad[tr, 0] = roll_lanes(
            jnp.where(lane >= 3 * STRIP, corner_up, ea_ref[tr, top]), STRIP
        )
        epad[tr, rows_e + 1] = roll_lanes(
            jnp.where(lane < STRIP, corner_dn, ea_ref[tr, 0]), -STRIP
        )
    efx = {
        r + 1: edge_flux_row(r, epad, ek_ref[r], eb, ebx, eby, level0) for r in (0, top)
    }

    bottom = slab_of(b_ref).astype(jnp.float32)
    bmy = lat_limits(bottom)
    bmx = bmx_ref[...]
    ends = (
        (1, -1, 0, 0, above_ref[4 * lat + 16 : 5 * lat + 16], True),
        (2, 0, 1, 0, slab_of(kh_ref, 0), False),
        (7, last, top + 1, 3, slab_of(kh_ref, last), False),
        (8, last + 1, top + 2, 3, below_ref[4 * lat + 16 : 5 * lat + 16], True),
    )
    spread = {}
    for m, (n, k, er, g, kappa_slab, only_z) in enumerate(ends):
        level = (base + k).astype(jnp.float32)
        level_z = jnp.where(level >= 1.0, level + 1.0, HUGE)
        level_h = jnp.where(level >= 0.0, level, HUGE)
        mx = level_h < bmx
        my = level_h < bmy
        mz = level_z < bottom
        kappa = jnp.where(level_h < bottom, 0.25 * kappa_slab, 0.0)
        gx, gy, gz = [], [], []
        for tr in range(2):
            slab, main = epad[tr, er], pad[tr, n]
            change = zonal_change(main, west_patch(slab, g), east_patch(slab, g), lane)
            gx.append(jnp.where(mx, change, 0.0))
            gy.append(diff(my, shift_north(main), shift_south(main)))
            gz.append(diff(mz, pad[tr, n + 1], pad[tr, n - 1]))
        fx, fy, fz = flux_xyz(gx, gy, gz, kappa, not only_z)
        for tr in range(2):
            fze[tr, m] = fz[tr]
            if not only_z:
                spread[k, tr] = divergence(fx[tr], fy[tr], efx[er][tr], g, lane)

    def vertical_flux(tr, k):
        place = {-1: 0, 0: 1, last: 2, last + 1: 3}.get(k)
        return fz_ref[tr, k] if place is None else fze[tr, place]

    z = [None, None]
    for k in range(levels):
        level = (base + k).astype(jnp.float32)
        wet = level < bottom
        for tr in range(2):
            change = vertical_flux(tr, k + 1) - vertical_flux(tr, k - 1)
            if k == 0 or k == last:
                change = change + spread[k, tr]
                start = pad[tr, 2 if k == 0 else 7]
            else:
                start = q_ref[tr, k]
            rhs = start + jnp.where(wet, change, 0.0)
            new = rhs * inv_ref[k]
            z[tr] = new if k == 0 else new + ei_ref[k] * z[tr]
        for tr in range(2):
            y_ref[tr, k] = z[tr]
    low = list(z)
    for k in range(last - 1, -1, -1):
        ratio = ratio_ref[k]
        z = [y_ref[tr, k] + ratio * z[tr] for tr in range(2)]
        for tr in range(2):
            y_ref[tr, k] = z[tr]
    for tr in range(2):
        near = jnp.where(upper, low[tr], z[tr])
        far = jnp.where(upper, z[tr], low[tr])
        m1_ref[tr] = jnp.where(outer, near, sign * (inside * near - cross * far))
        m2_ref[tr] = jnp.where(outer, share * near, far - share * near)


def finish_kernel(
    y_ref, a_ref, bb_ref, own_ref, r1_ref, r2_ref, r3_ref, out_hbm, out, sems
):
    levels = y_ref.shape[1]
    me = lax.axis_index("dep")
    upper = lax.rem(me, 2) == 0
    outer = (me == 0) | (me == 3)
    sign = jnp.where(me < 2, 1.0, -1.0)
    share, inv_t = own_ref[0], own_ref[1]
    inv_e = 1.0 / jnp.where(outer, r1_ref[2], own_ref[2])
    cross = share * inv_e
    inside = inv_t + share * cross
    tops, lows = [], []
    for tr in range(2):
        y_top, y_low = y_ref[tr, 0], y_ref[tr, levels - 1]
        near = jnp.where(upper, y_low, y_top)
        far = jnp.where(upper, y_top, y_low)
        mate, across = r1_ref[tr], r2_ref[tr] + r3_ref[tr]
        pair_flux = jnp.where(
            outer,
            mate + sign * (cross * across - inside * near),
            sign * (inside * (near - mate) + cross * (across - far)),
        )
        middle = sign * (inv_e * (across - far + share * near) - cross * mate)
        middle = jnp.where(outer, 0.0, middle)
        tops.append(jnp.where(upper, middle, pair_flux))
        lows.append(jnp.where(upper, pair_flux, middle))
    step, regs = levels // GROUPS, y_ref.shape[2] // 8
    copies = []
    for part in range(GROUPS):
        for k in range(part * step, (part + 1) * step):
            a, b = a_ref[k], bb_ref[k]
            new = [y_ref[tr, k] - tops[tr] * a + lows[tr] * b for tr in range(2)]
            for tr in range(2):
                for v in range(regs):
                    out[tr, k, pl.ds(v, 8, regs), :] = new[tr][8 * v : 8 * v + 8]
        for tr in range(2):
            span = (tr, pl.ds(part * step, step))
            copies.append(
                pltpu.make_async_copy(out.at[span], out_hbm.at[span], sems.at[tr, part])
            )
            copies[-1].start()
    for copy in copies:
        copy.wait()


def per_device(tracers, u_east, v_north, kappa_h, kappa_v, bottom):
    _, levels, lat, lon = tracers.shape
    rows_e = levels // GROUPS
    lon_n, dep_n = lax.axis_size("lon"), lax.axis_size("dep")
    east = [(i, (i + 1) % lon_n) for i in range(lon_n)]
    west = [(t, s) for s, t in east]
    slab = lat * lon * 4
    slabs = lambda *lead: f32(*lead, lat, lon)
    work = lambda *lead: pltpu.VMEM(lead + (lat, lon), jnp.float32)

    with jax.named_scope("pack"):
        sw, se, bp, ww, we, t0, t1, u, v, khb = call(
            pack_kernel,
            (slabs(rows_e),) * 2 + (slabs(),) + (slabs(rows_e - 1),) * 2 + (slabs(levels),) * 4
            + (slabs(2),),
            [
                work(levels), pltpu.VMEM((lat, lon), jnp.int32), work(rows_e), work(rows_e),
                pltpu.SemaphoreType.DMA((GROUPS, 4)), pltpu.SemaphoreType.DMA((2,)),
            ],
            (tracers, u_east, v_north, kappa_h, bottom), 10**6, 6 * levels * slab, 50.5,
            in_specs=[HBM] * 5,
        )
    with jax.named_scope("lon_halo"):
        r_east = lax.ppermute(ww, "lon", west)
        r_west = lax.ppermute(we, "lon", east)
    with jax.named_scope("factor"):
        inv, ei, ratio, a_end, b_end, abc, msg = call(
            factor_kernel, (slabs(levels),) * 5 + (slabs(3),) * 2, [],
            (kappa_v, bottom, khb), 10**7, 6 * levels * slab, 16,
        )
    swap = [(i, i ^ 1) for i in range(dep_n)]
    with jax.named_scope("pair_coefficients"):
        pair = lax.ppermute(msg, "dep", swap)
    half = levels // 2

    def advect_half(start, earlier):
        return call(
            functools.partial(advect_kernel, start), slabs(2, half),
            [work(2, 2 * half), work(5, half)],
            (t0, t1, u, v, bottom, earlier), 10**7, 4 * levels * slab, 16,
        )

    with jax.named_scope("advect_north"):
        north_half = advect_half(0, abc)
    with jax.named_scope("advect_south"):
        south_half = advect_half(half, abc)
    with jax.named_scope("own_strips"):
        own_strips, own_bottom = call(
            own_kernel, (slabs(4, rows_e), slabs()), [],
            (sw, se, bp, abc), 10**6, 8 * rows_e * slab, 16,
        )
    rows_pay = 5 * lat + 16
    with jax.named_scope("advect_edge"):
        ea, ek, eb, bmx, first, second, red = call(
            edge_kernel,
            (
                slabs(2, rows_e), slabs(rows_e), slabs(), slabs(),
                f32(rows_pay - lat, lon), f32(rows_pay + lat, lon), slabs(3),
            ),
            [
                work(2, 2 * rows_e), work(5, rows_e), work(4, rows_e),
                pltpu.VMEM((2, rows_pay, lon), jnp.float32),
            ],
            (own_strips, own_bottom, r_east, r_west, bottom, north_half, south_half, kappa_h, abc, pair),
            10**6, 3 * levels * slab, 16,
        )
    other = []
    for i in range(lon_n * dep_n):
        row, place = divmod(i, dep_n)
        if place in (0, dep_n - 1):
            other.append((i, (row ^ 1) * dep_n + place))
        else:
            other.append((i, i + 1 if place % 2 else i - 1))
    with jax.named_scope("dep_halo"):
        first = lax.ppermute(first, "dep", swap)
        second = lax.ppermute(second, ("lon", "dep"), other)
    with jax.named_scope("patch"):
        full, gx, efx = call(
            patch_kernel, (slabs(2, levels), slabs(2, levels), slabs(2, rows_e)),
            [work(2, rows_e + 2)],
            (north_half, south_half, ea, ek, eb), 10**7, 8 * levels * slab, 16,
        )
    with jax.named_scope("fluxes"):
        q_part, fz = call(
            flux_kernel, (slabs(2, levels), slabs(2, levels)), [work(3)],
            (full, gx, efx, bmx, bottom, kappa_h), 10**7, 10 * levels * slab, 16,
        )
    with jax.named_scope("solve"):
        y, m1, m2, own = call(
            solve_kernel, (slabs(2, levels), slabs(3), slabs(2), slabs(3)),
            [
                work(2, 10), work(2, rows_e + 2), work(2, 4),
                pltpu.VMEM((2, rows_pay, lon), jnp.float32),
            ],
            (
                full, q_part, fz, ea, ek, eb, bmx, bottom, kappa_h, first, second,
                inv, ei, ratio, red, pair,
            ),
            10**7, 12 * levels * slab, 24,
        )
    with jax.named_scope("interfaces"):
        m1 = lax.ppermute(m1, "dep", swap)
        m3 = lax.ppermute(m2, "dep", [(i, i ^ 3) for i in range(dep_n)])
        m2 = lax.ppermute(m2, "dep", [(i, i ^ 2) for i in range(dep_n)])
    with jax.named_scope("finish"):
        return call(
            finish_kernel, slabs(2, levels),
            [work(2, levels), pltpu.SemaphoreType.DMA((2, GROUPS))],
            (y, a_end, b_end, own, m1, m2, m3), 10**6, 6 * levels * slab, 16,
            out_specs=HBM,
        )


def solution(mesh):
    in_specs = (
        P(None, "dep", None, "lon"),
        P("dep", None, "lon"),
        P("dep", None, "lon"),
        P("dep", None, "lon"),
        P("dep", None, "lon"),
        P(None, "lon"),
    )
    out_specs = P(None, "dep", None, "lon")
    return jax.shard_map(
        per_device, mesh=mesh, in_specs=in_specs, out_specs=out_specs, check_vma=False
    )
```

```python
import functools

import jax
import jax.numpy as jnp
from jax import lax
from jax.experimental import pallas as pl
from jax.experimental.pallas import tpu as pltpu
from jax.sharding import PartitionSpec as P

SUB = 4
THERMAL = 0.2
HALINE = 0.8
GROUPS = 4
ROWS = 32
STRIP = 32
HUGE = 1e30
MIB = 1024 * 1024

VMEM = pl.BlockSpec(memory_space=pltpu.VMEM)
HBM = pl.BlockSpec(memory_space=pltpu.HBM)


def lane_ids(rows):
    return lax.broadcasted_iota(jnp.int32, (rows, 128), 1)


def roll_lanes(x, amount):
    amount = amount % 128
    return x if amount == 0 else pltpu.roll(x, amount, 1)


def shift_north(x):
    return jnp.concatenate([x[8:], pltpu.roll(x[:8], 7, 0)], axis=0)


def shift_south(x):
    return jnp.concatenate([pltpu.roll(x[-8:], 1, 0), x[:-8]], axis=0)


def rows_of(ref, v, *lead):
    return ref[(*lead, pl.ds(v, 8, ref.shape[-2] // 8), slice(None))]


def neighbours(regs, v):
    north = regs[v + 1] if v + 1 < len(regs) else pltpu.roll(regs[0], 7, 0)
    south = regs[v - 1] if v > 0 else pltpu.roll(regs[-1], 1, 0)
    return north, south


def slab_of(ref, *lead):
    return jnp.concatenate([rows_of(ref, v, *lead) for v in range(ref.shape[-2] // 8)], axis=0)


def call(body, out_shape, scratch, args, flops, in_bytes, limit, in_specs=None, out_specs=None):
    return pl.pallas_call(
        body,
        out_shape=out_shape,
        in_specs=in_specs or [VMEM] * len(args),
        out_specs=out_specs or jax.tree.map(lambda _: VMEM, out_shape),
        scratch_shapes=scratch,
        compiler_params=pltpu.CompilerParams(vmem_limit_bytes=int(limit * MIB)),
        cost_estimate=pl.CostEstimate(flops=flops, bytes_accessed=in_bytes, transcendentals=0),
    )(*args)


def f32(*shape):
    return jax.ShapeDtypeStruct(shape, jnp.float32)


def pack_kernel(
    t_hbm, u_hbm, v_hbm, kh_hbm, b_hbm,
    sw_ref, se_ref, bp_ref, ww_ref, we_ref, t0_ref, t1_ref, u_ref, v_ref, khb_ref,
    kh_buf, b_buf, first_buf, sems, more_sems,
):
    rows_e = u_ref.shape[0] // GROUPS
    lat = u_ref.shape[1]
    lane = lane_ids(lat)
    fields = ((t_hbm.at[0], t0_ref), (t_hbm.at[1], t1_ref), (u_hbm, u_ref), (v_hbm, v_ref))
    groups = [
        [
            pltpu.make_async_copy(
                src.at[pl.ds(g * rows_e, rows_e)], dst.at[pl.ds(g * rows_e, rows_e)], sems.at[g, n]
            )
            for n, (src, dst) in enumerate(fields)
        ]
        for g in range(GROUPS)
    ]
    tail = [
        pltpu.make_async_copy(b_hbm, b_buf, more_sems.at[0]),
        pltpu.make_async_copy(kh_hbm, kh_buf, more_sems.at[1]),
    ]
    for copy in sum(groups, []) + tail:
        copy.start()
    for g in range(GROUPS):
        for copy in groups[g]:
            copy.wait()
        for batch in (range(0, rows_e // 2), range(rows_e // 2, rows_e)):
            rolled = {
                (r, f): roll_lanes(slab_of(ref, g * rows_e + r), STRIP * g + 8 * f)
                for r in batch
                for f, ref in enumerate((t0_ref, t1_ref, u_ref, v_ref))
            }
            done = []
            for r in batch:
                low = rolled[r, 0]
                high = None
                if g > 0:
                    low = jnp.where(lane >= STRIP * g, low, sw_ref[r])
                    high = jnp.where(lane >= STRIP * g - 8, rolled[r, 0], se_ref[r])
                for f in range(1, 4):
                    start = STRIP * g + 8 * f
                    low = jnp.where(lane >= start, rolled[r, f], low)
                    if high is None:
                        high = rolled[r, f]
                    else:
                        high = jnp.where(lane >= start - 8, rolled[r, f], high)
                if g == GROUPS - 1:
                    high = jnp.where(lane >= 120, first_buf[r], high)
                done.append((r, low, high))
            for r, low, high in done:
                if g == 0:
                    first_buf[r] = rolled[r, 0]
                sw_ref[r] = low
                se_ref[r] = high
    for copy in tail:
        copy.wait()
    bottom = slab_of(b_buf).astype(jnp.float32)
    place = bottom
    for g in range(1, GROUPS):
        place = jnp.where(lane >= STRIP * g - 8, roll_lanes(bottom, STRIP * g), place)
    place = jnp.where(lane >= 120, bottom, place)
    bp_ref[...] = place

    def kappa(r):
        out = None
        for g in range(GROUPS):
            rolled = roll_lanes(slab_of(kh_buf, g * rows_e + r), STRIP * g + 23)
            out = rolled if g == 0 else jnp.where(lane >= STRIP * g + 8, rolled, out)
        return out

    khb_ref[0] = slab_of(kh_buf, 0)
    khb_ref[1] = slab_of(kh_buf, GROUPS * rows_e - 1)
    last = rows_e - 1
    kappa_last = kappa(last)
    lane_q = lane % STRIP
    low_last, high_last = sw_ref[last], se_ref[last]
    wires = []
    for r in range(last):
        k = kappa(r)
        low, high = sw_ref[r], se_ref[r]
        west = (low, roll_lanes(low, -2), roll_lanes(low, -4), roll_lanes(low, -6), k)
        east = (
            roll_lanes(high, 6), roll_lanes(high, 4), roll_lanes(high, 2), roll_lanes(high, -1),
            roll_lanes(k, 1),
        )
        west += (roll_lanes(low_last, 24 - 8 * r),)
        east += (roll_lanes(high_last, 5 if r == 3 else 30 - 8 * r),)
        if r == 3:
            west += (roll_lanes(kappa_last, 6),)
            east += (roll_lanes(kappa_last, 7),)
        else:
            west += (roll_lanes(place, 30 - 2 * r),)
            east += (roll_lanes(place, 36 - 2 * r),)
        starts = (6, 12, 18, 23, 24, 29 if r == 3 else 30)
        for ref, parts in ((ww_ref, west), (we_ref, east)):
            wire = parts[0]
            for start, part in zip(starts, parts[1:]):
                wire = jnp.where(lane_q >= start, part, wire)
            wires.append((ref, r, wire))
    for ref, r, wire in wires:
        ref[r] = wire


def advect_block(slabs, get_c, get_u, get_v, get_level, bx, by, buf, coef, put):
    regs = bx.shape[0] // 8
    for i, slab in enumerate(slabs):
        level = get_level(slab)
        um = jnp.where(level < bx, get_u(slab), 0.0)
        vm = jnp.where(level < by, get_v(slab), 0.0)
        uw = roll_lanes(um, 1)
        vs = shift_south(vm)
        coef[0, i] = (
            1.0
            - jnp.maximum(um, 0.0)
            + jnp.minimum(uw, 0.0)
            - jnp.maximum(vm, 0.0)
            + jnp.minimum(vs, 0.0)
        )
        coef[1, i] = -jnp.minimum(um, 0.0)
        coef[2, i] = jnp.maximum(uw, 0.0)
        coef[3, i] = -jnp.minimum(vm, 0.0)
        coef[4, i] = jnp.maximum(vs, 0.0)
        for tr in range(2):
            buf[0, 2 * i + tr] = get_c(tr, slab)
    for step in range(SUB):
        src, dst = step % 2, (step + 1) % 2
        for i, slab in enumerate(slabs):
            now = [
                [buf[src, 2 * i + tr, 8 * v : 8 * v + 8] for v in range(regs)] for tr in range(2)
            ]
            for v in range(regs):
                js = slice(8 * v, 8 * v + 8)
                a, b, c, d, e = (coef[n, i, js] for n in range(5))
                for tr in range(2):
                    here = now[tr][v]
                    north, south = neighbours(now[tr], v)
                    new = (
                        a * here
                        + b * roll_lanes(here, -1)
                        + c * roll_lanes(here, 1)
                        + d * north
                        + e * south
                    )
                    if step < SUB - 1:
                        buf[dst, 2 * i + tr, js] = new
                    else:
                        put(tr, slab, js, new)


def face_limits(bottom):
    lat = bottom.shape[0]
    rows = lax.broadcasted_iota(jnp.int32, bottom.shape, 0)
    north = jnp.where(rows == lat - 1, 0.0, shift_north(bottom))
    return jnp.minimum(bottom, roll_lanes(bottom, -1)), jnp.minimum(bottom, north)


def lat_limits(bottom):
    lat = bottom.shape[0]
    rows = lax.broadcasted_iota(jnp.int32, bottom.shape, 0)
    north = jnp.where(rows == lat - 1, 0.0, shift_north(bottom))
    south = jnp.where(rows == 0, 0.0, shift_south(bottom))
    return jnp.minimum(north, south)


def advect_kernel(start, t0_ref, t1_ref, u_ref, v_ref, b_ref, earlier_ref, out_ref, buf, coef):
    del earlier_ref
    count, lat = out_ref.shape[1], out_ref.shape[2]
    base = lax.axis_index("dep") * t0_ref.shape[0] + start
    bx, by = face_limits(slab_of(b_ref).astype(jnp.float32))

    def put(tr, slab, js, new):
        out_ref[tr, slab, js] = new

    advect_block(
        list(range(count)),
        lambda tr, s: slab_of((t0_ref, t1_ref)[tr], start + s),
        lambda s: slab_of(u_ref, start + s),
        lambda s: slab_of(v_ref, start + s),
        lambda s: (base + s).astype(jnp.float32),
        bx,
        by,
        buf,
        coef,
        put,
    )


def join(lane_q, own, east, west):
    halo = jnp.where(lane_q < 16, east, west)
    return jnp.where((lane_q >= 8) & (lane_q < 24), halo, own)


def west_patch(slab, g):
    return roll_lanes(slab, -(STRIP * g + 24))


def east_patch(slab, g):
    return roll_lanes(slab, 120 - STRIP * g)


def patched(main, slab, g, lane):
    return jnp.where(
        lane < 4, west_patch(slab, g), jnp.where(lane >= 124, east_patch(slab, g), main)
    )


def own_kernel(sw_ref, se_ref, bp_ref, earlier_ref, own_ref, ownb_ref):
    del earlier_ref
    rows_e, lat = sw_ref.shape[0], sw_ref.shape[1]
    lane_q = lane_ids(lat) % STRIP
    for r in range(rows_e):
        made = [
            jnp.where(
                lane_q < 16, roll_lanes(se_ref[r], 8 - 8 * f), roll_lanes(sw_ref[r], 24 - 8 * f)
            )
            for f in range(4)
        ]
        for f in range(4):
            own_ref[f, r] = made[f]
    place = bp_ref[...]
    ownb_ref[...] = jnp.where(lane_q < 16, roll_lanes(place, 8), roll_lanes(place, 24))


def pair_response(abc_ref, pair_ref, me):
    upper = lax.rem(me, 2) == 0
    low_pair = me < 2
    inv_t = 1.0 / (pair_ref[0] + jnp.where(upper, abc_ref[1], abc_ref[0]))
    c_pair = jnp.where(upper == low_pair, pair_ref[1], abc_ref[2])
    share = c_pair * inv_t
    return share, inv_t, jnp.where(upper, abc_ref[0], abc_ref[1]) - c_pair * share


def fold_strip(slab, place):
    lane = lane_ids(8)
    folded = jnp.zeros((8, 128), jnp.float32)
    for v in range(slab.shape[0] // 8):
        rolled = roll_lanes(slab[8 * v : 8 * v + 8], 16 * v - place)
        folded = jnp.where(lane >= 16 * v, rolled, folded)
    return folded


def unfold_strip(folded, place, regs):
    return jnp.concatenate([roll_lanes(folded, place - 16 * v) for v in range(regs)], axis=0)


def edge_kernel(
    own_ref, ownb_ref, re_ref, rw_ref, b_ref, north_half, south_half, kh_ref, abc_ref, pair_ref,
    ea_ref, ek_ref, eb_ref, bmx_ref, first_ref, second_ref, red_ref,
    buf, coef, fields, pay,
):
    levels, lat = kh_ref.shape[0], kh_ref.shape[1]
    rows_e = levels // GROUPS
    me = lax.axis_index("dep")
    base = me * levels
    parity = lax.rem(me, 2)
    up_ref, down_ref = pay.at[1 - parity], pay.at[parity]
    lane = lane_ids(lat)
    lane_q = lane % STRIP
    bottom = slab_of(b_ref).astype(jnp.float32)
    east = [roll_lanes(re_ref[r], 2 * r - 22) for r in range(3)]
    west = [roll_lanes(rw_ref[r], 2 * r - 12) for r in range(3)]
    eb = join(
        lane_q,
        ownb_ref[...],
        jnp.where(lane_q < 10, east[0], jnp.where(lane_q < 12, east[1], east[2])),
        jnp.where(lane_q < 20, west[0], jnp.where(lane_q < 22, west[1], west[2])),
    )
    eb_ref[...] = eb
    b_west = roll_lanes(jnp.where(lane == 127, west_patch(eb, 0), bottom), 1)
    b_east = roll_lanes(jnp.where(lane == 0, east_patch(eb, 0), bottom), -1)
    bmx_ref[...] = jnp.minimum(b_west, b_east)
    last = rows_e - 1
    for r in range(rows_e):
        at, shift_e, shift_w = (3, -21, -6) if r == last else (r, -15, 0)
        ek_ref[r] = jnp.where(
            lane_q < 16, roll_lanes(re_ref[at], shift_e), roll_lanes(rw_ref[at], shift_w)
        )
        made = []
        for f in range(4):
            at, start = (f, 24) if r == last else (r, 6 * f)
            made.append(
                join(
                    lane_q,
                    own_ref[f, r],
                    roll_lanes(re_ref[at], 8 - start),
                    roll_lanes(rw_ref[at], (19 if f == 3 else 18) - start),
                )
            )
        for f in range(4):
            fields[f, r] = made[f]
    bx, by = face_limits(eb)
    level0 = (base + (lane // STRIP) * rows_e).astype(jnp.float32)

    def put(tr, slab, js, new):
        ea_ref[tr, slab, js] = new

    advect_block(
        list(range(rows_e)),
        lambda tr, s: fields[tr, s],
        lambda s: fields[2, s],
        lambda s: fields[3, s],
        lambda s: level0 + float(s),
        bx,
        by,
        buf,
        coef,
        put,
    )
    top, half = rows_e - 1, levels // 2
    for tr in range(2):
        for n, (k, slab) in enumerate(((0, ea_ref[tr, 0]), (1, ea_ref[tr, 1]))):
            at = (2 * n + tr) * lat
            up_ref[at : at + lat] = patched(north_half[tr, k], slab, 0, lane)
        for n, (k, slab) in enumerate(
            ((half - 1, ea_ref[tr, top]), (half - 2, ea_ref[tr, top - 1]))
        ):
            at = (2 * n + tr) * lat
            down_ref[at : at + lat] = patched(south_half[tr, k], slab, 3, lane)
        at = 4 * lat + 8 * tr
        up_ref[at : at + 8] = fold_strip(ea_ref[tr, 0], 8)
        down_ref[at : at + 8] = fold_strip(ea_ref[tr, top], 3 * STRIP + 8)
    up_ref[4 * lat + 16 : 5 * lat + 16] = slab_of(kh_ref, 0)
    down_ref[4 * lat + 16 : 5 * lat + 16] = slab_of(kh_ref, levels - 1)
    first_ref[...] = pay[0, 0 : 4 * lat + 16]
    second_ref[0 : 5 * lat + 16] = pay[1]
    response = pair_response(abc_ref, pair_ref, me)
    for n in range(3):
        red_ref[n] = response[n]
    second_ref[5 * lat + 16 : 6 * lat + 16] = response[2]


def slopes(gx, gy, gz):
    rx, ry, rz = (-0.5 * THERMAL * g[0] + 0.5 * HALINE * g[1] for g in (gx, gy, gz))
    scale = rz / (1.0 + rx * rx + ry * ry + rz * rz)
    return rx * scale, ry * scale


def flux_xyz(gx, gy, gz, kappa, need_xy=True):
    sx, sy = slopes(gx, gy, gz)
    kx, ky = kappa * sx, kappa * sy
    kz = kx * sx + ky * sy
    fz = [kx * gx[n] + ky * gy[n] + kz * gz[n] for n in range(2)]
    if not need_xy:
        return None, None, fz
    fx = [kappa * gx[n] + kx * gz[n] for n in range(2)]
    fy = [kappa * gy[n] + ky * gz[n] for n in range(2)]
    return fx, fy, fz


def flux_x_edge(gx, gy, gz, kappa):
    sx, _ = slopes(gx, gy, gz)
    kx = kappa * sx
    return [kappa * gx[n] + kx * gz[n] for n in range(2)]


def diff(mask, high, low):
    return jnp.where(mask, high - low, 0.0)


def edge_flux_row(r, rows, ek, eb, ebx, eby, level0):
    level = level0 + r
    mx = level < ebx
    my = level < eby
    mz = (level + 1.0 < eb) & (level >= 1.0)
    kappa = jnp.where((level < eb) & (level >= 0.0), 0.25 * ek, 0.0)
    gx, gy, gz = [], [], []
    for tr in range(2):
        here = rows[tr, r + 1]
        gx.append(diff(mx, roll_lanes(here, -1), roll_lanes(here, 1)))
        gy.append(diff(my, shift_north(here), shift_south(here)))
        gz.append(diff(mz, rows[tr, r + 2], rows[tr, r]))
    return flux_x_edge(gx, gy, gz, kappa)


def edge_limits(eb):
    return (
        jnp.minimum(roll_lanes(eb, 1), roll_lanes(eb, -1)),
        lat_limits(eb),
    )


def zonal_change(fx, west, east, lane):
    return roll_lanes(jnp.where(lane == 0, east, fx), -1) - roll_lanes(
        jnp.where(lane == 127, west, fx), 1
    )


def divergence(fx, fy, slab, g, lane):
    return zonal_change(fx, west_patch(slab, g), east_patch(slab, g), lane) + (
        shift_north(fy) - shift_south(fy)
    )


def patch_kernel(
    north_half, south_half, ea_ref, ek_ref, eb_ref,
    full_ref, gx_ref, efx_ref,
    rows,
):
    levels, lat = full_ref.shape[1], full_ref.shape[2]
    rows_e = levels // GROUPS
    base = lax.axis_index("dep") * levels
    lane = lane_ids(lat)
    eb = eb_ref[...]
    ebx, eby = edge_limits(eb)
    level0 = (base + (lane // STRIP) * rows_e).astype(jnp.float32)
    for tr in range(2):
        for r in range(rows_e):
            rows[tr, r + 1] = ea_ref[tr, r]
        rows[tr, 0] = roll_lanes(ea_ref[tr, rows_e - 1], STRIP)
        rows[tr, rows_e + 1] = roll_lanes(ea_ref[tr, 0], -STRIP)
    found = [
        edge_flux_row(r, rows, ek_ref[r], eb, ebx, eby, level0) for r in range(rows_e)
    ]
    for r in range(rows_e):
        for tr in range(2):
            efx_ref[tr, r] = found[r][tr]

    lane = lane_ids(ROWS)
    units = [(g, slice(j, j + ROWS)) for g in range(GROUPS) for j in range(0, lat, ROWS)]

    def patch(r, _):
        def fetch(unit):
            g, js = unit
            strips = [ea_ref[tr, r, js] for tr in range(2)]
            half = (north_half, south_half)[2 * g // GROUPS]
            mains = [half[tr, g % (GROUPS // 2) * rows_e + r, js] for tr in range(2)]
            return [(west_patch(x, g), east_patch(x, g), y) for x, y in zip(strips, mains)]

        def put(unit, mains, rolled):
            g, js = unit
            for tr in range(2):
                full_ref[tr, g * rows_e + r, js] = mains[tr]
                gx_ref[tr, g * rows_e + r, js] = rolled[tr][0] - rolled[tr][1]

        waiting = None
        fetched = fetch(units[0])
        for n, unit in enumerate(units):
            now = fetched
            fetched = fetch(units[n + 1]) if n + 1 < len(units) else None
            mains, rolled = [], []
            for west, east, main in now:
                main = jnp.where(lane < 4, west, jnp.where(lane >= 124, east, main))
                mains.append(main)
                rolled.append(
                    (
                        roll_lanes(jnp.where(lane == 0, east, main), -1),
                        roll_lanes(jnp.where(lane == 127, west, main), 1),
                    )
                )
            if waiting is not None:
                put(*waiting)
            waiting = (unit, mains, rolled)
        put(*waiting)
        return 0

    lax.fori_loop(0, rows_e, patch, 0)


def flux_kernel(
    full_ref, gx_ref, efx_ref, bmx_ref, b_ref, kh_ref,
    q_ref, fz_ref,
    limits,
):
    levels, lat = full_ref.shape[1], full_ref.shape[2]
    rows_e = levels // GROUPS
    base = lax.axis_index("dep") * levels
    lane = lane_ids(lat)
    bottom = slab_of(b_ref).astype(jnp.float32)
    limits[0] = bmx_ref[...]
    limits[1] = lat_limits(bottom)
    limits[2] = bottom

    def north_rows(tr, k, j):
        if j + 8 + ROWS <= lat:
            return full_ref[tr, k, j + 8 : j + 8 + ROWS]
        return jnp.concatenate(
            [full_ref[tr, k, j + 8 : lat], pltpu.roll(full_ref[tr, k, 0:8], 7, 0)], axis=0
        )

    def south_rows(tr, k, j):
        if j >= 8:
            return full_ref[tr, k, j - 8 : j - 8 + ROWS]
        return jnp.concatenate(
            [pltpu.roll(full_ref[tr, k, lat - 8 : lat], 1, 0), full_ref[tr, k, 0 : ROWS - 8]],
            axis=0,
        )

    def fluxes(r, _):
        for g in range(GROUPS):
            k = g * rows_e + r
            above, below = jnp.maximum(k - 1, 0), jnp.minimum(k + 1, levels - 1)
            level = (base + k).astype(jnp.float32)
            level_z = jnp.where(level >= 1.0, level + 1.0, HUGE)
            sides = [
                (west_patch(efx_ref[tr, r], g), east_patch(efx_ref[tr, r], g)) for tr in range(2)
            ]
            fxs, fys, fzs = [[], []], [[], []], [[], []]
            for j in range(0, lat, ROWS):
                js = slice(j, j + ROWS)
                mx = level < limits[0, js]
                my = level < limits[1, js]
                mz = level_z < limits[2, js]
                kh = jnp.concatenate(
                    [rows_of(kh_ref, v, k) for v in range(j // 8, (j + ROWS) // 8)], axis=0
                )
                kappa = jnp.where(level < limits[2, js], 0.25 * kh, 0.0)
                gx, gy, gz = [], [], []
                for tr in range(2):
                    gx.append(jnp.where(mx, gx_ref[tr, k, js], 0.0))
                    gy.append(diff(my, north_rows(tr, k, j), south_rows(tr, k, j)))
                    gz.append(diff(mz, full_ref[tr, below, js], full_ref[tr, above, js]))
                fx, fy, fz = flux_xyz(gx, gy, gz, kappa)
                for tr in range(2):
                    fxs[tr].append(fx[tr])
                    fys[tr].append(fy[tr])
                    fzs[tr].append(fz[tr])
            wet = level < limits[2]
            new = []
            for tr in range(2):
                fy = jnp.concatenate(fys[tr], axis=0)
                change = zonal_change(jnp.concatenate(fxs[tr], axis=0), *sides[tr], lane)
                change = change + (shift_north(fy) - shift_south(fy))
                new.append(full_ref[tr, k] + jnp.where(wet, change, 0.0))
            for tr in range(2):
                q_ref[tr, k] = new[tr]
                fz_ref[tr, k] = jnp.concatenate(fzs[tr], axis=0)
        return 0

    lax.fori_loop(0, rows_e, fluxes, 0)


def factor_kernel(
    kv_ref, b_ref, khb_ref, inv_ref, ei_ref, ratio_ref, a_ref, bb_ref, abc_ref, msg_ref
):
    levels, lat = kv_ref.shape[0], kv_ref.shape[1]
    base = lax.axis_index("dep") * levels
    bottom = slab_of(b_ref).astype(jnp.float32)

    def coupling(k):
        level = (base + k).astype(jnp.float32)
        level = jnp.where(level >= 1.0, level, HUGE)
        return jnp.where(level < bottom, slab_of(kv_ref, k), 0.0)

    top = coupling(0)
    e = jnp.zeros((lat, 128), jnp.float32)
    q = e
    za = jnp.ones((lat, 128), jnp.float32)
    for k in range(levels):
        low = coupling(k + 1) if k + 1 < levels else jnp.zeros((lat, 128), jnp.float32)
        eq = 1.0 + e * q
        inv = 1.0 / (eq + low)
        inv_ref[k] = inv
        ei = e * inv
        ei_ref[k] = ei
        ratio_ref[k] = low * inv
        za = inv if k == 0 else za * ei
        a_ref[k] = za
        q = eq * inv
        e = low
    bb_ref[levels - 1] = inv
    b = inv
    a = za
    for k in range(levels - 2, -1, -1):
        ratio = ratio_ref[k]
        b = ratio * b
        a = a_ref[k] + ratio * a
        bb_ref[k] = b
        a_ref[k] = a
    a = a + jnp.where(top > 0.0, 1.0 / jnp.maximum(top, 1e-30), HUGE)
    abc_ref[0] = a
    abc_ref[1] = inv
    abc_ref[2] = b
    upper = lax.rem(lax.axis_index("dep"), 2) == 0
    msg_ref[0] = jnp.where(upper, inv, a)
    msg_ref[1] = b
    msg_ref[2] = jnp.where(upper, khb_ref[1], khb_ref[0])


def solve_kernel(
    full_ref, q_ref, fz_ref, ea_ref, ek_ref, eb_ref, bmx_ref, b_ref, kh_ref,
    first_ref, second_ref, inv_ref, ei_ref, ratio_ref, red_ref, pair_ref,
    y_ref, m1_ref, m2_ref, own_ref,
    pad, epad, fze, halo,
):
    levels, lat = q_ref.shape[1], q_ref.shape[2]
    rows_e = levels // GROUPS
    last = levels - 1
    top = rows_e - 1
    me = lax.axis_index("dep")
    base = me * levels
    parity = lax.rem(me, 2)
    outer = (me == 0) | (me == 3)
    upper = parity == 0
    sign = jnp.where(me < 2, 1.0, -1.0)
    lane = lane_ids(lat)
    halo[0, 0 : 4 * lat + 16] = first_ref[...]
    halo[0, 4 * lat + 16 : 5 * lat + 16] = pair_ref[2]
    halo[1] = second_ref[0 : 5 * lat + 16]
    above_ref, below_ref = halo.at[1 - parity], halo.at[parity]

    share = red_ref[0]
    both = red_ref[2] + second_ref[5 * lat + 16 : 6 * lat + 16]
    cross = share / both
    inside = red_ref[1] + share * cross
    for n, value in enumerate((share, red_ref[1], both)):
        own_ref[n] = value
    m1_ref[2] = both

    eb = eb_ref[...]
    ebx, eby = edge_limits(eb)
    level0 = (base + (lane // STRIP) * rows_e).astype(jnp.float32)
    for tr in range(2):
        pad[tr, 0] = above_ref[(2 + tr) * lat : (3 + tr) * lat]
        pad[tr, 1] = above_ref[tr * lat : (1 + tr) * lat]
        for n, k in enumerate((0, 1, 2, last - 2, last - 1, last)):
            pad[tr, n + 2] = full_ref[tr, k]
        pad[tr, 8] = below_ref[tr * lat : (1 + tr) * lat]
        pad[tr, 9] = below_ref[(2 + tr) * lat : (3 + tr) * lat]
        for r in range(rows_e):
            epad[tr, r + 1] = ea_ref[tr, r]
        at = 4 * lat + 8 * tr
        corner_up = unfold_strip(above_ref[at : at + 8], 3 * STRIP + 8, lat // 8)
        corner_dn = unfold_strip(below_ref[at : at + 8], 8, lat // 8)
        epad[tr, 0] = roll_lanes(
            jnp.where(lane >= 3 * STRIP, corner_up, ea_ref[tr, top]), STRIP
        )
        epad[tr, rows_e + 1] = roll_lanes(
            jnp.where(lane < STRIP, corner_dn, ea_ref[tr, 0]), -STRIP
        )
    efx = {
        r + 1: edge_flux_row(r, epad, ek_ref[r], eb, ebx, eby, level0) for r in (0, top)
    }

    bottom = slab_of(b_ref).astype(jnp.float32)
    bmy = lat_limits(bottom)
    bmx = bmx_ref[...]
    ends = (
        (1, -1, 0, 0, above_ref[4 * lat + 16 : 5 * lat + 16], True),
        (2, 0, 1, 0, slab_of(kh_ref, 0), False),
        (7, last, top + 1, 3, slab_of(kh_ref, last), False),
        (8, last + 1, top + 2, 3, below_ref[4 * lat + 16 : 5 * lat + 16], True),
    )
    spread = {}
    for m, (n, k, er, g, kappa_slab, only_z) in enumerate(ends):
        level = (base + k).astype(jnp.float32)
        level_z = jnp.where(level >= 1.0, level + 1.0, HUGE)
        level_h = jnp.where(level >= 0.0, level, HUGE)
        mx = level_h < bmx
        my = level_h < bmy
        mz = level_z < bottom
        kappa = jnp.where(level_h < bottom, 0.25 * kappa_slab, 0.0)
        gx, gy, gz = [], [], []
        for tr in range(2):
            slab, main = epad[tr, er], pad[tr, n]
            change = zonal_change(main, west_patch(slab, g), east_patch(slab, g), lane)
            gx.append(jnp.where(mx, change, 0.0))
            gy.append(diff(my, shift_north(main), shift_south(main)))
            gz.append(diff(mz, pad[tr, n + 1], pad[tr, n - 1]))
        fx, fy, fz = flux_xyz(gx, gy, gz, kappa, not only_z)
        for tr in range(2):
            fze[tr, m] = fz[tr]
            if not only_z:
                spread[k, tr] = divergence(fx[tr], fy[tr], efx[er][tr], g, lane)

    def vertical_flux(tr, k):
        place = {-1: 0, 0: 1, last: 2, last + 1: 3}.get(k)
        return fz_ref[tr, k] if place is None else fze[tr, place]

    z = [None, None]
    for k in range(levels):
        level = (base + k).astype(jnp.float32)
        wet = level < bottom
        for tr in range(2):
            change = vertical_flux(tr, k + 1) - vertical_flux(tr, k - 1)
            if k == 0 or k == last:
                change = change + spread[k, tr]
                start = pad[tr, 2 if k == 0 else 7]
            else:
                start = q_ref[tr, k]
            rhs = start + jnp.where(wet, change, 0.0)
            new = rhs * inv_ref[k]
            z[tr] = new if k == 0 else new + ei_ref[k] * z[tr]
        for tr in range(2):
            y_ref[tr, k] = z[tr]
    low = list(z)
    for k in range(last - 1, -1, -1):
        ratio = ratio_ref[k]
        z = [y_ref[tr, k] + ratio * z[tr] for tr in range(2)]
        for tr in range(2):
            y_ref[tr, k] = z[tr]
    for tr in range(2):
        near = jnp.where(upper, low[tr], z[tr])
        far = jnp.where(upper, z[tr], low[tr])
        m1_ref[tr] = jnp.where(outer, near, sign * (inside * near - cross * far))
        m2_ref[tr] = jnp.where(outer, share * near, far - share * near)


def finish_kernel(
    y_ref, a_ref, bb_ref, own_ref, r1_ref, r2_ref, r3_ref, out_hbm, out, sems
):
    levels = y_ref.shape[1]
    me = lax.axis_index("dep")
    upper = lax.rem(me, 2) == 0
    outer = (me == 0) | (me == 3)
    sign = jnp.where(me < 2, 1.0, -1.0)
    share, inv_t = own_ref[0], own_ref[1]
    inv_e = 1.0 / jnp.where(outer, r1_ref[2], own_ref[2])
    cross = share * inv_e
    inside = inv_t + share * cross
    tops, lows = [], []
    for tr in range(2):
        y_top, y_low = y_ref[tr, 0], y_ref[tr, levels - 1]
        near = jnp.where(upper, y_low, y_top)
        far = jnp.where(upper, y_top, y_low)
        mate, across = r1_ref[tr], r2_ref[tr] + r3_ref[tr]
        pair_flux = jnp.where(
            outer,
            mate + sign * (cross * across - inside * near),
            sign * (inside * (near - mate) + cross * (across - far)),
        )
        middle = sign * (inv_e * (across - far + share * near) - cross * mate)
        middle = jnp.where(outer, 0.0, middle)
        tops.append(jnp.where(upper, middle, pair_flux))
        lows.append(jnp.where(upper, pair_flux, middle))
    step, regs = levels // GROUPS, y_ref.shape[2] // 8
    copies = []
    for part in range(GROUPS):
        for k in range(part * step, (part + 1) * step):
            a, b = a_ref[k], bb_ref[k]
            new = [y_ref[tr, k] - tops[tr] * a + lows[tr] * b for tr in range(2)]
            for tr in range(2):
                for v in range(regs):
                    out[tr, k, pl.ds(v, 8, regs), :] = new[tr][8 * v : 8 * v + 8]
        for tr in range(2):
            span = (tr, pl.ds(part * step, step))
            copies.append(
                pltpu.make_async_copy(out.at[span], out_hbm.at[span], sems.at[tr, part])
            )
            copies[-1].start()
    for copy in copies:
        copy.wait()


def per_device(tracers, u_east, v_north, kappa_h, kappa_v, bottom):
    _, levels, lat, lon = tracers.shape
    rows_e = levels // GROUPS
    lon_n, dep_n = lax.axis_size("lon"), lax.axis_size("dep")
    east = [(i, (i + 1) % lon_n) for i in range(lon_n)]
    west = [(t, s) for s, t in east]
    slab = lat * lon * 4
    slabs = lambda *lead: f32(*lead, lat, lon)
    work = lambda *lead: pltpu.VMEM(lead + (lat, lon), jnp.float32)

    with jax.named_scope("pack"):
        sw, se, bp, ww, we, t0, t1, u, v, khb = call(
            pack_kernel,
            (slabs(rows_e),) * 2 + (slabs(),) + (slabs(rows_e - 1),) * 2 + (slabs(levels),) * 4
            + (slabs(2),),
            [
                work(levels), pltpu.VMEM((lat, lon), jnp.int32), work(rows_e),
                pltpu.SemaphoreType.DMA((GROUPS, 4)), pltpu.SemaphoreType.DMA((2,)),
            ],
            (tracers, u_east, v_north, kappa_h, bottom), 10**6, 6 * levels * slab, 50.5,
            in_specs=[HBM] * 5,
        )
    with jax.named_scope("lon_halo"):
        r_east = lax.ppermute(ww, "lon", west)
        r_west = lax.ppermute(we, "lon", east)
    with jax.named_scope("factor"):
        inv, ei, ratio, a_end, b_end, abc, msg = call(
            factor_kernel, (slabs(levels),) * 5 + (slabs(3),) * 2, [],
            (kappa_v, bottom, khb), 10**7, 6 * levels * slab, 16,
        )
    swap = [(i, i ^ 1) for i in range(dep_n)]
    with jax.named_scope("pair_coefficients"):
        pair = lax.ppermute(msg, "dep", swap)
    half = levels // 2

    def advect_half(start, earlier):
        return call(
            functools.partial(advect_kernel, start), slabs(2, half),
            [work(2, 2 * half), work(5, half)],
            (t0, t1, u, v, bottom, earlier), 10**7, 4 * levels * slab, 16,
        )

    with jax.named_scope("advect_north"):
        north_half = advect_half(0, abc)
    with jax.named_scope("advect_south"):
        south_half = advect_half(half, abc)
    with jax.named_scope("own_strips"):
        own_strips, own_bottom = call(
            own_kernel, (slabs(4, rows_e), slabs()), [],
            (sw, se, bp, abc), 10**6, 8 * rows_e * slab, 16,
        )
    rows_pay = 5 * lat + 16
    with jax.named_scope("advect_edge"):
        ea, ek, eb, bmx, first, second, red = call(
            edge_kernel,
            (
                slabs(2, rows_e), slabs(rows_e), slabs(), slabs(),
                f32(rows_pay - lat, lon), f32(rows_pay + lat, lon), slabs(3),
            ),
            [
                work(2, 2 * rows_e), work(5, rows_e), work(4, rows_e),
                pltpu.VMEM((2, rows_pay, lon), jnp.float32),
            ],
            (own_strips, own_bottom, r_east, r_west, bottom, north_half, south_half, kappa_h, abc, pair),
            10**6, 3 * levels * slab, 16,
        )
    other = []
    for i in range(lon_n * dep_n):
        row, place = divmod(i, dep_n)
        if place in (0, dep_n - 1):
            other.append((i, (row ^ 1) * dep_n + place))
        else:
            other.append((i, i + 1 if place % 2 else i - 1))
    with jax.named_scope("dep_halo"):
        first = lax.ppermute(first, "dep", swap)
        second = lax.ppermute(second, ("lon", "dep"), other)
    with jax.named_scope("patch"):
        full, gx, efx = call(
            patch_kernel, (slabs(2, levels), slabs(2, levels), slabs(2, rows_e)),
            [work(2, rows_e + 2)],
            (north_half, south_half, ea, ek, eb), 10**7, 8 * levels * slab, 16,
        )
    with jax.named_scope("fluxes"):
        q_part, fz = call(
            flux_kernel, (slabs(2, levels), slabs(2, levels)), [work(3)],
            (full, gx, efx, bmx, bottom, kappa_h), 10**7, 10 * levels * slab, 16,
        )
    with jax.named_scope("solve"):
        y, m1, m2, own = call(
            solve_kernel, (slabs(2, levels), slabs(3), slabs(2), slabs(3)),
            [
                work(2, 10), work(2, rows_e + 2), work(2, 4),
                pltpu.VMEM((2, rows_pay, lon), jnp.float32),
            ],
            (
                full, q_part, fz, ea, ek, eb, bmx, bottom, kappa_h, first, second,
                inv, ei, ratio, red, pair,
            ),
            10**7, 12 * levels * slab, 24,
        )
    with jax.named_scope("interfaces"):
        m1 = lax.ppermute(m1, "dep", swap)
        m3 = lax.ppermute(m2, "dep", [(i, i ^ 3) for i in range(dep_n)])
        m2 = lax.ppermute(m2, "dep", [(i, i ^ 2) for i in range(dep_n)])
    with jax.named_scope("finish"):
        return call(
            finish_kernel, slabs(2, levels),
            [work(2, levels), pltpu.SemaphoreType.DMA((2, GROUPS))],
            (y, a_end, b_end, own, m1, m2, m3), 10**6, 6 * levels * slab, 16,
            out_specs=HBM,
        )


def solution(mesh):
    in_specs = (
        P(None, "dep", None, "lon"),
        P("dep", None, "lon"),
        P("dep", None, "lon"),
        P("dep", None, "lon"),
        P("dep", None, "lon"),
        P(None, "lon"),
    )
    out_specs = P(None, "dep", None, "lon")
    return jax.shard_map(
        per_device, mesh=mesh, in_specs=in_specs, out_specs=out_specs, check_vma=False
    )
```

```python
import functools

import jax
import jax.numpy as jnp
from jax import lax
from jax.experimental import pallas as pl
from jax.experimental.pallas import tpu as pltpu
from jax.sharding import PartitionSpec as P

SUB = 4
THERMAL = 0.2
HALINE = 0.8
GROUPS = 4
ROWS = 32
STRIP = 32
HUGE = 1e30
MIB = 1024 * 1024

VMEM = pl.BlockSpec(memory_space=pltpu.VMEM)
HBM = pl.BlockSpec(memory_space=pltpu.HBM)


def lane_ids(rows):
    return lax.broadcasted_iota(jnp.int32, (rows, 128), 1)


def roll_lanes(x, amount):
    amount = amount % 128
    return x if amount == 0 else pltpu.roll(x, amount, 1)


def shift_north(x):
    return jnp.concatenate([x[8:], pltpu.roll(x[:8], 7, 0)], axis=0)


def shift_south(x):
    return jnp.concatenate([pltpu.roll(x[-8:], 1, 0), x[:-8]], axis=0)


def rows_of(ref, v, *lead):
    return ref[(*lead, pl.ds(v, 8, ref.shape[-2] // 8), slice(None))]


def neighbours(regs, v):
    north = regs[v + 1] if v + 1 < len(regs) else pltpu.roll(regs[0], 7, 0)
    south = regs[v - 1] if v > 0 else pltpu.roll(regs[-1], 1, 0)
    return north, south


def slab_of(ref, *lead):
    return jnp.concatenate([rows_of(ref, v, *lead) for v in range(ref.shape[-2] // 8)], axis=0)


def call(body, out_shape, scratch, args, flops, in_bytes, limit, in_specs=None, out_specs=None):
    return pl.pallas_call(
        body,
        out_shape=out_shape,
        in_specs=in_specs or [VMEM] * len(args),
        out_specs=out_specs or jax.tree.map(lambda _: VMEM, out_shape),
        scratch_shapes=scratch,
        compiler_params=pltpu.CompilerParams(vmem_limit_bytes=int(limit * MIB)),
        cost_estimate=pl.CostEstimate(flops=flops, bytes_accessed=in_bytes, transcendentals=0),
    )(*args)


def f32(*shape):
    return jax.ShapeDtypeStruct(shape, jnp.float32)


def pack_kernel(
    t_hbm, u_hbm, v_hbm, kh_hbm, b_hbm,
    sw_ref, se_ref, bp_ref, ww_ref, we_ref, t0_ref, t1_ref, u_ref, v_ref, khb_ref,
    kh_buf, b_buf, first_buf, sems, more_sems,
):
    rows_e = u_ref.shape[0] // GROUPS
    lat = u_ref.shape[1]
    lane = lane_ids(lat)
    fields = ((t_hbm.at[0], t0_ref), (t_hbm.at[1], t1_ref), (u_hbm, u_ref), (v_hbm, v_ref))
    groups = [
        [
            pltpu.make_async_copy(
                src.at[pl.ds(g * rows_e, rows_e)], dst.at[pl.ds(g * rows_e, rows_e)], sems.at[g, n]
            )
            for n, (src, dst) in enumerate(fields)
        ]
        for g in range(GROUPS)
    ]
    tail = [
        pltpu.make_async_copy(b_hbm, b_buf, more_sems.at[0]),
        pltpu.make_async_copy(kh_hbm, kh_buf, more_sems.at[1]),
    ]
    for copy in sum(groups, []) + tail:
        copy.start()
    for g in range(GROUPS):
        for copy in groups[g]:
            copy.wait()
        for batch in (range(0, rows_e // 2), range(rows_e // 2, rows_e)):
            rolled = {
                (r, f): roll_lanes(slab_of(ref, g * rows_e + r), STRIP * g + 8 * f)
                for r in batch
                for f, ref in enumerate((t0_ref, t1_ref, u_ref, v_ref))
            }
            done = []
            for r in batch:
                low = rolled[r, 0]
                high = None
                if g > 0:
                    low = jnp.where(lane >= STRIP * g, low, sw_ref[r])
                    high = jnp.where(lane >= STRIP * g - 8, rolled[r, 0], se_ref[r])
                for f in range(1, 4):
                    start = STRIP * g + 8 * f
                    low = jnp.where(lane >= start, rolled[r, f], low)
                    if high is None:
                        high = rolled[r, f]
                    else:
                        high = jnp.where(lane >= start - 8, rolled[r, f], high)
                if g == GROUPS - 1:
                    high = jnp.where(lane >= 120, first_buf[r], high)
                done.append((r, low, high))
            for r, low, high in done:
                if g == 0:
                    first_buf[r] = rolled[r, 0]
                sw_ref[r] = low
                se_ref[r] = high
    for copy in tail:
        copy.wait()
    bottom = slab_of(b_buf).astype(jnp.float32)
    place = bottom
    for g in range(1, GROUPS):
        place = jnp.where(lane >= STRIP * g - 8, roll_lanes(bottom, STRIP * g), place)
    place = jnp.where(lane >= 120, bottom, place)
    bp_ref[...] = place

    def kappa(r):
        out = None
        for g in range(GROUPS):
            rolled = roll_lanes(slab_of(kh_buf, g * rows_e + r), STRIP * g + 23)
            out = rolled if g == 0 else jnp.where(lane >= STRIP * g + 8, rolled, out)
        return out

    khb_ref[0] = slab_of(kh_buf, 0)
    khb_ref[1] = slab_of(kh_buf, GROUPS * rows_e - 1)
    last = rows_e - 1
    kappa_last = kappa(last)
    lane_q = lane % STRIP
    low_last, high_last = sw_ref[last], se_ref[last]
    wires = []
    for r in range(last):
        k = kappa(r)
        low, high = sw_ref[r], se_ref[r]
        west = (low, roll_lanes(low, -2), roll_lanes(low, -4), roll_lanes(low, -6), k)
        east = (
            roll_lanes(high, 6), roll_lanes(high, 4), roll_lanes(high, 2), roll_lanes(high, -1),
            roll_lanes(k, 1),
        )
        west += (roll_lanes(low_last, 24 - 8 * r),)
        east += (roll_lanes(high_last, 5 if r == 3 else 30 - 8 * r),)
        if r == 3:
            west += (roll_lanes(kappa_last, 6),)
            east += (roll_lanes(kappa_last, 7),)
        else:
            west += (roll_lanes(place, 30 - 2 * r),)
            east += (roll_lanes(place, 36 - 2 * r),)
        starts = (6, 12, 18, 23, 24, 29 if r == 3 else 30)
        for ref, parts in ((ww_ref, west), (we_ref, east)):
            wire = parts[0]
            for start, part in zip(starts, parts[1:]):
                wire = jnp.where(lane_q >= start, part, wire)
            wires.append((ref, r, wire))
    for ref, r, wire in wires:
        ref[r] = wire


def advect_block(slabs, get_c, get_u, get_v, get_level, bx, by, buf, coef, put):
    regs = bx.shape[0] // 8
    for i, slab in enumerate(slabs):
        level = get_level(slab)
        um = jnp.where(level < bx, get_u(slab), 0.0)
        vm = jnp.where(level < by, get_v(slab), 0.0)
        uw = roll_lanes(um, 1)
        vs = shift_south(vm)
        coef[0, i] = (
            1.0
            - jnp.maximum(um, 0.0)
            + jnp.minimum(uw, 0.0)
            - jnp.maximum(vm, 0.0)
            + jnp.minimum(vs, 0.0)
        )
        coef[1, i] = -jnp.minimum(um, 0.0)
        coef[2, i] = jnp.maximum(uw, 0.0)
        coef[3, i] = -jnp.minimum(vm, 0.0)
        coef[4, i] = jnp.maximum(vs, 0.0)
        for tr in range(2):
            buf[0, 2 * i + tr] = get_c(tr, slab)
    for step in range(SUB):
        src, dst = step % 2, (step + 1) % 2
        for i, slab in enumerate(slabs):
            now = [
                [buf[src, 2 * i + tr, 8 * v : 8 * v + 8] for v in range(regs)] for tr in range(2)
            ]
            for v in range(regs):
                js = slice(8 * v, 8 * v + 8)
                a, b, c, d, e = (coef[n, i, js] for n in range(5))
                for tr in range(2):
                    here = now[tr][v]
                    north, south = neighbours(now[tr], v)
                    new = (
                        a * here
                        + b * roll_lanes(here, -1)
                        + c * roll_lanes(here, 1)
                        + d * north
                        + e * south
                    )
                    if step < SUB - 1:
                        buf[dst, 2 * i + tr, js] = new
                    else:
                        put(tr, slab, js, new)


def face_limits(bottom):
    lat = bottom.shape[0]
    rows = lax.broadcasted_iota(jnp.int32, bottom.shape, 0)
    north = jnp.where(rows == lat - 1, 0.0, shift_north(bottom))
    return jnp.minimum(bottom, roll_lanes(bottom, -1)), jnp.minimum(bottom, north)


def lat_limits(bottom):
    lat = bottom.shape[0]
    rows = lax.broadcasted_iota(jnp.int32, bottom.shape, 0)
    north = jnp.where(rows == lat - 1, 0.0, shift_north(bottom))
    south = jnp.where(rows == 0, 0.0, shift_south(bottom))
    return jnp.minimum(north, south)


def advect_kernel(start, t0_ref, t1_ref, u_ref, v_ref, b_ref, earlier_ref, out_ref, buf, coef):
    del earlier_ref
    count, lat = out_ref.shape[1], out_ref.shape[2]
    base = lax.axis_index("dep") * t0_ref.shape[0] + start
    bx, by = face_limits(slab_of(b_ref).astype(jnp.float32))

    def put(tr, slab, js, new):
        out_ref[tr, slab, js] = new

    advect_block(
        list(range(count)),
        lambda tr, s: slab_of((t0_ref, t1_ref)[tr], start + s),
        lambda s: slab_of(u_ref, start + s),
        lambda s: slab_of(v_ref, start + s),
        lambda s: (base + s).astype(jnp.float32),
        bx,
        by,
        buf,
        coef,
        put,
    )


def join(lane_q, own, east, west):
    halo = jnp.where(lane_q < 16, east, west)
    return jnp.where((lane_q >= 8) & (lane_q < 24), halo, own)


def west_patch(slab, g):
    return roll_lanes(slab, -(STRIP * g + 24))


def east_patch(slab, g):
    return roll_lanes(slab, 120 - STRIP * g)


def patched(main, slab, g, lane):
    return jnp.where(
        lane < 4, west_patch(slab, g), jnp.where(lane >= 124, east_patch(slab, g), main)
    )


def own_kernel(sw_ref, se_ref, bp_ref, earlier_ref, own_ref, ownb_ref):
    del earlier_ref
    rows_e, lat = sw_ref.shape[0], sw_ref.shape[1]
    lane_q = lane_ids(lat) % STRIP
    for r in range(rows_e):
        made = [
            jnp.where(
                lane_q < 16, roll_lanes(se_ref[r], 8 - 8 * f), roll_lanes(sw_ref[r], 24 - 8 * f)
            )
            for f in range(4)
        ]
        for f in range(4):
            own_ref[f, r] = made[f]
    place = bp_ref[...]
    ownb_ref[...] = jnp.where(lane_q < 16, roll_lanes(place, 8), roll_lanes(place, 24))


def pair_response(abc_ref, pair_ref, me):
    upper = lax.rem(me, 2) == 0
    low_pair = me < 2
    inv_t = 1.0 / (pair_ref[0] + jnp.where(upper, abc_ref[1], abc_ref[0]))
    c_pair = jnp.where(upper == low_pair, pair_ref[1], abc_ref[2])
    share = c_pair * inv_t
    return share, inv_t, jnp.where(upper, abc_ref[0], abc_ref[1]) - c_pair * share


def fold_strip(slab, place):
    lane = lane_ids(8)
    folded = jnp.zeros((8, 128), jnp.float32)
    for v in range(slab.shape[0] // 8):
        rolled = roll_lanes(slab[8 * v : 8 * v + 8], 16 * v - place)
        folded = jnp.where(lane >= 16 * v, rolled, folded)
    return folded


def unfold_strip(folded, place, regs):
    return jnp.concatenate([roll_lanes(folded, place - 16 * v) for v in range(regs)], axis=0)


def edge_kernel(
    own_ref, ownb_ref, re_ref, rw_ref, b_ref, north_half, south_half, kh_ref, abc_ref, pair_ref,
    ea_ref, ek_ref, eb_ref, bmx_ref, first_ref, second_ref, red_ref,
    buf, coef, fields, pay,
):
    levels, lat = kh_ref.shape[0], kh_ref.shape[1]
    rows_e = levels // GROUPS
    me = lax.axis_index("dep")
    base = me * levels
    parity = lax.rem(me, 2)
    up_ref, down_ref = pay.at[1 - parity], pay.at[parity]
    lane = lane_ids(lat)
    lane_q = lane % STRIP
    bottom = slab_of(b_ref).astype(jnp.float32)
    east = [roll_lanes(re_ref[r], 2 * r - 22) for r in range(3)]
    west = [roll_lanes(rw_ref[r], 2 * r - 12) for r in range(3)]
    eb = join(
        lane_q,
        ownb_ref[...],
        jnp.where(lane_q < 10, east[0], jnp.where(lane_q < 12, east[1], east[2])),
        jnp.where(lane_q < 20, west[0], jnp.where(lane_q < 22, west[1], west[2])),
    )
    eb_ref[...] = eb
    b_west = roll_lanes(jnp.where(lane == 127, west_patch(eb, 0), bottom), 1)
    b_east = roll_lanes(jnp.where(lane == 0, east_patch(eb, 0), bottom), -1)
    bmx_ref[...] = jnp.minimum(b_west, b_east)
    last = rows_e - 1
    for r in range(rows_e):
        at, shift_e, shift_w = (3, -21, -6) if r == last else (r, -15, 0)
        ek_ref[r] = jnp.where(
            lane_q < 16, roll_lanes(re_ref[at], shift_e), roll_lanes(rw_ref[at], shift_w)
        )
        made = []
        for f in range(4):
            at, start = (f, 24) if r == last else (r, 6 * f)
            made.append(
                join(
                    lane_q,
                    own_ref[f, r],
                    roll_lanes(re_ref[at], 8 - start),
                    roll_lanes(rw_ref[at], (19 if f == 3 else 18) - start),
                )
            )
        for f in range(4):
            fields[f, r] = made[f]
    bx, by = face_limits(eb)
    level0 = (base + (lane // STRIP) * rows_e).astype(jnp.float32)

    def put(tr, slab, js, new):
        ea_ref[tr, slab, js] = new

    advect_block(
        list(range(rows_e)),
        lambda tr, s: fields[tr, s],
        lambda s: fields[2, s],
        lambda s: fields[3, s],
        lambda s: level0 + float(s),
        bx,
        by,
        buf,
        coef,
        put,
    )
    top, half = rows_e - 1, levels // 2
    for tr in range(2):
        for n, (k, slab) in enumerate(((0, ea_ref[tr, 0]), (1, ea_ref[tr, 1]))):
            at = (2 * n + tr) * lat
            up_ref[at : at + lat] = patched(north_half[tr, k], slab, 0, lane)
        for n, (k, slab) in enumerate(
            ((half - 1, ea_ref[tr, top]), (half - 2, ea_ref[tr, top - 1]))
        ):
            at = (2 * n + tr) * lat
            down_ref[at : at + lat] = patched(south_half[tr, k], slab, 3, lane)
        at = 4 * lat + 8 * tr
        up_ref[at : at + 8] = fold_strip(ea_ref[tr, 0], 8)
        down_ref[at : at + 8] = fold_strip(ea_ref[tr, top], 3 * STRIP + 8)
    up_ref[4 * lat + 16 : 5 * lat + 16] = slab_of(kh_ref, 0)
    down_ref[4 * lat + 16 : 5 * lat + 16] = slab_of(kh_ref, levels - 1)
    first_ref[...] = pay[0, 0 : 4 * lat + 16]
    second_ref[0 : 5 * lat + 16] = pay[1]
    response = pair_response(abc_ref, pair_ref, me)
    for n in range(3):
        red_ref[n] = response[n]
    second_ref[5 * lat + 16 : 6 * lat + 16] = response[2]


def slopes(gx, gy, gz):
    rx, ry, rz = (-0.5 * THERMAL * g[0] + 0.5 * HALINE * g[1] for g in (gx, gy, gz))
    scale = rz / (1.0 + rx * rx + ry * ry + rz * rz)
    return rx * scale, ry * scale


def flux_xyz(gx, gy, gz, kappa, need_xy=True):
    sx, sy = slopes(gx, gy, gz)
    kx, ky = kappa * sx, kappa * sy
    kz = kx * sx + ky * sy
    fz = [kx * gx[n] + ky * gy[n] + kz * gz[n] for n in range(2)]
    if not need_xy:
        return None, None, fz
    fx = [kappa * gx[n] + kx * gz[n] for n in range(2)]
    fy = [kappa * gy[n] + ky * gz[n] for n in range(2)]
    return fx, fy, fz


def flux_x_edge(gx, gy, gz, kappa):
    sx, _ = slopes(gx, gy, gz)
    kx = kappa * sx
    return [kappa * gx[n] + kx * gz[n] for n in range(2)]


def diff(mask, high, low):
    return jnp.where(mask, high - low, 0.0)


def edge_flux_row(r, rows, ek, eb, ebx, eby, level0):
    level = level0 + r
    mx = level < ebx
    my = level < eby
    mz = (level + 1.0 < eb) & (level >= 1.0)
    kappa = jnp.where((level < eb) & (level >= 0.0), 0.25 * ek, 0.0)
    gx, gy, gz = [], [], []
    for tr in range(2):
        here = rows[tr, r + 1]
        gx.append(diff(mx, roll_lanes(here, -1), roll_lanes(here, 1)))
        gy.append(diff(my, shift_north(here), shift_south(here)))
        gz.append(diff(mz, rows[tr, r + 2], rows[tr, r]))
    return flux_x_edge(gx, gy, gz, kappa)


def edge_limits(eb):
    return (
        jnp.minimum(roll_lanes(eb, 1), roll_lanes(eb, -1)),
        lat_limits(eb),
    )


def zonal_change(fx, west, east, lane):
    return roll_lanes(jnp.where(lane == 0, east, fx), -1) - roll_lanes(
        jnp.where(lane == 127, west, fx), 1
    )


def divergence(fx, fy, slab, g, lane):
    return zonal_change(fx, west_patch(slab, g), east_patch(slab, g), lane) + (
        shift_north(fy) - shift_south(fy)
    )


def patch_kernel(
    north_half, south_half, ea_ref, ek_ref, eb_ref,
    full_ref, gx_ref, efx_ref,
    rows,
):
    levels, lat = full_ref.shape[1], full_ref.shape[2]
    rows_e = levels // GROUPS
    base = lax.axis_index("dep") * levels
    lane = lane_ids(lat)
    eb = eb_ref[...]
    ebx, eby = edge_limits(eb)
    level0 = (base + (lane // STRIP) * rows_e).astype(jnp.float32)
    for tr in range(2):
        for r in range(rows_e):
            rows[tr, r + 1] = ea_ref[tr, r]
        rows[tr, 0] = roll_lanes(ea_ref[tr, rows_e - 1], STRIP)
        rows[tr, rows_e + 1] = roll_lanes(ea_ref[tr, 0], -STRIP)
    found = [
        edge_flux_row(r, rows, ek_ref[r], eb, ebx, eby, level0) for r in range(rows_e)
    ]
    for r in range(rows_e):
        for tr in range(2):
            efx_ref[tr, r] = found[r][tr]

    lane = lane_ids(ROWS)
    units = [(g, slice(j, j + ROWS)) for g in range(GROUPS) for j in range(0, lat, ROWS)]

    def patch(r, _):
        def fetch(unit):
            g, js = unit
            strips = [ea_ref[tr, r, js] for tr in range(2)]
            half = (north_half, south_half)[2 * g // GROUPS]
            mains = [half[tr, g % (GROUPS // 2) * rows_e + r, js] for tr in range(2)]
            return [(west_patch(x, g), east_patch(x, g), y) for x, y in zip(strips, mains)]

        def put(unit, mains, rolled):
            g, js = unit
            for tr in range(2):
                full_ref[tr, g * rows_e + r, js] = mains[tr]
                gx_ref[tr, g * rows_e + r, js] = rolled[tr][0] - rolled[tr][1]

        waiting = None
        fetched = fetch(units[0])
        for n, unit in enumerate(units):
            now = fetched
            fetched = fetch(units[n + 1]) if n + 1 < len(units) else None
            mains, rolled = [], []
            for west, east, main in now:
                main = jnp.where(lane < 4, west, jnp.where(lane >= 124, east, main))
                mains.append(main)
                rolled.append(
                    (
                        roll_lanes(jnp.where(lane == 0, east, main), -1),
                        roll_lanes(jnp.where(lane == 127, west, main), 1),
                    )
                )
            if waiting is not None:
                put(*waiting)
            waiting = (unit, mains, rolled)
        put(*waiting)
        return 0

    lax.fori_loop(0, rows_e, patch, 0)


def flux_kernel(
    full_ref, gx_ref, efx_ref, bmx_ref, b_ref, kh_ref,
    q_ref, fz_ref,
    limits,
):
    levels, lat = full_ref.shape[1], full_ref.shape[2]
    rows_e = levels // GROUPS
    base = lax.axis_index("dep") * levels
    lane = lane_ids(lat)
    bottom = slab_of(b_ref).astype(jnp.float32)
    limits[0] = bmx_ref[...]
    limits[1] = lat_limits(bottom)
    limits[2] = bottom

    def north_rows(tr, k, j):
        if j + 8 + ROWS <= lat:
            return full_ref[tr, k, j + 8 : j + 8 + ROWS]
        return jnp.concatenate(
            [full_ref[tr, k, j + 8 : lat], pltpu.roll(full_ref[tr, k, 0:8], 7, 0)], axis=0
        )

    def south_rows(tr, k, j):
        if j >= 8:
            return full_ref[tr, k, j - 8 : j - 8 + ROWS]
        return jnp.concatenate(
            [pltpu.roll(full_ref[tr, k, lat - 8 : lat], 1, 0), full_ref[tr, k, 0 : ROWS - 8]],
            axis=0,
        )

    def fluxes(r, _):
        for g in range(GROUPS):
            k = g * rows_e + r
            above, below = jnp.maximum(k - 1, 0), jnp.minimum(k + 1, levels - 1)
            level = (base + k).astype(jnp.float32)
            level_z = jnp.where(level >= 1.0, level + 1.0, HUGE)
            sides = [
                (west_patch(efx_ref[tr, r], g), east_patch(efx_ref[tr, r], g)) for tr in range(2)
            ]
            fxs, fys, fzs = [[], []], [[], []], [[], []]
            for j in range(0, lat, ROWS):
                js = slice(j, j + ROWS)
                mx = level < limits[0, js]
                my = level < limits[1, js]
                mz = level_z < limits[2, js]
                kh = jnp.concatenate(
                    [rows_of(kh_ref, v, k) for v in range(j // 8, (j + ROWS) // 8)], axis=0
                )
                kappa = jnp.where(level < limits[2, js], 0.25 * kh, 0.0)
                gx, gy, gz = [], [], []
                for tr in range(2):
                    gx.append(jnp.where(mx, gx_ref[tr, k, js], 0.0))
                    gy.append(diff(my, north_rows(tr, k, j), south_rows(tr, k, j)))
                    gz.append(diff(mz, full_ref[tr, below, js], full_ref[tr, above, js]))
                fx, fy, fz = flux_xyz(gx, gy, gz, kappa)
                for tr in range(2):
                    fxs[tr].append(fx[tr])
                    fys[tr].append(fy[tr])
                    fzs[tr].append(fz[tr])
            wet = level < limits[2]
            new = []
            for tr in range(2):
                fy = jnp.concatenate(fys[tr], axis=0)
                change = zonal_change(jnp.concatenate(fxs[tr], axis=0), *sides[tr], lane)
                change = change + (shift_north(fy) - shift_south(fy))
                new.append(full_ref[tr, k] + jnp.where(wet, change, 0.0))
            for tr in range(2):
                q_ref[tr, k] = new[tr]
                fz_ref[tr, k] = jnp.concatenate(fzs[tr], axis=0)
        return 0

    lax.fori_loop(0, rows_e, fluxes, 0)


def factor_kernel(
    kv_ref, b_ref, khb_ref, inv_ref, ei_ref, ratio_ref, a_ref, bb_ref, abc_ref, msg_ref
):
    levels, lat = kv_ref.shape[0], kv_ref.shape[1]
    base = lax.axis_index("dep") * levels
    bottom = slab_of(b_ref).astype(jnp.float32)

    def coupling(k):
        level = (base + k).astype(jnp.float32)
        level = jnp.where(level >= 1.0, level, HUGE)
        return jnp.where(level < bottom, slab_of(kv_ref, k), 0.0)

    top = coupling(0)
    e = jnp.zeros((lat, 128), jnp.float32)
    q = e
    za = jnp.ones((lat, 128), jnp.float32)
    for k in range(levels):
        low = coupling(k + 1) if k + 1 < levels else jnp.zeros((lat, 128), jnp.float32)
        eq = 1.0 + e * q
        inv = 1.0 / (eq + low)
        inv_ref[k] = inv
        ei = e * inv
        ei_ref[k] = ei
        ratio_ref[k] = low * inv
        za = inv if k == 0 else za * ei
        a_ref[k] = za
        q = eq * inv
        e = low
    bb_ref[levels - 1] = inv
    b = inv
    a = za
    for k in range(levels - 2, -1, -1):
        ratio = ratio_ref[k]
        b = ratio * b
        a = a_ref[k] + ratio * a
        bb_ref[k] = b
        a_ref[k] = a
    a = a + jnp.where(top > 0.0, 1.0 / jnp.maximum(top, 1e-30), HUGE)
    abc_ref[0] = a
    abc_ref[1] = inv
    abc_ref[2] = b
    upper = lax.rem(lax.axis_index("dep"), 2) == 0
    msg_ref[0] = jnp.where(upper, inv, a)
    msg_ref[1] = b
    msg_ref[2] = jnp.where(upper, khb_ref[1], khb_ref[0])


def solve_kernel(
    full_ref, q_ref, fz_ref, ea_ref, ek_ref, eb_ref, bmx_ref, b_ref, kh_ref,
    first_ref, second_ref, inv_ref, ei_ref, ratio_ref, red_ref, pair_ref,
    y_ref, send_ref, both_ref, own_ref,
    pad, epad, fze, halo,
):
    levels, lat = q_ref.shape[1], q_ref.shape[2]
    rows_e = levels // GROUPS
    last = levels - 1
    top = rows_e - 1
    me = lax.axis_index("dep")
    base = me * levels
    parity = lax.rem(me, 2)
    outer = (me == 0) | (me == 3)
    upper = parity == 0
    sign = jnp.where(me < 2, 1.0, -1.0)
    lane = lane_ids(lat)
    halo[0, 0 : 4 * lat + 16] = first_ref[...]
    halo[0, 4 * lat + 16 : 5 * lat + 16] = pair_ref[2]
    halo[1] = second_ref[0 : 5 * lat + 16]
    above_ref, below_ref = halo.at[1 - parity], halo.at[parity]

    share = red_ref[0]
    both = red_ref[2] + second_ref[5 * lat + 16 : 6 * lat + 16]
    cross = share / both
    inside = red_ref[1] + share * cross
    for n, value in enumerate((share, red_ref[1], both)):
        own_ref[n] = value
    both_ref[...] = both

    eb = eb_ref[...]
    ebx, eby = edge_limits(eb)
    level0 = (base + (lane // STRIP) * rows_e).astype(jnp.float32)
    for tr in range(2):
        pad[tr, 0] = above_ref[(2 + tr) * lat : (3 + tr) * lat]
        pad[tr, 1] = above_ref[tr * lat : (1 + tr) * lat]
        for n, k in enumerate((0, 1, 2, last - 2, last - 1, last)):
            pad[tr, n + 2] = full_ref[tr, k]
        pad[tr, 8] = below_ref[tr * lat : (1 + tr) * lat]
        pad[tr, 9] = below_ref[(2 + tr) * lat : (3 + tr) * lat]
        for r in range(rows_e):
            epad[tr, r + 1] = ea_ref[tr, r]
        at = 4 * lat + 8 * tr
        corner_up = unfold_strip(above_ref[at : at + 8], 3 * STRIP + 8, lat // 8)
        corner_dn = unfold_strip(below_ref[at : at + 8], 8, lat // 8)
        epad[tr, 0] = roll_lanes(
            jnp.where(lane >= 3 * STRIP, corner_up, ea_ref[tr, top]), STRIP
        )
        epad[tr, rows_e + 1] = roll_lanes(
            jnp.where(lane < STRIP, corner_dn, ea_ref[tr, 0]), -STRIP
        )
    efx = {
        r + 1: edge_flux_row(r, epad, ek_ref[r], eb, ebx, eby, level0) for r in (0, top)
    }

    bottom = slab_of(b_ref).astype(jnp.float32)
    bmy = lat_limits(bottom)
    bmx = bmx_ref[...]
    ends = (
        (1, -1, 0, 0, above_ref[4 * lat + 16 : 5 * lat + 16], True),
        (2, 0, 1, 0, slab_of(kh_ref, 0), False),
        (7, last, top + 1, 3, slab_of(kh_ref, last), False),
        (8, last + 1, top + 2, 3, below_ref[4 * lat + 16 : 5 * lat + 16], True),
    )
    spread = {}
    for m, (n, k, er, g, kappa_slab, only_z) in enumerate(ends):
        level = (base + k).astype(jnp.float32)
        level_z = jnp.where(level >= 1.0, level + 1.0, HUGE)
        level_h = jnp.where(level >= 0.0, level, HUGE)
        mx = level_h < bmx
        my = level_h < bmy
        mz = level_z < bottom
        kappa = jnp.where(level_h < bottom, 0.25 * kappa_slab, 0.0)
        gx, gy, gz = [], [], []
        for tr in range(2):
            slab, main = epad[tr, er], pad[tr, n]
            change = zonal_change(main, west_patch(slab, g), east_patch(slab, g), lane)
            gx.append(jnp.where(mx, change, 0.0))
            gy.append(diff(my, shift_north(main), shift_south(main)))
            gz.append(diff(mz, pad[tr, n + 1], pad[tr, n - 1]))
        fx, fy, fz = flux_xyz(gx, gy, gz, kappa, not only_z)
        for tr in range(2):
            fze[tr, m] = fz[tr]
            if not only_z:
                spread[k, tr] = divergence(fx[tr], fy[tr], efx[er][tr], g, lane)

    def vertical_flux(tr, k):
        place = {-1: 0, 0: 1, last: 2, last + 1: 3}.get(k)
        return fz_ref[tr, k] if place is None else fze[tr, place]

    z = [None, None]
    for k in range(levels):
        level = (base + k).astype(jnp.float32)
        wet = level < bottom
        for tr in range(2):
            change = vertical_flux(tr, k + 1) - vertical_flux(tr, k - 1)
            if k == 0 or k == last:
                change = change + spread[k, tr]
                start = pad[tr, 2 if k == 0 else 7]
            else:
                start = q_ref[tr, k]
            rhs = start + jnp.where(wet, change, 0.0)
            new = rhs * inv_ref[k]
            z[tr] = new if k == 0 else new + ei_ref[k] * z[tr]
        for tr in range(2):
            y_ref[tr, k] = z[tr]
    low = list(z)
    for k in range(last - 1, -1, -1):
        ratio = ratio_ref[k]
        z = [y_ref[tr, k] + ratio * z[tr] for tr in range(2)]
        for tr in range(2):
            y_ref[tr, k] = z[tr]
    for tr in range(2):
        near = jnp.where(upper, low[tr], z[tr])
        far = jnp.where(upper, z[tr], low[tr])
        value = jnp.where(outer, share * near, far - share * near)
        send_ref[me, tr] = value
        send_ref[lax.rem(me + 2, 4), tr] = value
        send_ref[3 - me, tr] = value
        send_ref[me + 1 - 2 * parity, tr] = jnp.where(
            outer, near, sign * (inside * near - cross * far)
        )


def finish_kernel(
    y_ref, a_ref, bb_ref, own_ref, both_ref, got_ref, out_hbm, out, sems
):
    levels = y_ref.shape[1]
    me = lax.axis_index("dep")
    upper = lax.rem(me, 2) == 0
    outer = (me == 0) | (me == 3)
    sign = jnp.where(me < 2, 1.0, -1.0)
    share, inv_t = own_ref[0], own_ref[1]
    inv_e = 1.0 / jnp.where(outer, both_ref[...], own_ref[2])
    cross = share * inv_e
    inside = inv_t + share * cross
    tops, lows = [], []
    for tr in range(2):
        y_top, y_low = y_ref[tr, 0], y_ref[tr, levels - 1]
        near = jnp.where(upper, y_low, y_top)
        far = jnp.where(upper, y_top, y_low)
        mate = got_ref[me + 1 - 2 * lax.rem(me, 2), tr]
        across = got_ref[lax.rem(me + 2, 4), tr] + got_ref[3 - me, tr]
        pair_flux = jnp.where(
            outer,
            mate + sign * (cross * across - inside * near),
            sign * (inside * (near - mate) + cross * (across - far)),
        )
        middle = sign * (inv_e * (across - far + share * near) - cross * mate)
        middle = jnp.where(outer, 0.0, middle)
        tops.append(jnp.where(upper, middle, pair_flux))
        lows.append(jnp.where(upper, pair_flux, middle))
    step, regs = levels // GROUPS, y_ref.shape[2] // 8
    copies = []
    for part in range(GROUPS):
        for k in range(part * step, (part + 1) * step):
            a, b = a_ref[k], bb_ref[k]
            new = [y_ref[tr, k] - tops[tr] * a + lows[tr] * b for tr in range(2)]
            for tr in range(2):
                for v in range(regs):
                    out[tr, k, pl.ds(v, 8, regs), :] = new[tr][8 * v : 8 * v + 8]
        for tr in range(2):
            span = (tr, pl.ds(part * step, step))
            copies.append(
                pltpu.make_async_copy(out.at[span], out_hbm.at[span], sems.at[tr, part])
            )
            copies[-1].start()
    for copy in copies:
        copy.wait()


def per_device(tracers, u_east, v_north, kappa_h, kappa_v, bottom):
    _, levels, lat, lon = tracers.shape
    rows_e = levels // GROUPS
    lon_n, dep_n = lax.axis_size("lon"), lax.axis_size("dep")
    east = [(i, (i + 1) % lon_n) for i in range(lon_n)]
    west = [(t, s) for s, t in east]
    slab = lat * lon * 4
    slabs = lambda *lead: f32(*lead, lat, lon)
    work = lambda *lead: pltpu.VMEM(lead + (lat, lon), jnp.float32)

    with jax.named_scope("pack"):
        sw, se, bp, ww, we, t0, t1, u, v, khb = call(
            pack_kernel,
            (slabs(rows_e),) * 2 + (slabs(),) + (slabs(rows_e - 1),) * 2 + (slabs(levels),) * 4
            + (slabs(2),),
            [
                work(levels), pltpu.VMEM((lat, lon), jnp.int32), work(rows_e),
                pltpu.SemaphoreType.DMA((GROUPS, 4)), pltpu.SemaphoreType.DMA((2,)),
            ],
            (tracers, u_east, v_north, kappa_h, bottom), 10**6, 6 * levels * slab, 50.5,
            in_specs=[HBM] * 5,
        )
    with jax.named_scope("lon_halo"):
        r_east = lax.ppermute(ww, "lon", west)
        r_west = lax.ppermute(we, "lon", east)
    with jax.named_scope("factor"):
        inv, ei, ratio, a_end, b_end, abc, msg = call(
            factor_kernel, (slabs(levels),) * 5 + (slabs(3),) * 2, [],
            (kappa_v, bottom, khb), 10**7, 6 * levels * slab, 16,
        )
    swap = [(i, i ^ 1) for i in range(dep_n)]
    with jax.named_scope("pair_coefficients"):
        pair = lax.ppermute(msg, "dep", swap)
    half = levels // 2

    def advect_half(start, earlier):
        return call(
            functools.partial(advect_kernel, start), slabs(2, half),
            [work(2, 2 * half), work(5, half)],
            (t0, t1, u, v, bottom, earlier), 10**7, 4 * levels * slab, 16,
        )

    with jax.named_scope("advect_north"):
        north_half = advect_half(0, abc)
    with jax.named_scope("advect_south"):
        south_half = advect_half(half, abc)
    with jax.named_scope("own_strips"):
        own_strips, own_bottom = call(
            own_kernel, (slabs(4, rows_e), slabs()), [],
            (sw, se, bp, abc), 10**6, 8 * rows_e * slab, 16,
        )
    rows_pay = 5 * lat + 16
    with jax.named_scope("advect_edge"):
        ea, ek, eb, bmx, first, second, red = call(
            edge_kernel,
            (
                slabs(2, rows_e), slabs(rows_e), slabs(), slabs(),
                f32(rows_pay - lat, lon), f32(rows_pay + lat, lon), slabs(3),
            ),
            [
                work(2, 2 * rows_e), work(5, rows_e), work(4, rows_e),
                pltpu.VMEM((2, rows_pay, lon), jnp.float32),
            ],
            (own_strips, own_bottom, r_east, r_west, bottom, north_half, south_half, kappa_h, abc, pair),
            10**6, 3 * levels * slab, 16,
        )
    other = []
    for i in range(lon_n * dep_n):
        row, place = divmod(i, dep_n)
        if place in (0, dep_n - 1):
            other.append((i, (row ^ 1) * dep_n + place))
        else:
            other.append((i, i + 1 if place % 2 else i - 1))
    with jax.named_scope("dep_halo"):
        first = lax.ppermute(first, "dep", swap)
        second = lax.ppermute(second, ("lon", "dep"), other)
    with jax.named_scope("patch"):
        full, gx, efx = call(
            patch_kernel, (slabs(2, levels), slabs(2, levels), slabs(2, rows_e)),
            [work(2, rows_e + 2)],
            (north_half, south_half, ea, ek, eb), 10**7, 8 * levels * slab, 16,
        )
    with jax.named_scope("fluxes"):
        q_part, fz = call(
            flux_kernel, (slabs(2, levels), slabs(2, levels)), [work(3)],
            (full, gx, efx, bmx, bottom, kappa_h), 10**7, 10 * levels * slab, 16,
        )
    with jax.named_scope("solve"):
        y, send, both, own = call(
            solve_kernel, (slabs(2, levels), slabs(dep_n, 2), slabs(), slabs(3)),
            [
                work(2, 10), work(2, rows_e + 2), work(2, 4),
                pltpu.VMEM((2, rows_pay, lon), jnp.float32),
            ],
            (
                full, q_part, fz, ea, ek, eb, bmx, bottom, kappa_h, first, second,
                inv, ei, ratio, red, pair,
            ),
            10**7, 12 * levels * slab, 24,
        )
    with jax.named_scope("interfaces"):
        both = lax.ppermute(both, "dep", swap)
        got = lax.all_to_all(send, "dep", 0, 0, tiled=True)
    with jax.named_scope("finish"):
        return call(
            finish_kernel, slabs(2, levels),
            [work(2, levels), pltpu.SemaphoreType.DMA((2, GROUPS))],
            (y, a_end, b_end, own, both, got), 10**6, 6 * levels * slab, 16,
            out_specs=HBM,
        )


def solution(mesh):
    in_specs = (
        P(None, "dep", None, "lon"),
        P("dep", None, "lon"),
        P("dep", None, "lon"),
        P("dep", None, "lon"),
        P("dep", None, "lon"),
        P(None, "lon"),
    )
    out_specs = P(None, "dep", None, "lon")
    return jax.shard_map(
        per_device, mesh=mesh, in_specs=in_specs, out_specs=out_specs, check_vma=False
    )
```

```python
import functools

import jax
import jax.numpy as jnp
from jax import lax
from jax.experimental import pallas as pl
from jax.experimental.pallas import tpu as pltpu
from jax.sharding import PartitionSpec as P

SUB = 4
THERMAL = 0.2
HALINE = 0.8
GROUPS = 4
ROWS = 32
STRIP = 32
HUGE = 1e30
MIB = 1024 * 1024

VMEM = pl.BlockSpec(memory_space=pltpu.VMEM)
HBM = pl.BlockSpec(memory_space=pltpu.HBM)


def lane_ids(rows):
    return lax.broadcasted_iota(jnp.int32, (rows, 128), 1)


def roll_lanes(x, amount):
    amount = amount % 128
    return x if amount == 0 else pltpu.roll(x, amount, 1)


def shift_north(x):
    return jnp.concatenate([x[8:], pltpu.roll(x[:8], 7, 0)], axis=0)


def shift_south(x):
    return jnp.concatenate([pltpu.roll(x[-8:], 1, 0), x[:-8]], axis=0)


def rows_of(ref, v, *lead):
    return ref[(*lead, pl.ds(v, 8, ref.shape[-2] // 8), slice(None))]


def neighbours(regs, v):
    north = regs[v + 1] if v + 1 < len(regs) else pltpu.roll(regs[0], 7, 0)
    south = regs[v - 1] if v > 0 else pltpu.roll(regs[-1], 1, 0)
    return north, south


def slab_of(ref, *lead):
    return jnp.concatenate([rows_of(ref, v, *lead) for v in range(ref.shape[-2] // 8)], axis=0)


def call(body, out_shape, scratch, args, flops, in_bytes, limit, in_specs=None, out_specs=None):
    return pl.pallas_call(
        body,
        out_shape=out_shape,
        in_specs=in_specs or [VMEM] * len(args),
        out_specs=out_specs or jax.tree.map(lambda _: VMEM, out_shape),
        scratch_shapes=scratch,
        compiler_params=pltpu.CompilerParams(vmem_limit_bytes=int(limit * MIB)),
        cost_estimate=pl.CostEstimate(flops=flops, bytes_accessed=in_bytes, transcendentals=0),
    )(*args)


def f32(*shape):
    return jax.ShapeDtypeStruct(shape, jnp.float32)


def pack_kernel(
    t_hbm, u_hbm, v_hbm, kh_hbm, b_hbm,
    sw_ref, se_ref, bp_ref, ww_ref, we_ref, t0_ref, t1_ref, u_ref, v_ref, khb_ref,
    kh_buf, b_buf, first_buf, sems, more_sems,
):
    rows_e = u_ref.shape[0] // GROUPS
    lat = u_ref.shape[1]
    lane = lane_ids(lat)
    fields = ((t_hbm.at[0], t0_ref), (t_hbm.at[1], t1_ref), (u_hbm, u_ref), (v_hbm, v_ref))
    groups = [
        [
            pltpu.make_async_copy(
                src.at[pl.ds(g * rows_e, rows_e)], dst.at[pl.ds(g * rows_e, rows_e)], sems.at[g, n]
            )
            for n, (src, dst) in enumerate(fields)
        ]
        for g in range(GROUPS)
    ]
    tail = [
        pltpu.make_async_copy(b_hbm, b_buf, more_sems.at[0]),
        pltpu.make_async_copy(kh_hbm, kh_buf, more_sems.at[1]),
    ]
    for copy in sum(groups, []) + tail:
        copy.start()
    for g in range(GROUPS):
        for copy in groups[g]:
            copy.wait()
        for batch in (range(0, rows_e // 2), range(rows_e // 2, rows_e)):
            rolled = {
                (r, f): roll_lanes(slab_of(ref, g * rows_e + r), STRIP * g + 8 * f)
                for r in batch
                for f, ref in enumerate((t0_ref, t1_ref, u_ref, v_ref))
            }
            done = []
            for r in batch:
                low = rolled[r, 0]
                high = None
                if g > 0:
                    low = jnp.where(lane >= STRIP * g, low, sw_ref[r])
                    high = jnp.where(lane >= STRIP * g - 8, rolled[r, 0], se_ref[r])
                for f in range(1, 4):
                    start = STRIP * g + 8 * f
                    low = jnp.where(lane >= start, rolled[r, f], low)
                    if high is None:
                        high = rolled[r, f]
                    else:
                        high = jnp.where(lane >= start - 8, rolled[r, f], high)
                if g == GROUPS - 1:
                    high = jnp.where(lane >= 120, first_buf[r], high)
                done.append((r, low, high))
            for r, low, high in done:
                if g == 0:
                    first_buf[r] = rolled[r, 0]
                sw_ref[r] = low
                se_ref[r] = high
    for copy in tail:
        copy.wait()
    bottom = slab_of(b_buf).astype(jnp.float32)
    place = bottom
    for g in range(1, GROUPS):
        place = jnp.where(lane >= STRIP * g - 8, roll_lanes(bottom, STRIP * g), place)
    place = jnp.where(lane >= 120, bottom, place)
    bp_ref[...] = place

    def kappa(r):
        out = None
        for g in range(GROUPS):
            rolled = roll_lanes(slab_of(kh_buf, g * rows_e + r), STRIP * g + 23)
            out = rolled if g == 0 else jnp.where(lane >= STRIP * g + 8, rolled, out)
        return out

    khb_ref[0] = slab_of(kh_buf, 0)
    khb_ref[1] = slab_of(kh_buf, GROUPS * rows_e - 1)
    last = rows_e - 1
    kappa_last = kappa(last)
    lane_q = lane % STRIP
    low_last, high_last = sw_ref[last], se_ref[last]
    wires = []
    for r in range(last):
        k = kappa(r)
        low, high = sw_ref[r], se_ref[r]
        west = (low, roll_lanes(low, -2), roll_lanes(low, -4), roll_lanes(low, -6), k)
        east = (
            roll_lanes(high, 6), roll_lanes(high, 4), roll_lanes(high, 2), roll_lanes(high, -1),
            roll_lanes(k, 1),
        )
        west += (roll_lanes(low_last, 24 - 8 * r),)
        east += (roll_lanes(high_last, 5 if r == 3 else 30 - 8 * r),)
        if r == 3:
            west += (roll_lanes(kappa_last, 6),)
            east += (roll_lanes(kappa_last, 7),)
        else:
            west += (roll_lanes(place, 30 - 2 * r),)
            east += (roll_lanes(place, 36 - 2 * r),)
        starts = (6, 12, 18, 23, 24, 29 if r == 3 else 30)
        for ref, parts in ((ww_ref, west), (we_ref, east)):
            wire = parts[0]
            for start, part in zip(starts, parts[1:]):
                wire = jnp.where(lane_q >= start, part, wire)
            wires.append((ref, r, wire))
    for ref, r, wire in wires:
        ref[r] = wire


def advect_block(slabs, get_c, get_u, get_v, get_level, bx, by, buf, coef, put):
    regs = bx.shape[0] // 8
    for i, slab in enumerate(slabs):
        level = get_level(slab)
        um = jnp.where(level < bx, get_u(slab), 0.0)
        vm = jnp.where(level < by, get_v(slab), 0.0)
        uw = roll_lanes(um, 1)
        vs = shift_south(vm)
        coef[0, i] = (
            1.0
            - jnp.maximum(um, 0.0)
            + jnp.minimum(uw, 0.0)
            - jnp.maximum(vm, 0.0)
            + jnp.minimum(vs, 0.0)
        )
        coef[1, i] = -jnp.minimum(um, 0.0)
        coef[2, i] = jnp.maximum(uw, 0.0)
        coef[3, i] = -jnp.minimum(vm, 0.0)
        coef[4, i] = jnp.maximum(vs, 0.0)
        for tr in range(2):
            buf[0, 2 * i + tr] = get_c(tr, slab)
    for step in range(SUB):
        src, dst = step % 2, (step + 1) % 2
        for i, slab in enumerate(slabs):
            now = [
                [buf[src, 2 * i + tr, 8 * v : 8 * v + 8] for v in range(regs)] for tr in range(2)
            ]
            for v in range(regs):
                js = slice(8 * v, 8 * v + 8)
                a, b, c, d, e = (coef[n, i, js] for n in range(5))
                for tr in range(2):
                    here = now[tr][v]
                    north, south = neighbours(now[tr], v)
                    new = (
                        a * here
                        + b * roll_lanes(here, -1)
                        + c * roll_lanes(here, 1)
                        + d * north
                        + e * south
                    )
                    if step < SUB - 1:
                        buf[dst, 2 * i + tr, js] = new
                    else:
                        put(tr, slab, js, new)


def face_limits(bottom):
    lat = bottom.shape[0]
    rows = lax.broadcasted_iota(jnp.int32, bottom.shape, 0)
    north = jnp.where(rows == lat - 1, 0.0, shift_north(bottom))
    return jnp.minimum(bottom, roll_lanes(bottom, -1)), jnp.minimum(bottom, north)


def lat_limits(bottom):
    lat = bottom.shape[0]
    rows = lax.broadcasted_iota(jnp.int32, bottom.shape, 0)
    north = jnp.where(rows == lat - 1, 0.0, shift_north(bottom))
    south = jnp.where(rows == 0, 0.0, shift_south(bottom))
    return jnp.minimum(north, south)


def advect_kernel(start, t0_ref, t1_ref, u_ref, v_ref, b_ref, earlier_ref, out_ref, buf, coef):
    del earlier_ref
    count, lat = out_ref.shape[1], out_ref.shape[2]
    base = lax.axis_index("dep") * t0_ref.shape[0] + start
    bx, by = face_limits(slab_of(b_ref).astype(jnp.float32))

    def put(tr, slab, js, new):
        out_ref[tr, slab, js] = new

    advect_block(
        list(range(count)),
        lambda tr, s: slab_of((t0_ref, t1_ref)[tr], start + s),
        lambda s: slab_of(u_ref, start + s),
        lambda s: slab_of(v_ref, start + s),
        lambda s: (base + s).astype(jnp.float32),
        bx,
        by,
        buf,
        coef,
        put,
    )


def join(lane_q, own, east, west):
    halo = jnp.where(lane_q < 16, east, west)
    return jnp.where((lane_q >= 8) & (lane_q < 24), halo, own)


def west_patch(slab, g):
    return roll_lanes(slab, -(STRIP * g + 24))


def east_patch(slab, g):
    return roll_lanes(slab, 120 - STRIP * g)


def patched(main, slab, g, lane):
    return jnp.where(
        lane < 4, west_patch(slab, g), jnp.where(lane >= 124, east_patch(slab, g), main)
    )


def own_kernel(sw_ref, se_ref, bp_ref, earlier_ref, own_ref, ownb_ref):
    del earlier_ref
    rows_e, lat = sw_ref.shape[0], sw_ref.shape[1]
    lane_q = lane_ids(lat) % STRIP
    for r in range(rows_e):
        made = [
            jnp.where(
                lane_q < 16, roll_lanes(se_ref[r], 8 - 8 * f), roll_lanes(sw_ref[r], 24 - 8 * f)
            )
            for f in range(4)
        ]
        for f in range(4):
            own_ref[f, r] = made[f]
    place = bp_ref[...]
    ownb_ref[...] = jnp.where(lane_q < 16, roll_lanes(place, 8), roll_lanes(place, 24))


def pair_response(abc_ref, pair_ref, me):
    upper = lax.rem(me, 2) == 0
    low_pair = me < 2
    inv_t = 1.0 / (pair_ref[0] + jnp.where(upper, abc_ref[1], abc_ref[0]))
    c_pair = jnp.where(upper == low_pair, pair_ref[1], abc_ref[2])
    share = c_pair * inv_t
    return share, inv_t, jnp.where(upper, abc_ref[0], abc_ref[1]) - c_pair * share


def fold_strip(slab, place):
    lane = lane_ids(8)
    folded = jnp.zeros((8, 128), jnp.float32)
    for v in range(slab.shape[0] // 8):
        rolled = roll_lanes(slab[8 * v : 8 * v + 8], 16 * v - place)
        folded = jnp.where(lane >= 16 * v, rolled, folded)
    return folded


def unfold_strip(folded, place, regs):
    return jnp.concatenate([roll_lanes(folded, place - 16 * v) for v in range(regs)], axis=0)


def edge_kernel(
    own_ref, ownb_ref, re_ref, rw_ref, b_ref, north_half, south_half, kh_ref, abc_ref, pair_ref,
    ea_ref, ek_ref, eb_ref, bmx_ref, first_ref, second_ref, red_ref,
    buf, coef, fields, pay,
):
    levels, lat = kh_ref.shape[0], kh_ref.shape[1]
    rows_e = levels // GROUPS
    me = lax.axis_index("dep")
    base = me * levels
    parity = lax.rem(me, 2)
    up_ref, down_ref = pay.at[1 - parity], pay.at[parity]
    lane = lane_ids(lat)
    lane_q = lane % STRIP
    bottom = slab_of(b_ref).astype(jnp.float32)
    east = [roll_lanes(re_ref[r], 2 * r - 22) for r in range(3)]
    west = [roll_lanes(rw_ref[r], 2 * r - 12) for r in range(3)]
    eb = join(
        lane_q,
        ownb_ref[...],
        jnp.where(lane_q < 10, east[0], jnp.where(lane_q < 12, east[1], east[2])),
        jnp.where(lane_q < 20, west[0], jnp.where(lane_q < 22, west[1], west[2])),
    )
    eb_ref[...] = eb
    b_west = roll_lanes(jnp.where(lane == 127, west_patch(eb, 0), bottom), 1)
    b_east = roll_lanes(jnp.where(lane == 0, east_patch(eb, 0), bottom), -1)
    bmx_ref[...] = jnp.minimum(b_west, b_east)
    last = rows_e - 1
    for r in range(rows_e):
        at, shift_e, shift_w = (3, -21, -6) if r == last else (r, -15, 0)
        ek_ref[r] = jnp.where(
            lane_q < 16, roll_lanes(re_ref[at], shift_e), roll_lanes(rw_ref[at], shift_w)
        )
        made = []
        for f in range(4):
            at, start = (f, 24) if r == last else (r, 6 * f)
            made.append(
                join(
                    lane_q,
                    own_ref[f, r],
                    roll_lanes(re_ref[at], 8 - start),
                    roll_lanes(rw_ref[at], (19 if f == 3 else 18) - start),
                )
            )
        for f in range(4):
            fields[f, r] = made[f]
    bx, by = face_limits(eb)
    level0 = (base + (lane // STRIP) * rows_e).astype(jnp.float32)

    def put(tr, slab, js, new):
        ea_ref[tr, slab, js] = new

    advect_block(
        list(range(rows_e)),
        lambda tr, s: fields[tr, s],
        lambda s: fields[2, s],
        lambda s: fields[3, s],
        lambda s: level0 + float(s),
        bx,
        by,
        buf,
        coef,
        put,
    )
    top, half = rows_e - 1, levels // 2
    for tr in range(2):
        for n, (k, slab) in enumerate(((0, ea_ref[tr, 0]), (1, ea_ref[tr, 1]))):
            at = (2 * n + tr) * lat
            up_ref[at : at + lat] = patched(north_half[tr, k], slab, 0, lane)
        for n, (k, slab) in enumerate(
            ((half - 1, ea_ref[tr, top]), (half - 2, ea_ref[tr, top - 1]))
        ):
            at = (2 * n + tr) * lat
            down_ref[at : at + lat] = patched(south_half[tr, k], slab, 3, lane)
        at = 4 * lat + 8 * tr
        up_ref[at : at + 8] = fold_strip(ea_ref[tr, 0], 8)
        down_ref[at : at + 8] = fold_strip(ea_ref[tr, top], 3 * STRIP + 8)
    up_ref[4 * lat + 16 : 5 * lat + 16] = slab_of(kh_ref, 0)
    down_ref[4 * lat + 16 : 5 * lat + 16] = slab_of(kh_ref, levels - 1)
    first_ref[...] = pay[0, 0 : 4 * lat + 16]
    second_ref[0 : 5 * lat + 16] = pay[1]
    response = pair_response(abc_ref, pair_ref, me)
    for n in range(3):
        red_ref[n] = response[n]
    second_ref[5 * lat + 16 : 6 * lat + 16] = response[2]


def slopes(gx, gy, gz):
    rx, ry, rz = (-0.5 * THERMAL * g[0] + 0.5 * HALINE * g[1] for g in (gx, gy, gz))
    scale = rz / (1.0 + rx * rx + ry * ry + rz * rz)
    return rx * scale, ry * scale


def flux_xyz(gx, gy, gz, kappa, need_xy=True):
    sx, sy = slopes(gx, gy, gz)
    kx, ky = kappa * sx, kappa * sy
    kz = kx * sx + ky * sy
    fz = [kx * gx[n] + ky * gy[n] + kz * gz[n] for n in range(2)]
    if not need_xy:
        return None, None, fz
    fx = [kappa * gx[n] + kx * gz[n] for n in range(2)]
    fy = [kappa * gy[n] + ky * gz[n] for n in range(2)]
    return fx, fy, fz


def flux_x_edge(gx, gy, gz, kappa):
    sx, _ = slopes(gx, gy, gz)
    kx = kappa * sx
    return [kappa * gx[n] + kx * gz[n] for n in range(2)]


def diff(mask, high, low):
    return jnp.where(mask, high - low, 0.0)


def edge_flux_row(r, rows, ek, eb, ebx, eby, level0):
    level = level0 + r
    mx = level < ebx
    my = level < eby
    mz = (level + 1.0 < eb) & (level >= 1.0)
    kappa = jnp.where((level < eb) & (level >= 0.0), 0.25 * ek, 0.0)
    gx, gy, gz = [], [], []
    for tr in range(2):
        here = rows[tr, r + 1]
        gx.append(diff(mx, roll_lanes(here, -1), roll_lanes(here, 1)))
        gy.append(diff(my, shift_north(here), shift_south(here)))
        gz.append(diff(mz, rows[tr, r + 2], rows[tr, r]))
    return flux_x_edge(gx, gy, gz, kappa)


def edge_limits(eb):
    return (
        jnp.minimum(roll_lanes(eb, 1), roll_lanes(eb, -1)),
        lat_limits(eb),
    )


def zonal_change(fx, west, east, lane):
    return roll_lanes(jnp.where(lane == 0, east, fx), -1) - roll_lanes(
        jnp.where(lane == 127, west, fx), 1
    )


def divergence(fx, fy, slab, g, lane):
    return zonal_change(fx, west_patch(slab, g), east_patch(slab, g), lane) + (
        shift_north(fy) - shift_south(fy)
    )


def patch_kernel(
    north_half, south_half, ea_ref, ek_ref, eb_ref,
    full_ref, gx_ref, efx_ref,
    rows,
):
    levels, lat = full_ref.shape[1], full_ref.shape[2]
    rows_e = levels // GROUPS
    base = lax.axis_index("dep") * levels
    lane = lane_ids(lat)
    eb = eb_ref[...]
    ebx, eby = edge_limits(eb)
    level0 = (base + (lane // STRIP) * rows_e).astype(jnp.float32)
    for tr in range(2):
        for r in range(rows_e):
            rows[tr, r + 1] = ea_ref[tr, r]
        rows[tr, 0] = roll_lanes(ea_ref[tr, rows_e - 1], STRIP)
        rows[tr, rows_e + 1] = roll_lanes(ea_ref[tr, 0], -STRIP)
    found = [
        edge_flux_row(r, rows, ek_ref[r], eb, ebx, eby, level0) for r in range(rows_e)
    ]
    for r in range(rows_e):
        for tr in range(2):
            efx_ref[tr, r] = found[r][tr]

    lane = lane_ids(ROWS)
    units = [(g, slice(j, j + ROWS)) for g in range(GROUPS) for j in range(0, lat, ROWS)]

    def patch(r, _):
        def fetch(unit):
            g, js = unit
            strips = [ea_ref[tr, r, js] for tr in range(2)]
            half = (north_half, south_half)[2 * g // GROUPS]
            mains = [half[tr, g % (GROUPS // 2) * rows_e + r, js] for tr in range(2)]
            return [(west_patch(x, g), east_patch(x, g), y) for x, y in zip(strips, mains)]

        def put(unit, mains, rolled):
            g, js = unit
            for tr in range(2):
                full_ref[tr, g * rows_e + r, js] = mains[tr]
                gx_ref[tr, g * rows_e + r, js] = rolled[tr][0] - rolled[tr][1]

        waiting = None
        fetched = fetch(units[0])
        for n, unit in enumerate(units):
            now = fetched
            fetched = fetch(units[n + 1]) if n + 1 < len(units) else None
            mains, rolled = [], []
            for west, east, main in now:
                main = jnp.where(lane < 4, west, jnp.where(lane >= 124, east, main))
                mains.append(main)
                rolled.append(
                    (
                        roll_lanes(jnp.where(lane == 0, east, main), -1),
                        roll_lanes(jnp.where(lane == 127, west, main), 1),
                    )
                )
            if waiting is not None:
                put(*waiting)
            waiting = (unit, mains, rolled)
        put(*waiting)
        return 0

    lax.fori_loop(0, rows_e, patch, 0)


def flux_kernel(
    full_ref, gx_ref, efx_ref, bmx_ref, b_ref, kh_ref,
    q_ref, fz_ref,
    limits,
):
    levels, lat = full_ref.shape[1], full_ref.shape[2]
    rows_e = levels // GROUPS
    base = lax.axis_index("dep") * levels
    lane = lane_ids(lat)
    bottom = slab_of(b_ref).astype(jnp.float32)
    limits[0] = bmx_ref[...]
    limits[1] = lat_limits(bottom)
    limits[2] = bottom

    def north_rows(tr, k, j):
        if j + 8 + ROWS <= lat:
            return full_ref[tr, k, j + 8 : j + 8 + ROWS]
        return jnp.concatenate(
            [full_ref[tr, k, j + 8 : lat], pltpu.roll(full_ref[tr, k, 0:8], 7, 0)], axis=0
        )

    def south_rows(tr, k, j):
        if j >= 8:
            return full_ref[tr, k, j - 8 : j - 8 + ROWS]
        return jnp.concatenate(
            [pltpu.roll(full_ref[tr, k, lat - 8 : lat], 1, 0), full_ref[tr, k, 0 : ROWS - 8]],
            axis=0,
        )

    def fluxes(r, _):
        for g in range(GROUPS):
            k = g * rows_e + r
            above, below = jnp.maximum(k - 1, 0), jnp.minimum(k + 1, levels - 1)
            level = (base + k).astype(jnp.float32)
            level_z = jnp.where(level >= 1.0, level + 1.0, HUGE)
            sides = [
                (west_patch(efx_ref[tr, r], g), east_patch(efx_ref[tr, r], g)) for tr in range(2)
            ]
            fxs, fys, fzs = [[], []], [[], []], [[], []]
            for j in range(0, lat, ROWS):
                js = slice(j, j + ROWS)
                mx = level < limits[0, js]
                my = level < limits[1, js]
                mz = level_z < limits[2, js]
                kh = jnp.concatenate(
                    [rows_of(kh_ref, v, k) for v in range(j // 8, (j + ROWS) // 8)], axis=0
                )
                kappa = jnp.where(level < limits[2, js], 0.25 * kh, 0.0)
                gx, gy, gz = [], [], []
                for tr in range(2):
                    gx.append(jnp.where(mx, gx_ref[tr, k, js], 0.0))
                    gy.append(diff(my, north_rows(tr, k, j), south_rows(tr, k, j)))
                    gz.append(diff(mz, full_ref[tr, below, js], full_ref[tr, above, js]))
                fx, fy, fz = flux_xyz(gx, gy, gz, kappa)
                for tr in range(2):
                    fxs[tr].append(fx[tr])
                    fys[tr].append(fy[tr])
                    fzs[tr].append(fz[tr])
            wet = level < limits[2]
            new = []
            for tr in range(2):
                fy = jnp.concatenate(fys[tr], axis=0)
                change = zonal_change(jnp.concatenate(fxs[tr], axis=0), *sides[tr], lane)
                change = change + (shift_north(fy) - shift_south(fy))
                new.append(full_ref[tr, k] + jnp.where(wet, change, 0.0))
            for tr in range(2):
                q_ref[tr, k] = new[tr]
                fz_ref[tr, k] = jnp.concatenate(fzs[tr], axis=0)
        return 0

    lax.fori_loop(0, rows_e, fluxes, 0)


def factor_kernel(
    kv_ref, b_ref, khb_ref, inv_ref, ei_ref, ratio_ref, a_ref, bb_ref, abc_ref, msg_ref
):
    levels, lat = kv_ref.shape[0], kv_ref.shape[1]
    base = lax.axis_index("dep") * levels
    bottom = slab_of(b_ref).astype(jnp.float32)

    def coupling(k):
        level = (base + k).astype(jnp.float32)
        level = jnp.where(level >= 1.0, level, HUGE)
        return jnp.where(level < bottom, slab_of(kv_ref, k), 0.0)

    top = coupling(0)
    e = jnp.zeros((lat, 128), jnp.float32)
    q = e
    za = jnp.ones((lat, 128), jnp.float32)
    for k in range(levels):
        low = coupling(k + 1) if k + 1 < levels else jnp.zeros((lat, 128), jnp.float32)
        eq = 1.0 + e * q
        inv = 1.0 / (eq + low)
        inv_ref[k] = inv
        ei = e * inv
        ei_ref[k] = ei
        ratio_ref[k] = low * inv
        za = inv if k == 0 else za * ei
        a_ref[k] = za
        q = eq * inv
        e = low
    bb_ref[levels - 1] = inv
    b = inv
    a = za
    for k in range(levels - 2, -1, -1):
        ratio = ratio_ref[k]
        b = ratio * b
        a = a_ref[k] + ratio * a
        bb_ref[k] = b
        a_ref[k] = a
    a = a + jnp.where(top > 0.0, 1.0 / jnp.maximum(top, 1e-30), HUGE)
    abc_ref[0] = a
    abc_ref[1] = inv
    abc_ref[2] = b
    upper = lax.rem(lax.axis_index("dep"), 2) == 0
    msg_ref[0] = jnp.where(upper, inv, a)
    msg_ref[1] = b
    msg_ref[2] = jnp.where(upper, khb_ref[1], khb_ref[0])


def solve_kernel(
    full_ref, q_ref, fz_ref, ea_ref, ek_ref, eb_ref, bmx_ref, b_ref, kh_ref,
    first_ref, second_ref, inv_ref, ei_ref, ratio_ref, red_ref, pair_ref,
    y_ref, m3_ref, m2_ref, m1_ref, both_ref, own_ref,
    pad, epad, fze, halo,
):
    levels, lat = q_ref.shape[1], q_ref.shape[2]
    rows_e = levels // GROUPS
    last = levels - 1
    top = rows_e - 1
    me = lax.axis_index("dep")
    base = me * levels
    parity = lax.rem(me, 2)
    outer = (me == 0) | (me == 3)
    upper = parity == 0
    sign = jnp.where(me < 2, 1.0, -1.0)
    lane = lane_ids(lat)
    halo[0, 0 : 4 * lat + 16] = first_ref[...]
    halo[0, 4 * lat + 16 : 5 * lat + 16] = pair_ref[2]
    halo[1] = second_ref[0 : 5 * lat + 16]
    above_ref, below_ref = halo.at[1 - parity], halo.at[parity]

    share = red_ref[0]
    both = red_ref[2] + second_ref[5 * lat + 16 : 6 * lat + 16]
    cross = share / both
    inside = red_ref[1] + share * cross
    for n, value in enumerate((share, red_ref[1], both)):
        own_ref[n] = value
    both_ref[...] = both

    eb = eb_ref[...]
    ebx, eby = edge_limits(eb)
    level0 = (base + (lane // STRIP) * rows_e).astype(jnp.float32)
    for tr in range(2):
        pad[tr, 0] = above_ref[(2 + tr) * lat : (3 + tr) * lat]
        pad[tr, 1] = above_ref[tr * lat : (1 + tr) * lat]
        for n, k in enumerate((0, 1, 2, last - 2, last - 1, last)):
            pad[tr, n + 2] = full_ref[tr, k]
        pad[tr, 8] = below_ref[tr * lat : (1 + tr) * lat]
        pad[tr, 9] = below_ref[(2 + tr) * lat : (3 + tr) * lat]
        for r in range(rows_e):
            epad[tr, r + 1] = ea_ref[tr, r]
        at = 4 * lat + 8 * tr
        corner_up = unfold_strip(above_ref[at : at + 8], 3 * STRIP + 8, lat // 8)
        corner_dn = unfold_strip(below_ref[at : at + 8], 8, lat // 8)
        epad[tr, 0] = roll_lanes(
            jnp.where(lane >= 3 * STRIP, corner_up, ea_ref[tr, top]), STRIP
        )
        epad[tr, rows_e + 1] = roll_lanes(
            jnp.where(lane < STRIP, corner_dn, ea_ref[tr, 0]), -STRIP
        )
    efx = {
        r + 1: edge_flux_row(r, epad, ek_ref[r], eb, ebx, eby, level0) for r in (0, top)
    }

    bottom = slab_of(b_ref).astype(jnp.float32)
    bmy = lat_limits(bottom)
    bmx = bmx_ref[...]
    ends = (
        (1, -1, 0, 0, above_ref[4 * lat + 16 : 5 * lat + 16], True),
        (2, 0, 1, 0, slab_of(kh_ref, 0), False),
        (7, last, top + 1, 3, slab_of(kh_ref, last), False),
        (8, last + 1, top + 2, 3, below_ref[4 * lat + 16 : 5 * lat + 16], True),
    )
    spread = {}
    for m, (n, k, er, g, kappa_slab, only_z) in enumerate(ends):
        level = (base + k).astype(jnp.float32)
        level_z = jnp.where(level >= 1.0, level + 1.0, HUGE)
        level_h = jnp.where(level >= 0.0, level, HUGE)
        mx = level_h < bmx
        my = level_h < bmy
        mz = level_z < bottom
        kappa = jnp.where(level_h < bottom, 0.25 * kappa_slab, 0.0)
        gx, gy, gz = [], [], []
        for tr in range(2):
            slab, main = epad[tr, er], pad[tr, n]
            change = zonal_change(main, west_patch(slab, g), east_patch(slab, g), lane)
            gx.append(jnp.where(mx, change, 0.0))
            gy.append(diff(my, shift_north(main), shift_south(main)))
            gz.append(diff(mz, pad[tr, n + 1], pad[tr, n - 1]))
        fx, fy, fz = flux_xyz(gx, gy, gz, kappa, not only_z)
        for tr in range(2):
            fze[tr, m] = fz[tr]
            if not only_z:
                spread[k, tr] = divergence(fx[tr], fy[tr], efx[er][tr], g, lane)

    def vertical_flux(tr, k):
        place = {-1: 0, 0: 1, last: 2, last + 1: 3}.get(k)
        return fz_ref[tr, k] if place is None else fze[tr, place]

    z = [None, None]
    for k in range(levels):
        level = (base + k).astype(jnp.float32)
        wet = level < bottom
        for tr in range(2):
            change = vertical_flux(tr, k + 1) - vertical_flux(tr, k - 1)
            if k == 0 or k == last:
                change = change + spread[k, tr]
                start = pad[tr, 2 if k == 0 else 7]
            else:
                start = q_ref[tr, k]
            rhs = start + jnp.where(wet, change, 0.0)
            new = rhs * inv_ref[k]
            z[tr] = new if k == 0 else new + ei_ref[k] * z[tr]
        for tr in range(2):
            y_ref[tr, k] = z[tr]
    low = list(z)
    for k in range(last - 1, -1, -1):
        ratio = ratio_ref[k]
        z = [y_ref[tr, k] + ratio * z[tr] for tr in range(2)]
        for tr in range(2):
            y_ref[tr, k] = z[tr]
    for tr in range(2):
        near = jnp.where(upper, low[tr], z[tr])
        far = jnp.where(upper, z[tr], low[tr])
        m1_ref[tr] = jnp.where(outer, near, sign * (inside * near - cross * far))
        value = jnp.where(outer, share * near, far - share * near)
        m2_ref[tr] = value
        m3_ref[tr] = value


def finish_kernel(
    y_ref, a_ref, bb_ref, own_ref, r3_ref, r2_ref, r1_ref, both_ref, out_hbm, out, sems
):
    levels = y_ref.shape[1]
    me = lax.axis_index("dep")
    upper = lax.rem(me, 2) == 0
    outer = (me == 0) | (me == 3)
    sign = jnp.where(me < 2, 1.0, -1.0)
    share, inv_t = own_ref[0], own_ref[1]
    inv_e = 1.0 / jnp.where(outer, both_ref[...], own_ref[2])
    cross = share * inv_e
    inside = inv_t + share * cross
    tops, lows = [], []
    for tr in range(2):
        y_top, y_low = y_ref[tr, 0], y_ref[tr, levels - 1]
        near = jnp.where(upper, y_low, y_top)
        far = jnp.where(upper, y_top, y_low)
        mate, across = r1_ref[tr], r2_ref[tr] + r3_ref[tr]
        pair_flux = jnp.where(
            outer,
            mate + sign * (cross * across - inside * near),
            sign * (inside * (near - mate) + cross * (across - far)),
        )
        middle = sign * (inv_e * (across - far + share * near) - cross * mate)
        middle = jnp.where(outer, 0.0, middle)
        tops.append(jnp.where(upper, middle, pair_flux))
        lows.append(jnp.where(upper, pair_flux, middle))
    step, regs = levels // GROUPS, y_ref.shape[2] // 8
    copies = []
    for part in range(GROUPS):
        for k in range(part * step, (part + 1) * step):
            a, b = a_ref[k], bb_ref[k]
            new = [y_ref[tr, k] - tops[tr] * a + lows[tr] * b for tr in range(2)]
            for tr in range(2):
                for v in range(regs):
                    out[tr, k, pl.ds(v, 8, regs), :] = new[tr][8 * v : 8 * v + 8]
        for tr in range(2):
            span = (tr, pl.ds(part * step, step))
            copies.append(
                pltpu.make_async_copy(out.at[span], out_hbm.at[span], sems.at[tr, part])
            )
            copies[-1].start()
    for copy in copies:
        copy.wait()


def per_device(tracers, u_east, v_north, kappa_h, kappa_v, bottom):
    _, levels, lat, lon = tracers.shape
    rows_e = levels // GROUPS
    lon_n, dep_n = lax.axis_size("lon"), lax.axis_size("dep")
    east = [(i, (i + 1) % lon_n) for i in range(lon_n)]
    west = [(t, s) for s, t in east]
    slab = lat * lon * 4
    slabs = lambda *lead: f32(*lead, lat, lon)
    work = lambda *lead: pltpu.VMEM(lead + (lat, lon), jnp.float32)

    with jax.named_scope("pack"):
        sw, se, bp, ww, we, t0, t1, u, v, khb = call(
            pack_kernel,
            (slabs(rows_e),) * 2 + (slabs(),) + (slabs(rows_e - 1),) * 2 + (slabs(levels),) * 4
            + (slabs(2),),
            [
                work(levels), pltpu.VMEM((lat, lon), jnp.int32), work(rows_e),
                pltpu.SemaphoreType.DMA((GROUPS, 4)), pltpu.SemaphoreType.DMA((2,)),
            ],
            (tracers, u_east, v_north, kappa_h, bottom), 10**6, 6 * levels * slab, 50.5,
            in_specs=[HBM] * 5,
        )
    with jax.named_scope("lon_halo"):
        r_east = lax.ppermute(ww, "lon", west)
        r_west = lax.ppermute(we, "lon", east)
    with jax.named_scope("factor"):
        inv, ei, ratio, a_end, b_end, abc, msg = call(
            factor_kernel, (slabs(levels),) * 5 + (slabs(3),) * 2, [],
            (kappa_v, bottom, khb), 10**7, 6 * levels * slab, 16,
        )
    swap = [(i, i ^ 1) for i in range(dep_n)]
    with jax.named_scope("pair_coefficients"):
        pair = lax.ppermute(msg, "dep", swap)
    half = levels // 2

    def advect_half(start, earlier):
        return call(
            functools.partial(advect_kernel, start), slabs(2, half),
            [work(2, 2 * half), work(5, half)],
            (t0, t1, u, v, bottom, earlier), 10**7, 4 * levels * slab, 16,
        )

    with jax.named_scope("advect_north"):
        north_half = advect_half(0, abc)
    with jax.named_scope("advect_south"):
        south_half = advect_half(half, abc)
    with jax.named_scope("own_strips"):
        own_strips, own_bottom = call(
            own_kernel, (slabs(4, rows_e), slabs()), [],
            (sw, se, bp, abc), 10**6, 8 * rows_e * slab, 16,
        )
    rows_pay = 5 * lat + 16
    with jax.named_scope("advect_edge"):
        ea, ek, eb, bmx, first, second, red = call(
            edge_kernel,
            (
                slabs(2, rows_e), slabs(rows_e), slabs(), slabs(),
                f32(rows_pay - lat, lon), f32(rows_pay + lat, lon), slabs(3),
            ),
            [
                work(2, 2 * rows_e), work(5, rows_e), work(4, rows_e),
                pltpu.VMEM((2, rows_pay, lon), jnp.float32),
            ],
            (own_strips, own_bottom, r_east, r_west, bottom, north_half, south_half, kappa_h, abc, pair),
            10**6, 3 * levels * slab, 16,
        )
    other = []
    for i in range(lon_n * dep_n):
        row, place = divmod(i, dep_n)
        if place in (0, dep_n - 1):
            other.append((i, (row ^ 1) * dep_n + place))
        else:
            other.append((i, i + 1 if place % 2 else i - 1))
    with jax.named_scope("dep_halo"):
        first = lax.ppermute(first, "dep", swap)
        second = lax.ppermute(second, ("lon", "dep"), other)
    with jax.named_scope("patch"):
        full, gx, efx = call(
            patch_kernel, (slabs(2, levels), slabs(2, levels), slabs(2, rows_e)),
            [work(2, rows_e + 2)],
            (north_half, south_half, ea, ek, eb), 10**7, 8 * levels * slab, 16,
        )
    with jax.named_scope("fluxes"):
        q_part, fz = call(
            flux_kernel, (slabs(2, levels), slabs(2, levels)), [work(3)],
            (full, gx, efx, bmx, bottom, kappa_h), 10**7, 10 * levels * slab, 16,
        )
    with jax.named_scope("solve"):
        y, m3, m2, m1, both, own = call(
            solve_kernel, (slabs(2, levels), slabs(2), slabs(2), slabs(2), slabs(), slabs(3)),
            [
                work(2, 10), work(2, rows_e + 2), work(2, 4),
                pltpu.VMEM((2, rows_pay, lon), jnp.float32),
            ],
            (
                full, q_part, fz, ea, ek, eb, bmx, bottom, kappa_h, first, second,
                inv, ei, ratio, red, pair,
            ),
            10**7, 12 * levels * slab, 24,
        )
    with jax.named_scope("interfaces"):
        m3 = lax.ppermute(m3, "dep", [(i, i ^ 3) for i in range(dep_n)])
        m2 = lax.ppermute(m2, "dep", [(i, i ^ 2) for i in range(dep_n)])
        m1 = lax.ppermute(m1, "dep", swap)
        both = lax.ppermute(both, "dep", swap)
    with jax.named_scope("finish"):
        return call(
            finish_kernel, slabs(2, levels),
            [work(2, levels), pltpu.SemaphoreType.DMA((2, GROUPS))],
            (y, a_end, b_end, own, m3, m2, m1, both), 10**6, 6 * levels * slab, 16,
            out_specs=HBM,
        )


def solution(mesh):
    in_specs = (
        P(None, "dep", None, "lon"),
        P("dep", None, "lon"),
        P("dep", None, "lon"),
        P("dep", None, "lon"),
        P("dep", None, "lon"),
        P(None, "lon"),
    )
    out_specs = P(None, "dep", None, "lon")
    return jax.shard_map(
        per_device, mesh=mesh, in_specs=in_specs, out_specs=out_specs, check_vma=False
    )
```

```python
import functools

import jax
import jax.numpy as jnp
from jax import lax
from jax.experimental import pallas as pl
from jax.experimental.pallas import tpu as pltpu
from jax.sharding import PartitionSpec as P

SUB = 4
THERMAL = 0.2
HALINE = 0.8
GROUPS = 4
ROWS = 32
STRIP = 32
HUGE = 1e30
MIB = 1024 * 1024

VMEM = pl.BlockSpec(memory_space=pltpu.VMEM)
HBM = pl.BlockSpec(memory_space=pltpu.HBM)


def lane_ids(rows):
    return lax.broadcasted_iota(jnp.int32, (rows, 128), 1)


def roll_lanes(x, amount):
    amount = amount % 128
    return x if amount == 0 else pltpu.roll(x, amount, 1)


def shift_north(x):
    return jnp.concatenate([x[8:], pltpu.roll(x[:8], 7, 0)], axis=0)


def shift_south(x):
    return jnp.concatenate([pltpu.roll(x[-8:], 1, 0), x[:-8]], axis=0)


def rows_of(ref, v, *lead):
    return ref[(*lead, pl.ds(v, 8, ref.shape[-2] // 8), slice(None))]


def neighbours(regs, v):
    north = regs[v + 1] if v + 1 < len(regs) else pltpu.roll(regs[0], 7, 0)
    south = regs[v - 1] if v > 0 else pltpu.roll(regs[-1], 1, 0)
    return north, south


def slab_of(ref, *lead):
    return jnp.concatenate([rows_of(ref, v, *lead) for v in range(ref.shape[-2] // 8)], axis=0)


def call(body, out_shape, scratch, args, flops, in_bytes, limit, in_specs=None, out_specs=None):
    return pl.pallas_call(
        body,
        out_shape=out_shape,
        in_specs=in_specs or [VMEM] * len(args),
        out_specs=out_specs or jax.tree.map(lambda _: VMEM, out_shape),
        scratch_shapes=scratch,
        compiler_params=pltpu.CompilerParams(vmem_limit_bytes=int(limit * MIB)),
        cost_estimate=pl.CostEstimate(flops=flops, bytes_accessed=in_bytes, transcendentals=0),
    )(*args)


def f32(*shape):
    return jax.ShapeDtypeStruct(shape, jnp.float32)


def pack_kernel(
    t_hbm, u_hbm, v_hbm, kh_hbm, b_hbm,
    sw_ref, se_ref, bp_ref, ww_ref, we_ref, t0_ref, t1_ref, u_ref, v_ref, khb_ref,
    kh_buf, b_buf, first_buf, kappa_buf, sems, more_sems,
):
    rows_e = u_ref.shape[0] // GROUPS
    lat = u_ref.shape[1]
    lane = lane_ids(lat)
    fields = ((t_hbm.at[0], t0_ref), (t_hbm.at[1], t1_ref), (u_hbm, u_ref), (v_hbm, v_ref))
    groups = [
        [
            pltpu.make_async_copy(
                src.at[pl.ds(g * rows_e, rows_e)], dst.at[pl.ds(g * rows_e, rows_e)], sems.at[g, n]
            )
            for n, (src, dst) in enumerate(fields)
        ]
        for g in range(GROUPS)
    ]
    tail = [
        pltpu.make_async_copy(b_hbm, b_buf, more_sems.at[0]),
        pltpu.make_async_copy(kh_hbm, kh_buf, more_sems.at[1]),
    ]
    half = GROUPS // 2
    for copy in sum(groups[:half], []) + tail + sum(groups[half:], []):
        copy.start()
    def arrange():
        for copy in tail:
            copy.wait()
        bottom = slab_of(b_buf).astype(jnp.float32)
        place = bottom
        for g in range(1, GROUPS):
            place = jnp.where(lane >= STRIP * g - 8, roll_lanes(bottom, STRIP * g), place)
        place = jnp.where(lane >= 120, bottom, place)
        bp_ref[...] = place

        def kappa(r):
            out = None
            for g in range(GROUPS):
                rolled = roll_lanes(slab_of(kh_buf, g * rows_e + r), STRIP * g + 23)
                out = rolled if g == 0 else jnp.where(lane >= STRIP * g + 8, rolled, out)
            return out

        arranged = [kappa(r) for r in range(rows_e)]
        for r in range(rows_e):
            kappa_buf[r] = arranged[r]
        khb_ref[0] = slab_of(kh_buf, 0)
        khb_ref[1] = slab_of(kh_buf, GROUPS * rows_e - 1)

    for g in range(GROUPS):
        if g == GROUPS // 2:
            arrange()
        for copy in groups[g]:
            copy.wait()
        for batch in (range(0, rows_e // 2), range(rows_e // 2, rows_e)):
            rolled = {
                (r, f): roll_lanes(slab_of(ref, g * rows_e + r), STRIP * g + 8 * f)
                for r in batch
                for f, ref in enumerate((t0_ref, t1_ref, u_ref, v_ref))
            }
            done = []
            for r in batch:
                low = rolled[r, 0]
                high = None
                if g > 0:
                    low = jnp.where(lane >= STRIP * g, low, sw_ref[r])
                    high = jnp.where(lane >= STRIP * g - 8, rolled[r, 0], se_ref[r])
                for f in range(1, 4):
                    start = STRIP * g + 8 * f
                    low = jnp.where(lane >= start, rolled[r, f], low)
                    if high is None:
                        high = rolled[r, f]
                    else:
                        high = jnp.where(lane >= start - 8, rolled[r, f], high)
                if g == GROUPS - 1:
                    high = jnp.where(lane >= 120, first_buf[r], high)
                done.append((r, low, high))
            for r, low, high in done:
                if g == 0:
                    first_buf[r] = rolled[r, 0]
                sw_ref[r] = low
                se_ref[r] = high
    last = rows_e - 1
    kappa_last, place = kappa_buf[last], bp_ref[...]
    lane_q = lane % STRIP
    low_last, high_last = sw_ref[last], se_ref[last]
    wires = []
    for r in range(last):
        k = kappa_buf[r]
        low, high = sw_ref[r], se_ref[r]
        west = (low, roll_lanes(low, -2), roll_lanes(low, -4), roll_lanes(low, -6), k)
        east = (
            roll_lanes(high, 6), roll_lanes(high, 4), roll_lanes(high, 2), roll_lanes(high, -1),
            roll_lanes(k, 1),
        )
        west += (roll_lanes(low_last, 24 - 8 * r),)
        east += (roll_lanes(high_last, 5 if r == 3 else 30 - 8 * r),)
        if r == 3:
            west += (roll_lanes(kappa_last, 6),)
            east += (roll_lanes(kappa_last, 7),)
        else:
            west += (roll_lanes(place, 30 - 2 * r),)
            east += (roll_lanes(place, 36 - 2 * r),)
        starts = (6, 12, 18, 23, 24, 29 if r == 3 else 30)
        for ref, parts in ((ww_ref, west), (we_ref, east)):
            wire = parts[0]
            for start, part in zip(starts, parts[1:]):
                wire = jnp.where(lane_q >= start, part, wire)
            wires.append((ref, r, wire))
    for ref, r, wire in wires:
        ref[r] = wire


def advect_block(slabs, get_c, get_u, get_v, get_level, bx, by, buf, coef, put):
    regs = bx.shape[0] // 8
    for i, slab in enumerate(slabs):
        level = get_level(slab)
        um = jnp.where(level < bx, get_u(slab), 0.0)
        vm = jnp.where(level < by, get_v(slab), 0.0)
        uw = roll_lanes(um, 1)
        vs = shift_south(vm)
        coef[0, i] = (
            1.0
            - jnp.maximum(um, 0.0)
            + jnp.minimum(uw, 0.0)
            - jnp.maximum(vm, 0.0)
            + jnp.minimum(vs, 0.0)
        )
        coef[1, i] = -jnp.minimum(um, 0.0)
        coef[2, i] = jnp.maximum(uw, 0.0)
        coef[3, i] = -jnp.minimum(vm, 0.0)
        coef[4, i] = jnp.maximum(vs, 0.0)
        for tr in range(2):
            buf[0, 2 * i + tr] = get_c(tr, slab)
    for step in range(SUB):
        src, dst = step % 2, (step + 1) % 2
        for i, slab in enumerate(slabs):
            now = [
                [buf[src, 2 * i + tr, 8 * v : 8 * v + 8] for v in range(regs)] for tr in range(2)
            ]
            for v in range(regs):
                js = slice(8 * v, 8 * v + 8)
                a, b, c, d, e = (coef[n, i, js] for n in range(5))
                for tr in range(2):
                    here = now[tr][v]
                    north, south = neighbours(now[tr], v)
                    new = (
                        a * here
                        + b * roll_lanes(here, -1)
                        + c * roll_lanes(here, 1)
                        + d * north
                        + e * south
                    )
                    if step < SUB - 1:
                        buf[dst, 2 * i + tr, js] = new
                    else:
                        put(tr, slab, js, new)


def face_limits(bottom):
    lat = bottom.shape[0]
    rows = lax.broadcasted_iota(jnp.int32, bottom.shape, 0)
    north = jnp.where(rows == lat - 1, 0.0, shift_north(bottom))
    return jnp.minimum(bottom, roll_lanes(bottom, -1)), jnp.minimum(bottom, north)


def lat_limits(bottom):
    lat = bottom.shape[0]
    rows = lax.broadcasted_iota(jnp.int32, bottom.shape, 0)
    north = jnp.where(rows == lat - 1, 0.0, shift_north(bottom))
    south = jnp.where(rows == 0, 0.0, shift_south(bottom))
    return jnp.minimum(north, south)


def advect_kernel(start, t0_ref, t1_ref, u_ref, v_ref, b_ref, earlier_ref, out_ref, buf, coef):
    del earlier_ref
    count, lat = out_ref.shape[1], out_ref.shape[2]
    base = lax.axis_index("dep") * t0_ref.shape[0] + start
    bx, by = face_limits(slab_of(b_ref).astype(jnp.float32))

    def put(tr, slab, js, new):
        out_ref[tr, slab, js] = new

    advect_block(
        list(range(count)),
        lambda tr, s: slab_of((t0_ref, t1_ref)[tr], start + s),
        lambda s: slab_of(u_ref, start + s),
        lambda s: slab_of(v_ref, start + s),
        lambda s: (base + s).astype(jnp.float32),
        bx,
        by,
        buf,
        coef,
        put,
    )


def join(lane_q, own, east, west):
    halo = jnp.where(lane_q < 16, east, west)
    return jnp.where((lane_q >= 8) & (lane_q < 24), halo, own)


def west_patch(slab, g):
    return roll_lanes(slab, -(STRIP * g + 24))


def east_patch(slab, g):
    return roll_lanes(slab, 120 - STRIP * g)


def patched(main, slab, g, lane):
    return jnp.where(
        lane < 4, west_patch(slab, g), jnp.where(lane >= 124, east_patch(slab, g), main)
    )


def own_kernel(sw_ref, se_ref, bp_ref, earlier_ref, own_ref, ownb_ref):
    del earlier_ref
    rows_e, lat = sw_ref.shape[0], sw_ref.shape[1]
    lane_q = lane_ids(lat) % STRIP
    for r in range(rows_e):
        made = [
            jnp.where(
                lane_q < 16, roll_lanes(se_ref[r], 8 - 8 * f), roll_lanes(sw_ref[r], 24 - 8 * f)
            )
            for f in range(4)
        ]
        for f in range(4):
            own_ref[f, r] = made[f]
    place = bp_ref[...]
    ownb_ref[...] = jnp.where(lane_q < 16, roll_lanes(place, 8), roll_lanes(place, 24))


def pair_response(abc_ref, pair_ref, me):
    upper = lax.rem(me, 2) == 0
    low_pair = me < 2
    inv_t = 1.0 / (pair_ref[0] + jnp.where(upper, abc_ref[1], abc_ref[0]))
    c_pair = jnp.where(upper == low_pair, pair_ref[1], abc_ref[2])
    share = c_pair * inv_t
    return share, inv_t, jnp.where(upper, abc_ref[0], abc_ref[1]) - c_pair * share


def fold_strip(slab, place):
    lane = lane_ids(8)
    folded = jnp.zeros((8, 128), jnp.float32)
    for v in range(slab.shape[0] // 8):
        rolled = roll_lanes(slab[8 * v : 8 * v + 8], 16 * v - place)
        folded = jnp.where(lane >= 16 * v, rolled, folded)
    return folded


def unfold_strip(folded, place, regs):
    return jnp.concatenate([roll_lanes(folded, place - 16 * v) for v in range(regs)], axis=0)


def edge_kernel(
    own_ref, ownb_ref, re_ref, rw_ref, b_ref, north_half, south_half, kh_ref, abc_ref, pair_ref,
    ea_ref, ek_ref, eb_ref, bmx_ref, first_ref, second_ref, red_ref,
    buf, coef, fields, pay,
):
    levels, lat = kh_ref.shape[0], kh_ref.shape[1]
    rows_e = levels // GROUPS
    me = lax.axis_index("dep")
    base = me * levels
    parity = lax.rem(me, 2)
    up_ref, down_ref = pay.at[1 - parity], pay.at[parity]
    lane = lane_ids(lat)
    lane_q = lane % STRIP
    bottom = slab_of(b_ref).astype(jnp.float32)
    east = [roll_lanes(re_ref[r], 2 * r - 22) for r in range(3)]
    west = [roll_lanes(rw_ref[r], 2 * r - 12) for r in range(3)]
    eb = join(
        lane_q,
        ownb_ref[...],
        jnp.where(lane_q < 10, east[0], jnp.where(lane_q < 12, east[1], east[2])),
        jnp.where(lane_q < 20, west[0], jnp.where(lane_q < 22, west[1], west[2])),
    )
    eb_ref[...] = eb
    b_west = roll_lanes(jnp.where(lane == 127, west_patch(eb, 0), bottom), 1)
    b_east = roll_lanes(jnp.where(lane == 0, east_patch(eb, 0), bottom), -1)
    bmx_ref[...] = jnp.minimum(b_west, b_east)
    last = rows_e - 1
    for r in range(rows_e):
        at, shift_e, shift_w = (3, -21, -6) if r == last else (r, -15, 0)
        ek_ref[r] = jnp.where(
            lane_q < 16, roll_lanes(re_ref[at], shift_e), roll_lanes(rw_ref[at], shift_w)
        )
        made = []
        for f in range(4):
            at, start = (f, 24) if r == last else (r, 6 * f)
            made.append(
                join(
                    lane_q,
                    own_ref[f, r],
                    roll_lanes(re_ref[at], 8 - start),
                    roll_lanes(rw_ref[at], (19 if f == 3 else 18) - start),
                )
            )
        for f in range(4):
            fields[f, r] = made[f]
    bx, by = face_limits(eb)
    level0 = (base + (lane // STRIP) * rows_e).astype(jnp.float32)

    def put(tr, slab, js, new):
        ea_ref[tr, slab, js] = new

    advect_block(
        list(range(rows_e)),
        lambda tr, s: fields[tr, s],
        lambda s: fields[2, s],
        lambda s: fields[3, s],
        lambda s: level0 + float(s),
        bx,
        by,
        buf,
        coef,
        put,
    )
    top, half = rows_e - 1, levels // 2
    for tr in range(2):
        for n, (k, slab) in enumerate(((0, ea_ref[tr, 0]), (1, ea_ref[tr, 1]))):
            at = (2 * n + tr) * lat
            up_ref[at : at + lat] = patched(north_half[tr, k], slab, 0, lane)
        for n, (k, slab) in enumerate(
            ((half - 1, ea_ref[tr, top]), (half - 2, ea_ref[tr, top - 1]))
        ):
            at = (2 * n + tr) * lat
            down_ref[at : at + lat] = patched(south_half[tr, k], slab, 3, lane)
        at = 4 * lat + 8 * tr
        up_ref[at : at + 8] = fold_strip(ea_ref[tr, 0], 8)
        down_ref[at : at + 8] = fold_strip(ea_ref[tr, top], 3 * STRIP + 8)
    up_ref[4 * lat + 16 : 5 * lat + 16] = slab_of(kh_ref, 0)
    down_ref[4 * lat + 16 : 5 * lat + 16] = slab_of(kh_ref, levels - 1)
    first_ref[...] = pay[0, 0 : 4 * lat + 16]
    second_ref[0 : 5 * lat + 16] = pay[1]
    response = pair_response(abc_ref, pair_ref, me)
    for n in range(3):
        red_ref[n] = response[n]
    second_ref[5 * lat + 16 : 6 * lat + 16] = response[2]


def slopes(gx, gy, gz):
    rx, ry, rz = (-0.5 * THERMAL * g[0] + 0.5 * HALINE * g[1] for g in (gx, gy, gz))
    scale = rz / (1.0 + rx * rx + ry * ry + rz * rz)
    return rx * scale, ry * scale


def flux_xyz(gx, gy, gz, kappa, need_xy=True):
    sx, sy = slopes(gx, gy, gz)
    kx, ky = kappa * sx, kappa * sy
    kz = kx * sx + ky * sy
    fz = [kx * gx[n] + ky * gy[n] + kz * gz[n] for n in range(2)]
    if not need_xy:
        return None, None, fz
    fx = [kappa * gx[n] + kx * gz[n] for n in range(2)]
    fy = [kappa * gy[n] + ky * gz[n] for n in range(2)]
    return fx, fy, fz


def flux_x_edge(gx, gy, gz, kappa):
    sx, _ = slopes(gx, gy, gz)
    kx = kappa * sx
    return [kappa * gx[n] + kx * gz[n] for n in range(2)]


def diff(mask, high, low):
    return jnp.where(mask, high - low, 0.0)


def edge_flux_row(r, rows, ek, eb, ebx, eby, level0):
    level = level0 + r
    mx = level < ebx
    my = level < eby
    mz = (level + 1.0 < eb) & (level >= 1.0)
    kappa = jnp.where((level < eb) & (level >= 0.0), 0.25 * ek, 0.0)
    gx, gy, gz = [], [], []
    for tr in range(2):
        here = rows[tr, r + 1]
        gx.append(diff(mx, roll_lanes(here, -1), roll_lanes(here, 1)))
        gy.append(diff(my, shift_north(here), shift_south(here)))
        gz.append(diff(mz, rows[tr, r + 2], rows[tr, r]))
    return flux_x_edge(gx, gy, gz, kappa)


def edge_limits(eb):
    return (
        jnp.minimum(roll_lanes(eb, 1), roll_lanes(eb, -1)),
        lat_limits(eb),
    )


def zonal_change(fx, west, east, lane):
    return roll_lanes(jnp.where(lane == 0, east, fx), -1) - roll_lanes(
        jnp.where(lane == 127, west, fx), 1
    )


def divergence(fx, fy, slab, g, lane):
    return zonal_change(fx, west_patch(slab, g), east_patch(slab, g), lane) + (
        shift_north(fy) - shift_south(fy)
    )


def patch_kernel(
    north_half, south_half, ea_ref, ek_ref, eb_ref,
    full_ref, gx_ref, efx_ref,
    rows,
):
    levels, lat = full_ref.shape[1], full_ref.shape[2]
    rows_e = levels // GROUPS
    base = lax.axis_index("dep") * levels
    lane = lane_ids(lat)
    eb = eb_ref[...]
    ebx, eby = edge_limits(eb)
    level0 = (base + (lane // STRIP) * rows_e).astype(jnp.float32)
    for tr in range(2):
        for r in range(rows_e):
            rows[tr, r + 1] = ea_ref[tr, r]
        rows[tr, 0] = roll_lanes(ea_ref[tr, rows_e - 1], STRIP)
        rows[tr, rows_e + 1] = roll_lanes(ea_ref[tr, 0], -STRIP)
    found = [
        edge_flux_row(r, rows, ek_ref[r], eb, ebx, eby, level0) for r in range(rows_e)
    ]
    for r in range(rows_e):
        for tr in range(2):
            efx_ref[tr, r] = found[r][tr]

    lane = lane_ids(ROWS)
    units = [(g, slice(j, j + ROWS)) for g in range(GROUPS) for j in range(0, lat, ROWS)]

    def patch(r, _):
        def fetch(unit):
            g, js = unit
            strips = [ea_ref[tr, r, js] for tr in range(2)]
            half = (north_half, south_half)[2 * g // GROUPS]
            mains = [half[tr, g % (GROUPS // 2) * rows_e + r, js] for tr in range(2)]
            return [(west_patch(x, g), east_patch(x, g), y) for x, y in zip(strips, mains)]

        def put(unit, mains, rolled):
            g, js = unit
            for tr in range(2):
                full_ref[tr, g * rows_e + r, js] = mains[tr]
                gx_ref[tr, g * rows_e + r, js] = rolled[tr][0] - rolled[tr][1]

        waiting = None
        fetched = fetch(units[0])
        for n, unit in enumerate(units):
            now = fetched
            fetched = fetch(units[n + 1]) if n + 1 < len(units) else None
            mains, rolled = [], []
            for west, east, main in now:
                main = jnp.where(lane < 4, west, jnp.where(lane >= 124, east, main))
                mains.append(main)
                rolled.append(
                    (
                        roll_lanes(jnp.where(lane == 0, east, main), -1),
                        roll_lanes(jnp.where(lane == 127, west, main), 1),
                    )
                )
            if waiting is not None:
                put(*waiting)
            waiting = (unit, mains, rolled)
        put(*waiting)
        return 0

    lax.fori_loop(0, rows_e, patch, 0)


def flux_kernel(
    full_ref, gx_ref, efx_ref, bmx_ref, b_ref, kh_ref,
    q_ref, fz_ref,
    limits,
):
    levels, lat = full_ref.shape[1], full_ref.shape[2]
    rows_e = levels // GROUPS
    base = lax.axis_index("dep") * levels
    lane = lane_ids(lat)
    bottom = slab_of(b_ref).astype(jnp.float32)
    limits[0] = bmx_ref[...]
    limits[1] = lat_limits(bottom)
    limits[2] = bottom

    def north_rows(tr, k, j):
        if j + 8 + ROWS <= lat:
            return full_ref[tr, k, j + 8 : j + 8 + ROWS]
        return jnp.concatenate(
            [full_ref[tr, k, j + 8 : lat], pltpu.roll(full_ref[tr, k, 0:8], 7, 0)], axis=0
        )

    def south_rows(tr, k, j):
        if j >= 8:
            return full_ref[tr, k, j - 8 : j - 8 + ROWS]
        return jnp.concatenate(
            [pltpu.roll(full_ref[tr, k, lat - 8 : lat], 1, 0), full_ref[tr, k, 0 : ROWS - 8]],
            axis=0,
        )

    def fluxes(r, _):
        for g in range(GROUPS):
            k = g * rows_e + r
            above, below = jnp.maximum(k - 1, 0), jnp.minimum(k + 1, levels - 1)
            level = (base + k).astype(jnp.float32)
            level_z = jnp.where(level >= 1.0, level + 1.0, HUGE)
            sides = [
                (west_patch(efx_ref[tr, r], g), east_patch(efx_ref[tr, r], g)) for tr in range(2)
            ]
            fxs, fys, fzs = [[], []], [[], []], [[], []]
            for j in range(0, lat, ROWS):
                js = slice(j, j + ROWS)
                mx = level < limits[0, js]
                my = level < limits[1, js]
                mz = level_z < limits[2, js]
                kh = jnp.concatenate(
                    [rows_of(kh_ref, v, k) for v in range(j // 8, (j + ROWS) // 8)], axis=0
                )
                kappa = jnp.where(level < limits[2, js], 0.25 * kh, 0.0)
                gx, gy, gz = [], [], []
                for tr in range(2):
                    gx.append(jnp.where(mx, gx_ref[tr, k, js], 0.0))
                    gy.append(diff(my, north_rows(tr, k, j), south_rows(tr, k, j)))
                    gz.append(diff(mz, full_ref[tr, below, js], full_ref[tr, above, js]))
                fx, fy, fz = flux_xyz(gx, gy, gz, kappa)
                for tr in range(2):
                    fxs[tr].append(fx[tr])
                    fys[tr].append(fy[tr])
                    fzs[tr].append(fz[tr])
            wet = level < limits[2]
            new = []
            for tr in range(2):
                fy = jnp.concatenate(fys[tr], axis=0)
                change = zonal_change(jnp.concatenate(fxs[tr], axis=0), *sides[tr], lane)
                change = change + (shift_north(fy) - shift_south(fy))
                new.append(full_ref[tr, k] + jnp.where(wet, change, 0.0))
            for tr in range(2):
                q_ref[tr, k] = new[tr]
                fz_ref[tr, k] = jnp.concatenate(fzs[tr], axis=0)
        return 0

    lax.fori_loop(0, rows_e, fluxes, 0)


def factor_kernel(
    kv_ref, b_ref, khb_ref, inv_ref, ei_ref, ratio_ref, a_ref, bb_ref, abc_ref, msg_ref
):
    levels, lat = kv_ref.shape[0], kv_ref.shape[1]
    base = lax.axis_index("dep") * levels
    bottom = slab_of(b_ref).astype(jnp.float32)

    def coupling(k):
        level = (base + k).astype(jnp.float32)
        level = jnp.where(level >= 1.0, level, HUGE)
        return jnp.where(level < bottom, slab_of(kv_ref, k), 0.0)

    top = coupling(0)
    e = jnp.zeros((lat, 128), jnp.float32)
    q = e
    za = jnp.ones((lat, 128), jnp.float32)
    for k in range(levels):
        low = coupling(k + 1) if k + 1 < levels else jnp.zeros((lat, 128), jnp.float32)
        eq = 1.0 + e * q
        inv = 1.0 / (eq + low)
        inv_ref[k] = inv
        ei = e * inv
        ei_ref[k] = ei
        ratio_ref[k] = low * inv
        za = inv if k == 0 else za * ei
        a_ref[k] = za
        q = eq * inv
        e = low
    bb_ref[levels - 1] = inv
    b = inv
    a = za
    for k in range(levels - 2, -1, -1):
        ratio = ratio_ref[k]
        b = ratio * b
        a = a_ref[k] + ratio * a
        bb_ref[k] = b
        a_ref[k] = a
    a = a + jnp.where(top > 0.0, 1.0 / jnp.maximum(top, 1e-30), HUGE)
    abc_ref[0] = a
    abc_ref[1] = inv
    abc_ref[2] = b
    upper = lax.rem(lax.axis_index("dep"), 2) == 0
    msg_ref[0] = jnp.where(upper, inv, a)
    msg_ref[1] = b
    msg_ref[2] = jnp.where(upper, khb_ref[1], khb_ref[0])


def solve_kernel(
    full_ref, q_ref, fz_ref, ea_ref, ek_ref, eb_ref, bmx_ref, b_ref, kh_ref,
    first_ref, second_ref, inv_ref, ei_ref, ratio_ref, red_ref, pair_ref,
    y_ref, m3_ref, m2_ref, m1_ref, both_ref, own_ref,
    pad, epad, fze, halo,
):
    levels, lat = q_ref.shape[1], q_ref.shape[2]
    rows_e = levels // GROUPS
    last = levels - 1
    top = rows_e - 1
    me = lax.axis_index("dep")
    base = me * levels
    parity = lax.rem(me, 2)
    outer = (me == 0) | (me == 3)
    upper = parity == 0
    sign = jnp.where(me < 2, 1.0, -1.0)
    lane = lane_ids(lat)
    halo[0, 0 : 4 * lat + 16] = first_ref[...]
    halo[0, 4 * lat + 16 : 5 * lat + 16] = pair_ref[2]
    halo[1] = second_ref[0 : 5 * lat + 16]
    above_ref, below_ref = halo.at[1 - parity], halo.at[parity]

    share = red_ref[0]
    both = red_ref[2] + second_ref[5 * lat + 16 : 6 * lat + 16]
    cross = share / both
    inside = red_ref[1] + share * cross
    for n, value in enumerate((share, red_ref[1], both)):
        own_ref[n] = value
    both_ref[...] = both

    eb = eb_ref[...]
    ebx, eby = edge_limits(eb)
    level0 = (base + (lane // STRIP) * rows_e).astype(jnp.float32)
    for tr in range(2):
        pad[tr, 0] = above_ref[(2 + tr) * lat : (3 + tr) * lat]
        pad[tr, 1] = above_ref[tr * lat : (1 + tr) * lat]
        for n, k in enumerate((0, 1, 2, last - 2, last - 1, last)):
            pad[tr, n + 2] = full_ref[tr, k]
        pad[tr, 8] = below_ref[tr * lat : (1 + tr) * lat]
        pad[tr, 9] = below_ref[(2 + tr) * lat : (3 + tr) * lat]
        for r in range(rows_e):
            epad[tr, r + 1] = ea_ref[tr, r]
        at = 4 * lat + 8 * tr
        corner_up = unfold_strip(above_ref[at : at + 8], 3 * STRIP + 8, lat // 8)
        corner_dn = unfold_strip(below_ref[at : at + 8], 8, lat // 8)
        epad[tr, 0] = roll_lanes(
            jnp.where(lane >= 3 * STRIP, corner_up, ea_ref[tr, top]), STRIP
        )
        epad[tr, rows_e + 1] = roll_lanes(
            jnp.where(lane < STRIP, corner_dn, ea_ref[tr, 0]), -STRIP
        )
    efx = {
        r + 1: edge_flux_row(r, epad, ek_ref[r], eb, ebx, eby, level0) for r in (0, top)
    }

    bottom = slab_of(b_ref).astype(jnp.float32)
    bmy = lat_limits(bottom)
    bmx = bmx_ref[...]
    ends = (
        (1, -1, 0, 0, above_ref[4 * lat + 16 : 5 * lat + 16], True),
        (2, 0, 1, 0, slab_of(kh_ref, 0), False),
        (7, last, top + 1, 3, slab_of(kh_ref, last), False),
        (8, last + 1, top + 2, 3, below_ref[4 * lat + 16 : 5 * lat + 16], True),
    )
    spread = {}
    for m, (n, k, er, g, kappa_slab, only_z) in enumerate(ends):
        level = (base + k).astype(jnp.float32)
        level_z = jnp.where(level >= 1.0, level + 1.0, HUGE)
        level_h = jnp.where(level >= 0.0, level, HUGE)
        mx = level_h < bmx
        my = level_h < bmy
        mz = level_z < bottom
        kappa = jnp.where(level_h < bottom, 0.25 * kappa_slab, 0.0)
        gx, gy, gz = [], [], []
        for tr in range(2):
            slab, main = epad[tr, er], pad[tr, n]
            change = zonal_change(main, west_patch(slab, g), east_patch(slab, g), lane)
            gx.append(jnp.where(mx, change, 0.0))
            gy.append(diff(my, shift_north(main), shift_south(main)))
            gz.append(diff(mz, pad[tr, n + 1], pad[tr, n - 1]))
        fx, fy, fz = flux_xyz(gx, gy, gz, kappa, not only_z)
        for tr in range(2):
            fze[tr, m] = fz[tr]
            if not only_z:
                spread[k, tr] = divergence(fx[tr], fy[tr], efx[er][tr], g, lane)

    def vertical_flux(tr, k):
        place = {-1: 0, 0: 1, last: 2, last + 1: 3}.get(k)
        return fz_ref[tr, k] if place is None else fze[tr, place]

    z = [None, None]
    for k in range(levels):
        level = (base + k).astype(jnp.float32)
        wet = level < bottom
        for tr in range(2):
            change = vertical_flux(tr, k + 1) - vertical_flux(tr, k - 1)
            if k == 0 or k == last:
                change = change + spread[k, tr]
                start = pad[tr, 2 if k == 0 else 7]
            else:
                start = q_ref[tr, k]
            rhs = start + jnp.where(wet, change, 0.0)
            new = rhs * inv_ref[k]
            z[tr] = new if k == 0 else new + ei_ref[k] * z[tr]
        for tr in range(2):
            y_ref[tr, k] = z[tr]
    low = list(z)
    for k in range(last - 1, -1, -1):
        ratio = ratio_ref[k]
        z = [y_ref[tr, k] + ratio * z[tr] for tr in range(2)]
        for tr in range(2):
            y_ref[tr, k] = z[tr]
    for tr in range(2):
        near = jnp.where(upper, low[tr], z[tr])
        far = jnp.where(upper, z[tr], low[tr])
        m1_ref[tr] = jnp.where(outer, near, sign * (inside * near - cross * far))
        value = jnp.where(outer, share * near, far - share * near)
        m2_ref[tr] = value
        m3_ref[tr] = value


def finish_kernel(
    y_ref, a_ref, bb_ref, own_ref, r3_ref, r2_ref, r1_ref, both_ref, out_hbm, out, sems
):
    levels = y_ref.shape[1]
    me = lax.axis_index("dep")
    upper = lax.rem(me, 2) == 0
    outer = (me == 0) | (me == 3)
    sign = jnp.where(me < 2, 1.0, -1.0)
    share, inv_t = own_ref[0], own_ref[1]
    inv_e = 1.0 / jnp.where(outer, both_ref[...], own_ref[2])
    cross = share * inv_e
    inside = inv_t + share * cross
    tops, lows = [], []
    for tr in range(2):
        y_top, y_low = y_ref[tr, 0], y_ref[tr, levels - 1]
        near = jnp.where(upper, y_low, y_top)
        far = jnp.where(upper, y_top, y_low)
        mate, across = r1_ref[tr], r2_ref[tr] + r3_ref[tr]
        pair_flux = jnp.where(
            outer,
            mate + sign * (cross * across - inside * near),
            sign * (inside * (near - mate) + cross * (across - far)),
        )
        middle = sign * (inv_e * (across - far + share * near) - cross * mate)
        middle = jnp.where(outer, 0.0, middle)
        tops.append(jnp.where(upper, middle, pair_flux))
        lows.append(jnp.where(upper, pair_flux, middle))
    step, regs = levels // GROUPS, y_ref.shape[2] // 8
    copies = []
    for part in range(GROUPS):
        for k in range(part * step, (part + 1) * step):
            a, b = a_ref[k], bb_ref[k]
            new = [y_ref[tr, k] - tops[tr] * a + lows[tr] * b for tr in range(2)]
            for tr in range(2):
                for v in range(regs):
                    out[tr, k, pl.ds(v, 8, regs), :] = new[tr][8 * v : 8 * v + 8]
        for tr in range(2):
            span = (tr, pl.ds(part * step, step))
            copies.append(
                pltpu.make_async_copy(out.at[span], out_hbm.at[span], sems.at[tr, part])
            )
            copies[-1].start()
    for copy in copies:
        copy.wait()


def per_device(tracers, u_east, v_north, kappa_h, kappa_v, bottom):
    _, levels, lat, lon = tracers.shape
    rows_e = levels // GROUPS
    lon_n, dep_n = lax.axis_size("lon"), lax.axis_size("dep")
    east = [(i, (i + 1) % lon_n) for i in range(lon_n)]
    west = [(t, s) for s, t in east]
    slab = lat * lon * 4
    slabs = lambda *lead: f32(*lead, lat, lon)
    work = lambda *lead: pltpu.VMEM(lead + (lat, lon), jnp.float32)

    with jax.named_scope("pack"):
        sw, se, bp, ww, we, t0, t1, u, v, khb = call(
            pack_kernel,
            (slabs(rows_e),) * 2 + (slabs(),) + (slabs(rows_e - 1),) * 2 + (slabs(levels),) * 4
            + (slabs(2),),
            [
                work(levels), pltpu.VMEM((lat, lon), jnp.int32), work(rows_e), work(rows_e),
                pltpu.SemaphoreType.DMA((GROUPS, 4)), pltpu.SemaphoreType.DMA((2,)),
            ],
            (tracers, u_east, v_north, kappa_h, bottom), 10**6, 6 * levels * slab, 50.5,
            in_specs=[HBM] * 5,
        )
    with jax.named_scope("lon_halo"):
        r_east = lax.ppermute(ww, "lon", west)
        r_west = lax.ppermute(we, "lon", east)
    with jax.named_scope("factor"):
        inv, ei, ratio, a_end, b_end, abc, msg = call(
            factor_kernel, (slabs(levels),) * 5 + (slabs(3),) * 2, [],
            (kappa_v, bottom, khb), 10**7, 6 * levels * slab, 16,
        )
    swap = [(i, i ^ 1) for i in range(dep_n)]
    with jax.named_scope("pair_coefficients"):
        pair = lax.ppermute(msg, "dep", swap)
    half = levels // 2

    def advect_half(start, earlier):
        return call(
            functools.partial(advect_kernel, start), slabs(2, half),
            [work(2, 2 * half), work(5, half)],
            (t0, t1, u, v, bottom, earlier), 10**7, 4 * levels * slab, 16,
        )

    with jax.named_scope("advect_north"):
        north_half = advect_half(0, abc)
    with jax.named_scope("advect_south"):
        south_half = advect_half(half, abc)
    with jax.named_scope("own_strips"):
        own_strips, own_bottom = call(
            own_kernel, (slabs(4, rows_e), slabs()), [],
            (sw, se, bp, abc), 10**6, 8 * rows_e * slab, 16,
        )
    rows_pay = 5 * lat + 16
    with jax.named_scope("advect_edge"):
        ea, ek, eb, bmx, first, second, red = call(
            edge_kernel,
            (
                slabs(2, rows_e), slabs(rows_e), slabs(), slabs(),
                f32(rows_pay - lat, lon), f32(rows_pay + lat, lon), slabs(3),
            ),
            [
                work(2, 2 * rows_e), work(5, rows_e), work(4, rows_e),
                pltpu.VMEM((2, rows_pay, lon), jnp.float32),
            ],
            (own_strips, own_bottom, r_east, r_west, bottom, north_half, south_half, kappa_h, abc, pair),
            10**6, 3 * levels * slab, 16,
        )
    other = []
    for i in range(lon_n * dep_n):
        row, place = divmod(i, dep_n)
        if place in (0, dep_n - 1):
            other.append((i, (row ^ 1) * dep_n + place))
        else:
            other.append((i, i + 1 if place % 2 else i - 1))
    with jax.named_scope("dep_halo"):
        first = lax.ppermute(first, "dep", swap)
        second = lax.ppermute(second, ("lon", "dep"), other)
    with jax.named_scope("patch"):
        full, gx, efx = call(
            patch_kernel, (slabs(2, levels), slabs(2, levels), slabs(2, rows_e)),
            [work(2, rows_e + 2)],
            (north_half, south_half, ea, ek, eb), 10**7, 8 * levels * slab, 16,
        )
    with jax.named_scope("fluxes"):
        q_part, fz = call(
            flux_kernel, (slabs(2, levels), slabs(2, levels)), [work(3)],
            (full, gx, efx, bmx, bottom, kappa_h), 10**7, 10 * levels * slab, 16,
        )
    with jax.named_scope("solve"):
        y, m3, m2, m1, both, own = call(
            solve_kernel, (slabs(2, levels), slabs(2), slabs(2), slabs(2), slabs(), slabs(3)),
            [
                work(2, 10), work(2, rows_e + 2), work(2, 4),
                pltpu.VMEM((2, rows_pay, lon), jnp.float32),
            ],
            (
                full, q_part, fz, ea, ek, eb, bmx, bottom, kappa_h, first, second,
                inv, ei, ratio, red, pair,
            ),
            10**7, 12 * levels * slab, 24,
        )
    with jax.named_scope("interfaces"):
        m3 = lax.ppermute(m3, "dep", [(i, i ^ 3) for i in range(dep_n)])
        m2 = lax.ppermute(m2, "dep", [(i, i ^ 2) for i in range(dep_n)])
        m1 = lax.ppermute(m1, "dep", swap)
        both = lax.ppermute(both, "dep", swap)
    with jax.named_scope("finish"):
        return call(
            finish_kernel, slabs(2, levels),
            [work(2, levels), pltpu.SemaphoreType.DMA((2, GROUPS))],
            (y, a_end, b_end, own, m3, m2, m1, both), 10**6, 6 * levels * slab, 16,
            out_specs=HBM,
        )


def solution(mesh):
    in_specs = (
        P(None, "dep", None, "lon"),
        P("dep", None, "lon"),
        P("dep", None, "lon"),
        P("dep", None, "lon"),
        P("dep", None, "lon"),
        P(None, "lon"),
    )
    out_specs = P(None, "dep", None, "lon")
    return jax.shard_map(
        per_device, mesh=mesh, in_specs=in_specs, out_specs=out_specs, check_vma=False
    )
```

```python
import functools

import jax
import jax.numpy as jnp
from jax import lax
from jax.experimental import pallas as pl
from jax.experimental.pallas import tpu as pltpu
from jax.sharding import PartitionSpec as P

SUB = 4
THERMAL = 0.2
HALINE = 0.8
GROUPS = 4
ROWS = 32
STRIP = 32
HUGE = 1e30
MIB = 1024 * 1024

VMEM = pl.BlockSpec(memory_space=pltpu.VMEM)
HBM = pl.BlockSpec(memory_space=pltpu.HBM)


def lane_ids(rows):
    return lax.broadcasted_iota(jnp.int32, (rows, 128), 1)


def roll_lanes(x, amount):
    amount = amount % 128
    return x if amount == 0 else pltpu.roll(x, amount, 1)


def shift_north(x):
    return jnp.concatenate([x[8:], pltpu.roll(x[:8], 7, 0)], axis=0)


def shift_south(x):
    return jnp.concatenate([pltpu.roll(x[-8:], 1, 0), x[:-8]], axis=0)


def rows_of(ref, v, *lead):
    return ref[(*lead, pl.ds(v, 8, ref.shape[-2] // 8), slice(None))]


def neighbours(regs, v):
    north = regs[v + 1] if v + 1 < len(regs) else pltpu.roll(regs[0], 7, 0)
    south = regs[v - 1] if v > 0 else pltpu.roll(regs[-1], 1, 0)
    return north, south


def slab_of(ref, *lead):
    return jnp.concatenate([rows_of(ref, v, *lead) for v in range(ref.shape[-2] // 8)], axis=0)


def call(body, out_shape, scratch, args, flops, in_bytes, limit, in_specs=None, out_specs=None):
    return pl.pallas_call(
        body,
        out_shape=out_shape,
        in_specs=in_specs or [VMEM] * len(args),
        out_specs=out_specs or jax.tree.map(lambda _: VMEM, out_shape),
        scratch_shapes=scratch,
        compiler_params=pltpu.CompilerParams(vmem_limit_bytes=int(limit * MIB)),
        cost_estimate=pl.CostEstimate(flops=flops, bytes_accessed=in_bytes, transcendentals=0),
    )(*args)


def f32(*shape):
    return jax.ShapeDtypeStruct(shape, jnp.float32)


def pack_kernel(
    t_hbm, u_hbm, v_hbm, kh_hbm, b_hbm,
    sw_ref, se_ref, bp_ref, ww_ref, we_ref, t0_ref, t1_ref, u_ref, v_ref, khb_ref,
    kh_buf, b_buf, first_buf, sems, more_sems,
):
    rows_e = u_ref.shape[0] // GROUPS
    lat = u_ref.shape[1]
    lane = lane_ids(lat)
    fields = ((t_hbm.at[0], t0_ref), (t_hbm.at[1], t1_ref), (u_hbm, u_ref), (v_hbm, v_ref))
    groups = [
        [
            pltpu.make_async_copy(
                src.at[pl.ds(g * rows_e, rows_e)], dst.at[pl.ds(g * rows_e, rows_e)], sems.at[g, n]
            )
            for n, (src, dst) in enumerate(fields)
        ]
        for g in range(GROUPS)
    ]
    tail = [
        pltpu.make_async_copy(b_hbm, b_buf, more_sems.at[0]),
        pltpu.make_async_copy(kh_hbm, kh_buf, more_sems.at[1]),
    ]
    for copy in sum(groups, []) + tail:
        copy.start()
    for g in range(GROUPS):
        for copy in groups[g]:
            copy.wait()
        for batch in (range(0, rows_e // 2), range(rows_e // 2, rows_e)):
            rolled = {
                (r, f): roll_lanes(slab_of(ref, g * rows_e + r), STRIP * g + 8 * f)
                for r in batch
                for f, ref in enumerate((t0_ref, t1_ref, u_ref, v_ref))
            }
            done = []
            for r in batch:
                low = rolled[r, 0]
                high = None
                if g > 0:
                    low = jnp.where(lane >= STRIP * g, low, sw_ref[r])
                    high = jnp.where(lane >= STRIP * g - 8, rolled[r, 0], se_ref[r])
                for f in range(1, 4):
                    start = STRIP * g + 8 * f
                    low = jnp.where(lane >= start, rolled[r, f], low)
                    if high is None:
                        high = rolled[r, f]
                    else:
                        high = jnp.where(lane >= start - 8, rolled[r, f], high)
                if g == GROUPS - 1:
                    high = jnp.where(lane >= 120, first_buf[r], high)
                done.append((r, low, high))
            for r, low, high in done:
                if g == 0:
                    first_buf[r] = rolled[r, 0]
                sw_ref[r] = low
                se_ref[r] = high
    for copy in tail:
        copy.wait()
    bottom = slab_of(b_buf).astype(jnp.float32)
    place = bottom
    for g in range(1, GROUPS):
        place = jnp.where(lane >= STRIP * g - 8, roll_lanes(bottom, STRIP * g), place)
    place = jnp.where(lane >= 120, bottom, place)
    bp_ref[...] = place

    def kappa(r):
        out = None
        for g in range(GROUPS):
            rolled = roll_lanes(slab_of(kh_buf, g * rows_e + r), STRIP * g + 23)
            out = rolled if g == 0 else jnp.where(lane >= STRIP * g + 8, rolled, out)
        return out

    khb_ref[0] = slab_of(kh_buf, 0)
    khb_ref[1] = slab_of(kh_buf, GROUPS * rows_e - 1)
    last = rows_e - 1
    kappa_last = kappa(last)
    lane_q = lane % STRIP
    low_last, high_last = sw_ref[last], se_ref[last]
    wires = []
    for r in range(last):
        k = kappa(r)
        low, high = sw_ref[r], se_ref[r]
        west = (low, roll_lanes(low, -2), roll_lanes(low, -4), roll_lanes(low, -6), k)
        east = (
            roll_lanes(high, 6), roll_lanes(high, 4), roll_lanes(high, 2), roll_lanes(high, -1),
            roll_lanes(k, 1),
        )
        west += (roll_lanes(low_last, 24 - 8 * r),)
        east += (roll_lanes(high_last, 5 if r == 3 else 30 - 8 * r),)
        if r == 3:
            west += (roll_lanes(kappa_last, 6),)
            east += (roll_lanes(kappa_last, 7),)
        else:
            west += (roll_lanes(place, 30 - 2 * r),)
            east += (roll_lanes(place, 36 - 2 * r),)
        starts = (6, 12, 18, 23, 24, 29 if r == 3 else 30)
        for ref, parts in ((ww_ref, west), (we_ref, east)):
            wire = parts[0]
            for start, part in zip(starts, parts[1:]):
                wire = jnp.where(lane_q >= start, part, wire)
            wires.append((ref, r, wire))
    for ref, r, wire in wires:
        ref[r] = wire


def advect_block(slabs, get_c, get_u, get_v, get_level, bx, by, buf, coef, put):
    regs = bx.shape[0] // 8

    def masked(slab):
        level = get_level(slab)
        um = jnp.where(level < bx, get_u(slab), 0.0)
        vm = jnp.where(level < by, get_v(slab), 0.0)
        return um, vm, roll_lanes(um, 1), shift_south(vm)

    following = masked(slabs[0])
    for i, slab in enumerate(slabs):
        um, vm, uw, vs = following
        if i + 1 < len(slabs):
            following = masked(slabs[i + 1])
        now = [get_c(tr, slab) for tr in range(2)]
        coef[0, i] = (
            1.0
            - jnp.maximum(um, 0.0)
            + jnp.minimum(uw, 0.0)
            - jnp.maximum(vm, 0.0)
            + jnp.minimum(vs, 0.0)
        )
        coef[1, i] = -jnp.minimum(um, 0.0)
        coef[2, i] = jnp.maximum(uw, 0.0)
        coef[3, i] = -jnp.minimum(vm, 0.0)
        coef[4, i] = jnp.maximum(vs, 0.0)
        for tr in range(2):
            buf[0, 2 * i + tr] = now[tr]
    for step in range(SUB):
        src, dst = step % 2, (step + 1) % 2
        for i, slab in enumerate(slabs):
            now = [
                [buf[src, 2 * i + tr, 8 * v : 8 * v + 8] for v in range(regs)] for tr in range(2)
            ]
            for v in range(regs):
                js = slice(8 * v, 8 * v + 8)
                a, b, c, d, e = (coef[n, i, js] for n in range(5))
                for tr in range(2):
                    here = now[tr][v]
                    north, south = neighbours(now[tr], v)
                    new = (
                        a * here
                        + b * roll_lanes(here, -1)
                        + c * roll_lanes(here, 1)
                        + d * north
                        + e * south
                    )
                    if step < SUB - 1:
                        buf[dst, 2 * i + tr, js] = new
                    else:
                        put(tr, slab, js, new)


def face_limits(bottom):
    lat = bottom.shape[0]
    rows = lax.broadcasted_iota(jnp.int32, bottom.shape, 0)
    north = jnp.where(rows == lat - 1, 0.0, shift_north(bottom))
    return jnp.minimum(bottom, roll_lanes(bottom, -1)), jnp.minimum(bottom, north)


def lat_limits(bottom):
    lat = bottom.shape[0]
    rows = lax.broadcasted_iota(jnp.int32, bottom.shape, 0)
    north = jnp.where(rows == lat - 1, 0.0, shift_north(bottom))
    south = jnp.where(rows == 0, 0.0, shift_south(bottom))
    return jnp.minimum(north, south)


def advect_kernel(start, t0_ref, t1_ref, u_ref, v_ref, b_ref, earlier_ref, out_ref, buf, coef):
    del earlier_ref
    count, lat = out_ref.shape[1], out_ref.shape[2]
    base = lax.axis_index("dep") * t0_ref.shape[0] + start
    bx, by = face_limits(slab_of(b_ref).astype(jnp.float32))

    def put(tr, slab, js, new):
        out_ref[tr, slab, js] = new

    advect_block(
        list(range(count)),
        lambda tr, s: slab_of((t0_ref, t1_ref)[tr], start + s),
        lambda s: slab_of(u_ref, start + s),
        lambda s: slab_of(v_ref, start + s),
        lambda s: (base + s).astype(jnp.float32),
        bx,
        by,
        buf,
        coef,
        put,
    )


def join(lane_q, own, east, west):
    halo = jnp.where(lane_q < 16, east, west)
    return jnp.where((lane_q >= 8) & (lane_q < 24), halo, own)


def west_patch(slab, g):
    return roll_lanes(slab, -(STRIP * g + 24))


def east_patch(slab, g):
    return roll_lanes(slab, 120 - STRIP * g)


def patched(main, slab, g, lane):
    return jnp.where(
        lane < 4, west_patch(slab, g), jnp.where(lane >= 124, east_patch(slab, g), main)
    )


def own_kernel(sw_ref, se_ref, bp_ref, earlier_ref, own_ref, ownb_ref):
    del earlier_ref
    rows_e, lat = sw_ref.shape[0], sw_ref.shape[1]
    lane_q = lane_ids(lat) % STRIP
    for r in range(rows_e):
        made = [
            jnp.where(
                lane_q < 16, roll_lanes(se_ref[r], 8 - 8 * f), roll_lanes(sw_ref[r], 24 - 8 * f)
            )
            for f in range(4)
        ]
        for f in range(4):
            own_ref[f, r] = made[f]
    place = bp_ref[...]
    ownb_ref[...] = jnp.where(lane_q < 16, roll_lanes(place, 8), roll_lanes(place, 24))


def pair_response(abc_ref, pair_ref, me):
    upper = lax.rem(me, 2) == 0
    low_pair = me < 2
    inv_t = 1.0 / (pair_ref[0] + jnp.where(upper, abc_ref[1], abc_ref[0]))
    c_pair = jnp.where(upper == low_pair, pair_ref[1], abc_ref[2])
    share = c_pair * inv_t
    return share, inv_t, jnp.where(upper, abc_ref[0], abc_ref[1]) - c_pair * share


def fold_strip(slab, place):
    lane = lane_ids(8)
    folded = jnp.zeros((8, 128), jnp.float32)
    for v in range(slab.shape[0] // 8):
        rolled = roll_lanes(slab[8 * v : 8 * v + 8], 16 * v - place)
        folded = jnp.where(lane >= 16 * v, rolled, folded)
    return folded


def unfold_strip(folded, place, regs):
    return jnp.concatenate([roll_lanes(folded, place - 16 * v) for v in range(regs)], axis=0)


def edge_kernel(
    own_ref, ownb_ref, re_ref, rw_ref, b_ref, north_half, south_half, kh_ref, abc_ref, pair_ref,
    ea_ref, ek_ref, eb_ref, bmx_ref, first_ref, second_ref, red_ref,
    buf, coef, fields, pay,
):
    levels, lat = kh_ref.shape[0], kh_ref.shape[1]
    rows_e = levels // GROUPS
    me = lax.axis_index("dep")
    base = me * levels
    parity = lax.rem(me, 2)
    up_ref, down_ref = pay.at[1 - parity], pay.at[parity]
    lane = lane_ids(lat)
    lane_q = lane % STRIP
    bottom = slab_of(b_ref).astype(jnp.float32)
    east = [roll_lanes(re_ref[r], 2 * r - 22) for r in range(3)]
    west = [roll_lanes(rw_ref[r], 2 * r - 12) for r in range(3)]
    eb = join(
        lane_q,
        ownb_ref[...],
        jnp.where(lane_q < 10, east[0], jnp.where(lane_q < 12, east[1], east[2])),
        jnp.where(lane_q < 20, west[0], jnp.where(lane_q < 22, west[1], west[2])),
    )
    eb_ref[...] = eb
    b_west = roll_lanes(jnp.where(lane == 127, west_patch(eb, 0), bottom), 1)
    b_east = roll_lanes(jnp.where(lane == 0, east_patch(eb, 0), bottom), -1)
    bmx_ref[...] = jnp.minimum(b_west, b_east)
    last = rows_e - 1
    for r in range(rows_e):
        at, shift_e, shift_w = (3, -21, -6) if r == last else (r, -15, 0)
        ek_ref[r] = jnp.where(
            lane_q < 16, roll_lanes(re_ref[at], shift_e), roll_lanes(rw_ref[at], shift_w)
        )
        made = []
        for f in range(4):
            at, start = (f, 24) if r == last else (r, 6 * f)
            made.append(
                join(
                    lane_q,
                    own_ref[f, r],
                    roll_lanes(re_ref[at], 8 - start),
                    roll_lanes(rw_ref[at], (19 if f == 3 else 18) - start),
                )
            )
        for f in range(4):
            fields[f, r] = made[f]
    bx, by = face_limits(eb)
    level0 = (base + (lane // STRIP) * rows_e).astype(jnp.float32)

    def put(tr, slab, js, new):
        ea_ref[tr, slab, js] = new

    advect_block(
        list(range(rows_e)),
        lambda tr, s: fields[tr, s],
        lambda s: fields[2, s],
        lambda s: fields[3, s],
        lambda s: level0 + float(s),
        bx,
        by,
        buf,
        coef,
        put,
    )
    top, half = rows_e - 1, levels // 2
    for tr in range(2):
        for n, (k, slab) in enumerate(((0, ea_ref[tr, 0]), (1, ea_ref[tr, 1]))):
            at = (2 * n + tr) * lat
            up_ref[at : at + lat] = patched(north_half[tr, k], slab, 0, lane)
        for n, (k, slab) in enumerate(
            ((half - 1, ea_ref[tr, top]), (half - 2, ea_ref[tr, top - 1]))
        ):
            at = (2 * n + tr) * lat
            down_ref[at : at + lat] = patched(south_half[tr, k], slab, 3, lane)
        at = 4 * lat + 8 * tr
        up_ref[at : at + 8] = fold_strip(ea_ref[tr, 0], 8)
        down_ref[at : at + 8] = fold_strip(ea_ref[tr, top], 3 * STRIP + 8)
    up_ref[4 * lat + 16 : 5 * lat + 16] = slab_of(kh_ref, 0)
    down_ref[4 * lat + 16 : 5 * lat + 16] = slab_of(kh_ref, levels - 1)
    first_ref[...] = pay[0, 0 : 4 * lat + 16]
    second_ref[0 : 5 * lat + 16] = pay[1]
    response = pair_response(abc_ref, pair_ref, me)
    for n in range(3):
        red_ref[n] = response[n]
    second_ref[5 * lat + 16 : 6 * lat + 16] = response[2]


def slopes(gx, gy, gz):
    rx, ry, rz = (-0.5 * THERMAL * g[0] + 0.5 * HALINE * g[1] for g in (gx, gy, gz))
    scale = rz / (1.0 + rx * rx + ry * ry + rz * rz)
    return rx * scale, ry * scale


def flux_xyz(gx, gy, gz, kappa, need_xy=True):
    sx, sy = slopes(gx, gy, gz)
    kx, ky = kappa * sx, kappa * sy
    kz = kx * sx + ky * sy
    fz = [kx * gx[n] + ky * gy[n] + kz * gz[n] for n in range(2)]
    if not need_xy:
        return None, None, fz
    fx = [kappa * gx[n] + kx * gz[n] for n in range(2)]
    fy = [kappa * gy[n] + ky * gz[n] for n in range(2)]
    return fx, fy, fz


def flux_x_edge(gx, gy, gz, kappa):
    sx, _ = slopes(gx, gy, gz)
    kx = kappa * sx
    return [kappa * gx[n] + kx * gz[n] for n in range(2)]


def diff(mask, high, low):
    return jnp.where(mask, high - low, 0.0)


def edge_flux_row(r, rows, ek, eb, ebx, eby, level0):
    level = level0 + r
    mx = level < ebx
    my = level < eby
    mz = (level + 1.0 < eb) & (level >= 1.0)
    kappa = jnp.where((level < eb) & (level >= 0.0), 0.25 * ek, 0.0)
    gx, gy, gz = [], [], []
    for tr in range(2):
        here = rows[tr, r + 1]
        gx.append(diff(mx, roll_lanes(here, -1), roll_lanes(here, 1)))
        gy.append(diff(my, shift_north(here), shift_south(here)))
        gz.append(diff(mz, rows[tr, r + 2], rows[tr, r]))
    return flux_x_edge(gx, gy, gz, kappa)


def edge_limits(eb):
    return (
        jnp.minimum(roll_lanes(eb, 1), roll_lanes(eb, -1)),
        lat_limits(eb),
    )


def zonal_change(fx, west, east, lane):
    return roll_lanes(jnp.where(lane == 0, east, fx), -1) - roll_lanes(
        jnp.where(lane == 127, west, fx), 1
    )


def divergence(fx, fy, slab, g, lane):
    return zonal_change(fx, west_patch(slab, g), east_patch(slab, g), lane) + (
        shift_north(fy) - shift_south(fy)
    )


def patch_kernel(
    north_half, south_half, ea_ref, ek_ref, eb_ref,
    full_ref, gx_ref, efx_ref,
    rows,
):
    levels, lat = full_ref.shape[1], full_ref.shape[2]
    rows_e = levels // GROUPS
    base = lax.axis_index("dep") * levels
    lane = lane_ids(lat)
    eb = eb_ref[...]
    ebx, eby = edge_limits(eb)
    level0 = (base + (lane // STRIP) * rows_e).astype(jnp.float32)
    for tr in range(2):
        for r in range(rows_e):
            rows[tr, r + 1] = ea_ref[tr, r]
        rows[tr, 0] = roll_lanes(ea_ref[tr, rows_e - 1], STRIP)
        rows[tr, rows_e + 1] = roll_lanes(ea_ref[tr, 0], -STRIP)
    found = [
        edge_flux_row(r, rows, ek_ref[r], eb, ebx, eby, level0) for r in range(rows_e)
    ]
    for r in range(rows_e):
        for tr in range(2):
            efx_ref[tr, r] = found[r][tr]

    lane = lane_ids(ROWS)
    units = [(g, slice(j, j + ROWS)) for g in range(GROUPS) for j in range(0, lat, ROWS)]

    def patch(r, _):
        def fetch(unit):
            g, js = unit
            strips = [ea_ref[tr, r, js] for tr in range(2)]
            half = (north_half, south_half)[2 * g // GROUPS]
            mains = [half[tr, g % (GROUPS // 2) * rows_e + r, js] for tr in range(2)]
            return [(west_patch(x, g), east_patch(x, g), y) for x, y in zip(strips, mains)]

        def put(unit, mains, rolled):
            g, js = unit
            for tr in range(2):
                full_ref[tr, g * rows_e + r, js] = mains[tr]
                gx_ref[tr, g * rows_e + r, js] = rolled[tr][0] - rolled[tr][1]

        waiting = None
        fetched = fetch(units[0])
        for n, unit in enumerate(units):
            now = fetched
            fetched = fetch(units[n + 1]) if n + 1 < len(units) else None
            mains, rolled = [], []
            for west, east, main in now:
                main = jnp.where(lane < 4, west, jnp.where(lane >= 124, east, main))
                mains.append(main)
                rolled.append(
                    (
                        roll_lanes(jnp.where(lane == 0, east, main), -1),
                        roll_lanes(jnp.where(lane == 127, west, main), 1),
                    )
                )
            if waiting is not None:
                put(*waiting)
            waiting = (unit, mains, rolled)
        put(*waiting)
        return 0

    lax.fori_loop(0, rows_e, patch, 0)


def flux_kernel(
    full_ref, gx_ref, efx_ref, bmx_ref, b_ref, kh_ref,
    q_ref, fz_ref,
    limits,
):
    levels, lat = full_ref.shape[1], full_ref.shape[2]
    rows_e = levels // GROUPS
    base = lax.axis_index("dep") * levels
    lane = lane_ids(lat)
    bottom = slab_of(b_ref).astype(jnp.float32)
    limits[0] = bmx_ref[...]
    limits[1] = lat_limits(bottom)
    limits[2] = bottom

    def north_rows(tr, k, j):
        if j + 8 + ROWS <= lat:
            return full_ref[tr, k, j + 8 : j + 8 + ROWS]
        return jnp.concatenate(
            [full_ref[tr, k, j + 8 : lat], pltpu.roll(full_ref[tr, k, 0:8], 7, 0)], axis=0
        )

    def south_rows(tr, k, j):
        if j >= 8:
            return full_ref[tr, k, j - 8 : j - 8 + ROWS]
        return jnp.concatenate(
            [pltpu.roll(full_ref[tr, k, lat - 8 : lat], 1, 0), full_ref[tr, k, 0 : ROWS - 8]],
            axis=0,
        )

    def fluxes(r, _):
        for g in range(GROUPS):
            k = g * rows_e + r
            above, below = jnp.maximum(k - 1, 0), jnp.minimum(k + 1, levels - 1)
            level = (base + k).astype(jnp.float32)
            level_z = jnp.where(level >= 1.0, level + 1.0, HUGE)
            sides = [
                (west_patch(efx_ref[tr, r], g), east_patch(efx_ref[tr, r], g)) for tr in range(2)
            ]
            fxs, fys, fzs = [[], []], [[], []], [[], []]
            for j in range(0, lat, ROWS):
                js = slice(j, j + ROWS)
                mx = level < limits[0, js]
                my = level < limits[1, js]
                mz = level_z < limits[2, js]
                kh = jnp.concatenate(
                    [rows_of(kh_ref, v, k) for v in range(j // 8, (j + ROWS) // 8)], axis=0
                )
                kappa = jnp.where(level < limits[2, js], 0.25 * kh, 0.0)
                gx, gy, gz = [], [], []
                for tr in range(2):
                    gx.append(jnp.where(mx, gx_ref[tr, k, js], 0.0))
                    gy.append(diff(my, north_rows(tr, k, j), south_rows(tr, k, j)))
                    gz.append(diff(mz, full_ref[tr, below, js], full_ref[tr, above, js]))
                fx, fy, fz = flux_xyz(gx, gy, gz, kappa)
                for tr in range(2):
                    fxs[tr].append(fx[tr])
                    fys[tr].append(fy[tr])
                    fzs[tr].append(fz[tr])
            wet = level < limits[2]
            new = []
            for tr in range(2):
                fy = jnp.concatenate(fys[tr], axis=0)
                change = zonal_change(jnp.concatenate(fxs[tr], axis=0), *sides[tr], lane)
                change = change + (shift_north(fy) - shift_south(fy))
                new.append(full_ref[tr, k] + jnp.where(wet, change, 0.0))
            for tr in range(2):
                q_ref[tr, k] = new[tr]
                fz_ref[tr, k] = jnp.concatenate(fzs[tr], axis=0)
        return 0

    lax.fori_loop(0, rows_e, fluxes, 0)


def factor_kernel(
    kv_ref, b_ref, khb_ref, inv_ref, ei_ref, ratio_ref, a_ref, bb_ref, abc_ref, msg_ref
):
    levels, lat = kv_ref.shape[0], kv_ref.shape[1]
    base = lax.axis_index("dep") * levels
    bottom = slab_of(b_ref).astype(jnp.float32)

    def coupling(k):
        level = (base + k).astype(jnp.float32)
        level = jnp.where(level >= 1.0, level, HUGE)
        return jnp.where(level < bottom, slab_of(kv_ref, k), 0.0)

    top = coupling(0)
    e = jnp.zeros((lat, 128), jnp.float32)
    q = e
    za = jnp.ones((lat, 128), jnp.float32)
    for k in range(levels):
        low = coupling(k + 1) if k + 1 < levels else jnp.zeros((lat, 128), jnp.float32)
        eq = 1.0 + e * q
        inv = 1.0 / (eq + low)
        inv_ref[k] = inv
        ei = e * inv
        ei_ref[k] = ei
        ratio_ref[k] = low * inv
        za = inv if k == 0 else za * ei
        a_ref[k] = za
        q = eq * inv
        e = low
    bb_ref[levels - 1] = inv
    b = inv
    a = za
    for k in range(levels - 2, -1, -1):
        ratio = ratio_ref[k]
        b = ratio * b
        a = a_ref[k] + ratio * a
        bb_ref[k] = b
        a_ref[k] = a
    a = a + jnp.where(top > 0.0, 1.0 / jnp.maximum(top, 1e-30), HUGE)
    abc_ref[0] = a
    abc_ref[1] = inv
    abc_ref[2] = b
    upper = lax.rem(lax.axis_index("dep"), 2) == 0
    msg_ref[0] = jnp.where(upper, inv, a)
    msg_ref[1] = b
    msg_ref[2] = jnp.where(upper, khb_ref[1], khb_ref[0])


def solve_kernel(
    full_ref, q_ref, fz_ref, ea_ref, ek_ref, eb_ref, bmx_ref, b_ref, kh_ref,
    first_ref, second_ref, inv_ref, ei_ref, ratio_ref, red_ref, pair_ref,
    y_ref, m3_ref, m2_ref, m1_ref, both_ref, own_ref,
    pad, epad, halo,
):
    levels, lat = q_ref.shape[1], q_ref.shape[2]
    rows_e = levels // GROUPS
    last = levels - 1
    top = rows_e - 1
    me = lax.axis_index("dep")
    base = me * levels
    parity = lax.rem(me, 2)
    outer = (me == 0) | (me == 3)
    upper = parity == 0
    sign = jnp.where(me < 2, 1.0, -1.0)
    lane = lane_ids(lat)
    halo[0, 0 : 4 * lat + 16] = first_ref[...]
    halo[0, 4 * lat + 16 : 5 * lat + 16] = pair_ref[2]
    halo[1] = second_ref[0 : 5 * lat + 16]
    above_ref, below_ref = halo.at[1 - parity], halo.at[parity]

    share = red_ref[0]
    both = red_ref[2] + second_ref[5 * lat + 16 : 6 * lat + 16]
    cross = share / both
    inside = red_ref[1] + share * cross
    for n, value in enumerate((share, red_ref[1], both)):
        own_ref[n] = value
    both_ref[...] = both

    eb = eb_ref[...]
    ebx, eby = edge_limits(eb)
    level0 = (base + (lane // STRIP) * rows_e).astype(jnp.float32)
    for tr in range(2):
        pad[tr, 0] = above_ref[(2 + tr) * lat : (3 + tr) * lat]
        pad[tr, 1] = above_ref[tr * lat : (1 + tr) * lat]
        for n, k in enumerate((0, 1, 2, last - 2, last - 1, last)):
            pad[tr, n + 2] = full_ref[tr, k]
        pad[tr, 8] = below_ref[tr * lat : (1 + tr) * lat]
        pad[tr, 9] = below_ref[(2 + tr) * lat : (3 + tr) * lat]
        for r in range(rows_e):
            epad[tr, r + 1] = ea_ref[tr, r]
        at = 4 * lat + 8 * tr
        corner_up = unfold_strip(above_ref[at : at + 8], 3 * STRIP + 8, lat // 8)
        corner_dn = unfold_strip(below_ref[at : at + 8], 8, lat // 8)
        epad[tr, 0] = roll_lanes(
            jnp.where(lane >= 3 * STRIP, corner_up, ea_ref[tr, top]), STRIP
        )
        epad[tr, rows_e + 1] = roll_lanes(
            jnp.where(lane < STRIP, corner_dn, ea_ref[tr, 0]), -STRIP
        )
    efx = {
        r + 1: edge_flux_row(r, epad, ek_ref[r], eb, ebx, eby, level0) for r in (0, top)
    }

    bottom = slab_of(b_ref).astype(jnp.float32)
    bmy = lat_limits(bottom)
    bmx = bmx_ref[...]
    ends = (
        (1, -1, 0, 0, above_ref[4 * lat + 16 : 5 * lat + 16], True),
        (2, 0, 1, 0, slab_of(kh_ref, 0), False),
        (7, last, top + 1, 3, slab_of(kh_ref, last), False),
        (8, last + 1, top + 2, 3, below_ref[4 * lat + 16 : 5 * lat + 16], True),
    )
    spread, end_flux = {}, {}
    for n, k, er, g, kappa_slab, only_z in ends:
        level = (base + k).astype(jnp.float32)
        level_z = jnp.where(level >= 1.0, level + 1.0, HUGE)
        level_h = jnp.where(level >= 0.0, level, HUGE)
        mx = level_h < bmx
        my = level_h < bmy
        mz = level_z < bottom
        kappa = jnp.where(level_h < bottom, 0.25 * kappa_slab, 0.0)
        gx, gy, gz = [], [], []
        for tr in range(2):
            slab, main = epad[tr, er], pad[tr, n]
            change = zonal_change(main, west_patch(slab, g), east_patch(slab, g), lane)
            gx.append(jnp.where(mx, change, 0.0))
            gy.append(diff(my, shift_north(main), shift_south(main)))
            gz.append(diff(mz, pad[tr, n + 1], pad[tr, n - 1]))
        fx, fy, fz = flux_xyz(gx, gy, gz, kappa, not only_z)
        for tr in range(2):
            end_flux[k, tr] = fz[tr]
            if not only_z:
                spread[k, tr] = divergence(fx[tr], fy[tr], efx[er][tr], g, lane)

    def vertical_flux(tr, k):
        return end_flux[k, tr] if (k, tr) in end_flux else fz_ref[tr, k]

    z = [None, None]
    for pair in range(0, levels, 2):
        made = []
        for k in (pair, pair + 1):
            level = (base + k).astype(jnp.float32)
            wet = level < bottom
            for tr in range(2):
                change = vertical_flux(tr, k + 1) - vertical_flux(tr, k - 1)
                if k == 0 or k == last:
                    change = change + spread[k, tr]
                    start = pad[tr, 2 if k == 0 else 7]
                else:
                    start = q_ref[tr, k]
                rhs = start + jnp.where(wet, change, 0.0)
                new = rhs * inv_ref[k]
                z[tr] = new if k == 0 else new + ei_ref[k] * z[tr]
                made.append((tr, k, z[tr]))
        for tr, k, new in made:
            y_ref[tr, k] = new
    low = list(z)
    for pair in range(last - 1, -1, -2):
        made = []
        for k in (pair, pair - 1):
            if k < 0:
                continue
            ratio = ratio_ref[k]
            z = [y_ref[tr, k] + ratio * z[tr] for tr in range(2)]
            made += [(tr, k, z[tr]) for tr in range(2)]
        for tr, k, new in made:
            y_ref[tr, k] = new
    for tr in range(2):
        near = jnp.where(upper, low[tr], z[tr])
        far = jnp.where(upper, z[tr], low[tr])
        m1_ref[tr] = jnp.where(outer, near, sign * (inside * near - cross * far))
        value = jnp.where(outer, share * near, far - share * near)
        m2_ref[tr] = value
        m3_ref[tr] = value


def finish_kernel(
    y_ref, a_ref, bb_ref, own_ref, r3_ref, r2_ref, r1_ref, both_ref, out_hbm, out, sems
):
    levels = y_ref.shape[1]
    me = lax.axis_index("dep")
    upper = lax.rem(me, 2) == 0
    outer = (me == 0) | (me == 3)
    sign = jnp.where(me < 2, 1.0, -1.0)
    share, inv_t = own_ref[0], own_ref[1]
    inv_e = 1.0 / jnp.where(outer, both_ref[...], own_ref[2])
    cross = share * inv_e
    inside = inv_t + share * cross
    tops, lows = [], []
    for tr in range(2):
        y_top, y_low = y_ref[tr, 0], y_ref[tr, levels - 1]
        near = jnp.where(upper, y_low, y_top)
        far = jnp.where(upper, y_top, y_low)
        mate, across = r1_ref[tr], r2_ref[tr] + r3_ref[tr]
        pair_flux = jnp.where(
            outer,
            mate + sign * (cross * across - inside * near),
            sign * (inside * (near - mate) + cross * (across - far)),
        )
        middle = sign * (inv_e * (across - far + share * near) - cross * mate)
        middle = jnp.where(outer, 0.0, middle)
        tops.append(jnp.where(upper, middle, pair_flux))
        lows.append(jnp.where(upper, pair_flux, middle))
    step, regs = 2, y_ref.shape[2] // 8
    copies = []
    for part in range(levels // step):
        made = {}
        for k in range(part * step, (part + 1) * step):
            a, b = a_ref[k], bb_ref[k]
            for tr in range(2):
                made[tr, k] = y_ref[tr, k] - tops[tr] * a + lows[tr] * b
        for (tr, k), new in made.items():
            for v in range(regs):
                out[tr, k, pl.ds(v, 8, regs), :] = new[8 * v : 8 * v + 8]
        for tr in range(2):
            span = (tr, pl.ds(part * step, step))
            copies.append(
                pltpu.make_async_copy(out.at[span], out_hbm.at[span], sems.at[tr, part])
            )
            copies[-1].start()
    for copy in copies:
        copy.wait()


def per_device(tracers, u_east, v_north, kappa_h, kappa_v, bottom):
    _, levels, lat, lon = tracers.shape
    rows_e = levels // GROUPS
    lon_n, dep_n = lax.axis_size("lon"), lax.axis_size("dep")
    east = [(i, (i + 1) % lon_n) for i in range(lon_n)]
    west = [(t, s) for s, t in east]
    slab = lat * lon * 4
    slabs = lambda *lead: f32(*lead, lat, lon)
    work = lambda *lead: pltpu.VMEM(lead + (lat, lon), jnp.float32)

    with jax.named_scope("pack"):
        sw, se, bp, ww, we, t0, t1, u, v, khb = call(
            pack_kernel,
            (slabs(rows_e),) * 2 + (slabs(),) + (slabs(rows_e - 1),) * 2 + (slabs(levels),) * 4
            + (slabs(2),),
            [
                work(levels), pltpu.VMEM((lat, lon), jnp.int32), work(rows_e),
                pltpu.SemaphoreType.DMA((GROUPS, 4)), pltpu.SemaphoreType.DMA((2,)),
            ],
            (tracers, u_east, v_north, kappa_h, bottom), 10**6, 6 * levels * slab, 50.5,
            in_specs=[HBM] * 5,
        )
    with jax.named_scope("lon_halo"):
        r_east = lax.ppermute(ww, "lon", west)
        r_west = lax.ppermute(we, "lon", east)
    with jax.named_scope("factor"):
        inv, ei, ratio, a_end, b_end, abc, msg = call(
            factor_kernel, (slabs(levels),) * 5 + (slabs(3),) * 2, [],
            (kappa_v, bottom, khb), 10**7, 6 * levels * slab, 16,
        )
    swap = [(i, i ^ 1) for i in range(dep_n)]
    with jax.named_scope("pair_coefficients"):
        pair = lax.ppermute(msg, "dep", swap)
    half = levels // 2

    def advect_half(start, earlier):
        return call(
            functools.partial(advect_kernel, start), slabs(2, half),
            [work(2, 2 * half), work(5, half)],
            (t0, t1, u, v, bottom, earlier), 10**7, 4 * levels * slab, 16,
        )

    with jax.named_scope("advect_north"):
        north_half = advect_half(0, abc)
    with jax.named_scope("advect_south"):
        south_half = advect_half(half, abc)
    with jax.named_scope("own_strips"):
        own_strips, own_bottom = call(
            own_kernel, (slabs(4, rows_e), slabs()), [],
            (sw, se, bp, abc), 10**6, 8 * rows_e * slab, 16,
        )
    rows_pay = 5 * lat + 16
    with jax.named_scope("advect_edge"):
        ea, ek, eb, bmx, first, second, red = call(
            edge_kernel,
            (
                slabs(2, rows_e), slabs(rows_e), slabs(), slabs(),
                f32(rows_pay - lat, lon), f32(rows_pay + lat, lon), slabs(3),
            ),
            [
                work(2, 2 * rows_e), work(5, rows_e), work(4, rows_e),
                pltpu.VMEM((2, rows_pay, lon), jnp.float32),
            ],
            (own_strips, own_bottom, r_east, r_west, bottom, north_half, south_half, kappa_h, abc, pair),
            10**6, 3 * levels * slab, 16,
        )
    other = []
    for i in range(lon_n * dep_n):
        row, place = divmod(i, dep_n)
        if place in (0, dep_n - 1):
            other.append((i, (row ^ 1) * dep_n + place))
        else:
            other.append((i, i + 1 if place % 2 else i - 1))
    with jax.named_scope("dep_halo"):
        first = lax.ppermute(first, "dep", swap)
        second = lax.ppermute(second, ("lon", "dep"), other)
    with jax.named_scope("patch"):
        full, gx, efx = call(
            patch_kernel, (slabs(2, levels), slabs(2, levels), slabs(2, rows_e)),
            [work(2, rows_e + 2)],
            (north_half, south_half, ea, ek, eb), 10**7, 8 * levels * slab, 16,
        )
    with jax.named_scope("fluxes"):
        q_part, fz = call(
            flux_kernel, (slabs(2, levels), slabs(2, levels)), [work(3)],
            (full, gx, efx, bmx, bottom, kappa_h), 10**7, 10 * levels * slab, 16,
        )
    with jax.named_scope("solve"):
        y, m3, m2, m1, both, own = call(
            solve_kernel, (slabs(2, levels), slabs(2), slabs(2), slabs(2), slabs(), slabs(3)),
            [
                work(2, 10), work(2, rows_e + 2),
                pltpu.VMEM((2, rows_pay, lon), jnp.float32),
            ],
            (
                full, q_part, fz, ea, ek, eb, bmx, bottom, kappa_h, first, second,
                inv, ei, ratio, red, pair,
            ),
            10**7, 12 * levels * slab, 24,
        )
    with jax.named_scope("interfaces"):
        m3 = lax.ppermute(m3, "dep", [(i, i ^ 3) for i in range(dep_n)])
        m2 = lax.ppermute(m2, "dep", [(i, i ^ 2) for i in range(dep_n)])
        m1 = lax.ppermute(m1, "dep", swap)
        both = lax.ppermute(both, "dep", swap)
    with jax.named_scope("finish"):
        return call(
            finish_kernel, slabs(2, levels),
            [work(2, levels), pltpu.SemaphoreType.DMA((2, levels // 2))],
            (y, a_end, b_end, own, m3, m2, m1, both), 10**6, 6 * levels * slab, 16,
            out_specs=HBM,
        )


def solution(mesh):
    in_specs = (
        P(None, "dep", None, "lon"),
        P("dep", None, "lon"),
        P("dep", None, "lon"),
        P("dep", None, "lon"),
        P("dep", None, "lon"),
        P(None, "lon"),
    )
    out_specs = P(None, "dep", None, "lon")
    return jax.shard_map(
        per_device, mesh=mesh, in_specs=in_specs, out_specs=out_specs, check_vma=False
    )
```

```python
import functools

import jax
import jax.numpy as jnp
from jax import lax
from jax.experimental import pallas as pl
from jax.experimental.pallas import tpu as pltpu
from jax.sharding import PartitionSpec as P

SUB = 4
THERMAL = 0.2
HALINE = 0.8
GROUPS = 4
ROWS = 32
STRIP = 32
HUGE = 1e30
MIB = 1024 * 1024

VMEM = pl.BlockSpec(memory_space=pltpu.VMEM)
HBM = pl.BlockSpec(memory_space=pltpu.HBM)


def lane_ids(rows):
    return lax.broadcasted_iota(jnp.int32, (rows, 128), 1)


def roll_lanes(x, amount):
    amount = amount % 128
    return x if amount == 0 else pltpu.roll(x, amount, 1)


def shift_north(x):
    return jnp.concatenate([x[8:], pltpu.roll(x[:8], 7, 0)], axis=0)


def shift_south(x):
    return jnp.concatenate([pltpu.roll(x[-8:], 1, 0), x[:-8]], axis=0)


def rows_of(ref, v, *lead):
    return ref[(*lead, pl.ds(v, 8, ref.shape[-2] // 8), slice(None))]


def neighbours(regs, v):
    north = regs[v + 1] if v + 1 < len(regs) else pltpu.roll(regs[0], 7, 0)
    south = regs[v - 1] if v > 0 else pltpu.roll(regs[-1], 1, 0)
    return north, south


def slab_of(ref, *lead):
    return jnp.concatenate([rows_of(ref, v, *lead) for v in range(ref.shape[-2] // 8)], axis=0)


def call(body, out_shape, scratch, args, flops, in_bytes, limit, in_specs=None, out_specs=None):
    return pl.pallas_call(
        body,
        out_shape=out_shape,
        in_specs=in_specs or [VMEM] * len(args),
        out_specs=out_specs or jax.tree.map(lambda _: VMEM, out_shape),
        scratch_shapes=scratch,
        compiler_params=pltpu.CompilerParams(vmem_limit_bytes=int(limit * MIB)),
        cost_estimate=pl.CostEstimate(flops=flops, bytes_accessed=in_bytes, transcendentals=0),
    )(*args)


def f32(*shape):
    return jax.ShapeDtypeStruct(shape, jnp.float32)


def pack_kernel(
    t_hbm, u_hbm, v_hbm, kh_hbm, b_hbm,
    sw_ref, se_ref, bp_ref, ww_ref, we_ref, t0_ref, t1_ref, u_ref, v_ref, khb_ref,
    kh_buf, b_buf, first_buf, sems, more_sems,
):
    rows_e = u_ref.shape[0] // GROUPS
    lat = u_ref.shape[1]
    lane = lane_ids(lat)
    fields = ((t_hbm.at[0], t0_ref), (t_hbm.at[1], t1_ref), (u_hbm, u_ref), (v_hbm, v_ref))
    groups = [
        [
            pltpu.make_async_copy(
                src.at[pl.ds(g * rows_e, rows_e)], dst.at[pl.ds(g * rows_e, rows_e)], sems.at[g, n]
            )
            for n, (src, dst) in enumerate(fields)
        ]
        for g in range(GROUPS)
    ]
    tail = [
        pltpu.make_async_copy(b_hbm, b_buf, more_sems.at[0]),
        pltpu.make_async_copy(kh_hbm, kh_buf, more_sems.at[1]),
    ]
    for copy in sum(groups, []) + tail:
        copy.start()
    for g in range(GROUPS):
        for copy in groups[g]:
            copy.wait()
        for batch in (range(0, rows_e // 2), range(rows_e // 2, rows_e)):
            rolled = {
                (r, f): roll_lanes(slab_of(ref, g * rows_e + r), STRIP * g + 8 * f)
                for r in batch
                for f, ref in enumerate((t0_ref, t1_ref, u_ref, v_ref))
            }
            done = []
            for r in batch:
                low = rolled[r, 0]
                high = None
                if g > 0:
                    low = jnp.where(lane >= STRIP * g, low, sw_ref[r])
                    high = jnp.where(lane >= STRIP * g - 8, rolled[r, 0], se_ref[r])
                for f in range(1, 4):
                    start = STRIP * g + 8 * f
                    low = jnp.where(lane >= start, rolled[r, f], low)
                    if high is None:
                        high = rolled[r, f]
                    else:
                        high = jnp.where(lane >= start - 8, rolled[r, f], high)
                if g == GROUPS - 1:
                    high = jnp.where(lane >= 120, first_buf[r], high)
                done.append((r, low, high))
            for r, low, high in done:
                if g == 0:
                    first_buf[r] = rolled[r, 0]
                sw_ref[r] = low
                se_ref[r] = high
    for copy in tail:
        copy.wait()
    bottom = slab_of(b_buf).astype(jnp.float32)
    place = bottom
    for g in range(1, GROUPS):
        place = jnp.where(lane >= STRIP * g - 8, roll_lanes(bottom, STRIP * g), place)
    place = jnp.where(lane >= 120, bottom, place)
    bp_ref[...] = place

    def kappa(r):
        out = None
        for g in range(GROUPS):
            rolled = roll_lanes(slab_of(kh_buf, g * rows_e + r), STRIP * g + 23)
            out = rolled if g == 0 else jnp.where(lane >= STRIP * g + 8, rolled, out)
        return out

    khb_ref[0] = slab_of(kh_buf, 0)
    khb_ref[1] = slab_of(kh_buf, GROUPS * rows_e - 1)
    last = rows_e - 1
    kappa_last = kappa(last)
    lane_q = lane % STRIP
    low_last, high_last = sw_ref[last], se_ref[last]
    wires = []
    for r in range(last):
        k = kappa(r)
        low, high = sw_ref[r], se_ref[r]
        west = (low, roll_lanes(low, -2), roll_lanes(low, -4), roll_lanes(low, -6), k)
        east = (
            roll_lanes(high, 6), roll_lanes(high, 4), roll_lanes(high, 2), roll_lanes(high, -1),
            roll_lanes(k, 1),
        )
        west += (roll_lanes(low_last, 24 - 8 * r),)
        east += (roll_lanes(high_last, 5 if r == 3 else 30 - 8 * r),)
        if r == 3:
            west += (roll_lanes(kappa_last, 6),)
            east += (roll_lanes(kappa_last, 7),)
        else:
            west += (roll_lanes(place, 30 - 2 * r),)
            east += (roll_lanes(place, 36 - 2 * r),)
        starts = (6, 12, 18, 23, 24, 29 if r == 3 else 30)
        for ref, parts in ((ww_ref, west), (we_ref, east)):
            wire = parts[0]
            for start, part in zip(starts, parts[1:]):
                wire = jnp.where(lane_q >= start, part, wire)
            wires.append((ref, r, wire))
    for ref, r, wire in wires:
        ref[r] = wire


def advect_block(slabs, get_c, get_u, get_v, get_level, bx, by, buf, coef, put):
    regs = bx.shape[0] // 8
    for i, slab in enumerate(slabs):
        level = get_level(slab)
        um = jnp.where(level < bx, get_u(slab), 0.0)
        vm = jnp.where(level < by, get_v(slab), 0.0)
        uw = roll_lanes(um, 1)
        vs = shift_south(vm)
        coef[0, i] = (
            1.0
            - jnp.maximum(um, 0.0)
            + jnp.minimum(uw, 0.0)
            - jnp.maximum(vm, 0.0)
            + jnp.minimum(vs, 0.0)
        )
        coef[1, i] = -jnp.minimum(um, 0.0)
        coef[2, i] = jnp.maximum(uw, 0.0)
        coef[3, i] = -jnp.minimum(vm, 0.0)
        coef[4, i] = jnp.maximum(vs, 0.0)
        for tr in range(2):
            buf[0, 2 * i + tr] = get_c(tr, slab)
    for step in range(SUB):
        src, dst = step % 2, (step + 1) % 2
        for i, slab in enumerate(slabs):
            now = [
                [buf[src, 2 * i + tr, 8 * v : 8 * v + 8] for v in range(regs)] for tr in range(2)
            ]
            for v in range(regs):
                js = slice(8 * v, 8 * v + 8)
                a, b, c, d, e = (coef[n, i, js] for n in range(5))
                for tr in range(2):
                    here = now[tr][v]
                    north, south = neighbours(now[tr], v)
                    new = (
                        a * here
                        + b * roll_lanes(here, -1)
                        + c * roll_lanes(here, 1)
                        + d * north
                        + e * south
                    )
                    if step < SUB - 1:
                        buf[dst, 2 * i + tr, js] = new
                    else:
                        put(tr, slab, js, new)


def face_limits(bottom):
    lat = bottom.shape[0]
    rows = lax.broadcasted_iota(jnp.int32, bottom.shape, 0)
    north = jnp.where(rows == lat - 1, 0.0, shift_north(bottom))
    return jnp.minimum(bottom, roll_lanes(bottom, -1)), jnp.minimum(bottom, north)


def lat_limits(bottom):
    lat = bottom.shape[0]
    rows = lax.broadcasted_iota(jnp.int32, bottom.shape, 0)
    north = jnp.where(rows == lat - 1, 0.0, shift_north(bottom))
    south = jnp.where(rows == 0, 0.0, shift_south(bottom))
    return jnp.minimum(north, south)


def advect_kernel(start, t0_ref, t1_ref, u_ref, v_ref, b_ref, earlier_ref, out_ref, buf, coef):
    del earlier_ref
    count, lat = out_ref.shape[1], out_ref.shape[2]
    base = lax.axis_index("dep") * t0_ref.shape[0] + start
    bx, by = face_limits(slab_of(b_ref).astype(jnp.float32))

    def put(tr, slab, js, new):
        out_ref[tr, slab, js] = new

    advect_block(
        list(range(count)),
        lambda tr, s: slab_of((t0_ref, t1_ref)[tr], start + s),
        lambda s: slab_of(u_ref, start + s),
        lambda s: slab_of(v_ref, start + s),
        lambda s: (base + s).astype(jnp.float32),
        bx,
        by,
        buf,
        coef,
        put,
    )


def join(lane_q, own, east, west):
    halo = jnp.where(lane_q < 16, east, west)
    return jnp.where((lane_q >= 8) & (lane_q < 24), halo, own)


def west_patch(slab, g):
    return roll_lanes(slab, -(STRIP * g + 24))


def east_patch(slab, g):
    return roll_lanes(slab, 120 - STRIP * g)


def patched(main, slab, g, lane):
    return jnp.where(
        lane < 4, west_patch(slab, g), jnp.where(lane >= 124, east_patch(slab, g), main)
    )


def own_kernel(sw_ref, se_ref, bp_ref, earlier_ref, own_ref, ownb_ref):
    del earlier_ref
    rows_e, lat = sw_ref.shape[0], sw_ref.shape[1]
    lane_q = lane_ids(lat) % STRIP
    for r in range(rows_e):
        made = [
            jnp.where(
                lane_q < 16, roll_lanes(se_ref[r], 8 - 8 * f), roll_lanes(sw_ref[r], 24 - 8 * f)
            )
            for f in range(4)
        ]
        for f in range(4):
            own_ref[f, r] = made[f]
    place = bp_ref[...]
    ownb_ref[...] = jnp.where(lane_q < 16, roll_lanes(place, 8), roll_lanes(place, 24))


def pair_response(abc_ref, pair_ref, me):
    upper = lax.rem(me, 2) == 0
    low_pair = me < 2
    inv_t = 1.0 / (pair_ref[0] + jnp.where(upper, abc_ref[1], abc_ref[0]))
    c_pair = jnp.where(upper == low_pair, pair_ref[1], abc_ref[2])
    share = c_pair * inv_t
    return share, inv_t, jnp.where(upper, abc_ref[0], abc_ref[1]) - c_pair * share


def fold_strip(slab, place):
    lane = lane_ids(8)
    folded = jnp.zeros((8, 128), jnp.float32)
    for v in range(slab.shape[0] // 8):
        rolled = roll_lanes(slab[8 * v : 8 * v + 8], 16 * v - place)
        folded = jnp.where(lane >= 16 * v, rolled, folded)
    return folded


def unfold_strip(folded, place, regs):
    return jnp.concatenate([roll_lanes(folded, place - 16 * v) for v in range(regs)], axis=0)


def edge_kernel(
    own_ref, ownb_ref, re_ref, rw_ref, b_ref, north_half, south_half, kh_ref, abc_ref, pair_ref,
    ea_ref, ek_ref, eb_ref, bmx_ref, first_ref, second_ref, red_ref,
    buf, coef, fields, pay,
):
    levels, lat = kh_ref.shape[0], kh_ref.shape[1]
    rows_e = levels // GROUPS
    me = lax.axis_index("dep")
    base = me * levels
    parity = lax.rem(me, 2)
    up_ref, down_ref = pay.at[1 - parity], pay.at[parity]
    lane = lane_ids(lat)
    lane_q = lane % STRIP
    bottom = slab_of(b_ref).astype(jnp.float32)
    east = [roll_lanes(re_ref[r], 2 * r - 22) for r in range(3)]
    west = [roll_lanes(rw_ref[r], 2 * r - 12) for r in range(3)]
    eb = join(
        lane_q,
        ownb_ref[...],
        jnp.where(lane_q < 10, east[0], jnp.where(lane_q < 12, east[1], east[2])),
        jnp.where(lane_q < 20, west[0], jnp.where(lane_q < 22, west[1], west[2])),
    )
    eb_ref[...] = eb
    b_west = roll_lanes(jnp.where(lane == 127, west_patch(eb, 0), bottom), 1)
    b_east = roll_lanes(jnp.where(lane == 0, east_patch(eb, 0), bottom), -1)
    bmx_ref[...] = jnp.minimum(b_west, b_east)
    last = rows_e - 1
    for r in range(rows_e):
        at, shift_e, shift_w = (3, -21, -6) if r == last else (r, -15, 0)
        ek_ref[r] = jnp.where(
            lane_q < 16, roll_lanes(re_ref[at], shift_e), roll_lanes(rw_ref[at], shift_w)
        )
        made = []
        for f in range(4):
            at, start = (f, 24) if r == last else (r, 6 * f)
            made.append(
                join(
                    lane_q,
                    own_ref[f, r],
                    roll_lanes(re_ref[at], 8 - start),
                    roll_lanes(rw_ref[at], (19 if f == 3 else 18) - start),
                )
            )
        for f in range(4):
            fields[f, r] = made[f]
    bx, by = face_limits(eb)
    level0 = (base + (lane // STRIP) * rows_e).astype(jnp.float32)

    def put(tr, slab, js, new):
        ea_ref[tr, slab, js] = new

    advect_block(
        list(range(rows_e)),
        lambda tr, s: fields[tr, s],
        lambda s: fields[2, s],
        lambda s: fields[3, s],
        lambda s: level0 + float(s),
        bx,
        by,
        buf,
        coef,
        put,
    )
    top, half = rows_e - 1, levels // 2
    for tr in range(2):
        for n, (k, slab) in enumerate(((0, ea_ref[tr, 0]), (1, ea_ref[tr, 1]))):
            at = (2 * n + tr) * lat
            up_ref[at : at + lat] = patched(north_half[tr, k], slab, 0, lane)
        for n, (k, slab) in enumerate(
            ((half - 1, ea_ref[tr, top]), (half - 2, ea_ref[tr, top - 1]))
        ):
            at = (2 * n + tr) * lat
            down_ref[at : at + lat] = patched(south_half[tr, k], slab, 3, lane)
        at = 4 * lat + 8 * tr
        up_ref[at : at + 8] = fold_strip(ea_ref[tr, 0], 8)
        down_ref[at : at + 8] = fold_strip(ea_ref[tr, top], 3 * STRIP + 8)
    up_ref[4 * lat + 16 : 5 * lat + 16] = slab_of(kh_ref, 0)
    down_ref[4 * lat + 16 : 5 * lat + 16] = slab_of(kh_ref, levels - 1)
    first_ref[...] = pay[0, 0 : 4 * lat + 16]
    second_ref[0 : 5 * lat + 16] = pay[1]
    response = pair_response(abc_ref, pair_ref, me)
    for n in range(3):
        red_ref[n] = response[n]
    second_ref[5 * lat + 16 : 6 * lat + 16] = response[2]


def slopes(gx, gy, gz):
    rx, ry, rz = (-0.5 * THERMAL * g[0] + 0.5 * HALINE * g[1] for g in (gx, gy, gz))
    scale = rz / (1.0 + rx * rx + ry * ry + rz * rz)
    return rx * scale, ry * scale


def flux_xyz(gx, gy, gz, kappa, need_xy=True):
    sx, sy = slopes(gx, gy, gz)
    kx, ky = kappa * sx, kappa * sy
    kz = kx * sx + ky * sy
    fz = [kx * gx[n] + ky * gy[n] + kz * gz[n] for n in range(2)]
    if not need_xy:
        return None, None, fz
    fx = [kappa * gx[n] + kx * gz[n] for n in range(2)]
    fy = [kappa * gy[n] + ky * gz[n] for n in range(2)]
    return fx, fy, fz


def flux_x_edge(gx, gy, gz, kappa):
    sx, _ = slopes(gx, gy, gz)
    kx = kappa * sx
    return [kappa * gx[n] + kx * gz[n] for n in range(2)]


def diff(mask, high, low):
    return jnp.where(mask, high - low, 0.0)


def edge_flux_row(r, rows, ek, eb, ebx, eby, level0):
    level = level0 + r
    mx = level < ebx
    my = level < eby
    mz = (level + 1.0 < eb) & (level >= 1.0)
    kappa = jnp.where((level < eb) & (level >= 0.0), 0.25 * ek, 0.0)
    gx, gy, gz = [], [], []
    for tr in range(2):
        here = rows[tr, r + 1]
        gx.append(diff(mx, roll_lanes(here, -1), roll_lanes(here, 1)))
        gy.append(diff(my, shift_north(here), shift_south(here)))
        gz.append(diff(mz, rows[tr, r + 2], rows[tr, r]))
    return flux_x_edge(gx, gy, gz, kappa)


def edge_limits(eb):
    return (
        jnp.minimum(roll_lanes(eb, 1), roll_lanes(eb, -1)),
        lat_limits(eb),
    )


def zonal_change(fx, west, east, lane):
    return roll_lanes(jnp.where(lane == 0, east, fx), -1) - roll_lanes(
        jnp.where(lane == 127, west, fx), 1
    )


def divergence(fx, fy, slab, g, lane):
    return zonal_change(fx, west_patch(slab, g), east_patch(slab, g), lane) + (
        shift_north(fy) - shift_south(fy)
    )


def patch_kernel(
    north_half, south_half, ea_ref, ek_ref, eb_ref,
    full_ref, gx_ref, efx_ref,
    rows,
):
    levels, lat = full_ref.shape[1], full_ref.shape[2]
    rows_e = levels // GROUPS
    base = lax.axis_index("dep") * levels
    lane = lane_ids(lat)
    eb = eb_ref[...]
    ebx, eby = edge_limits(eb)
    level0 = (base + (lane // STRIP) * rows_e).astype(jnp.float32)
    for tr in range(2):
        for r in range(rows_e):
            rows[tr, r + 1] = ea_ref[tr, r]
        rows[tr, 0] = roll_lanes(ea_ref[tr, rows_e - 1], STRIP)
        rows[tr, rows_e + 1] = roll_lanes(ea_ref[tr, 0], -STRIP)
    found = [
        edge_flux_row(r, rows, ek_ref[r], eb, ebx, eby, level0) for r in range(rows_e)
    ]
    for r in range(rows_e):
        for tr in range(2):
            efx_ref[tr, r] = found[r][tr]

    lane = lane_ids(ROWS)
    units = [(g, slice(j, j + ROWS)) for g in range(GROUPS) for j in range(0, lat, ROWS)]

    def patch(r, _):
        def fetch(unit):
            g, js = unit
            strips = [ea_ref[tr, r, js] for tr in range(2)]
            half = (north_half, south_half)[2 * g // GROUPS]
            mains = [half[tr, g % (GROUPS // 2) * rows_e + r, js] for tr in range(2)]
            return [(west_patch(x, g), east_patch(x, g), y) for x, y in zip(strips, mains)]

        def put(unit, mains, rolled):
            g, js = unit
            for tr in range(2):
                full_ref[tr, g * rows_e + r, js] = mains[tr]
                gx_ref[tr, g * rows_e + r, js] = rolled[tr][0] - rolled[tr][1]

        waiting = None
        fetched = fetch(units[0])
        for n, unit in enumerate(units):
            now = fetched
            fetched = fetch(units[n + 1]) if n + 1 < len(units) else None
            mains, rolled = [], []
            for west, east, main in now:
                main = jnp.where(lane < 4, west, jnp.where(lane >= 124, east, main))
                mains.append(main)
                rolled.append(
                    (
                        roll_lanes(jnp.where(lane == 0, east, main), -1),
                        roll_lanes(jnp.where(lane == 127, west, main), 1),
                    )
                )
            if waiting is not None:
                put(*waiting)
            waiting = (unit, mains, rolled)
        put(*waiting)
        return 0

    lax.fori_loop(0, rows_e, patch, 0)


def flux_kernel(
    full_ref, gx_ref, efx_ref, bmx_ref, b_ref, kh_ref,
    q_ref, fz_ref,
    limits,
):
    levels, lat = full_ref.shape[1], full_ref.shape[2]
    rows_e = levels // GROUPS
    base = lax.axis_index("dep") * levels
    lane = lane_ids(lat)
    bottom = slab_of(b_ref).astype(jnp.float32)
    limits[0] = bmx_ref[...]
    limits[1] = lat_limits(bottom)
    limits[2] = bottom

    def north_rows(tr, k, j):
        if j + 8 + ROWS <= lat:
            return full_ref[tr, k, j + 8 : j + 8 + ROWS]
        return jnp.concatenate(
            [full_ref[tr, k, j + 8 : lat], pltpu.roll(full_ref[tr, k, 0:8], 7, 0)], axis=0
        )

    def south_rows(tr, k, j):
        if j >= 8:
            return full_ref[tr, k, j - 8 : j - 8 + ROWS]
        return jnp.concatenate(
            [pltpu.roll(full_ref[tr, k, lat - 8 : lat], 1, 0), full_ref[tr, k, 0 : ROWS - 8]],
            axis=0,
        )

    def fluxes(r, _):
        for g in range(GROUPS):
            k = g * rows_e + r
            above, below = jnp.maximum(k - 1, 0), jnp.minimum(k + 1, levels - 1)
            level = (base + k).astype(jnp.float32)
            level_z = jnp.where(level >= 1.0, level + 1.0, HUGE)
            sides = [
                (west_patch(efx_ref[tr, r], g), east_patch(efx_ref[tr, r], g)) for tr in range(2)
            ]
            fxs, fys, fzs = [[], []], [[], []], [[], []]
            for j in range(0, lat, ROWS):
                js = slice(j, j + ROWS)
                mx = level < limits[0, js]
                my = level < limits[1, js]
                mz = level_z < limits[2, js]
                kh = jnp.concatenate(
                    [rows_of(kh_ref, v, k) for v in range(j // 8, (j + ROWS) // 8)], axis=0
                )
                kappa = jnp.where(level < limits[2, js], 0.25 * kh, 0.0)
                gx, gy, gz = [], [], []
                for tr in range(2):
                    gx.append(jnp.where(mx, gx_ref[tr, k, js], 0.0))
                    gy.append(diff(my, north_rows(tr, k, j), south_rows(tr, k, j)))
                    gz.append(diff(mz, full_ref[tr, below, js], full_ref[tr, above, js]))
                fx, fy, fz = flux_xyz(gx, gy, gz, kappa)
                for tr in range(2):
                    fxs[tr].append(fx[tr])
                    fys[tr].append(fy[tr])
                    fzs[tr].append(fz[tr])
            wet = level < limits[2]
            new = []
            for tr in range(2):
                fy = jnp.concatenate(fys[tr], axis=0)
                change = zonal_change(jnp.concatenate(fxs[tr], axis=0), *sides[tr], lane)
                change = change + (shift_north(fy) - shift_south(fy))
                new.append(full_ref[tr, k] + jnp.where(wet, change, 0.0))
            for tr in range(2):
                q_ref[tr, k] = new[tr]
                fz_ref[tr, k] = jnp.concatenate(fzs[tr], axis=0)
        return 0

    lax.fori_loop(0, rows_e, fluxes, 0)


def factor_kernel(
    kv_ref, b_ref, khb_ref, inv_ref, ei_ref, ratio_ref, a_ref, bb_ref, abc_ref, msg_ref
):
    levels, lat = kv_ref.shape[0], kv_ref.shape[1]
    base = lax.axis_index("dep") * levels
    bottom = slab_of(b_ref).astype(jnp.float32)

    def coupling(k):
        level = (base + k).astype(jnp.float32)
        level = jnp.where(level >= 1.0, level, HUGE)
        return jnp.where(level < bottom, slab_of(kv_ref, k), 0.0)

    top = coupling(0)
    e = jnp.zeros((lat, 128), jnp.float32)
    q = e
    za = jnp.ones((lat, 128), jnp.float32)
    for k in range(levels):
        low = coupling(k + 1) if k + 1 < levels else jnp.zeros((lat, 128), jnp.float32)
        eq = 1.0 + e * q
        inv = 1.0 / (eq + low)
        inv_ref[k] = inv
        ei = e * inv
        ei_ref[k] = ei
        ratio_ref[k] = low * inv
        za = inv if k == 0 else za * ei
        a_ref[k] = za
        q = eq * inv
        e = low
    bb_ref[levels - 1] = inv
    b = inv
    a = za
    for k in range(levels - 2, -1, -1):
        ratio = ratio_ref[k]
        b = ratio * b
        a = a_ref[k] + ratio * a
        bb_ref[k] = b
        a_ref[k] = a
    a = a + jnp.where(top > 0.0, 1.0 / jnp.maximum(top, 1e-30), HUGE)
    abc_ref[0] = a
    abc_ref[1] = inv
    abc_ref[2] = b
    upper = lax.rem(lax.axis_index("dep"), 2) == 0
    msg_ref[0] = jnp.where(upper, inv, a)
    msg_ref[1] = b
    msg_ref[2] = jnp.where(upper, khb_ref[1], khb_ref[0])


def solve_kernel(
    full_ref, q_ref, fz_ref, ea_ref, ek_ref, eb_ref, bmx_ref, b_ref, kh_ref,
    first_ref, second_ref, inv_ref, ei_ref, ratio_ref, red_ref, pair_ref,
    y_ref, m2_ref, m3_ref, m1_ref, both_ref, own_ref,
    pad, epad, fze, halo,
):
    levels, lat = q_ref.shape[1], q_ref.shape[2]
    rows_e = levels // GROUPS
    last = levels - 1
    top = rows_e - 1
    me = lax.axis_index("dep")
    base = me * levels
    parity = lax.rem(me, 2)
    outer = (me == 0) | (me == 3)
    upper = parity == 0
    sign = jnp.where(me < 2, 1.0, -1.0)
    lane = lane_ids(lat)
    halo[0, 0 : 4 * lat + 16] = first_ref[...]
    halo[0, 4 * lat + 16 : 5 * lat + 16] = pair_ref[2]
    halo[1] = second_ref[0 : 5 * lat + 16]
    above_ref, below_ref = halo.at[1 - parity], halo.at[parity]

    share = red_ref[0]
    both = red_ref[2] + second_ref[5 * lat + 16 : 6 * lat + 16]
    cross = share / both
    inside = red_ref[1] + share * cross
    for n, value in enumerate((share, red_ref[1], both)):
        own_ref[n] = value
    both_ref[...] = both

    eb = eb_ref[...]
    ebx, eby = edge_limits(eb)
    level0 = (base + (lane // STRIP) * rows_e).astype(jnp.float32)
    for tr in range(2):
        pad[tr, 0] = above_ref[(2 + tr) * lat : (3 + tr) * lat]
        pad[tr, 1] = above_ref[tr * lat : (1 + tr) * lat]
        for n, k in enumerate((0, 1, 2, last - 2, last - 1, last)):
            pad[tr, n + 2] = full_ref[tr, k]
        pad[tr, 8] = below_ref[tr * lat : (1 + tr) * lat]
        pad[tr, 9] = below_ref[(2 + tr) * lat : (3 + tr) * lat]
        for r in range(rows_e):
            epad[tr, r + 1] = ea_ref[tr, r]
        at = 4 * lat + 8 * tr
        corner_up = unfold_strip(above_ref[at : at + 8], 3 * STRIP + 8, lat // 8)
        corner_dn = unfold_strip(below_ref[at : at + 8], 8, lat // 8)
        epad[tr, 0] = roll_lanes(
            jnp.where(lane >= 3 * STRIP, corner_up, ea_ref[tr, top]), STRIP
        )
        epad[tr, rows_e + 1] = roll_lanes(
            jnp.where(lane < STRIP, corner_dn, ea_ref[tr, 0]), -STRIP
        )
    efx = {
        r + 1: edge_flux_row(r, epad, ek_ref[r], eb, ebx, eby, level0) for r in (0, top)
    }

    bottom = slab_of(b_ref).astype(jnp.float32)
    bmy = lat_limits(bottom)
    bmx = bmx_ref[...]
    ends = (
        (1, -1, 0, 0, above_ref[4 * lat + 16 : 5 * lat + 16], True),
        (2, 0, 1, 0, slab_of(kh_ref, 0), False),
        (7, last, top + 1, 3, slab_of(kh_ref, last), False),
        (8, last + 1, top + 2, 3, below_ref[4 * lat + 16 : 5 * lat + 16], True),
    )
    spread = {}
    for m, (n, k, er, g, kappa_slab, only_z) in enumerate(ends):
        level = (base + k).astype(jnp.float32)
        level_z = jnp.where(level >= 1.0, level + 1.0, HUGE)
        level_h = jnp.where(level >= 0.0, level, HUGE)
        mx = level_h < bmx
        my = level_h < bmy
        mz = level_z < bottom
        kappa = jnp.where(level_h < bottom, 0.25 * kappa_slab, 0.0)
        gx, gy, gz = [], [], []
        for tr in range(2):
            slab, main = epad[tr, er], pad[tr, n]
            change = zonal_change(main, west_patch(slab, g), east_patch(slab, g), lane)
            gx.append(jnp.where(mx, change, 0.0))
            gy.append(diff(my, shift_north(main), shift_south(main)))
            gz.append(diff(mz, pad[tr, n + 1], pad[tr, n - 1]))
        fx, fy, fz = flux_xyz(gx, gy, gz, kappa, not only_z)
        for tr in range(2):
            fze[tr, m] = fz[tr]
            if not only_z:
                spread[k, tr] = divergence(fx[tr], fy[tr], efx[er][tr], g, lane)

    def vertical_flux(tr, k):
        place = {-1: 0, 0: 1, last: 2, last + 1: 3}.get(k)
        return fz_ref[tr, k] if place is None else fze[tr, place]

    z = [None, None]
    for k in range(levels):
        level = (base + k).astype(jnp.float32)
        wet = level < bottom
        for tr in range(2):
            change = vertical_flux(tr, k + 1) - vertical_flux(tr, k - 1)
            if k == 0 or k == last:
                change = change + spread[k, tr]
                start = pad[tr, 2 if k == 0 else 7]
            else:
                start = q_ref[tr, k]
            rhs = start + jnp.where(wet, change, 0.0)
            new = rhs * inv_ref[k]
            z[tr] = new if k == 0 else new + ei_ref[k] * z[tr]
        for tr in range(2):
            y_ref[tr, k] = z[tr]
    low = list(z)
    for k in range(last - 1, -1, -1):
        ratio = ratio_ref[k]
        z = [y_ref[tr, k] + ratio * z[tr] for tr in range(2)]
        for tr in range(2):
            y_ref[tr, k] = z[tr]
    for tr in range(2):
        near = jnp.where(upper, low[tr], z[tr])
        far = jnp.where(upper, z[tr], low[tr])
        m1_ref[tr] = jnp.where(outer, near, sign * (inside * near - cross * far))
        value = jnp.where(outer, share * near, far - share * near)
        m2_ref[tr] = value
        m3_ref[tr] = value


def finish_kernel(
    y_ref, a_ref, bb_ref, own_ref, r2_ref, r3_ref, r1_ref, both_ref, out_hbm, out, sems
):
    levels = y_ref.shape[1]
    me = lax.axis_index("dep")
    upper = lax.rem(me, 2) == 0
    outer = (me == 0) | (me == 3)
    sign = jnp.where(me < 2, 1.0, -1.0)
    share, inv_t = own_ref[0], own_ref[1]
    inv_e = 1.0 / jnp.where(outer, both_ref[...], own_ref[2])
    cross = share * inv_e
    inside = inv_t + share * cross
    tops, lows = [], []
    for tr in range(2):
        y_top, y_low = y_ref[tr, 0], y_ref[tr, levels - 1]
        near = jnp.where(upper, y_low, y_top)
        far = jnp.where(upper, y_top, y_low)
        mate, across = r1_ref[tr], r2_ref[tr] + r3_ref[tr]
        pair_flux = jnp.where(
            outer,
            mate + sign * (cross * across - inside * near),
            sign * (inside * (near - mate) + cross * (across - far)),
        )
        middle = sign * (inv_e * (across - far + share * near) - cross * mate)
        middle = jnp.where(outer, 0.0, middle)
        tops.append(jnp.where(upper, middle, pair_flux))
        lows.append(jnp.where(upper, pair_flux, middle))
    step, regs = levels // GROUPS, y_ref.shape[2] // 8
    copies = []
    for part in range(GROUPS):
        for k in range(part * step, (part + 1) * step):
            a, b = a_ref[k], bb_ref[k]
            new = [y_ref[tr, k] - tops[tr] * a + lows[tr] * b for tr in range(2)]
            for tr in range(2):
                for v in range(regs):
                    out[tr, k, pl.ds(v, 8, regs), :] = new[tr][8 * v : 8 * v + 8]
        for tr in range(2):
            span = (tr, pl.ds(part * step, step))
            copies.append(
                pltpu.make_async_copy(out.at[span], out_hbm.at[span], sems.at[tr, part])
            )
            copies[-1].start()
    for copy in copies:
        copy.wait()


def per_device(tracers, u_east, v_north, kappa_h, kappa_v, bottom):
    _, levels, lat, lon = tracers.shape
    rows_e = levels // GROUPS
    lon_n, dep_n = lax.axis_size("lon"), lax.axis_size("dep")
    east = [(i, (i + 1) % lon_n) for i in range(lon_n)]
    west = [(t, s) for s, t in east]
    slab = lat * lon * 4
    slabs = lambda *lead: f32(*lead, lat, lon)
    work = lambda *lead: pltpu.VMEM(lead + (lat, lon), jnp.float32)

    with jax.named_scope("pack"):
        sw, se, bp, ww, we, t0, t1, u, v, khb = call(
            pack_kernel,
            (slabs(rows_e),) * 2 + (slabs(),) + (slabs(rows_e - 1),) * 2 + (slabs(levels),) * 4
            + (slabs(2),),
            [
                work(levels), pltpu.VMEM((lat, lon), jnp.int32), work(rows_e),
                pltpu.SemaphoreType.DMA((GROUPS, 4)), pltpu.SemaphoreType.DMA((2,)),
            ],
            (tracers, u_east, v_north, kappa_h, bottom), 10**6, 6 * levels * slab, 50.5,
            in_specs=[HBM] * 5,
        )
    with jax.named_scope("lon_halo"):
        r_east = lax.ppermute(ww, "lon", west)
        r_west = lax.ppermute(we, "lon", east)
    with jax.named_scope("factor"):
        inv, ei, ratio, a_end, b_end, abc, msg = call(
            factor_kernel, (slabs(levels),) * 5 + (slabs(3),) * 2, [],
            (kappa_v, bottom, khb), 10**7, 6 * levels * slab, 16,
        )
    swap = [(i, i ^ 1) for i in range(dep_n)]
    with jax.named_scope("pair_coefficients"):
        pair = lax.ppermute(msg, "dep", swap)
    half = levels // 2

    def advect_half(start, earlier):
        return call(
            functools.partial(advect_kernel, start), slabs(2, half),
            [work(2, 2 * half), work(5, half)],
            (t0, t1, u, v, bottom, earlier), 10**7, 4 * levels * slab, 16,
        )

    with jax.named_scope("advect_north"):
        north_half = advect_half(0, abc)
    with jax.named_scope("advect_south"):
        south_half = advect_half(half, abc)
    with jax.named_scope("own_strips"):
        own_strips, own_bottom = call(
            own_kernel, (slabs(4, rows_e), slabs()), [],
            (sw, se, bp, abc), 10**6, 8 * rows_e * slab, 16,
        )
    rows_pay = 5 * lat + 16
    with jax.named_scope("advect_edge"):
        ea, ek, eb, bmx, first, second, red = call(
            edge_kernel,
            (
                slabs(2, rows_e), slabs(rows_e), slabs(), slabs(),
                f32(rows_pay - lat, lon), f32(rows_pay + lat, lon), slabs(3),
            ),
            [
                work(2, 2 * rows_e), work(5, rows_e), work(4, rows_e),
                pltpu.VMEM((2, rows_pay, lon), jnp.float32),
            ],
            (own_strips, own_bottom, r_east, r_west, bottom, north_half, south_half, kappa_h, abc, pair),
            10**6, 3 * levels * slab, 16,
        )
    other = []
    for i in range(lon_n * dep_n):
        row, place = divmod(i, dep_n)
        if place in (0, dep_n - 1):
            other.append((i, (row ^ 1) * dep_n + place))
        else:
            other.append((i, i + 1 if place % 2 else i - 1))
    with jax.named_scope("dep_halo"):
        first = lax.ppermute(first, "dep", swap)
        second = lax.ppermute(second, ("lon", "dep"), other)
    with jax.named_scope("patch"):
        full, gx, efx = call(
            patch_kernel, (slabs(2, levels), slabs(2, levels), slabs(2, rows_e)),
            [work(2, rows_e + 2)],
            (north_half, south_half, ea, ek, eb), 10**7, 8 * levels * slab, 16,
        )
    with jax.named_scope("fluxes"):
        q_part, fz = call(
            flux_kernel, (slabs(2, levels), slabs(2, levels)), [work(3)],
            (full, gx, efx, bmx, bottom, kappa_h), 10**7, 10 * levels * slab, 16,
        )
    with jax.named_scope("solve"):
        y, m2, m3, m1, both, own = call(
            solve_kernel, (slabs(2, levels), slabs(2), slabs(2), slabs(2), slabs(), slabs(3)),
            [
                work(2, 10), work(2, rows_e + 2), work(2, 4),
                pltpu.VMEM((2, rows_pay, lon), jnp.float32),
            ],
            (
                full, q_part, fz, ea, ek, eb, bmx, bottom, kappa_h, first, second,
                inv, ei, ratio, red, pair,
            ),
            10**7, 12 * levels * slab, 24,
        )
    with jax.named_scope("interfaces"):
        m2 = lax.ppermute(m2, "dep", [(i, i ^ 2) for i in range(dep_n)])
        m3 = lax.ppermute(m3, "dep", [(i, i ^ 3) for i in range(dep_n)])
        m1 = lax.ppermute(m1, "dep", swap)
        both = lax.ppermute(both, "dep", swap)
    with jax.named_scope("finish"):
        return call(
            finish_kernel, slabs(2, levels),
            [work(2, levels), pltpu.SemaphoreType.DMA((2, GROUPS))],
            (y, a_end, b_end, own, m2, m3, m1, both), 10**6, 6 * levels * slab, 16,
            out_specs=HBM,
        )


def solution(mesh):
    in_specs = (
        P(None, "dep", None, "lon"),
        P("dep", None, "lon"),
        P("dep", None, "lon"),
        P("dep", None, "lon"),
        P("dep", None, "lon"),
        P(None, "lon"),
    )
    out_specs = P(None, "dep", None, "lon")
    return jax.shard_map(
        per_device, mesh=mesh, in_specs=in_specs, out_specs=out_specs, check_vma=False
    )
```

```python
import functools

import jax
import jax.numpy as jnp
from jax import lax
from jax.experimental import pallas as pl
from jax.experimental.pallas import tpu as pltpu
from jax.sharding import PartitionSpec as P

SUB = 4
THERMAL = 0.2
HALINE = 0.8
GROUPS = 4
ROWS = 32
STRIP = 32
HUGE = 1e30
MIB = 1024 * 1024

VMEM = pl.BlockSpec(memory_space=pltpu.VMEM)
HBM = pl.BlockSpec(memory_space=pltpu.HBM)


def lane_ids(rows):
    return lax.broadcasted_iota(jnp.int32, (rows, 128), 1)


def roll_lanes(x, amount):
    amount = amount % 128
    return x if amount == 0 else pltpu.roll(x, amount, 1)


def shift_north(x):
    return jnp.concatenate([x[8:], pltpu.roll(x[:8], 7, 0)], axis=0)


def shift_south(x):
    return jnp.concatenate([pltpu.roll(x[-8:], 1, 0), x[:-8]], axis=0)


def rows_of(ref, v, *lead):
    return ref[(*lead, pl.ds(v, 8, ref.shape[-2] // 8), slice(None))]


def neighbours(regs, v):
    north = regs[v + 1] if v + 1 < len(regs) else pltpu.roll(regs[0], 7, 0)
    south = regs[v - 1] if v > 0 else pltpu.roll(regs[-1], 1, 0)
    return north, south


def slab_of(ref, *lead):
    return jnp.concatenate([rows_of(ref, v, *lead) for v in range(ref.shape[-2] // 8)], axis=0)


def call(body, out_shape, scratch, args, flops, in_bytes, limit, in_specs=None, out_specs=None):
    return pl.pallas_call(
        body,
        out_shape=out_shape,
        in_specs=in_specs or [VMEM] * len(args),
        out_specs=out_specs or jax.tree.map(lambda _: VMEM, out_shape),
        scratch_shapes=scratch,
        compiler_params=pltpu.CompilerParams(vmem_limit_bytes=int(limit * MIB)),
        cost_estimate=pl.CostEstimate(flops=flops, bytes_accessed=in_bytes, transcendentals=0),
    )(*args)


def f32(*shape):
    return jax.ShapeDtypeStruct(shape, jnp.float32)


def pack_kernel(
    t_hbm, u_hbm, v_hbm, kh_hbm, b_hbm,
    sw_ref, se_ref, bp_ref, ww_ref, we_ref, t0_ref, t1_ref, u_ref, v_ref, khb_ref,
    kh_buf, b_buf, first_buf, sems, more_sems,
):
    rows_e = u_ref.shape[0] // GROUPS
    lat = u_ref.shape[1]
    lane = lane_ids(lat)
    fields = ((t_hbm.at[0], t0_ref), (t_hbm.at[1], t1_ref), (u_hbm, u_ref), (v_hbm, v_ref))
    groups = [
        [
            pltpu.make_async_copy(
                src.at[pl.ds(g * rows_e, rows_e)], dst.at[pl.ds(g * rows_e, rows_e)], sems.at[g, n]
            )
            for n, (src, dst) in enumerate(fields)
        ]
        for g in range(GROUPS)
    ]
    tail = [
        pltpu.make_async_copy(b_hbm, b_buf, more_sems.at[0]),
        pltpu.make_async_copy(kh_hbm, kh_buf, more_sems.at[1]),
    ]
    for copy in sum(groups, []) + tail:
        copy.start()
    for g in range(GROUPS):
        for copy in groups[g]:
            copy.wait()
        for batch in (range(0, rows_e // 2), range(rows_e // 2, rows_e)):
            rolled = {
                (r, f): roll_lanes(slab_of(ref, g * rows_e + r), STRIP * g + 8 * f)
                for r in batch
                for f, ref in enumerate((t0_ref, t1_ref, u_ref, v_ref))
            }
            done = []
            for r in batch:
                low = rolled[r, 0]
                high = None
                if g > 0:
                    low = jnp.where(lane >= STRIP * g, low, sw_ref[r])
                    high = jnp.where(lane >= STRIP * g - 8, rolled[r, 0], se_ref[r])
                for f in range(1, 4):
                    start = STRIP * g + 8 * f
                    low = jnp.where(lane >= start, rolled[r, f], low)
                    if high is None:
                        high = rolled[r, f]
                    else:
                        high = jnp.where(lane >= start - 8, rolled[r, f], high)
                if g == GROUPS - 1:
                    high = jnp.where(lane >= 120, first_buf[r], high)
                done.append((r, low, high))
            for r, low, high in done:
                if g == 0:
                    first_buf[r] = rolled[r, 0]
                sw_ref[r] = low
                se_ref[r] = high
    for copy in tail:
        copy.wait()
    bottom = slab_of(b_buf).astype(jnp.float32)
    place = bottom
    for g in range(1, GROUPS):
        place = jnp.where(lane >= STRIP * g - 8, roll_lanes(bottom, STRIP * g), place)
    place = jnp.where(lane >= 120, bottom, place)
    bp_ref[...] = place

    def kappa(r):
        out = None
        for g in range(GROUPS):
            rolled = roll_lanes(slab_of(kh_buf, g * rows_e + r), STRIP * g + 23)
            out = rolled if g == 0 else jnp.where(lane >= STRIP * g + 8, rolled, out)
        return out

    khb_ref[0] = slab_of(kh_buf, 0)
    khb_ref[1] = slab_of(kh_buf, GROUPS * rows_e - 1)
    last = rows_e - 1
    kappa_last = kappa(last)
    lane_q = lane % STRIP
    low_last, high_last = sw_ref[last], se_ref[last]
    wires = []
    for r in range(last):
        k = kappa(r)
        low, high = sw_ref[r], se_ref[r]
        west = (low, roll_lanes(low, -2), roll_lanes(low, -4), roll_lanes(low, -6), k)
        east = (
            roll_lanes(high, -2), roll_lanes(high, -4), roll_lanes(high, -7), roll_lanes(k, -5),
        )
        west += (roll_lanes(low_last, 24 - 8 * r),)
        east += (roll_lanes(high_last, -1 if r == 3 else 24 - 8 * r),)
        if r == 3:
            west += (roll_lanes(kappa_last, 6),)
            east += (roll_lanes(kappa_last, 1), high)
        else:
            pair = roll_lanes(place, 30 - 2 * r)
            west += (pair,)
            east += (pair, high)
        starts = (6, 12, 18, 23, 24, 29 if r == 3 else 30)
        starts_e = (6, 12, 17, 18, 23 if r == 3 else 24, 26)
        for ref, parts, starts in ((ww_ref, west, starts), (we_ref, east, starts_e)):
            wire = parts[0]
            for start, part in zip(starts, parts[1:]):
                wire = jnp.where(lane_q >= start, part, wire)
            wires.append((ref, r, wire))
    for ref, r, wire in wires:
        ref[r] = wire


def advect_block(slabs, get_c, get_u, get_v, get_level, bx, by, buf, coef, put):
    regs = bx.shape[0] // 8
    for i, slab in enumerate(slabs):
        level = get_level(slab)
        um = jnp.where(level < bx, get_u(slab), 0.0)
        vm = jnp.where(level < by, get_v(slab), 0.0)
        uw = roll_lanes(um, 1)
        vs = shift_south(vm)
        coef[0, i] = (
            1.0
            - jnp.maximum(um, 0.0)
            + jnp.minimum(uw, 0.0)
            - jnp.maximum(vm, 0.0)
            + jnp.minimum(vs, 0.0)
        )
        coef[1, i] = -jnp.minimum(um, 0.0)
        coef[2, i] = jnp.maximum(uw, 0.0)
        coef[3, i] = -jnp.minimum(vm, 0.0)
        coef[4, i] = jnp.maximum(vs, 0.0)
        for tr in range(2):
            buf[0, 2 * i + tr] = get_c(tr, slab)
    for step in range(SUB):
        src, dst = step % 2, (step + 1) % 2
        for i, slab in enumerate(slabs):
            now = [
                [buf[src, 2 * i + tr, 8 * v : 8 * v + 8] for v in range(regs)] for tr in range(2)
            ]
            for v in range(regs):
                js = slice(8 * v, 8 * v + 8)
                a, b, c, d, e = (coef[n, i, js] for n in range(5))
                for tr in range(2):
                    here = now[tr][v]
                    north, south = neighbours(now[tr], v)
                    new = (
                        a * here
                        + b * roll_lanes(here, -1)
                        + c * roll_lanes(here, 1)
                        + d * north
                        + e * south
                    )
                    if step < SUB - 1:
                        buf[dst, 2 * i + tr, js] = new
                    else:
                        put(tr, slab, js, new)


def face_limits(bottom):
    lat = bottom.shape[0]
    rows = lax.broadcasted_iota(jnp.int32, bottom.shape, 0)
    north = jnp.where(rows == lat - 1, 0.0, shift_north(bottom))
    return jnp.minimum(bottom, roll_lanes(bottom, -1)), jnp.minimum(bottom, north)


def lat_limits(bottom):
    lat = bottom.shape[0]
    rows = lax.broadcasted_iota(jnp.int32, bottom.shape, 0)
    north = jnp.where(rows == lat - 1, 0.0, shift_north(bottom))
    south = jnp.where(rows == 0, 0.0, shift_south(bottom))
    return jnp.minimum(north, south)


def advect_kernel(start, t0_ref, t1_ref, u_ref, v_ref, b_ref, earlier_ref, out_ref, buf, coef):
    del earlier_ref
    count, lat = out_ref.shape[1], out_ref.shape[2]
    base = lax.axis_index("dep") * t0_ref.shape[0] + start
    bx, by = face_limits(slab_of(b_ref).astype(jnp.float32))

    def put(tr, slab, js, new):
        out_ref[tr, slab, js] = new

    advect_block(
        list(range(count)),
        lambda tr, s: slab_of((t0_ref, t1_ref)[tr], start + s),
        lambda s: slab_of(u_ref, start + s),
        lambda s: slab_of(v_ref, start + s),
        lambda s: (base + s).astype(jnp.float32),
        bx,
        by,
        buf,
        coef,
        put,
    )


def join(lane_q, own, east, west):
    halo = jnp.where(lane_q < 16, east, west)
    return jnp.where((lane_q >= 8) & (lane_q < 24), halo, own)


def west_patch(slab, g):
    return roll_lanes(slab, -(STRIP * g + 24))


def east_patch(slab, g):
    return roll_lanes(slab, 120 - STRIP * g)


def patched(main, slab, g, lane):
    return jnp.where(
        lane < 4, west_patch(slab, g), jnp.where(lane >= 124, east_patch(slab, g), main)
    )


def own_kernel(sw_ref, se_ref, bp_ref, earlier_ref, own_ref, ownb_ref):
    del earlier_ref
    rows_e, lat = sw_ref.shape[0], sw_ref.shape[1]
    lane_q = lane_ids(lat) % STRIP
    for r in range(rows_e):
        made = [
            jnp.where(
                lane_q < 16, roll_lanes(se_ref[r], 8 - 8 * f), roll_lanes(sw_ref[r], 24 - 8 * f)
            )
            for f in range(4)
        ]
        for f in range(4):
            own_ref[f, r] = made[f]
    place = bp_ref[...]
    ownb_ref[...] = jnp.where(lane_q < 16, roll_lanes(place, 8), roll_lanes(place, 24))


def pair_response(abc_ref, pair_ref, me):
    upper = lax.rem(me, 2) == 0
    low_pair = me < 2
    inv_t = 1.0 / (pair_ref[0] + jnp.where(upper, abc_ref[1], abc_ref[0]))
    c_pair = jnp.where(upper == low_pair, pair_ref[1], abc_ref[2])
    share = c_pair * inv_t
    return share, inv_t, jnp.where(upper, abc_ref[0], abc_ref[1]) - c_pair * share


def fold_strip(slab, place):
    lane = lane_ids(8)
    folded = jnp.zeros((8, 128), jnp.float32)
    for v in range(slab.shape[0] // 8):
        rolled = roll_lanes(slab[8 * v : 8 * v + 8], 16 * v - place)
        folded = jnp.where(lane >= 16 * v, rolled, folded)
    return folded


def unfold_strip(folded, place, regs):
    return jnp.concatenate([roll_lanes(folded, place - 16 * v) for v in range(regs)], axis=0)


def edge_kernel(
    own_ref, ownb_ref, re_ref, rw_ref, b_ref, north_half, south_half, kh_ref, abc_ref, pair_ref,
    ea_ref, ek_ref, eb_ref, bmx_ref, first_ref, second_ref, red_ref,
    buf, coef, fields, pay,
):
    levels, lat = kh_ref.shape[0], kh_ref.shape[1]
    rows_e = levels // GROUPS
    me = lax.axis_index("dep")
    base = me * levels
    parity = lax.rem(me, 2)
    up_ref, down_ref = pay.at[1 - parity], pay.at[parity]
    lane = lane_ids(lat)
    lane_q = lane % STRIP
    bottom = slab_of(b_ref).astype(jnp.float32)
    east = [roll_lanes(re_ref[r], 2 * r - 22) for r in range(3)]
    west = [roll_lanes(rw_ref[r], 2 * r - 6) for r in range(3)]
    eb = join(
        lane_q,
        ownb_ref[...],
        jnp.where(lane_q < 10, east[0], jnp.where(lane_q < 12, east[1], east[2])),
        jnp.where(lane_q < 20, west[0], jnp.where(lane_q < 22, west[1], west[2])),
    )
    eb_ref[...] = eb
    b_west = roll_lanes(jnp.where(lane == 127, west_patch(eb, 0), bottom), 1)
    b_east = roll_lanes(jnp.where(lane == 0, east_patch(eb, 0), bottom), -1)
    bmx_ref[...] = jnp.minimum(b_west, b_east)
    last = rows_e - 1
    for r in range(rows_e):
        at, shift_e, shift_w = (3, -21, 0) if r == last else (r, -15, 6)
        ek_ref[r] = jnp.where(
            lane_q < 16, roll_lanes(re_ref[at], shift_e), roll_lanes(rw_ref[at], shift_w)
        )
        made = []
        for f in range(4):
            at, start = (f, 24) if r == last else (r, 6 * f)
            made.append(
                join(
                    lane_q,
                    own_ref[f, r],
                    roll_lanes(re_ref[at], 8 - start),
                    roll_lanes(rw_ref[at], (f == 3) if r == last else (24, 18, 12, 7)[f]),
                )
            )
        for f in range(4):
            fields[f, r] = made[f]
    bx, by = face_limits(eb)
    level0 = (base + (lane // STRIP) * rows_e).astype(jnp.float32)

    def put(tr, slab, js, new):
        ea_ref[tr, slab, js] = new

    advect_block(
        list(range(rows_e)),
        lambda tr, s: fields[tr, s],
        lambda s: fields[2, s],
        lambda s: fields[3, s],
        lambda s: level0 + float(s),
        bx,
        by,
        buf,
        coef,
        put,
    )
    top, half = rows_e - 1, levels // 2
    for tr in range(2):
        for n, (k, slab) in enumerate(((0, ea_ref[tr, 0]), (1, ea_ref[tr, 1]))):
            at = (2 * n + tr) * lat
            up_ref[at : at + lat] = patched(north_half[tr, k], slab, 0, lane)
        for n, (k, slab) in enumerate(
            ((half - 1, ea_ref[tr, top]), (half - 2, ea_ref[tr, top - 1]))
        ):
            at = (2 * n + tr) * lat
            down_ref[at : at + lat] = patched(south_half[tr, k], slab, 3, lane)
        at = 4 * lat + 8 * tr
        up_ref[at : at + 8] = fold_strip(ea_ref[tr, 0], 8)
        down_ref[at : at + 8] = fold_strip(ea_ref[tr, top], 3 * STRIP + 8)
    up_ref[4 * lat + 16 : 5 * lat + 16] = slab_of(kh_ref, 0)
    down_ref[4 * lat + 16 : 5 * lat + 16] = slab_of(kh_ref, levels - 1)
    first_ref[...] = pay[0, 0 : 4 * lat + 16]
    second_ref[0 : 5 * lat + 16] = pay[1]
    response = pair_response(abc_ref, pair_ref, me)
    for n in range(3):
        red_ref[n] = response[n]
    second_ref[5 * lat + 16 : 6 * lat + 16] = response[2]


def slopes(gx, gy, gz):
    rx, ry, rz = (-0.5 * THERMAL * g[0] + 0.5 * HALINE * g[1] for g in (gx, gy, gz))
    scale = rz / (1.0 + rx * rx + ry * ry + rz * rz)
    return rx * scale, ry * scale


def flux_xyz(gx, gy, gz, kappa, need_xy=True):
    sx, sy = slopes(gx, gy, gz)
    kx, ky = kappa * sx, kappa * sy
    kz = kx * sx + ky * sy
    fz = [kx * gx[n] + ky * gy[n] + kz * gz[n] for n in range(2)]
    if not need_xy:
        return None, None, fz
    fx = [kappa * gx[n] + kx * gz[n] for n in range(2)]
    fy = [kappa * gy[n] + ky * gz[n] for n in range(2)]
    return fx, fy, fz


def flux_x_edge(gx, gy, gz, kappa):
    sx, _ = slopes(gx, gy, gz)
    kx = kappa * sx
    return [kappa * gx[n] + kx * gz[n] for n in range(2)]


def diff(mask, high, low):
    return jnp.where(mask, high - low, 0.0)


def edge_flux_row(r, rows, ek, eb, ebx, eby, level0):
    level = level0 + r
    mx = level < ebx
    my = level < eby
    mz = (level + 1.0 < eb) & (level >= 1.0)
    kappa = jnp.where((level < eb) & (level >= 0.0), 0.25 * ek, 0.0)
    gx, gy, gz = [], [], []
    for tr in range(2):
        here = rows[tr, r + 1]
        gx.append(diff(mx, roll_lanes(here, -1), roll_lanes(here, 1)))
        gy.append(diff(my, shift_north(here), shift_south(here)))
        gz.append(diff(mz, rows[tr, r + 2], rows[tr, r]))
    return flux_x_edge(gx, gy, gz, kappa)


def edge_limits(eb):
    return (
        jnp.minimum(roll_lanes(eb, 1), roll_lanes(eb, -1)),
        lat_limits(eb),
    )


def zonal_change(fx, west, east, lane):
    return roll_lanes(jnp.where(lane == 0, east, fx), -1) - roll_lanes(
        jnp.where(lane == 127, west, fx), 1
    )


def divergence(fx, fy, slab, g, lane):
    return zonal_change(fx, west_patch(slab, g), east_patch(slab, g), lane) + (
        shift_north(fy) - shift_south(fy)
    )


def patch_kernel(
    north_half, south_half, ea_ref, ek_ref, eb_ref,
    full_ref, gx_ref, efx_ref,
    rows,
):
    levels, lat = full_ref.shape[1], full_ref.shape[2]
    rows_e = levels // GROUPS
    base = lax.axis_index("dep") * levels
    lane = lane_ids(lat)
    eb = eb_ref[...]
    ebx, eby = edge_limits(eb)
    level0 = (base + (lane // STRIP) * rows_e).astype(jnp.float32)
    for tr in range(2):
        for r in range(rows_e):
            rows[tr, r + 1] = ea_ref[tr, r]
        rows[tr, 0] = roll_lanes(ea_ref[tr, rows_e - 1], STRIP)
        rows[tr, rows_e + 1] = roll_lanes(ea_ref[tr, 0], -STRIP)
    found = [
        edge_flux_row(r, rows, ek_ref[r], eb, ebx, eby, level0) for r in range(rows_e)
    ]
    for r in range(rows_e):
        for tr in range(2):
            efx_ref[tr, r] = found[r][tr]

    lane = lane_ids(ROWS)
    units = [(g, slice(j, j + ROWS)) for g in range(GROUPS) for j in range(0, lat, ROWS)]

    def patch(r, _):
        def fetch(unit):
            g, js = unit
            strips = [ea_ref[tr, r, js] for tr in range(2)]
            half = (north_half, south_half)[2 * g // GROUPS]
            mains = [half[tr, g % (GROUPS // 2) * rows_e + r, js] for tr in range(2)]
            return [(west_patch(x, g), east_patch(x, g), y) for x, y in zip(strips, mains)]

        def put(unit, mains, rolled):
            g, js = unit
            for tr in range(2):
                full_ref[tr, g * rows_e + r, js] = mains[tr]
                gx_ref[tr, g * rows_e + r, js] = rolled[tr][0] - rolled[tr][1]

        waiting = None
        fetched = fetch(units[0])
        for n, unit in enumerate(units):
            now = fetched
            fetched = fetch(units[n + 1]) if n + 1 < len(units) else None
            mains, rolled = [], []
            for west, east, main in now:
                main = jnp.where(lane < 4, west, jnp.where(lane >= 124, east, main))
                mains.append(main)
                rolled.append(
                    (
                        roll_lanes(jnp.where(lane == 0, east, main), -1),
                        roll_lanes(jnp.where(lane == 127, west, main), 1),
                    )
                )
            if waiting is not None:
                put(*waiting)
            waiting = (unit, mains, rolled)
        put(*waiting)
        return 0

    lax.fori_loop(0, rows_e, patch, 0)


def flux_kernel(
    full_ref, gx_ref, efx_ref, bmx_ref, b_ref, kh_ref,
    q_ref, fz_ref,
    limits,
):
    levels, lat = full_ref.shape[1], full_ref.shape[2]
    rows_e = levels // GROUPS
    base = lax.axis_index("dep") * levels
    lane = lane_ids(lat)
    bottom = slab_of(b_ref).astype(jnp.float32)
    limits[0] = bmx_ref[...]
    limits[1] = lat_limits(bottom)
    limits[2] = bottom

    def north_rows(tr, k, j):
        if j + 8 + ROWS <= lat:
            return full_ref[tr, k, j + 8 : j + 8 + ROWS]
        return jnp.concatenate(
            [full_ref[tr, k, j + 8 : lat], pltpu.roll(full_ref[tr, k, 0:8], 7, 0)], axis=0
        )

    def south_rows(tr, k, j):
        if j >= 8:
            return full_ref[tr, k, j - 8 : j - 8 + ROWS]
        return jnp.concatenate(
            [pltpu.roll(full_ref[tr, k, lat - 8 : lat], 1, 0), full_ref[tr, k, 0 : ROWS - 8]],
            axis=0,
        )

    def fluxes(r, _):
        for g in range(GROUPS):
            k = g * rows_e + r
            above, below = jnp.maximum(k - 1, 0), jnp.minimum(k + 1, levels - 1)
            level = (base + k).astype(jnp.float32)
            level_z = jnp.where(level >= 1.0, level + 1.0, HUGE)
            sides = [
                (west_patch(efx_ref[tr, r], g), east_patch(efx_ref[tr, r], g)) for tr in range(2)
            ]
            fxs, fys, fzs = [[], []], [[], []], [[], []]
            for j in range(0, lat, ROWS):
                js = slice(j, j + ROWS)
                mx = level < limits[0, js]
                my = level < limits[1, js]
                mz = level_z < limits[2, js]
                kh = jnp.concatenate(
                    [rows_of(kh_ref, v, k) for v in range(j // 8, (j + ROWS) // 8)], axis=0
                )
                kappa = jnp.where(level < limits[2, js], 0.25 * kh, 0.0)
                gx, gy, gz = [], [], []
                for tr in range(2):
                    gx.append(jnp.where(mx, gx_ref[tr, k, js], 0.0))
                    gy.append(diff(my, north_rows(tr, k, j), south_rows(tr, k, j)))
                    gz.append(diff(mz, full_ref[tr, below, js], full_ref[tr, above, js]))
                fx, fy, fz = flux_xyz(gx, gy, gz, kappa)
                for tr in range(2):
                    fxs[tr].append(fx[tr])
                    fys[tr].append(fy[tr])
                    fzs[tr].append(fz[tr])
            wet = level < limits[2]
            new = []
            for tr in range(2):
                fy = jnp.concatenate(fys[tr], axis=0)
                change = zonal_change(jnp.concatenate(fxs[tr], axis=0), *sides[tr], lane)
                change = change + (shift_north(fy) - shift_south(fy))
                new.append(full_ref[tr, k] + jnp.where(wet, change, 0.0))
            for tr in range(2):
                q_ref[tr, k] = new[tr]
                fz_ref[tr, k] = jnp.concatenate(fzs[tr], axis=0)
        return 0

    lax.fori_loop(0, rows_e, fluxes, 0)


def factor_kernel(
    kv_ref, b_ref, khb_ref, inv_ref, ei_ref, ratio_ref, a_ref, bb_ref, abc_ref, msg_ref
):
    levels, lat = kv_ref.shape[0], kv_ref.shape[1]
    base = lax.axis_index("dep") * levels
    bottom = slab_of(b_ref).astype(jnp.float32)

    def coupling(k):
        level = (base + k).astype(jnp.float32)
        level = jnp.where(level >= 1.0, level, HUGE)
        return jnp.where(level < bottom, slab_of(kv_ref, k), 0.0)

    top = coupling(0)
    e = jnp.zeros((lat, 128), jnp.float32)
    q = e
    za = jnp.ones((lat, 128), jnp.float32)
    for k in range(levels):
        low = coupling(k + 1) if k + 1 < levels else jnp.zeros((lat, 128), jnp.float32)
        eq = 1.0 + e * q
        inv = 1.0 / (eq + low)
        inv_ref[k] = inv
        ei = e * inv
        ei_ref[k] = ei
        ratio_ref[k] = low * inv
        za = inv if k == 0 else za * ei
        a_ref[k] = za
        q = eq * inv
        e = low
    bb_ref[levels - 1] = inv
    b = inv
    a = za
    for k in range(levels - 2, -1, -1):
        ratio = ratio_ref[k]
        b = ratio * b
        a = a_ref[k] + ratio * a
        bb_ref[k] = b
        a_ref[k] = a
    a = a + jnp.where(top > 0.0, 1.0 / jnp.maximum(top, 1e-30), HUGE)
    abc_ref[0] = a
    abc_ref[1] = inv
    abc_ref[2] = b
    upper = lax.rem(lax.axis_index("dep"), 2) == 0
    msg_ref[0] = jnp.where(upper, inv, a)
    msg_ref[1] = b
    msg_ref[2] = jnp.where(upper, khb_ref[1], khb_ref[0])


def solve_kernel(
    full_ref, q_ref, fz_ref, ea_ref, ek_ref, eb_ref, bmx_ref, b_ref, kh_ref,
    first_ref, second_ref, inv_ref, ei_ref, ratio_ref, red_ref, pair_ref,
    y_ref, m2_ref, m3_ref, m1_ref, both_ref, own_ref,
    pad, epad, fze, halo,
):
    levels, lat = q_ref.shape[1], q_ref.shape[2]
    rows_e = levels // GROUPS
    last = levels - 1
    top = rows_e - 1
    me = lax.axis_index("dep")
    base = me * levels
    parity = lax.rem(me, 2)
    outer = (me == 0) | (me == 3)
    upper = parity == 0
    sign = jnp.where(me < 2, 1.0, -1.0)
    lane = lane_ids(lat)
    halo[0, 0 : 4 * lat + 16] = first_ref[...]
    halo[0, 4 * lat + 16 : 5 * lat + 16] = pair_ref[2]
    halo[1] = second_ref[0 : 5 * lat + 16]
    above_ref, below_ref = halo.at[1 - parity], halo.at[parity]

    share = red_ref[0]
    both = red_ref[2] + second_ref[5 * lat + 16 : 6 * lat + 16]
    cross = share / both
    inside = red_ref[1] + share * cross
    for n, value in enumerate((share, red_ref[1], both)):
        own_ref[n] = value
    both_ref[...] = both

    eb = eb_ref[...]
    ebx, eby = edge_limits(eb)
    level0 = (base + (lane // STRIP) * rows_e).astype(jnp.float32)
    for tr in range(2):
        pad[tr, 0] = above_ref[(2 + tr) * lat : (3 + tr) * lat]
        pad[tr, 1] = above_ref[tr * lat : (1 + tr) * lat]
        for n, k in enumerate((0, 1, 2, last - 2, last - 1, last)):
            pad[tr, n + 2] = full_ref[tr, k]
        pad[tr, 8] = below_ref[tr * lat : (1 + tr) * lat]
        pad[tr, 9] = below_ref[(2 + tr) * lat : (3 + tr) * lat]
        for r in range(rows_e):
            epad[tr, r + 1] = ea_ref[tr, r]
        at = 4 * lat + 8 * tr
        corner_up = unfold_strip(above_ref[at : at + 8], 3 * STRIP + 8, lat // 8)
        corner_dn = unfold_strip(below_ref[at : at + 8], 8, lat // 8)
        epad[tr, 0] = roll_lanes(
            jnp.where(lane >= 3 * STRIP, corner_up, ea_ref[tr, top]), STRIP
        )
        epad[tr, rows_e + 1] = roll_lanes(
            jnp.where(lane < STRIP, corner_dn, ea_ref[tr, 0]), -STRIP
        )
    efx = {
        r + 1: edge_flux_row(r, epad, ek_ref[r], eb, ebx, eby, level0) for r in (0, top)
    }

    bottom = slab_of(b_ref).astype(jnp.float32)
    bmy = lat_limits(bottom)
    bmx = bmx_ref[...]
    ends = (
        (1, -1, 0, 0, above_ref[4 * lat + 16 : 5 * lat + 16], True),
        (2, 0, 1, 0, slab_of(kh_ref, 0), False),
        (7, last, top + 1, 3, slab_of(kh_ref, last), False),
        (8, last + 1, top + 2, 3, below_ref[4 * lat + 16 : 5 * lat + 16], True),
    )
    spread = {}
    for m, (n, k, er, g, kappa_slab, only_z) in enumerate(ends):
        level = (base + k).astype(jnp.float32)
        level_z = jnp.where(level >= 1.0, level + 1.0, HUGE)
        level_h = jnp.where(level >= 0.0, level, HUGE)
        mx = level_h < bmx
        my = level_h < bmy
        mz = level_z < bottom
        kappa = jnp.where(level_h < bottom, 0.25 * kappa_slab, 0.0)
        gx, gy, gz = [], [], []
        for tr in range(2):
            slab, main = epad[tr, er], pad[tr, n]
            change = zonal_change(main, west_patch(slab, g), east_patch(slab, g), lane)
            gx.append(jnp.where(mx, change, 0.0))
            gy.append(diff(my, shift_north(main), shift_south(main)))
            gz.append(diff(mz, pad[tr, n + 1], pad[tr, n - 1]))
        fx, fy, fz = flux_xyz(gx, gy, gz, kappa, not only_z)
        for tr in range(2):
            fze[tr, m] = fz[tr]
            if not only_z:
                spread[k, tr] = divergence(fx[tr], fy[tr], efx[er][tr], g, lane)

    def vertical_flux(tr, k):
        place = {-1: 0, 0: 1, last: 2, last + 1: 3}.get(k)
        return fz_ref[tr, k] if place is None else fze[tr, place]

    z = [None, None]
    for k in range(levels):
        level = (base + k).astype(jnp.float32)
        wet = level < bottom
        for tr in range(2):
            change = vertical_flux(tr, k + 1) - vertical_flux(tr, k - 1)
            if k == 0 or k == last:
                change = change + spread[k, tr]
                start = pad[tr, 2 if k == 0 else 7]
            else:
                start = q_ref[tr, k]
            rhs = start + jnp.where(wet, change, 0.0)
            new = rhs * inv_ref[k]
            z[tr] = new if k == 0 else new + ei_ref[k] * z[tr]
        for tr in range(2):
            y_ref[tr, k] = z[tr]
    low = list(z)
    for k in range(last - 1, -1, -1):
        ratio = ratio_ref[k]
        z = [y_ref[tr, k] + ratio * z[tr] for tr in range(2)]
        for tr in range(2):
            y_ref[tr, k] = z[tr]
    for tr in range(2):
        near = jnp.where(upper, low[tr], z[tr])
        far = jnp.where(upper, z[tr], low[tr])
        m1_ref[tr] = jnp.where(outer, near, sign * (inside * near - cross * far))
        value = jnp.where(outer, share * near, far - share * near)
        m2_ref[tr] = value
        m3_ref[tr] = value


def finish_kernel(
    y_ref, a_ref, bb_ref, own_ref, r2_ref, r3_ref, r1_ref, both_ref, out_hbm, out, sems
):
    levels = y_ref.shape[1]
    me = lax.axis_index("dep")
    upper = lax.rem(me, 2) == 0
    outer = (me == 0) | (me == 3)
    sign = jnp.where(me < 2, 1.0, -1.0)
    share, inv_t = own_ref[0], own_ref[1]
    inv_e = 1.0 / jnp.where(outer, both_ref[...], own_ref[2])
    cross = share * inv_e
    inside = inv_t + share * cross
    tops, lows = [], []
    for tr in range(2):
        y_top, y_low = y_ref[tr, 0], y_ref[tr, levels - 1]
        near = jnp.where(upper, y_low, y_top)
        far = jnp.where(upper, y_top, y_low)
        mate, across = r1_ref[tr], r2_ref[tr] + r3_ref[tr]
        pair_flux = jnp.where(
            outer,
            mate + sign * (cross * across - inside * near),
            sign * (inside * (near - mate) + cross * (across - far)),
        )
        middle = sign * (inv_e * (across - far + share * near) - cross * mate)
        middle = jnp.where(outer, 0.0, middle)
        tops.append(jnp.where(upper, middle, pair_flux))
        lows.append(jnp.where(upper, pair_flux, middle))
    step, regs = levels // GROUPS, y_ref.shape[2] // 8
    copies = []
    for part in range(GROUPS):
        for k in range(part * step, (part + 1) * step):
            a, b = a_ref[k], bb_ref[k]
            new = [y_ref[tr, k] - tops[tr] * a + lows[tr] * b for tr in range(2)]
            for tr in range(2):
                for v in range(regs):
                    out[tr, k, pl.ds(v, 8, regs), :] = new[tr][8 * v : 8 * v + 8]
        span = (slice(None), pl.ds(part * step, step))
        copies.append(pltpu.make_async_copy(out.at[span], out_hbm.at[span], sems.at[part]))
        copies[-1].start()
    for copy in copies:
        copy.wait()


def per_device(tracers, u_east, v_north, kappa_h, kappa_v, bottom):
    _, levels, lat, lon = tracers.shape
    rows_e = levels // GROUPS
    lon_n, dep_n = lax.axis_size("lon"), lax.axis_size("dep")
    east = [(i, (i + 1) % lon_n) for i in range(lon_n)]
    west = [(t, s) for s, t in east]
    slab = lat * lon * 4
    slabs = lambda *lead: f32(*lead, lat, lon)
    work = lambda *lead: pltpu.VMEM(lead + (lat, lon), jnp.float32)

    with jax.named_scope("pack"):
        sw, se, bp, ww, we, t0, t1, u, v, khb = call(
            pack_kernel,
            (slabs(rows_e),) * 2 + (slabs(),) + (slabs(rows_e - 1),) * 2 + (slabs(levels),) * 4
            + (slabs(2),),
            [
                work(levels), pltpu.VMEM((lat, lon), jnp.int32), work(rows_e),
                pltpu.SemaphoreType.DMA((GROUPS, 4)), pltpu.SemaphoreType.DMA((2,)),
            ],
            (tracers, u_east, v_north, kappa_h, bottom), 10**6, 6 * levels * slab, 50.5,
            in_specs=[HBM] * 5,
        )
    with jax.named_scope("lon_halo"):
        r_east = lax.ppermute(ww, "lon", west)
        r_west = lax.ppermute(we, "lon", east)
    with jax.named_scope("factor"):
        inv, ei, ratio, a_end, b_end, abc, msg = call(
            factor_kernel, (slabs(levels),) * 5 + (slabs(3),) * 2, [],
            (kappa_v, bottom, khb), 10**7, 6 * levels * slab, 16,
        )
    swap = [(i, i ^ 1) for i in range(dep_n)]
    with jax.named_scope("pair_coefficients"):
        pair = lax.ppermute(msg, "dep", swap)
    half = levels // 2

    def advect_half(start, earlier):
        return call(
            functools.partial(advect_kernel, start), slabs(2, half),
            [work(2, 2 * half), work(5, half)],
            (t0, t1, u, v, bottom, earlier), 10**7, 4 * levels * slab, 16,
        )

    with jax.named_scope("advect_north"):
        north_half = advect_half(0, abc)
    with jax.named_scope("advect_south"):
        south_half = advect_half(half, abc)
    with jax.named_scope("own_strips"):
        own_strips, own_bottom = call(
            own_kernel, (slabs(4, rows_e), slabs()), [],
            (sw, se, bp, abc), 10**6, 8 * rows_e * slab, 16,
        )
    rows_pay = 5 * lat + 16
    with jax.named_scope("advect_edge"):
        ea, ek, eb, bmx, first, second, red = call(
            edge_kernel,
            (
                slabs(2, rows_e), slabs(rows_e), slabs(), slabs(),
                f32(rows_pay - lat, lon), f32(rows_pay + lat, lon), slabs(3),
            ),
            [
                work(2, 2 * rows_e), work(5, rows_e), work(4, rows_e),
                pltpu.VMEM((2, rows_pay, lon), jnp.float32),
            ],
            (own_strips, own_bottom, r_east, r_west, bottom, north_half, south_half, kappa_h, abc, pair),
            10**6, 3 * levels * slab, 16,
        )
    other = []
    for i in range(lon_n * dep_n):
        row, place = divmod(i, dep_n)
        if place in (0, dep_n - 1):
            other.append((i, (row ^ 1) * dep_n + place))
        else:
            other.append((i, i + 1 if place % 2 else i - 1))
    with jax.named_scope("dep_halo"):
        first = lax.ppermute(first, "dep", swap)
        second = lax.ppermute(second, ("lon", "dep"), other)
    with jax.named_scope("patch"):
        full, gx, efx = call(
            patch_kernel, (slabs(2, levels), slabs(2, levels), slabs(2, rows_e)),
            [work(2, rows_e + 2)],
            (north_half, south_half, ea, ek, eb), 10**7, 8 * levels * slab, 16,
        )
    with jax.named_scope("fluxes"):
        q_part, fz = call(
            flux_kernel, (slabs(2, levels), slabs(2, levels)), [work(3)],
            (full, gx, efx, bmx, bottom, kappa_h), 10**7, 10 * levels * slab, 16,
        )
    with jax.named_scope("solve"):
        y, m2, m3, m1, both, own = call(
            solve_kernel, (slabs(2, levels), slabs(2), slabs(2), slabs(2), slabs(), slabs(3)),
            [
                work(2, 10), work(2, rows_e + 2), work(2, 4),
                pltpu.VMEM((2, rows_pay, lon), jnp.float32),
            ],
            (
                full, q_part, fz, ea, ek, eb, bmx, bottom, kappa_h, first, second,
                inv, ei, ratio, red, pair,
            ),
            10**7, 12 * levels * slab, 24,
        )
    with jax.named_scope("interfaces"):
        m2 = lax.ppermute(m2, "dep", [(i, i ^ 2) for i in range(dep_n)])
        m3 = lax.ppermute(m3, "dep", [(i, i ^ 3) for i in range(dep_n)])
        m1 = lax.ppermute(m1, "dep", swap)
        both = lax.ppermute(both, "dep", swap)
    with jax.named_scope("finish"):
        return call(
            finish_kernel, slabs(2, levels),
            [work(2, levels), pltpu.SemaphoreType.DMA((GROUPS,))],
            (y, a_end, b_end, own, m2, m3, m1, both), 10**6, 6 * levels * slab, 16,
            out_specs=HBM,
        )


def solution(mesh):
    in_specs = (
        P(None, "dep", None, "lon"),
        P("dep", None, "lon"),
        P("dep", None, "lon"),
        P("dep", None, "lon"),
        P("dep", None, "lon"),
        P(None, "lon"),
    )
    out_specs = P(None, "dep", None, "lon")
    return jax.shard_map(
        per_device, mesh=mesh, in_specs=in_specs, out_specs=out_specs, check_vma=False
    )
```
